32 devices in a mesh: dp: 8 (over z, x), tensor: 4 (over y, core).
Axes of the slice: x: 2, y: 2, z: 4, core: 2. Of those that a mesh axis runs over, the one named last changes fastest.
Arguments:
- layer_in: bfloat16 [2, 4096, 1536], P(None, 'dp'), may hold values from -6 to 6
- short_lengths: int32 [8, 4], P('dp'), may hold values from 1 to 160, 512 in all within a row
- long_lengths: int32 [8, 3], P('dp'), may hold values from 1 to 256, 512 in all within a row
- norm1_gain: float32 [1536], replicated, may hold values from 0.5 to 1.5
- query_weight: bfloat16 [1536, 1536], P(None, 'tensor'), may hold values from -0.15625 to 0.15625
- key_weight: bfloat16 [1536, 1536], P(None, 'tensor'), may hold values from -0.15625 to 0.15625
- value_weight: bfloat16 [1536, 1536], P(None, 'tensor'), may hold values from -0.15625 to 0.15625
- lambda_param: float32 [12, 256], P('tensor'), may hold values from -0.12 to 0.12
- sub_gain: float32 [12, 128], P('tensor'), may hold values from 0.5 to 1.5
- out_weight: bfloat16 [1536, 1536], P('tensor'), may hold values from -0.625 to 0.625
- norm2_gain: float32 [1536], replicated, may hold values from 0.5 to 1.5
- gate_weight: bfloat16 [1536, 4096], P(None, 'tensor'), may hold values from -0.15625 to 0.15625
- up_weight: bfloat16 [1536, 4096], P(None, 'tensor'), may hold values from -0.15625 to 0.15625
- down_weight: bfloat16 [4096, 1536], P('tensor'), may hold values from -0.125 to 0.125
- out_cotangent: bfloat16 [2, 4096, 1536], P(None, 'dp'), may hold values from -6 to 6
Outputs:
- layer_out: bfloat16 [2, 4096, 1536], P(None, 'dp')
- grad_in: bfloat16 [2, 4096, 1536], P(None, 'dp')
- grad_norm1: float32 [1536], P('dp')
- grad_query: float32 [1536, 1536], P('dp', 'tensor')
- grad_key: float32 [1536, 1536], P('dp', 'tensor')
- grad_value: float32 [1536, 1536], P('dp', 'tensor')
- grad_lambda: float32 [12, 256], P('tensor', 'dp')
- grad_sub_gain: float32 [12, 128], P('tensor', 'dp')
- grad_out: float32 [1536, 1536], P('tensor', 'dp')
- grad_norm2: float32 [1536], P('dp')
- grad_gate: float32 [1536, 4096], P('dp', 'tensor')
- grad_up: float32 [1536, 4096], P('dp', 'tensor')
- grad_down: float32 [4096, 1536], P('tensor', 'dp')
The draws below stay inside these ranges and needn't reach their ends.
Inputs may be any that keep to these rules, and one draw needn't show every extreme that they name: `short_lengths`: each row gives, in order, the lengths of the documents packed into one block of 512 rows of micro-batch 0; a row sums to 512. `long_lengths`: each row gives, in order, the lengths of the documents packed into one block of 512 rows of micro-batch 1; a row sums to 512.
All inputs are finite; a program needn't handle non-finite values.
Results may differ from the reference program's by a relative error of at most 0.015.
The reference program's roundings to bfloat16 on the way count: a program that leaves them out, or rounds other values in their place, can miss the bound.
Values sent between devices are 32-bit elements; how exact they have to be, the bound alone decides.
A program may use at most 256 MiB of HBM per device.

```python
import math
import jax
import jax.numpy as jnp
import numpy as np
from jax import lax

D = 1536
H = 12
QK = 64
VD = 128
FF = 4096
TOK_MB = 512
SHORT_DOCS = 4
LONG_DOCS = 3
TOKENS = 4096
N_DP = 8


def steps_of(stream_key, shape, pieces, least, top_value):
    def one(axis_at, parts):
        draws = jax.random.uniform(jax.random.fold_in(jax.random.fold_in(stream_key, 6), axis_at), (parts,), jnp.float32, least / len(pieces), top_value / len(pieces))
        return jnp.repeat(jnp.exp(draws), shape[axis_at] // parts).reshape((-1,) + (1,) * (len(shape) - axis_at - 1))

    factor_of = one(*pieces[0])
    for cut in pieces[1:]:
        factor_of = factor_of * one(*cut)
    return factor_of


def profile(count, total, limit, lean):
    loads = [(1 << 20) // math.isqrt(standing ** lean) + 1 for standing in range(2, count + 1)]
    rest, holding = total - limit - (count - 1), [1] * (count - 1)
    while rest > 0:
        candidates = [i for i in range(count - 1) if holding[i] < limit]
        whole, remaining = sum([loads[i] for i in candidates]), rest
        for i in candidates:
            extra = min(limit - holding[i], max(1, remaining * loads[i] // whole), rest)
            holding[i] = holding[i] + extra
            rest = rest - extra
    return np.array([limit] + holding)


def ragged_sizes(key, number_of, total, bound, skew):
    if number_of == 2:
        one = jax.random.randint(key, (), max(1, total - bound), min(bound, total - 1) + 1)
        return jnp.stack([one, total - one])
    tallies = jnp.asarray(profile(number_of, total, bound, skew), jnp.int32)
    twos = (number_of - 1) // 2
    source_of, taker = tallies[1:1 + 2 * twos:2], tallies[2:2 + 2 * twos:2]
    room = jnp.minimum(source_of - 1, bound - taker)
    moved = jax.random.randint(jax.random.fold_in(key, 1), (twos,), 0, 1 << 20) % (room + 1)
    tallies = tallies.at[1:1 + 2 * twos:2].set(source_of - moved).at[2:2 + 2 * twos:2].set(taker + moved)
    return tallies[jax.random.permutation(jax.random.fold_in(key, 2), number_of)]


def bell_draw(own_key, dims, width, limit, cuts=(), kind=jnp.bfloat16):
    drawn = jax.random.normal(own_key, dims, jnp.float32) * width
    if len(cuts) > 0:
        drawn = steps_of(own_key, dims, cuts, -0.22, 0.18) * drawn
    return jnp.clip(drawn, min=-limit, max=limit).astype(kind)


def setup_inputs(seed: int = 0) -> dict:
    keys = jax.random.split(jax.random.key(seed), 16)
    layer_in = bell_draw(keys[0], (2, TOKENS, D), 1.0, 6.0, ((1, 8),))
    short_lengths = jax.vmap(lambda own: ragged_sizes(own, SHORT_DOCS, TOK_MB, TOK_MB // 4 + TOK_MB // 16, 1))(jax.random.split(keys[1], N_DP)).reshape((N_DP, SHORT_DOCS)).astype(jnp.int32)
    long_lengths = jax.vmap(lambda own: ragged_sizes(own, LONG_DOCS, TOK_MB, TOK_MB // 2, 0))(jax.random.split(keys[2], N_DP)).reshape((N_DP, LONG_DOCS)).astype(jnp.int32)
    norm1_gain = jnp.clip(1.0 + 0.1 * jax.random.normal(keys[3], (D,), jnp.float32), 0.5, 1.5)
    query_weight = bell_draw(keys[4], (D, H * 2 * QK), D ** -0.5, 0.15625, ((1, 4),))
    key_weight = bell_draw(keys[5], (D, H * 2 * QK), D ** -0.5, 0.15625, ((1, 4),))
    value_weight = bell_draw(keys[6], (D, H * VD), D ** -0.5, 0.15625, ((1, 4),))
    lambda_param = jnp.clip(jax.random.uniform(keys[7], (H, 4 * QK), jnp.float32, -0.12, 0.12) * steps_of(keys[7], (H, 4 * QK), ((0, 4),), -0.4, 0.0), -0.12, 0.12)
    sub_gain = jnp.clip(1.0 + 0.1 * jax.random.normal(keys[8], (H, VD), jnp.float32), 0.5, 1.5)
    out_weight = bell_draw(keys[9], (H * VD, D), (D // 16) ** -0.5, 0.625, ((0, 4),))
    norm2_gain = jnp.clip(1.0 + 0.1 * jax.random.normal(keys[10], (D,), jnp.float32), 0.5, 1.5)
    gate_weight = bell_draw(keys[11], (D, FF), D ** -0.5, 0.15625, ((1, 4),))
    up_weight = bell_draw(keys[12], (D, FF), D ** -0.5, 0.15625, ((1, 4),))
    down_weight = bell_draw(keys[13], (FF, D), (FF // 2) ** -0.5, 0.125, ((0, 4),))
    out_cotangent = bell_draw(keys[14], (2, TOKENS, D), 1.0, 6.0, ((1, 8),))
    return dict(layer_in=layer_in, short_lengths=short_lengths, long_lengths=long_lengths, norm1_gain=norm1_gain, query_weight=query_weight, key_weight=key_weight, value_weight=value_weight, lambda_param=lambda_param, sub_gain=sub_gain, out_weight=out_weight, norm2_gain=norm2_gain, gate_weight=gate_weight, up_weight=up_weight, down_weight=down_weight, out_cotangent=out_cotangent)


@jax.custom_vjp
def low(v):
    return lax.optimization_barrier(v.astype(jnp.bfloat16)).astype(jnp.float32)

@jax.custom_vjp
def low_back(v):
    return v

def low_keep(v):
    return (low(v), None)

def low_pass(kept, grad):
    return (grad,)

def back_keep(v):
    return (v, None)

def back_low(kept, grad):
    return (low(grad),)
low.defvjp(low_keep, low_pass)
low_back.defvjp(back_keep, back_low)
norm_epsilon = 1e-05
lambda_base = 0.8 - 0.6 * math.exp(-0.3 * 11.0)
rotary_base = 10000.0
floor_score = -60.0

def rms_scale(values):
    return values * lax.rsqrt(lax.optimization_barrier(jnp.mean(values * values, axis=-1, keepdims=True)) + norm_epsilon)

def doc_tables(lengths, row_count):
    lengths = lengths.astype(jnp.int32)
    doc_ends = jnp.cumsum(lengths, dtype=jnp.int32)
    places = jnp.arange(row_count, dtype=jnp.int32)
    passed = (places[:, None] >= doc_ends[None, :]).astype(jnp.int32)
    segment = lax.optimization_barrier(jnp.sum(passed, axis=1, dtype=jnp.int32))
    starts = lax.optimization_barrier(jnp.sum(passed * lengths[None, :], axis=1, dtype=jnp.int32))
    allowed = (segment[:, None] == segment[None, :]) & (places[None, :] <= places[:, None])
    return ((places - starts).astype(jnp.int32), allowed)

def rotary_tables(position, map_width):
    half_width = map_width // 2
    frequency = rotary_base ** (-2.0 * jnp.arange(half_width, dtype=jnp.float32) / map_width)
    angles = position.astype(jnp.float32)[:, None] * frequency[None, :]
    return (jnp.cos(angles), jnp.sin(angles))

def rotate(values, cosine_table, sine_table):
    half_width = values.shape[-1] // 2
    first_half = values[..., :half_width]
    second_half = values[..., half_width:]
    cos_wide = cosine_table[:, None, None, :]
    sin_wide = sine_table[:, None, None, :]
    return jnp.concatenate([first_half * cos_wide - second_half * sin_wide, second_half * cos_wide + first_half * sin_wide], axis=-1)

def masked_softmax(scores, allowed):
    row_max = lax.optimization_barrier(jnp.max(jnp.where(allowed, scores, floor_score), axis=-1, keepdims=True))
    shifted = jnp.where(allowed, scores - row_max, 0.0)
    expanded = jnp.where(allowed, jnp.exp(shifted), 0.0)
    return expanded / lax.optimization_barrier(jnp.sum(expanded, axis=-1, keepdims=True))

def block_forward(row_values, weight_set, allowed, cosine_table, sine_table):
    norm1_gain, query_weight, key_weight, value_weight, lambda_param, sub_gain, out_weight, norm2_gain, gate_weight, up_weight, down_weight = weight_set
    highest = lax.Precision.HIGHEST
    row_count = row_values.shape[0]
    head_count = lambda_param.shape[0]
    map_width = lambda_param.shape[1] // 4
    value_width = sub_gain.shape[1]
    score_scale = map_width ** (-0.5)
    normed_one = low(rms_scale(row_values) * norm1_gain)
    query_raw = jnp.dot(normed_one, query_weight, precision=highest).reshape(row_count, head_count, 2, map_width)
    query_rows = low(rotate(low_back(query_raw), cosine_table, sine_table))
    key_raw = jnp.dot(normed_one, key_weight, precision=highest).reshape(row_count, head_count, 2, map_width)
    key_rows = low(rotate(low_back(key_raw), cosine_table, sine_table))
    value_rows = low(low_back(jnp.dot(normed_one, value_weight, precision=highest))).reshape(row_count, head_count, value_width)
    lambda_parts = lambda_param.reshape(head_count, 4, map_width)
    lambda_head = jnp.exp(lax.optimization_barrier(jnp.sum(lambda_parts[:, 0] * lambda_parts[:, 1], axis=-1))) - jnp.exp(lax.optimization_barrier(jnp.sum(lambda_parts[:, 2] * lambda_parts[:, 3], axis=-1))) + lambda_base
    scores = jnp.einsum('thmd,shmd->hmts', query_rows, key_rows, precision=highest) * score_scale
    scores = low_back(scores)
    softmax_maps = masked_softmax(scores, allowed[None, None])
    combined = low(softmax_maps[:, 0] - lambda_head[:, None, None] * softmax_maps[:, 1])
    mixed = jnp.einsum('hts,shd->thd', combined, value_rows, precision=highest)
    mixed = low_back(mixed)
    heads_out = low(rms_scale(mixed) * sub_gain[None] * (1.0 - lambda_base)).reshape(row_count, head_count * value_width)
    attended = low_back(jnp.dot(heads_out, out_weight, precision=highest))
    middle = row_values + attended
    normed_two = low(rms_scale(middle) * norm2_gain)
    gate_pre = low_back(jnp.dot(normed_two, gate_weight, precision=highest))
    upward = low_back(jnp.dot(normed_two, up_weight, precision=highest))
    hidden = low(jax.nn.silu(gate_pre) * upward)
    return middle + low_back(jnp.dot(hidden, down_weight, precision=highest))

def reference(layer_in, short_lengths, long_lengths, norm1_gain, query_weight, key_weight, value_weight, lambda_param, sub_gain, out_weight, norm2_gain, gate_weight, up_weight, down_weight, out_cotangent):
    weight_set = tuple((member.astype(jnp.float32) for member in (norm1_gain, query_weight, key_weight, value_weight, lambda_param, sub_gain, out_weight, norm2_gain, gate_weight, up_weight, down_weight)))

    def row_step(running_sum, member):
        row_in, row_cot, lengths = member
        position, allowed = doc_tables(lengths, TOK_MB)
        cosine_table, sine_table = rotary_tables(position, QK)

        def forward(row_values, weights_now):
            return block_forward(row_values, weights_now, allowed, cosine_table, sine_table)
        result, pullback = jax.vjp(forward, row_in.astype(jnp.float32), weight_set)
        grad_row, grad_weights = pullback(row_cot.astype(jnp.float32))
        running_sum = tuple((running + addend.astype(running.dtype) for running, addend in zip(running_sum, grad_weights)))
        return (running_sum, (result.astype(jnp.bfloat16), grad_row.astype(jnp.bfloat16)))
    totals = tuple((jnp.zeros(member.shape, jnp.float32) for member in weight_set))
    out_blocks = []
    grad_blocks = []
    for batch_index, lengths_all in ((0, short_lengths), (1, long_lengths)):
        rows_in = layer_in[batch_index].reshape(N_DP, TOK_MB, D)
        cotangents = out_cotangent[batch_index].reshape(N_DP, TOK_MB, D)
        totals, (result_rows, grad_rows) = lax.scan(row_step, totals, (rows_in, cotangents, lengths_all.astype(jnp.int32)))
        out_blocks.append(result_rows.reshape(TOKENS, D))
        grad_blocks.append(grad_rows.reshape(TOKENS, D))
    return (jnp.stack(out_blocks), jnp.stack(grad_blocks), totals[0], totals[1], totals[2], totals[3], totals[4], totals[5], totals[6], totals[7], totals[8], totals[9], totals[10])
```

```python
import math

import jax
import jax.numpy as jnp
from jax import lax
from jax.sharding import PartitionSpec as P

norm_epsilon = 1e-05
lambda_base = 0.8 - 0.6 * math.exp(-0.3 * 11.0)
rotary_base = 10000.0
floor_score = -60.0


def doc_tables(lengths, row_count):
    doc_ends = jnp.cumsum(lengths, dtype=jnp.int32)
    places = jnp.arange(row_count, dtype=jnp.int32)
    passed = (places[:, None] >= doc_ends[None, :]).astype(jnp.int32)
    segment = jnp.sum(passed, axis=1, dtype=jnp.int32)
    starts = jnp.sum(passed * lengths[None, :], axis=1, dtype=jnp.int32)
    allowed = (segment[:, None] == segment[None, :]) & (places[None, :] <= places[:, None])
    return (places - starts, allowed)


def rotary_tables(position, map_width):
    half_width = map_width // 2
    frequency = rotary_base ** (-2.0 * jnp.arange(half_width, dtype=jnp.float32) / map_width)
    angles = position.astype(jnp.float32)[:, None] * frequency[None, :]
    return (jnp.cos(angles), jnp.sin(angles))


def rotate(values, cosine_table, sine_table):
    half_width = values.shape[-1] // 2
    first_half = values[..., :half_width]
    second_half = values[..., half_width:]
    cos_wide = cosine_table[:, None, None, :]
    sin_wide = sine_table[:, None, None, :]
    return jnp.concatenate(
        [
            first_half * cos_wide - second_half * sin_wide,
            second_half * cos_wide + first_half * sin_wide,
        ],
        axis=-1,
    )


def rotate_back(values, cosine_table, sine_table):
    half_width = values.shape[-1] // 2
    first_half = values[..., :half_width]
    second_half = values[..., half_width:]
    cos_wide = cosine_table[:, None, None, :]
    sin_wide = sine_table[:, None, None, :]
    return jnp.concatenate(
        [
            first_half * cos_wide + second_half * sin_wide,
            second_half * cos_wide - first_half * sin_wide,
        ],
        axis=-1,
    )


def f32_dot(left, right):
    return jnp.dot(left, right, preferred_element_type=jnp.float32)


def dot_t(left, right):
    return lax.dot_general(
        left, right, (((1,), (1,)), ((), ())), preferred_element_type=jnp.float32
    )


def dot_rows(left, right):
    return lax.dot_general(
        left, right, (((0,), (0,)), ((), ())), preferred_element_type=jnp.float32
    )


def flip(values, axis_name, bit):
    size = lax.axis_size(axis_name)
    return lax.ppermute(values, axis_name, [(i, i ^ bit) for i in range(size)])


def half_rows(values, which):
    count = values.shape[0] // 2
    return lax.dynamic_slice_in_dim(values, which * count, count, 0)


def mine_first(values, core):
    return jnp.concatenate([half_rows(values, core), half_rows(values, 1 - core)], axis=0)


def in_order(values, core):
    half = values.shape[0] // 2
    swapped = jnp.concatenate([values[half:], values[:half]], 0)
    return jnp.where(core == 0, values, swapped)


def tensor_sum(keep, send):
    half = keep + flip(send, "tensor", 1)
    return half + flip(half, "tensor", 2)


def with_other(mine):
    return jnp.concatenate([mine, flip(mine, "tensor", 1)], axis=0)


def line_scatter(parts, dp_count):
    line = dp_count // 2
    place = lax.axis_index("dp") // 2
    up_in = None
    down_in = None
    own = parts
    for step in range(line - 1):
        up_at = jnp.clip(line - 1 - step + place, 0, line - 1)
        down_at = jnp.clip(step - line + 1 + place, 0, line - 1)
        up_out = lax.dynamic_index_in_dim(own, up_at, 0, keepdims=False)
        down_out = lax.dynamic_index_in_dim(own, down_at, 0, keepdims=False)
        if up_in is not None:
            up_out = up_out + up_in
            down_out = down_out + down_in
        up_in = lax.ppermute(
            up_out, "dp", [(2 * z + x, 2 * z + 2 + x) for z in range(step + 1) for x in range(2)]
        )
        down_in = lax.ppermute(
            down_out,
            "dp",
            [
                (2 * z + x, 2 * z - 2 + x)
                for z in range(line - 1, line - 2 - step, -1)
                for x in range(2)
            ],
        )
    return lax.dynamic_index_in_dim(own, place, 0, keepdims=False) + up_in + down_in


def pair_columns(values, dp_count):
    rows, width = values.shape
    line = dp_count // 2
    side = lax.axis_index("dp") % 2
    cut = values.reshape(rows, line, 2, width // dp_count)
    pick = lambda which: lax.dynamic_index_in_dim(cut, which, 2, keepdims=False).reshape(
        rows, width // 2
    )
    return pick(1 - side), pick(side)


def weight_scatter(pair, right, dp_count):
    send_left, keep_left = pair
    received = flip(dot_rows(send_left, right), "dp", 1)
    summed = dot_rows(keep_left, right) + received
    line = dp_count // 2
    return line_scatter(summed.reshape(line, -1, summed.shape[-1]), dp_count)


def rms_back(incoming, values, inverse_root):
    return inverse_root * incoming - values * inverse_root**3 * jnp.mean(
        incoming * values, axis=-1, keepdims=True
    )


def root_of(values):
    return lax.rsqrt(jnp.mean(values * values, axis=-1, keepdims=True) + norm_epsilon)


def attention_forward(row_in, lengths, weight_set, core):
    (norm1_gain, query_weight, key_weight, value_weight, lambda_param, sub_gain, out_weight) = (
        weight_set
    )
    row_count = row_in.shape[0]
    head_count = lambda_param.shape[0]
    map_width = lambda_param.shape[1] // 4
    value_width = sub_gain.shape[1]
    score_scale = map_width ** (-0.5)
    position, allowed = doc_tables(lengths, row_count)
    cosine_table, sine_table = rotary_tables(position, map_width)
    inputs = row_in.astype(jnp.float32)
    normed_one = (inputs * root_of(inputs) * norm1_gain).astype(jnp.bfloat16)
    query_raw = f32_dot(normed_one, query_weight).reshape(row_count, head_count, 2, map_width)
    query_rows = rotate(query_raw, cosine_table, sine_table).astype(jnp.bfloat16)
    key_raw = f32_dot(normed_one, key_weight).reshape(row_count, head_count, 2, map_width)
    key_rows = rotate(key_raw, cosine_table, sine_table).astype(jnp.bfloat16)
    value_rows = (
        f32_dot(normed_one, value_weight)
        .astype(jnp.bfloat16)
        .reshape(row_count, head_count, value_width)
    )
    lambda_parts = lambda_param.reshape(head_count, 4, map_width)
    first_exp = jnp.exp(jnp.sum(lambda_parts[:, 0] * lambda_parts[:, 1], axis=-1))
    second_exp = jnp.exp(jnp.sum(lambda_parts[:, 2] * lambda_parts[:, 3], axis=-1))
    lambda_head = first_exp - second_exp + lambda_base
    scores = (
        jnp.einsum("thmd,shmd->hmts", query_rows, key_rows, preferred_element_type=jnp.float32)
        * score_scale
    )
    row_max = jnp.max(jnp.where(allowed, scores, floor_score), axis=-1, keepdims=True)
    expanded = jnp.where(allowed, jnp.exp(jnp.where(allowed, scores - row_max, 0.0)), 0.0)
    row_total = jnp.sum(expanded, axis=-1, keepdims=True)
    log_total = row_max + jnp.log(row_total)
    softmax_maps = expanded / row_total
    combined = (softmax_maps[:, 0] - lambda_head[:, None, None] * softmax_maps[:, 1]).astype(
        jnp.bfloat16
    )
    mixed = jnp.einsum("hts,shd->thd", combined, value_rows, preferred_element_type=jnp.float32)
    root_sub = root_of(mixed)
    sub_scale = sub_gain * (1.0 - lambda_base)
    heads_out = (
        (mixed * root_sub * sub_scale)
        .astype(jnp.bfloat16)
        .reshape(row_count, head_count * value_width)
    )
    send = f32_dot(half_rows(heads_out, 1 - core), out_weight)
    keep = f32_dot(half_rows(heads_out, core), out_weight)
    kept = (
        allowed, cosine_table, sine_table, normed_one, query_rows, key_rows, value_rows,
        lambda_parts, first_exp, second_exp, lambda_head, log_total, mixed, root_sub, sub_scale,
        heads_out,
    )
    return keep, send, kept


def attention_backward(grad_attended, kept, weight_set, core):
    (query_weight, key_weight, value_weight, out_weight) = weight_set
    (
        allowed, cosine_table, sine_table, normed_one, query_rows, key_rows, value_rows,
        lambda_parts, first_exp, second_exp, lambda_head, log_total, mixed, root_sub, sub_scale,
        heads_out,
    ) = kept
    row_count, head_count, value_width = value_rows.shape
    map_width = query_rows.shape[-1]
    score_scale = map_width ** (-0.5)
    grad_heads = dot_t(grad_attended, out_weight).reshape(row_count, head_count, value_width)
    grad_sub = jnp.sum(grad_heads * mixed * root_sub, axis=0) * (1.0 - lambda_base)
    grad_mixed = rms_back(grad_heads * sub_scale, mixed, root_sub).astype(jnp.bfloat16)
    scores = (
        jnp.einsum("thmd,shmd->hmts", query_rows, key_rows, preferred_element_type=jnp.float32)
        * score_scale
    )
    maps_again = jnp.where(allowed, jnp.exp(jnp.where(allowed, scores - log_total, 0.0)), 0.0)
    first_map = maps_again[:, 0]
    second_map = maps_again[:, 1]
    combined_again = (first_map - lambda_head[:, None, None] * second_map).astype(jnp.bfloat16)
    grad_combined = jnp.einsum(
        "thd,shd->hts", grad_mixed, value_rows, preferred_element_type=jnp.float32
    )
    grad_value = (
        jnp.einsum("hts,thd->shd", combined_again, grad_mixed, preferred_element_type=jnp.float32)
        .astype(jnp.bfloat16)
        .reshape(row_count, head_count * value_width)
    )
    grad_lambda_head = -jnp.sum(grad_combined * second_map, axis=(1, 2))
    grad_first = first_map * (
        grad_combined - jnp.sum(grad_combined * first_map, axis=-1, keepdims=True)
    )
    second_in = -lambda_head[:, None, None] * grad_combined
    grad_second = second_map * (second_in - jnp.sum(second_in * second_map, axis=-1, keepdims=True))
    grad_scores = jnp.stack([grad_first, grad_second], axis=1).astype(jnp.bfloat16)
    grad_query_roped = (
        jnp.einsum("hmts,shmd->thmd", grad_scores, key_rows, preferred_element_type=jnp.float32)
        * score_scale
    )
    grad_key_roped = (
        jnp.einsum("hmts,thmd->shmd", grad_scores, query_rows, preferred_element_type=jnp.float32)
        * score_scale
    )
    grad_query = (
        rotate_back(grad_query_roped, cosine_table, sine_table)
        .astype(jnp.bfloat16)
        .reshape(row_count, head_count * 2 * map_width)
    )
    grad_key = (
        rotate_back(grad_key_roped, cosine_table, sine_table)
        .astype(jnp.bfloat16)
        .reshape(row_count, head_count * 2 * map_width)
    )

    def partial(which):
        return (
            dot_t(half_rows(grad_query, which), query_weight)
            + dot_t(half_rows(grad_key, which), key_weight)
            + dot_t(half_rows(grad_value, which), value_weight)
        )

    send = partial(1 - core)
    keep = partial(core)
    first_scale = (grad_lambda_head * first_exp)[:, None]
    second_scale = (grad_lambda_head * second_exp)[:, None]
    lambda_grad = jnp.stack(
        [
            first_scale * lambda_parts[:, 1],
            first_scale * lambda_parts[:, 0],
            -second_scale * lambda_parts[:, 3],
            -second_scale * lambda_parts[:, 2],
        ],
        axis=1,
    ).reshape(head_count, 4 * map_width)
    return keep, send, grad_query, grad_key, grad_value, lambda_grad, grad_sub


def feed_forward(normed_two, cot_rows, gate_weight, up_weight, down_weight):
    half = normed_two.shape[0] // 2
    gate_pre = f32_dot(normed_two, gate_weight)
    upward = f32_dot(normed_two, up_weight)
    sigmoid_gate = jax.nn.sigmoid(gate_pre)
    hidden = (gate_pre * sigmoid_gate * upward).astype(jnp.bfloat16)
    grad_hidden = dot_t(cot_rows, down_weight)
    grad_gate_pre = (
        grad_hidden * upward * sigmoid_gate * (1.0 + gate_pre * (1.0 - sigmoid_gate))
    ).astype(jnp.bfloat16)
    grad_up_pre = (grad_hidden * gate_pre * sigmoid_gate).astype(jnp.bfloat16)

    def back(at):
        return dot_t(grad_gate_pre[at], gate_weight) + dot_t(grad_up_pre[at], up_weight)

    send_back = back(slice(half, None))
    keep_back = back(slice(0, half))
    send_fed = f32_dot(hidden[half:], down_weight)
    keep_fed = f32_dot(hidden[:half], down_weight)
    return (keep_back, send_back), (keep_fed, send_fed), hidden, grad_gate_pre, grad_up_pre


def on_device(
    layer_in,
    short_lengths,
    long_lengths,
    norm1_gain,
    query_weight,
    key_weight,
    value_weight,
    lambda_param,
    sub_gain,
    out_weight,
    norm2_gain,
    gate_weight,
    up_weight,
    down_weight,
    out_cotangent,
):
    dp_count = lax.axis_size("dp")
    core = lax.axis_index("tensor") % 2
    head_count, lambda_width = lambda_param.shape
    value_width = sub_gain.shape[1]
    doc_lengths = (short_lengths[0], long_lengths[0])
    attention_weights = (
        norm1_gain, query_weight, key_weight, value_weight, lambda_param, sub_gain, out_weight,
    )
    cots = [mine_first(out_cotangent[m], core) for m in range(2)]
    cot_pair = pair_columns(jnp.concatenate(cots, 0), dp_count)
    half = cots[0].shape[0] // 2
    rows_in = [mine_first(layer_in[m], core).astype(jnp.float32) for m in range(2)]
    inputs = [rows_in[m][:half] for m in range(2)]
    front = [attention_forward(layer_in[m], doc_lengths[m], attention_weights, core) for m in range(2)]
    kept = [front[m][2] for m in range(2)]
    attended, middle, root_two, normed_two, ffn = [], [], [], [], []
    for m in range(2):
        attended.append(tensor_sum(front[m][0], front[m][1]))
        middle.append(inputs[m] + attended[m])
        root_two.append(root_of(middle[m]))
        normed_two.append((with_other(middle[m] * root_two[m]) * norm2_gain).astype(jnp.bfloat16))
        ffn.append(feed_forward(normed_two[m], cots[m], gate_weight, up_weight, down_weight))
    both = lambda index: jnp.concatenate([ffn[0][index], ffn[1][index]], 0)
    normed_two_pair = pair_columns(jnp.concatenate(normed_two, 0), dp_count)
    grad_down = weight_scatter(cot_pair, both(2), dp_count)
    grad_gate = weight_scatter(normed_two_pair, both(3), dp_count)
    grad_up = weight_scatter(normed_two_pair, both(4), dp_count)
    grad_norm2 = 0.0
    grad_norm1 = 0.0
    through_two, grad_attended, back = [], [], []
    for m in range(2):
        grad_normed_two = tensor_sum(*ffn[m][0])
        grad_norm2 = grad_norm2 + jnp.sum(grad_normed_two * middle[m] * root_two[m], axis=0)
        through_two.append(rms_back(grad_normed_two * norm2_gain, middle[m], root_two[m]))
        grad_middle = cots[m].astype(jnp.float32) + with_other(through_two[m])
        grad_attended.append(in_order(grad_middle, core).astype(jnp.bfloat16))
        back.append(
            attention_backward(
                grad_attended[m], kept[m], (query_weight, key_weight, value_weight, out_weight), core
            )
        )
    heads_both = jnp.concatenate([kept[0][-1], kept[1][-1]], 0)
    grad_out = weight_scatter(
        pair_columns(jnp.concatenate(grad_attended, 0), dp_count), heads_both, dp_count
    )
    normed_one_pair = pair_columns(jnp.concatenate([kept[0][3], kept[1][3]], 0), dp_count)
    grad_query, grad_key, grad_value = [
        weight_scatter(normed_one_pair, jnp.concatenate([back[0][i], back[1][i]], 0), dp_count)
        for i in (2, 3, 4)
    ]
    out_blocks, grad_blocks = [], []
    for m in range(2):
        fed = tensor_sum(*ffn[m][1])
        out_rows = rows_in[m] + with_other(attended[m] + fed)
        out_blocks.append(in_order(out_rows, core).astype(jnp.bfloat16))
        grad_normed_one = tensor_sum(back[m][0], back[m][1])
        root_one = root_of(inputs[m])
        grad_norm1 = grad_norm1 + jnp.sum(grad_normed_one * inputs[m] * root_one, axis=0)
        through = through_two[m] + rms_back(grad_normed_one * norm1_gain, inputs[m], root_one)
        grad_rows = cots[m].astype(jnp.float32) + with_other(through)
        grad_blocks.append(in_order(grad_rows, core).astype(jnp.bfloat16))
    norms = jnp.stack([grad_norm1, grad_norm2])
    norms = norms + flip(norms, "tensor", 1)
    small = [
        norms,
        back[0][5] + back[1][5],
        back[0][6] + back[1][6],
    ]
    width = norms.shape[-1]
    packed = jnp.concatenate(
        [
            part.reshape(part.shape[0], dp_count, -1).transpose(1, 0, 2).reshape(dp_count, -1)
            for part in small
        ],
        axis=1,
    )
    pairs = packed.reshape(dp_count // 2, 2, 1, -1)
    side = lax.axis_index("dp") % 2
    send = lax.dynamic_index_in_dim(pairs, 1 - side, 1, keepdims=False)
    keep = lax.dynamic_index_in_dim(pairs, side, 1, keepdims=False)
    small_sum = line_scatter(keep + flip(send, "dp", 1), dp_count)[0]
    sizes = [2 * width // dp_count, head_count * lambda_width // dp_count]
    norm_sum, lambda_sum, sub_sum = jnp.split(small_sum, [sizes[0], sizes[0] + sizes[1]])
    norm_sum = norm_sum.reshape(2, -1)
    return (
        jnp.stack(out_blocks),
        jnp.stack(grad_blocks),
        norm_sum[0],
        grad_query,
        grad_key,
        grad_value,
        lambda_sum.reshape(head_count, -1),
        sub_sum.reshape(head_count, -1),
        grad_out.T,
        norm_sum[1],
        grad_gate,
        grad_up,
        grad_down.T,
    )


def solution(mesh):
    return jax.shard_map(
        on_device,
        mesh=mesh,
        in_specs=(
            P(None, "dp", None),
            P("dp", None),
            P("dp", None),
            P(),
            P(None, "tensor"),
            P(None, "tensor"),
            P(None, "tensor"),
            P("tensor", None),
            P("tensor", None),
            P("tensor", None),
            P(),
            P(None, "tensor"),
            P(None, "tensor"),
            P("tensor", None),
            P(None, "dp", None),
        ),
        out_specs=(
            P(None, "dp", None),
            P(None, "dp", None),
            P("dp"),
            P("dp", "tensor"),
            P("dp", "tensor"),
            P("dp", "tensor"),
            P("tensor", "dp"),
            P("tensor", "dp"),
            P("tensor", "dp"),
            P("dp"),
            P("dp", "tensor"),
            P("dp", "tensor"),
            P("tensor", "dp"),
        ),
        check_vma=False,
    )
```

```python
import functools
import math

import jax
import jax.numpy as jnp
from jax import lax
from jax.experimental import pallas as pl
from jax.experimental.pallas import tpu as pltpu
from jax.sharding import PartitionSpec as P

norm_epsilon = 1e-05
lambda_base = 0.8 - 0.6 * math.exp(-0.3 * 11.0)
rotary_base = 10000.0
floor_score = -60.0
chunk_columns = 256
send_slots = 3
held_slots = 4
MESH = pl.DeviceIdType.MESH


def doc_tables(lengths, row_count):
    doc_ends = jnp.cumsum(lengths, dtype=jnp.int32)
    places = jnp.arange(row_count, dtype=jnp.int32)
    passed = (places[:, None] >= doc_ends[None, :]).astype(jnp.int32)
    segment = jnp.sum(passed, axis=1, dtype=jnp.int32)
    starts = jnp.sum(passed * lengths[None, :], axis=1, dtype=jnp.int32)
    allowed = (segment[:, None] == segment[None, :]) & (places[None, :] <= places[:, None])
    return (places - starts, allowed)


def rotary_tables(position, map_width):
    half_width = map_width // 2
    frequency = rotary_base ** (-2.0 * jnp.arange(half_width, dtype=jnp.float32) / map_width)
    angles = position.astype(jnp.float32)[:, None] * frequency[None, :]
    return (jnp.cos(angles), jnp.sin(angles))


def rotate(values, cosine_table, sine_table):
    half_width = values.shape[-1] // 2
    first_half = values[..., :half_width]
    second_half = values[..., half_width:]
    cos_wide = cosine_table[:, None, None, :]
    sin_wide = sine_table[:, None, None, :]
    return jnp.concatenate(
        [
            first_half * cos_wide - second_half * sin_wide,
            second_half * cos_wide + first_half * sin_wide,
        ],
        axis=-1,
    )


def rotate_back(values, cosine_table, sine_table):
    half_width = values.shape[-1] // 2
    first_half = values[..., :half_width]
    second_half = values[..., half_width:]
    cos_wide = cosine_table[:, None, None, :]
    sin_wide = sine_table[:, None, None, :]
    return jnp.concatenate(
        [
            first_half * cos_wide + second_half * sin_wide,
            second_half * cos_wide - first_half * sin_wide,
        ],
        axis=-1,
    )


def f32_dot(left, right):
    return jnp.dot(left, right, preferred_element_type=jnp.float32)


def dot_t(left, right):
    return lax.dot_general(
        left, right, (((1,), (1,)), ((), ())), preferred_element_type=jnp.float32
    )


def dot_rows(left, right):
    return lax.dot_general(
        left, right, (((0,), (0,)), ((), ())), preferred_element_type=jnp.float32
    )


def flip(values, axis_name, bit):
    size = lax.axis_size(axis_name)
    return lax.ppermute(values, axis_name, [(i, i ^ bit) for i in range(size)])


def half_rows(values, which):
    count = values.shape[0] // 2
    return lax.dynamic_slice_in_dim(values, which * count, count, 0)


def mine_first(values, core):
    return jnp.concatenate([half_rows(values, core), half_rows(values, 1 - core)], axis=0)


def in_order(values, core):
    half = values.shape[0] // 2
    swapped = jnp.concatenate([values[half:], values[:half]], 0)
    return jnp.where(core == 0, values, swapped)


def tensor_sum(keep, send):
    half = keep + flip(send, "tensor", 1)
    return half + flip(half, "tensor", 2)


def with_other(mine):
    return jnp.concatenate([mine, flip(mine, "tensor", 1)], axis=0)


def line_scatter(parts, dp_count):
    line = dp_count // 2
    place = lax.axis_index("dp") // 2
    up_in = None
    down_in = None
    own = parts
    for step in range(line - 1):
        up_at = jnp.clip(line - 1 - step + place, 0, line - 1)
        down_at = jnp.clip(step - line + 1 + place, 0, line - 1)
        up_out = lax.dynamic_index_in_dim(own, up_at, 0, keepdims=False)
        down_out = lax.dynamic_index_in_dim(own, down_at, 0, keepdims=False)
        if up_in is not None:
            up_out = up_out + up_in
            down_out = down_out + down_in
        up_in = lax.ppermute(
            up_out, "dp", [(2 * z + x, 2 * z + 2 + x) for z in range(step + 1) for x in range(2)]
        )
        down_in = lax.ppermute(
            down_out,
            "dp",
            [
                (2 * z + x, 2 * z - 2 + x)
                for z in range(line - 1, line - 2 - step, -1)
                for x in range(2)
            ],
        )
    return lax.dynamic_index_in_dim(own, place, 0, keepdims=False) + up_in + down_in


def scatter_kernel(plan, line, left_count, right_count, *refs):
    lefts, refs = refs[:left_count], refs[left_count:]
    rights, refs = refs[:right_count], refs[right_count:]
    outs, scratch = refs[:right_count], refs[right_count:]
    send, held, total, landed, pair_out, pair_in, line_out, line_in, credit, out_sem = scratch
    me = lax.axis_index("dp")
    place, side = me // 2, me % 2
    other = me + 1 - 2 * side
    steps = line - 1
    count = len(plan)
    ring = total.shape[0]

    barrier = pltpu.get_barrier_semaphore()
    pl.semaphore_signal(barrier, inc=1, device_id={"dp": other}, device_id_type=MESH)

    @pl.when(place > 0)
    def _():
        pl.semaphore_signal(barrier, inc=1, device_id={"dp": me - 2}, device_id_type=MESH)

    @pl.when(place < line - 1)
    def _():
        pl.semaphore_signal(barrier, inc=1, device_id={"dp": me + 2}, device_id_type=MESH)

    has_below = jnp.where(place > 0, 1, 0)
    has_above = jnp.where(place < line - 1, 1, 0)
    pl.semaphore_wait(barrier, 1 + has_below + has_above)

    def compute(c):
        left, right, first, width = plan[c]

        def block(at, carry):
            columns = rights[right][:, first : first + width]
            send[c % send_slots, at, :, :width] = f32_dot(lefts[left][at, 1 - side], columns)
            total[c % ring, at, :, :width] = f32_dot(lefts[left][at, side], columns)
            return carry

        lax.fori_loop(0, line, block, 0)

    def pair_copy(c):
        width = plan[c][3]
        return pltpu.make_async_remote_copy(
            src_ref=send.at[c % send_slots, :, :, :width],
            dst_ref=held.at[c % held_slots, :, :, :width],
            send_sem=pair_out.at[c % send_slots],
            recv_sem=pair_in.at[c % held_slots],
            device_id={"dp": other},
            device_id_type=MESH,
        )

    def pair_finish(c):
        width = plan[c][3]
        pair_copy(c).wait_recv()

        def block(at, carry):
            total[c % ring, at, :, :width] += held[c % held_slots, at, :, :width]
            return carry

        lax.fori_loop(0, line, block, 0)
        pair_copy(c).wait_send()

    def line_copy(c, step, way):
        width = plan[c][3]
        block = line - 1 - step + place if way == 0 else place + step - line + 1
        return pltpu.make_async_remote_copy(
            src_ref=total.at[c % ring, block, :, :width],
            dst_ref=landed.at[way, step, c % 2, :, :width],
            send_sem=line_out.at[way, step, c % 2],
            recv_sem=line_in.at[way, step, c % 2],
            device_id={"dp": me + 2 - 4 * way},
            device_id_type=MESH,
        )

    def line_sends(step, way):
        if way == 0:
            return (place <= step) & (place < line - 1)
        return (place >= line - 1 - step) & (place > 0)

    def line_start(c, step):
        for way in range(2):

            @pl.when(line_sends(step, way))
            def _():
                if c >= 2:
                    pl.semaphore_wait(credit.at[way, step], 1)
                line_copy(c, step, way).start()

    def line_finish(c, step):
        width = plan[c][3]
        for way in range(2):
            if way == 0:
                gets = (place > 0) & (place - 1 <= step)
                block = line - 2 - step + place
            else:
                gets = (place < line - 1) & (place + 1 >= line - 1 - step)
                block = place + step - line + 2

            @pl.when(gets)
            def _():
                pltpu.make_async_remote_copy(
                    src_ref=total.at[c % ring, block, :, :width],
                    dst_ref=landed.at[way, step, c % 2, :, :width],
                    send_sem=line_out.at[way, step, c % 2],
                    recv_sem=line_in.at[way, step, c % 2],
                    device_id={"dp": me - 2 + 4 * way},
                    device_id_type=MESH,
                ).wait_recv()
                total[c % ring, block, :, :width] += landed[way, step, c % 2, :, :width]
                if c + 2 < count:
                    pl.semaphore_signal(
                        credit.at[way, step],
                        inc=1,
                        device_id={"dp": me - 2 + 4 * way},
                        device_id_type=MESH,
                    )

            @pl.when(line_sends(step, way))
            def _():
                line_copy(c, step, way).wait_send()

    def out_copy(c):
        left, right, first, width = plan[c]
        return pltpu.make_async_copy(
            total.at[c % ring, place, :, :width],
            outs[right].at[:, first : first + width],
            out_sem.at[c % ring],
        )

    compute(0)
    pair_copy(0).start()
    if count > 1:
        compute(1)
    for slot in range(count + steps + 1):
        for step in range(steps):
            c = slot - 2 - step
            if 0 <= c < count:
                line_finish(c, step)
        if 0 <= slot - 1 < count:
            pair_finish(slot - 1)
        for step in range(steps):
            c = slot - 1 - step
            if 0 <= c < count:
                line_start(c, step)
        if slot + 1 < count:
            pair_copy(slot + 1).start()
        done = slot - 1 - steps
        if 0 <= done < count:
            out_copy(done).start()
        if slot + 2 < count:
            if slot + 2 >= ring:
                out_copy(slot + 2 - ring).wait()
            compute(slot + 2)
    for c in range(max(0, count - ring), count):
        out_copy(c).wait()


def weight_scatter(lefts, rights, pairs, dp_count, collective_id):
    line = dp_count // 2
    tokens, depth = lefts[0].shape
    rows = depth // dp_count
    lefts = [left.T.reshape(line, 2, rows, tokens) for left in lefts]
    plan = []
    for left, right in pairs:
        width = rights[right].shape[1]
        for first in range(0, width, chunk_columns):
            plan.append((left, right, first, min(chunk_columns, width - first)))
    ring = line + 4
    wide = (line, rows, chunk_columns)
    flops = 2 * tokens * depth * sum(item[3] for item in plan)
    return pl.pallas_call(
        functools.partial(scatter_kernel, tuple(plan), line, len(lefts), len(rights)),
        out_shape=[
            jax.ShapeDtypeStruct((rows, right.shape[1]), jnp.float32) for right in rights
        ],
        in_specs=[pl.BlockSpec(memory_space=pltpu.VMEM)] * (len(lefts) + len(rights)),
        out_specs=[pl.BlockSpec(memory_space=pl.ANY)] * len(rights),
        scratch_shapes=[
            pltpu.VMEM((send_slots,) + wide, jnp.float32),
            pltpu.VMEM((held_slots,) + wide, jnp.float32),
            pltpu.VMEM((ring,) + wide, jnp.float32),
            pltpu.VMEM((2, line - 1, 2, rows, chunk_columns), jnp.float32),
            pltpu.SemaphoreType.DMA((send_slots,)),
            pltpu.SemaphoreType.DMA((held_slots,)),
            pltpu.SemaphoreType.DMA((2, line - 1, 2)),
            pltpu.SemaphoreType.DMA((2, line - 1, 2)),
            pltpu.SemaphoreType.REGULAR((2, line - 1)),
            pltpu.SemaphoreType.DMA((ring,)),
        ],
        compiler_params=pltpu.CompilerParams(
            collective_id=collective_id, has_side_effects=True, vmem_limit_bytes=48 * 1024 * 1024
        ),
        cost_estimate=pl.CostEstimate(flops=flops, bytes_accessed=flops // 16, transcendentals=0),
    )(*lefts, *rights)


def rms_back(incoming, values, inverse_root):
    return inverse_root * incoming - values * inverse_root**3 * jnp.mean(
        incoming * values, axis=-1, keepdims=True
    )


def root_of(values):
    return lax.rsqrt(jnp.mean(values * values, axis=-1, keepdims=True) + norm_epsilon)


def attention_forward(row_in, lengths, weight_set, core):
    (norm1_gain, query_weight, key_weight, value_weight, lambda_param, sub_gain, out_weight) = (
        weight_set
    )
    row_count = row_in.shape[0]
    head_count = lambda_param.shape[0]
    map_width = lambda_param.shape[1] // 4
    value_width = sub_gain.shape[1]
    score_scale = map_width ** (-0.5)
    position, allowed = doc_tables(lengths, row_count)
    cosine_table, sine_table = rotary_tables(position, map_width)
    inputs = row_in.astype(jnp.float32)
    normed_one = (inputs * root_of(inputs) * norm1_gain).astype(jnp.bfloat16)
    query_raw = f32_dot(normed_one, query_weight).reshape(row_count, head_count, 2, map_width)
    query_rows = rotate(query_raw, cosine_table, sine_table).astype(jnp.bfloat16)
    key_raw = f32_dot(normed_one, key_weight).reshape(row_count, head_count, 2, map_width)
    key_rows = rotate(key_raw, cosine_table, sine_table).astype(jnp.bfloat16)
    value_rows = (
        f32_dot(normed_one, value_weight)
        .astype(jnp.bfloat16)
        .reshape(row_count, head_count, value_width)
    )
    lambda_parts = lambda_param.reshape(head_count, 4, map_width)
    first_exp = jnp.exp(jnp.sum(lambda_parts[:, 0] * lambda_parts[:, 1], axis=-1))
    second_exp = jnp.exp(jnp.sum(lambda_parts[:, 2] * lambda_parts[:, 3], axis=-1))
    lambda_head = first_exp - second_exp + lambda_base
    scores = (
        jnp.einsum("thmd,shmd->hmts", query_rows, key_rows, preferred_element_type=jnp.float32)
        * score_scale
    )
    row_max = jnp.max(jnp.where(allowed, scores, floor_score), axis=-1, keepdims=True)
    expanded = jnp.where(allowed, jnp.exp(jnp.where(allowed, scores - row_max, 0.0)), 0.0)
    row_total = jnp.sum(expanded, axis=-1, keepdims=True)
    log_total = row_max + jnp.log(row_total)
    softmax_maps = expanded / row_total
    combined = (softmax_maps[:, 0] - lambda_head[:, None, None] * softmax_maps[:, 1]).astype(
        jnp.bfloat16
    )
    mixed = jnp.einsum("hts,shd->thd", combined, value_rows, preferred_element_type=jnp.float32)
    root_sub = root_of(mixed)
    sub_scale = sub_gain * (1.0 - lambda_base)
    heads_out = (
        (mixed * root_sub * sub_scale)
        .astype(jnp.bfloat16)
        .reshape(row_count, head_count * value_width)
    )
    send = f32_dot(half_rows(heads_out, 1 - core), out_weight)
    keep = f32_dot(half_rows(heads_out, core), out_weight)
    kept = (
        allowed, cosine_table, sine_table, normed_one, query_rows, key_rows, value_rows,
        lambda_parts, first_exp, second_exp, lambda_head, log_total, mixed, root_sub, sub_scale,
        heads_out,
    )
    return keep, send, kept


def attention_backward(grad_attended, kept, weight_set, core):
    (query_weight, key_weight, value_weight, out_weight) = weight_set
    (
        allowed, cosine_table, sine_table, normed_one, query_rows, key_rows, value_rows,
        lambda_parts, first_exp, second_exp, lambda_head, log_total, mixed, root_sub, sub_scale,
        heads_out,
    ) = kept
    row_count, head_count, value_width = value_rows.shape
    map_width = query_rows.shape[-1]
    score_scale = map_width ** (-0.5)
    grad_heads = dot_t(grad_attended, out_weight).reshape(row_count, head_count, value_width)
    grad_sub = jnp.sum(grad_heads * mixed * root_sub, axis=0) * (1.0 - lambda_base)
    grad_mixed = rms_back(grad_heads * sub_scale, mixed, root_sub).astype(jnp.bfloat16)
    scores = (
        jnp.einsum("thmd,shmd->hmts", query_rows, key_rows, preferred_element_type=jnp.float32)
        * score_scale
    )
    maps_again = jnp.where(allowed, jnp.exp(jnp.where(allowed, scores - log_total, 0.0)), 0.0)
    first_map = maps_again[:, 0]
    second_map = maps_again[:, 1]
    combined_again = (first_map - lambda_head[:, None, None] * second_map).astype(jnp.bfloat16)
    grad_combined = jnp.einsum(
        "thd,shd->hts", grad_mixed, value_rows, preferred_element_type=jnp.float32
    )
    grad_value = (
        jnp.einsum("hts,thd->shd", combined_again, grad_mixed, preferred_element_type=jnp.float32)
        .astype(jnp.bfloat16)
        .reshape(row_count, head_count * value_width)
    )
    grad_lambda_head = -jnp.sum(grad_combined * second_map, axis=(1, 2))
    grad_first = first_map * (
        grad_combined - jnp.sum(grad_combined * first_map, axis=-1, keepdims=True)
    )
    second_in = -lambda_head[:, None, None] * grad_combined
    grad_second = second_map * (second_in - jnp.sum(second_in * second_map, axis=-1, keepdims=True))
    grad_scores = jnp.stack([grad_first, grad_second], axis=1).astype(jnp.bfloat16)
    grad_query_roped = (
        jnp.einsum("hmts,shmd->thmd", grad_scores, key_rows, preferred_element_type=jnp.float32)
        * score_scale
    )
    grad_key_roped = (
        jnp.einsum("hmts,thmd->shmd", grad_scores, query_rows, preferred_element_type=jnp.float32)
        * score_scale
    )
    grad_query = (
        rotate_back(grad_query_roped, cosine_table, sine_table)
        .astype(jnp.bfloat16)
        .reshape(row_count, head_count * 2 * map_width)
    )
    grad_key = (
        rotate_back(grad_key_roped, cosine_table, sine_table)
        .astype(jnp.bfloat16)
        .reshape(row_count, head_count * 2 * map_width)
    )

    def partial(which):
        return (
            dot_t(half_rows(grad_query, which), query_weight)
            + dot_t(half_rows(grad_key, which), key_weight)
            + dot_t(half_rows(grad_value, which), value_weight)
        )

    send = partial(1 - core)
    keep = partial(core)
    first_scale = (grad_lambda_head * first_exp)[:, None]
    second_scale = (grad_lambda_head * second_exp)[:, None]
    lambda_grad = jnp.stack(
        [
            first_scale * lambda_parts[:, 1],
            first_scale * lambda_parts[:, 0],
            -second_scale * lambda_parts[:, 3],
            -second_scale * lambda_parts[:, 2],
        ],
        axis=1,
    ).reshape(head_count, 4 * map_width)
    return keep, send, grad_query, grad_key, grad_value, lambda_grad, grad_sub


def feed_forward(normed_two, cot_rows, gate_weight, up_weight, down_weight):
    half = normed_two.shape[0] // 2
    gate_pre = f32_dot(normed_two, gate_weight)
    upward = f32_dot(normed_two, up_weight)
    sigmoid_gate = jax.nn.sigmoid(gate_pre)
    hidden = (gate_pre * sigmoid_gate * upward).astype(jnp.bfloat16)
    grad_hidden = dot_t(cot_rows, down_weight)
    grad_gate_pre = (
        grad_hidden * upward * sigmoid_gate * (1.0 + gate_pre * (1.0 - sigmoid_gate))
    ).astype(jnp.bfloat16)
    grad_up_pre = (grad_hidden * gate_pre * sigmoid_gate).astype(jnp.bfloat16)

    def back(at):
        return dot_t(grad_gate_pre[at], gate_weight) + dot_t(grad_up_pre[at], up_weight)

    send_back = back(slice(half, None))
    keep_back = back(slice(0, half))
    send_fed = f32_dot(hidden[half:], down_weight)
    keep_fed = f32_dot(hidden[:half], down_weight)
    return (keep_back, send_back), (keep_fed, send_fed), hidden, grad_gate_pre, grad_up_pre


def on_device(
    layer_in,
    short_lengths,
    long_lengths,
    norm1_gain,
    query_weight,
    key_weight,
    value_weight,
    lambda_param,
    sub_gain,
    out_weight,
    norm2_gain,
    gate_weight,
    up_weight,
    down_weight,
    out_cotangent,
):
    dp_count = lax.axis_size("dp")
    core = lax.axis_index("tensor") % 2
    head_count, lambda_width = lambda_param.shape
    value_width = sub_gain.shape[1]
    doc_lengths = (short_lengths[0], long_lengths[0])
    attention_weights = (
        norm1_gain, query_weight, key_weight, value_weight, lambda_param, sub_gain, out_weight,
    )
    cots = [mine_first(out_cotangent[m], core) for m in range(2)]
    half = cots[0].shape[0] // 2
    rows_in = [mine_first(layer_in[m], core).astype(jnp.float32) for m in range(2)]
    inputs = [rows_in[m][:half] for m in range(2)]
    front = [attention_forward(layer_in[m], doc_lengths[m], attention_weights, core) for m in range(2)]
    kept = [front[m][2] for m in range(2)]
    attended, middle, root_two, normed_two, ffn = [], [], [], [], []
    for m in range(2):
        attended.append(tensor_sum(front[m][0], front[m][1]))
        middle.append(inputs[m] + attended[m])
        root_two.append(root_of(middle[m]))
        normed_two.append((with_other(middle[m] * root_two[m]) * norm2_gain).astype(jnp.bfloat16))
        ffn.append(feed_forward(normed_two[m], cots[m], gate_weight, up_weight, down_weight))
    both = lambda index: jnp.concatenate([ffn[0][index], ffn[1][index]], 0)
    grad_down, grad_gate, grad_up = weight_scatter(
        [jnp.concatenate(cots, 0), jnp.concatenate(normed_two, 0)],
        [both(2), both(3), both(4)],
        [(0, 0), (1, 1), (1, 2)],
        dp_count,
        0,
    )
    grad_norm2 = 0.0
    grad_norm1 = 0.0
    through_two, grad_attended, back = [], [], []
    for m in range(2):
        grad_normed_two = tensor_sum(*ffn[m][0])
        grad_norm2 = grad_norm2 + jnp.sum(grad_normed_two * middle[m] * root_two[m], axis=0)
        through_two.append(rms_back(grad_normed_two * norm2_gain, middle[m], root_two[m]))
        grad_middle = cots[m].astype(jnp.float32) + with_other(through_two[m])
        grad_attended.append(in_order(grad_middle, core).astype(jnp.bfloat16))
        back.append(
            attention_backward(
                grad_attended[m], kept[m], (query_weight, key_weight, value_weight, out_weight), core
            )
        )
    heads_both = jnp.concatenate([kept[0][-1], kept[1][-1]], 0)
    grad_rows = jnp.concatenate(
        [jnp.concatenate([back[m][i] for i in (2, 3, 4)], 1) for m in range(2)], 0
    )
    grad_out, grad_qkv = weight_scatter(
        [jnp.concatenate(grad_attended, 0), jnp.concatenate([kept[0][3], kept[1][3]], 0)],
        [heads_both, grad_rows],
        [(0, 0), (1, 1)],
        dp_count,
        1,
    )
    grad_query, grad_key, grad_value = jnp.split(grad_qkv, 3, axis=1)
    out_blocks, grad_blocks = [], []
    for m in range(2):
        fed = tensor_sum(*ffn[m][1])
        out_rows = rows_in[m] + with_other(attended[m] + fed)
        out_blocks.append(in_order(out_rows, core).astype(jnp.bfloat16))
        grad_normed_one = tensor_sum(back[m][0], back[m][1])
        root_one = root_of(inputs[m])
        grad_norm1 = grad_norm1 + jnp.sum(grad_normed_one * inputs[m] * root_one, axis=0)
        through = through_two[m] + rms_back(grad_normed_one * norm1_gain, inputs[m], root_one)
        grad_rows = cots[m].astype(jnp.float32) + with_other(through)
        grad_blocks.append(in_order(grad_rows, core).astype(jnp.bfloat16))
    norms = jnp.stack([grad_norm1, grad_norm2])
    norms = norms + flip(norms, "tensor", 1)
    small = [
        norms,
        back[0][5] + back[1][5],
        back[0][6] + back[1][6],
    ]
    width = norms.shape[-1]
    packed = jnp.concatenate(
        [
            part.reshape(part.shape[0], dp_count, -1).transpose(1, 0, 2).reshape(dp_count, -1)
            for part in small
        ],
        axis=1,
    )
    pairs = packed.reshape(dp_count // 2, 2, 1, -1)
    side = lax.axis_index("dp") % 2
    send = lax.dynamic_index_in_dim(pairs, 1 - side, 1, keepdims=False)
    keep = lax.dynamic_index_in_dim(pairs, side, 1, keepdims=False)
    small_sum = line_scatter(keep + flip(send, "dp", 1), dp_count)[0]
    sizes = [2 * width // dp_count, head_count * lambda_width // dp_count]
    norm_sum, lambda_sum, sub_sum = jnp.split(small_sum, [sizes[0], sizes[0] + sizes[1]])
    norm_sum = norm_sum.reshape(2, -1)
    return (
        jnp.stack(out_blocks),
        jnp.stack(grad_blocks),
        norm_sum[0],
        grad_query,
        grad_key,
        grad_value,
        lambda_sum.reshape(head_count, -1),
        sub_sum.reshape(head_count, -1),
        grad_out.T,
        norm_sum[1],
        grad_gate,
        grad_up,
        grad_down.T,
    )


def solution(mesh):
    return jax.shard_map(
        on_device,
        mesh=mesh,
        in_specs=(
            P(None, "dp", None),
            P("dp", None),
            P("dp", None),
            P(),
            P(None, "tensor"),
            P(None, "tensor"),
            P(None, "tensor"),
            P("tensor", None),
            P("tensor", None),
            P("tensor", None),
            P(),
            P(None, "tensor"),
            P(None, "tensor"),
            P("tensor", None),
            P(None, "dp", None),
        ),
        out_specs=(
            P(None, "dp", None),
            P(None, "dp", None),
            P("dp"),
            P("dp", "tensor"),
            P("dp", "tensor"),
            P("dp", "tensor"),
            P("tensor", "dp"),
            P("tensor", "dp"),
            P("tensor", "dp"),
            P("dp"),
            P("dp", "tensor"),
            P("dp", "tensor"),
            P("tensor", "dp"),
        ),
        check_vma=False,
    )
```

```python
import functools
import math

import jax
import jax.numpy as jnp
from jax import lax
from jax.experimental import pallas as pl
from jax.experimental.pallas import tpu as pltpu
from jax.sharding import PartitionSpec as P

norm_epsilon = 1e-05
lambda_base = 0.8 - 0.6 * math.exp(-0.3 * 11.0)
rotary_base = 10000.0
closed_score = -1e30
block_rows = 128
longest_document = 256
chunk_columns = 256
send_slots = 3
held_slots = 4
MESH = pl.DeviceIdType.MESH


def doc_tables(lengths, row_count):
    doc_ends = jnp.cumsum(lengths, dtype=jnp.int32)
    places = jnp.arange(row_count, dtype=jnp.int32)
    passed = (places[:, None] >= doc_ends[None, :]).astype(jnp.int32)
    segment = jnp.sum(passed, axis=1, dtype=jnp.int32)
    starts = jnp.sum(passed * lengths[None, :], axis=1, dtype=jnp.int32)
    return (places - starts, segment)


def rotary_tables(position, map_width):
    half_width = map_width // 2
    frequency = rotary_base ** (-2.0 * jnp.arange(half_width, dtype=jnp.float32) / map_width)
    angles = position.astype(jnp.float32)[:, None] * frequency[None, :]
    cosine, sine = jnp.cos(angles), jnp.sin(angles)
    return (
        jnp.concatenate([cosine] * 4, axis=1),
        jnp.concatenate([-sine, sine, -sine, sine], axis=1),
    )


def turn(values, cosine, sine):
    width = values.shape[-1]
    quarter = width // 4
    lane = lax.broadcasted_iota(jnp.int32, values.shape, 1)
    partner = jnp.where(
        lane % (2 * quarter) < quarter,
        pltpu.roll(values, width - quarter, 1),
        pltpu.roll(values, quarter, 1),
    )
    return values * cosine + partner * sine


def map_of(values, which):
    lane = lax.broadcasted_iota(jnp.int32, values.shape, 1)
    mine = (lane >= values.shape[-1] // 2) == (which == 1)
    return jnp.where(mine, values, jnp.zeros_like(values))


def key_range(block):
    first = max(0, block * block_rows - longest_document + 1) // block_rows * block_rows
    return first, (block + 1) * block_rows


def open_pairs(block, segment_column, segment_row):
    first, last = key_range(block)
    rows = pl.ds(block * block_rows, block_rows)
    shape = (block_rows, last - first)
    row_at = lax.broadcasted_iota(jnp.int32, shape, 0) + block * block_rows
    key_at = lax.broadcasted_iota(jnp.int32, shape, 1) + first
    return (segment_column[rows, :] == segment_row[:, first:last]) & (key_at <= row_at)


def softmax_map(query, key, opened, scale):
    scores = jnp.where(opened, dot_t(query, key) * scale, closed_score)
    expanded = jnp.exp(scores - jnp.max(scores, axis=-1, keepdims=True))
    return expanded * (1.0 / jnp.sum(expanded, axis=-1, keepdims=True))


def f32_dot(left, right):
    return jnp.dot(left, right, preferred_element_type=jnp.float32)


def dot_t(left, right):
    return lax.dot_general(
        left, right, (((1,), (1,)), ((), ())), preferred_element_type=jnp.float32
    )


def dot_rows(left, right):
    return lax.dot_general(
        left, right, (((0,), (0,)), ((), ())), preferred_element_type=jnp.float32
    )


def flip(values, axis_name, bit):
    size = lax.axis_size(axis_name)
    return lax.ppermute(values, axis_name, [(i, i ^ bit) for i in range(size)])


def half_rows(values, which):
    count = values.shape[0] // 2
    return lax.dynamic_slice_in_dim(values, which * count, count, 0)


def mine_first(values, core):
    return jnp.concatenate([half_rows(values, core), half_rows(values, 1 - core)], axis=0)


def in_order(values, core):
    half = values.shape[0] // 2
    swapped = jnp.concatenate([values[half:], values[:half]], 0)
    return jnp.where(core == 0, values, swapped)


def tensor_sum(keep, send):
    half = keep + flip(send, "tensor", 1)
    return half + flip(half, "tensor", 2)


def with_other(mine):
    return jnp.concatenate([mine, flip(mine, "tensor", 1)], axis=0)


def line_scatter(parts, dp_count):
    line = dp_count // 2
    place = lax.axis_index("dp") // 2
    up_in = None
    down_in = None
    own = parts
    for step in range(line - 1):
        up_at = jnp.clip(line - 1 - step + place, 0, line - 1)
        down_at = jnp.clip(step - line + 1 + place, 0, line - 1)
        up_out = lax.dynamic_index_in_dim(own, up_at, 0, keepdims=False)
        down_out = lax.dynamic_index_in_dim(own, down_at, 0, keepdims=False)
        if up_in is not None:
            up_out = up_out + up_in
            down_out = down_out + down_in
        up_in = lax.ppermute(
            up_out, "dp", [(2 * z + x, 2 * z + 2 + x) for z in range(step + 1) for x in range(2)]
        )
        down_in = lax.ppermute(
            down_out,
            "dp",
            [
                (2 * z + x, 2 * z - 2 + x)
                for z in range(line - 1, line - 2 - step, -1)
                for x in range(2)
            ],
        )
    return lax.dynamic_index_in_dim(own, place, 0, keepdims=False) + up_in + down_in


def scatter_kernel(plan, line, left_count, right_count, *refs):
    lefts, refs = refs[:left_count], refs[left_count:]
    rights, refs = refs[:right_count], refs[right_count:]
    outs, scratch = refs[:right_count], refs[right_count:]
    send, held, total, landed, pair_out, pair_in, line_out, line_in, credit, out_sem = scratch
    me = lax.axis_index("dp")
    place, side = me // 2, me % 2
    other = me + 1 - 2 * side
    steps = line - 1
    count = len(plan)
    ring = total.shape[0]

    barrier = pltpu.get_barrier_semaphore()
    pl.semaphore_signal(barrier, inc=1, device_id={"dp": other}, device_id_type=MESH)

    @pl.when(place > 0)
    def _():
        pl.semaphore_signal(barrier, inc=1, device_id={"dp": me - 2}, device_id_type=MESH)

    @pl.when(place < line - 1)
    def _():
        pl.semaphore_signal(barrier, inc=1, device_id={"dp": me + 2}, device_id_type=MESH)

    has_below = jnp.where(place > 0, 1, 0)
    has_above = jnp.where(place < line - 1, 1, 0)
    pl.semaphore_wait(barrier, 1 + has_below + has_above)

    def compute(c):
        left, right, first, width = plan[c]

        def block(at, carry):
            columns = rights[right][:, first : first + width]
            send[c % send_slots, at, :, :width] = f32_dot(lefts[left][at, 1 - side], columns)
            total[c % ring, at, :, :width] = f32_dot(lefts[left][at, side], columns)
            return carry

        lax.fori_loop(0, line, block, 0)

    def pair_copy(c):
        width = plan[c][3]
        return pltpu.make_async_remote_copy(
            src_ref=send.at[c % send_slots, :, :, :width],
            dst_ref=held.at[c % held_slots, :, :, :width],
            send_sem=pair_out.at[c % send_slots],
            recv_sem=pair_in.at[c % held_slots],
            device_id={"dp": other},
            device_id_type=MESH,
        )

    def pair_finish(c):
        width = plan[c][3]
        pair_copy(c).wait_recv()

        def block(at, carry):
            total[c % ring, at, :, :width] += held[c % held_slots, at, :, :width]
            return carry

        lax.fori_loop(0, line, block, 0)
        pair_copy(c).wait_send()

    def line_copy(c, step, way):
        width = plan[c][3]
        block = line - 1 - step + place if way == 0 else place + step - line + 1
        return pltpu.make_async_remote_copy(
            src_ref=total.at[c % ring, block, :, :width],
            dst_ref=landed.at[way, step, c % 2, :, :width],
            send_sem=line_out.at[way, step, c % 2],
            recv_sem=line_in.at[way, step, c % 2],
            device_id={"dp": me + 2 - 4 * way},
            device_id_type=MESH,
        )

    def line_sends(step, way):
        if way == 0:
            return (place <= step) & (place < line - 1)
        return (place >= line - 1 - step) & (place > 0)

    def line_start(c, step):
        for way in range(2):

            @pl.when(line_sends(step, way))
            def _():
                if c >= 2:
                    pl.semaphore_wait(credit.at[way, step], 1)
                line_copy(c, step, way).start()

    def line_finish(c, step):
        width = plan[c][3]
        for way in range(2):
            if way == 0:
                gets = (place > 0) & (place - 1 <= step)
                block = line - 2 - step + place
            else:
                gets = (place < line - 1) & (place + 1 >= line - 1 - step)
                block = place + step - line + 2

            @pl.when(gets)
            def _():
                pltpu.make_async_remote_copy(
                    src_ref=total.at[c % ring, block, :, :width],
                    dst_ref=landed.at[way, step, c % 2, :, :width],
                    send_sem=line_out.at[way, step, c % 2],
                    recv_sem=line_in.at[way, step, c % 2],
                    device_id={"dp": me - 2 + 4 * way},
                    device_id_type=MESH,
                ).wait_recv()
                total[c % ring, block, :, :width] += landed[way, step, c % 2, :, :width]
                if c + 2 < count:
                    pl.semaphore_signal(
                        credit.at[way, step],
                        inc=1,
                        device_id={"dp": me - 2 + 4 * way},
                        device_id_type=MESH,
                    )

            @pl.when(line_sends(step, way))
            def _():
                line_copy(c, step, way).wait_send()

    def out_copy(c):
        left, right, first, width = plan[c]
        return pltpu.make_async_copy(
            total.at[c % ring, place, :, :width],
            outs[right].at[:, first : first + width],
            out_sem.at[c % ring],
        )

    compute(0)
    pair_copy(0).start()
    if count > 1:
        compute(1)
    for slot in range(count + steps + 1):
        for step in range(steps):
            c = slot - 2 - step
            if 0 <= c < count:
                line_finish(c, step)
        if 0 <= slot - 1 < count:
            pair_finish(slot - 1)
        for step in range(steps):
            c = slot - 1 - step
            if 0 <= c < count:
                line_start(c, step)
        if slot + 1 < count:
            pair_copy(slot + 1).start()
        done = slot - 1 - steps
        if 0 <= done < count:
            out_copy(done).start()
        if slot + 2 < count:
            if slot + 2 >= ring:
                out_copy(slot + 2 - ring).wait()
            compute(slot + 2)
    for c in range(max(0, count - ring), count):
        out_copy(c).wait()


def weight_scatter(lefts, rights, pairs, dp_count, collective_id):
    line = dp_count // 2
    tokens, depth = lefts[0].shape
    rows = depth // dp_count
    lefts = [left.T.reshape(line, 2, rows, tokens) for left in lefts]
    plan = []
    for left, right in pairs:
        width = rights[right].shape[1]
        for first in range(0, width, chunk_columns):
            plan.append((left, right, first, min(chunk_columns, width - first)))
    ring = line + 4
    wide = (line, rows, chunk_columns)
    flops = 2 * tokens * depth * sum(item[3] for item in plan)
    return pl.pallas_call(
        functools.partial(scatter_kernel, tuple(plan), line, len(lefts), len(rights)),
        out_shape=[
            jax.ShapeDtypeStruct((rows, right.shape[1]), jnp.float32) for right in rights
        ],
        in_specs=[pl.BlockSpec(memory_space=pltpu.VMEM)] * (len(lefts) + len(rights)),
        out_specs=[pl.BlockSpec(memory_space=pl.ANY)] * len(rights),
        scratch_shapes=[
            pltpu.VMEM((send_slots,) + wide, jnp.float32),
            pltpu.VMEM((held_slots,) + wide, jnp.float32),
            pltpu.VMEM((ring,) + wide, jnp.float32),
            pltpu.VMEM((2, line - 1, 2, rows, chunk_columns), jnp.float32),
            pltpu.SemaphoreType.DMA((send_slots,)),
            pltpu.SemaphoreType.DMA((held_slots,)),
            pltpu.SemaphoreType.DMA((2, line - 1, 2)),
            pltpu.SemaphoreType.DMA((2, line - 1, 2)),
            pltpu.SemaphoreType.REGULAR((2, line - 1)),
            pltpu.SemaphoreType.DMA((ring,)),
        ],
        compiler_params=pltpu.CompilerParams(
            collective_id=collective_id, has_side_effects=True, vmem_limit_bytes=48 * 1024 * 1024
        ),
        cost_estimate=pl.CostEstimate(flops=flops, bytes_accessed=flops // 16, transcendentals=0),
    )(*lefts, *rights)


def rms_back(incoming, values, inverse_root):
    return inverse_root * incoming - values * inverse_root**3 * jnp.mean(
        incoming * values, axis=-1, keepdims=True
    )


def root_of(values):
    return lax.rsqrt(jnp.mean(values * values, axis=-1, keepdims=True) + norm_epsilon)


def forward_kernel(
    lam, rows, gain, query_weight, key_weight, value_weight, cosine, sine, segment_column,
    segment_row, sub_scale, normed_one, query, key, value, mixed, heads_out,
):
    head_count, width = sub_scale.shape
    scale = (width // 2) ** (-0.5)
    values = rows[...].astype(jnp.float32)
    normed_one[...] = (values * root_of(values) * gain[...]).astype(jnp.bfloat16)
    raw_query = f32_dot(normed_one[...], query_weight[...])
    raw_key = f32_dot(normed_one[...], key_weight[...])
    value[...] = f32_dot(normed_one[...], value_weight[...]).astype(jnp.bfloat16)
    for head in range(head_count):
        at = slice(head * width, (head + 1) * width)
        query[:, at] = turn(raw_query[:, at], cosine[...], sine[...]).astype(jnp.bfloat16)
        key[:, at] = turn(raw_key[:, at], cosine[...], sine[...]).astype(jnp.bfloat16)
    for block in range(rows.shape[0] // block_rows):
        first, last = key_range(block)
        here = slice(block * block_rows, last)
        opened = open_pairs(block, segment_column, segment_row)
        for head in range(head_count):
            at = slice(head * width, (head + 1) * width)
            keys = key[first:last, at]
            maps = [softmax_map(map_of(query[here, at], c), keys, opened, scale) for c in range(2)]
            combined = (maps[0] - lam[head] * maps[1]).astype(jnp.bfloat16)
            out = f32_dot(combined, value[first:last, at])
            mixed[here, at] = out
            heads_out[here, at] = (out * root_of(out) * sub_scale[head : head + 1, :]).astype(
                jnp.bfloat16
            )


def backward_kernel(
    lam, grad_attended, out_weight, query, key, value, mixed, cosine, sine, segment_column,
    segment_row, sub_scale, grad_rows, grad_sub, grad_lam, grad_heads, grad_mixed, grad_key,
    grad_value,
):
    head_count, width = sub_scale.shape
    row_count = query.shape[0]
    inner = head_count * width
    scale = (width // 2) ** (-0.5)
    grad_heads[...] = dot_t(grad_attended[...], out_weight[...])
    for head in range(head_count):
        at = slice(head * width, (head + 1) * width)
        heads = mixed[:, at]
        root = root_of(heads)
        grads = grad_heads[:, at]
        grad_sub[head : head + 1, :] = jnp.sum(grads * heads * root, axis=0, keepdims=True) * (
            1.0 - lambda_base
        )
        grad_mixed[:, at] = rms_back(grads * sub_scale[head : head + 1, :], heads, root).astype(
            jnp.bfloat16
        )
    grad_key[...] = jnp.zeros_like(grad_key)
    grad_value[...] = jnp.zeros_like(grad_value)
    lam_sums = [0.0] * head_count
    for block in range(row_count // block_rows):
        first, last = key_range(block)
        here = slice(block * block_rows, last)
        opened = open_pairs(block, segment_column, segment_row)
        for head in range(head_count):
            at = slice(head * width, (head + 1) * width)
            keys = key[first:last, at]
            queries = [map_of(query[here, at], c) for c in range(2)]
            maps = [softmax_map(queries[c], keys, opened, scale) for c in range(2)]
            mixes = grad_mixed[here, at]
            combined = (maps[0] - lam[head] * maps[1]).astype(jnp.bfloat16)
            grad_value[first:last, at] += dot_rows(combined, mixes)
            grads = dot_t(mixes, value[first:last, at])
            first_sum = jnp.sum(grads * maps[0], axis=-1, keepdims=True)
            second_sum = jnp.sum(grads * maps[1], axis=-1, keepdims=True)
            lam_sums[head] = lam_sums[head] + jnp.sum(second_sum, axis=0, keepdims=True)
            score_grads = [
                (maps[0] * (grads - first_sum)).astype(jnp.bfloat16),
                (maps[1] * (-lam[head] * (grads - second_sum))).astype(jnp.bfloat16),
            ]
            grad_query = f32_dot(score_grads[0], map_of(keys, 0)) + f32_dot(
                score_grads[1], map_of(keys, 1)
            )
            grad_rows[here, at] = turn(
                grad_query * scale, cosine[here, :], -sine[here, :]
            ).astype(jnp.bfloat16)
            grad_key[first:last, at] += dot_rows(score_grads[0], queries[0]) + dot_rows(
                score_grads[1], queries[1]
            )
    for head in range(head_count):
        at = slice(head * width, (head + 1) * width)
        grad_rows[:, inner + head * width : inner + (head + 1) * width] = turn(
            grad_key[:, at] * scale, cosine[...], -sine[...]
        ).astype(jnp.bfloat16)
        grad_lam[head : head + 1, :] = jnp.broadcast_to(-lam_sums[head], (1, width))
    grad_rows[:, 2 * inner :] = grad_value[...].astype(jnp.bfloat16)


def in_vmem(count):
    return [pl.BlockSpec(memory_space=pltpu.VMEM)] * count


def attention_forward(row_in, tables, lam, sub_scale, norm1_gain, projections):
    row_count, depth = row_in.shape
    inner = projections[0].shape[1]
    narrow = jax.ShapeDtypeStruct((row_count, inner), jnp.bfloat16)
    return pl.pallas_call(
        forward_kernel,
        out_shape=[
            jax.ShapeDtypeStruct((row_count, depth), jnp.bfloat16),
            narrow,
            narrow,
            narrow,
            jax.ShapeDtypeStruct((row_count, inner), jnp.float32),
            narrow,
        ],
        in_specs=[pl.BlockSpec(memory_space=pltpu.SMEM)] + in_vmem(10),
        out_specs=in_vmem(6),
        compiler_params=pltpu.CompilerParams(vmem_limit_bytes=32 * 1024 * 1024),
        cost_estimate=pl.CostEstimate(
            flops=12 * row_count * depth * inner, bytes_accessed=8 << 20, transcendentals=0
        ),
    )(lam, row_in, norm1_gain[None, :], *projections, *tables, sub_scale)


def attention_backward(grad_attended, out_weight, kept, tables, lam, sub_scale):
    row_count, depth = grad_attended.shape
    head_count, width = sub_scale.shape
    inner = out_weight.shape[0]
    small = jax.ShapeDtypeStruct((head_count, width), jnp.float32)
    return pl.pallas_call(
        backward_kernel,
        out_shape=[jax.ShapeDtypeStruct((row_count, 3 * inner), jnp.bfloat16), small, small],
        in_specs=[pl.BlockSpec(memory_space=pltpu.SMEM)] + in_vmem(11),
        out_specs=in_vmem(3),
        scratch_shapes=[
            pltpu.VMEM((row_count, inner), jnp.float32),
            pltpu.VMEM((row_count, inner), jnp.bfloat16),
            pltpu.VMEM((row_count, inner), jnp.float32),
            pltpu.VMEM((row_count, inner), jnp.float32),
        ],
        compiler_params=pltpu.CompilerParams(vmem_limit_bytes=32 * 1024 * 1024),
        cost_estimate=pl.CostEstimate(
            flops=12 * row_count * depth * inner, bytes_accessed=8 << 20, transcendentals=0
        ),
    )(lam, grad_attended, out_weight, *kept, *tables, sub_scale)


def through_projections(grad_rows, projections, core):
    inner = projections[0].shape[1]

    def partial(which):
        rows = half_rows(grad_rows, which)
        return sum(
            dot_t(rows[:, i * inner : (i + 1) * inner], projections[i]) for i in range(3)
        )

    return partial(core), partial(1 - core)


def feed_forward(normed_two, cot_rows, gate_weight, up_weight, down_weight):
    half = normed_two.shape[0] // 2
    gate_pre = f32_dot(normed_two, gate_weight)
    upward = f32_dot(normed_two, up_weight)
    sigmoid_gate = jax.nn.sigmoid(gate_pre)
    hidden = (gate_pre * sigmoid_gate * upward).astype(jnp.bfloat16)
    grad_hidden = dot_t(cot_rows, down_weight)
    grad_gate_pre = (
        grad_hidden * upward * sigmoid_gate * (1.0 + gate_pre * (1.0 - sigmoid_gate))
    ).astype(jnp.bfloat16)
    grad_up_pre = (grad_hidden * gate_pre * sigmoid_gate).astype(jnp.bfloat16)

    def back(at):
        return dot_t(grad_gate_pre[at], gate_weight) + dot_t(grad_up_pre[at], up_weight)

    send_back = back(slice(half, None))
    keep_back = back(slice(0, half))
    send_fed = f32_dot(hidden[half:], down_weight)
    keep_fed = f32_dot(hidden[:half], down_weight)
    return (keep_back, send_back), (keep_fed, send_fed), hidden, grad_gate_pre, grad_up_pre


def on_device(
    layer_in,
    short_lengths,
    long_lengths,
    norm1_gain,
    query_weight,
    key_weight,
    value_weight,
    lambda_param,
    sub_gain,
    out_weight,
    norm2_gain,
    gate_weight,
    up_weight,
    down_weight,
    out_cotangent,
):
    dp_count = lax.axis_size("dp")
    core = lax.axis_index("tensor") % 2
    head_count, lambda_width = lambda_param.shape
    doc_lengths = (short_lengths[0], long_lengths[0])
    map_width = lambda_width // 4
    projections = (query_weight, key_weight, value_weight)
    lambda_parts = lambda_param.reshape(head_count, 4, map_width)
    first_exp = jnp.exp(jnp.sum(lambda_parts[:, 0] * lambda_parts[:, 1], axis=-1))
    second_exp = jnp.exp(jnp.sum(lambda_parts[:, 2] * lambda_parts[:, 3], axis=-1))
    lam = first_exp - second_exp + lambda_base
    sub_scale = sub_gain * (1.0 - lambda_base)
    tables = []
    for m in range(2):
        position, segment = doc_tables(doc_lengths[m], layer_in.shape[1])
        tables.append(
            rotary_tables(position, map_width) + (segment[:, None], segment[None, :])
        )
    cots = [mine_first(out_cotangent[m], core) for m in range(2)]
    half = cots[0].shape[0] // 2
    rows_in = [mine_first(layer_in[m], core).astype(jnp.float32) for m in range(2)]
    inputs = [rows_in[m][:half] for m in range(2)]
    front = [
        attention_forward(layer_in[m], tables[m], lam, sub_scale, norm1_gain, projections)
        for m in range(2)
    ]
    heads = [front[m][5] for m in range(2)]
    attended, middle, root_two, normed_two, ffn = [], [], [], [], []
    for m in range(2):
        keep = f32_dot(half_rows(heads[m], core), out_weight)
        send = f32_dot(half_rows(heads[m], 1 - core), out_weight)
        attended.append(tensor_sum(keep, send))
        middle.append(inputs[m] + attended[m])
        root_two.append(root_of(middle[m]))
        normed_two.append((with_other(middle[m] * root_two[m]) * norm2_gain).astype(jnp.bfloat16))
        ffn.append(feed_forward(normed_two[m], cots[m], gate_weight, up_weight, down_weight))
    both = lambda index: jnp.concatenate([ffn[0][index], ffn[1][index]], 0)
    grad_down, grad_gate, grad_up = weight_scatter(
        [jnp.concatenate(cots, 0), jnp.concatenate(normed_two, 0)],
        [both(2), both(3), both(4)],
        [(0, 0), (1, 1), (1, 2)],
        dp_count,
        0,
    )
    grad_norm2 = 0.0
    grad_norm1 = 0.0
    through_two, grad_attended, back = [], [], []
    for m in range(2):
        grad_normed_two = tensor_sum(*ffn[m][0])
        grad_norm2 = grad_norm2 + jnp.sum(grad_normed_two * middle[m] * root_two[m], axis=0)
        through_two.append(rms_back(grad_normed_two * norm2_gain, middle[m], root_two[m]))
        grad_middle = cots[m].astype(jnp.float32) + with_other(through_two[m])
        grad_attended.append(in_order(grad_middle, core).astype(jnp.bfloat16))
        back.append(
            attention_backward(
                grad_attended[m], out_weight, front[m][1:5], tables[m], lam, sub_scale
            )
        )
    grad_out, grad_qkv = weight_scatter(
        [jnp.concatenate(grad_attended, 0), jnp.concatenate([front[0][0], front[1][0]], 0)],
        [jnp.concatenate(heads, 0), jnp.concatenate([back[0][0], back[1][0]], 0)],
        [(0, 0), (1, 1)],
        dp_count,
        1,
    )
    grad_query, grad_key, grad_value = jnp.split(grad_qkv, 3, axis=1)
    out_blocks, grad_blocks = [], []
    for m in range(2):
        fed = tensor_sum(*ffn[m][1])
        out_rows = rows_in[m] + with_other(attended[m] + fed)
        out_blocks.append(in_order(out_rows, core).astype(jnp.bfloat16))
        grad_normed_one = tensor_sum(*through_projections(back[m][0], projections, core))
        root_one = root_of(inputs[m])
        grad_norm1 = grad_norm1 + jnp.sum(grad_normed_one * inputs[m] * root_one, axis=0)
        through = through_two[m] + rms_back(grad_normed_one * norm1_gain, inputs[m], root_one)
        grad_rows = cots[m].astype(jnp.float32) + with_other(through)
        grad_blocks.append(in_order(grad_rows, core).astype(jnp.bfloat16))
    norms = jnp.stack([grad_norm1, grad_norm2])
    norms = norms + flip(norms, "tensor", 1)
    grad_lam = (back[0][2] + back[1][2])[:, :1]
    first_scale = grad_lam * first_exp[:, None]
    second_scale = grad_lam * second_exp[:, None]
    lambda_grad = jnp.concatenate(
        [
            first_scale * lambda_parts[:, 1],
            first_scale * lambda_parts[:, 0],
            -second_scale * lambda_parts[:, 3],
            -second_scale * lambda_parts[:, 2],
        ],
        axis=1,
    )
    small = [norms, lambda_grad, back[0][1] + back[1][1]]
    width = norms.shape[-1]
    packed = jnp.concatenate(
        [
            part.reshape(part.shape[0], dp_count, -1).transpose(1, 0, 2).reshape(dp_count, -1)
            for part in small
        ],
        axis=1,
    )
    pairs = packed.reshape(dp_count // 2, 2, 1, -1)
    side = lax.axis_index("dp") % 2
    send = lax.dynamic_index_in_dim(pairs, 1 - side, 1, keepdims=False)
    keep = lax.dynamic_index_in_dim(pairs, side, 1, keepdims=False)
    small_sum = line_scatter(keep + flip(send, "dp", 1), dp_count)[0]
    sizes = [2 * width // dp_count, head_count * lambda_width // dp_count]
    norm_sum, lambda_sum, sub_sum = jnp.split(small_sum, [sizes[0], sizes[0] + sizes[1]])
    norm_sum = norm_sum.reshape(2, -1)
    return (
        jnp.stack(out_blocks),
        jnp.stack(grad_blocks),
        norm_sum[0],
        grad_query,
        grad_key,
        grad_value,
        lambda_sum.reshape(head_count, -1),
        sub_sum.reshape(head_count, -1),
        grad_out.T,
        norm_sum[1],
        grad_gate,
        grad_up,
        grad_down.T,
    )


def solution(mesh):
    return jax.shard_map(
        on_device,
        mesh=mesh,
        in_specs=(
            P(None, "dp", None),
            P("dp", None),
            P("dp", None),
            P(),
            P(None, "tensor"),
            P(None, "tensor"),
            P(None, "tensor"),
            P("tensor", None),
            P("tensor", None),
            P("tensor", None),
            P(),
            P(None, "tensor"),
            P(None, "tensor"),
            P("tensor", None),
            P(None, "dp", None),
        ),
        out_specs=(
            P(None, "dp", None),
            P(None, "dp", None),
            P("dp"),
            P("dp", "tensor"),
            P("dp", "tensor"),
            P("dp", "tensor"),
            P("tensor", "dp"),
            P("tensor", "dp"),
            P("tensor", "dp"),
            P("dp"),
            P("dp", "tensor"),
            P("dp", "tensor"),
            P("tensor", "dp"),
        ),
        check_vma=False,
    )
```

```python
import functools
import math

import jax
import jax.numpy as jnp
from jax import lax
from jax.experimental import pallas as pl
from jax.experimental.pallas import tpu as pltpu
from jax.sharding import PartitionSpec as P

norm_epsilon = 1e-05
lambda_base = 0.8 - 0.6 * math.exp(-0.3 * 11.0)
rotary_base = 10000.0
closed_score = -1e30
block_rows = 128
longest_document = 256
row_group = 16
send_slots = 3
held_slots = 4
MESH = pl.DeviceIdType.MESH


def doc_tables(lengths, row_count):
    doc_ends = jnp.cumsum(lengths, dtype=jnp.int32)
    places = jnp.arange(row_count, dtype=jnp.int32)
    passed = (places[:, None] >= doc_ends[None, :]).astype(jnp.int32)
    segment = jnp.sum(passed, axis=1, dtype=jnp.int32)
    starts = jnp.sum(passed * lengths[None, :], axis=1, dtype=jnp.int32)
    return (places - starts, segment)


def rotary_tables(position, map_width):
    half_width = map_width // 2
    frequency = rotary_base ** (-2.0 * jnp.arange(half_width, dtype=jnp.float32) / map_width)
    angles = position.astype(jnp.float32)[:, None] * frequency[None, :]
    cosine, sine = jnp.cos(angles), jnp.sin(angles)
    return (
        jnp.concatenate([cosine] * 4, axis=1),
        jnp.concatenate([-sine, sine, -sine, sine], axis=1),
    )


def turn(values, cosine, sine):
    width = values.shape[-1]
    quarter = width // 4
    lane = lax.broadcasted_iota(jnp.int32, values.shape, 1)
    partner = jnp.where(
        lane % (2 * quarter) < quarter,
        pltpu.roll(values, width - quarter, 1),
        pltpu.roll(values, quarter, 1),
    )
    return values * cosine + partner * sine


def map_of(values, which):
    lane = lax.broadcasted_iota(jnp.int32, values.shape, 1)
    mine = (lane >= values.shape[-1] // 2) == (which == 1)
    return jnp.where(mine, values, jnp.zeros_like(values))


def key_range(block):
    first = max(0, block * block_rows - longest_document + 1) // block_rows * block_rows
    return first, (block + 1) * block_rows


def open_pairs(block, segment_column, segment_row):
    first, last = key_range(block)
    rows = pl.ds(block * block_rows, block_rows)
    shape = (block_rows, last - first)
    row_at = lax.broadcasted_iota(jnp.int32, shape, 0) + block * block_rows
    key_at = lax.broadcasted_iota(jnp.int32, shape, 1) + first
    return (segment_column[rows, :] == segment_row[:, first:last]) & (key_at <= row_at)


def softmax_map(query, key, opened, scale):
    scores = jnp.where(opened, dot_t(query, key) * scale, closed_score)
    expanded = jnp.exp(scores - jnp.max(scores, axis=-1, keepdims=True))
    return expanded * (1.0 / jnp.sum(expanded, axis=-1, keepdims=True))


def f32_dot(left, right):
    return jnp.dot(left, right, preferred_element_type=jnp.float32)


def dot_t(left, right):
    return lax.dot_general(
        left, right, (((1,), (1,)), ((), ())), preferred_element_type=jnp.float32
    )


def dot_rows(left, right):
    return lax.dot_general(
        left, right, (((0,), (0,)), ((), ())), preferred_element_type=jnp.float32
    )


def flip(values, axis_name, bit):
    size = lax.axis_size(axis_name)
    return lax.ppermute(values, axis_name, [(i, i ^ bit) for i in range(size)])


def half_rows(values, which):
    count = values.shape[0] // 2
    return lax.dynamic_slice_in_dim(values, which * count, count, 0)


def mine_first(values, core):
    return jnp.concatenate([half_rows(values, core), half_rows(values, 1 - core)], axis=0)


def tensor_sum(keep, send):
    half = keep + flip(send, "tensor", 1)
    return half + flip(half, "tensor", 2)


def with_other(mine):
    return jnp.concatenate([mine, flip(mine, "tensor", 1)], axis=0)


def rms_back(incoming, values, inverse_root):
    return inverse_root * incoming - values * inverse_root**3 * jnp.mean(
        incoming * values, axis=-1, keepdims=True
    )


def root_of(values):
    return lax.rsqrt(jnp.mean(values * values, axis=-1, keepdims=True) + norm_epsilon)


def forward_kernel(
    lam, rows, gain, query_weight, key_weight, value_weight, cosine, sine, segment_column,
    segment_row, sub_scale, normed_one, query, key, value, mixed, heads_out,
):
    head_count, width = sub_scale.shape
    scale = (width // 2) ** (-0.5)
    values = rows[...].astype(jnp.float32)
    normed_one[...] = (values * root_of(values) * gain[...]).astype(jnp.bfloat16)
    raw_query = f32_dot(normed_one[...], query_weight[...])
    raw_key = f32_dot(normed_one[...], key_weight[...])
    value[...] = f32_dot(normed_one[...], value_weight[...]).astype(jnp.bfloat16)
    for head in range(head_count):
        at = slice(head * width, (head + 1) * width)
        query[:, at] = turn(raw_query[:, at], cosine[...], sine[...]).astype(jnp.bfloat16)
        key[:, at] = turn(raw_key[:, at], cosine[...], sine[...]).astype(jnp.bfloat16)
    for block in range(rows.shape[0] // block_rows):
        first, last = key_range(block)
        here = slice(block * block_rows, last)
        opened = open_pairs(block, segment_column, segment_row)
        for head in range(head_count):
            at = slice(head * width, (head + 1) * width)
            keys = key[first:last, at]
            maps = [softmax_map(map_of(query[here, at], c), keys, opened, scale) for c in range(2)]
            combined = (maps[0] - lam[head] * maps[1]).astype(jnp.bfloat16)
            out = f32_dot(combined, value[first:last, at])
            mixed[here, at] = out
            heads_out[here, at] = (out * root_of(out) * sub_scale[head : head + 1, :]).astype(
                jnp.bfloat16
            )


def backward_kernel(
    lam, grad_attended, out_weight, query, key, value, mixed, cosine, sine, segment_column,
    segment_row, sub_scale, grad_rows, grad_sub, grad_lam, grad_heads, grad_mixed, grad_key,
    grad_value,
):
    head_count, width = sub_scale.shape
    row_count = query.shape[0]
    inner = head_count * width
    scale = (width // 2) ** (-0.5)
    grad_heads[...] = dot_t(grad_attended[...], out_weight[...])
    for head in range(head_count):
        at = slice(head * width, (head + 1) * width)
        heads = mixed[:, at]
        root = root_of(heads)
        grads = grad_heads[:, at]
        grad_sub[head : head + 1, :] = jnp.sum(grads * heads * root, axis=0, keepdims=True) * (
            1.0 - lambda_base
        )
        grad_mixed[:, at] = rms_back(grads * sub_scale[head : head + 1, :], heads, root).astype(
            jnp.bfloat16
        )
    grad_key[...] = jnp.zeros_like(grad_key)
    grad_value[...] = jnp.zeros_like(grad_value)
    lam_sums = [0.0] * head_count
    for block in range(row_count // block_rows):
        first, last = key_range(block)
        here = slice(block * block_rows, last)
        opened = open_pairs(block, segment_column, segment_row)
        for head in range(head_count):
            at = slice(head * width, (head + 1) * width)
            keys = key[first:last, at]
            queries = [map_of(query[here, at], c) for c in range(2)]
            maps = [softmax_map(queries[c], keys, opened, scale) for c in range(2)]
            mixes = grad_mixed[here, at]
            combined = (maps[0] - lam[head] * maps[1]).astype(jnp.bfloat16)
            grad_value[first:last, at] += dot_rows(combined, mixes)
            grads = dot_t(mixes, value[first:last, at])
            first_sum = jnp.sum(grads * maps[0], axis=-1, keepdims=True)
            second_sum = jnp.sum(grads * maps[1], axis=-1, keepdims=True)
            lam_sums[head] = lam_sums[head] + jnp.sum(second_sum, axis=0, keepdims=True)
            score_grads = [
                (maps[0] * (grads - first_sum)).astype(jnp.bfloat16),
                (maps[1] * (-lam[head] * (grads - second_sum))).astype(jnp.bfloat16),
            ]
            grad_query = f32_dot(score_grads[0], map_of(keys, 0)) + f32_dot(
                score_grads[1], map_of(keys, 1)
            )
            grad_rows[here, at] = turn(
                grad_query * scale, cosine[here, :], -sine[here, :]
            ).astype(jnp.bfloat16)
            grad_key[first:last, at] += dot_rows(score_grads[0], queries[0]) + dot_rows(
                score_grads[1], queries[1]
            )
    for head in range(head_count):
        at = slice(head * width, (head + 1) * width)
        grad_rows[:, inner + head * width : inner + (head + 1) * width] = turn(
            grad_key[:, at] * scale, cosine[...], -sine[...]
        ).astype(jnp.bfloat16)
        grad_lam[head : head + 1, :] = jnp.broadcast_to(-lam_sums[head], (1, width))
    grad_rows[:, 2 * inner :] = grad_value[...].astype(jnp.bfloat16)


def in_vmem(count):
    return [pl.BlockSpec(memory_space=pltpu.VMEM)] * count


class Reducer:
    def __init__(self, plan, line, refs):
        self.plan, self.line = plan, line
        (
            self.send, self.held, self.total, self.landed, self.pair_out, self.pair_in,
            self.line_out, self.line_in, self.credit, self.out_sem,
        ) = refs
        self.me = lax.axis_index("dp")
        self.place, self.side = self.me // 2, self.me % 2
        self.other = self.me + 1 - 2 * self.side
        self.steps = line - 1
        self.ring = self.total.shape[0]
        self.rows = self.total.shape[2]

    def compute(self, c):
        item = self.plan[c]
        width = item.width
        left, right = item.left(), item.right()

        def block(at, carry):
            first = pl.multiple_of(2 * at * self.rows, self.rows)
            columns = right[...]
            away = left[pl.ds(first + (1 - self.side) * self.rows, self.rows), :]
            here = left[pl.ds(first + self.side * self.rows, self.rows), :]
            self.send[c % send_slots, at, :, :width] = f32_dot(away, columns)
            self.total[c % self.ring, at, :, :width] = f32_dot(here, columns)
            return carry

        lax.fori_loop(0, self.line, block, 0)
        item.computed()

    def pair_copy(self, c):
        width = self.plan[c].width
        return pltpu.make_async_remote_copy(
            src_ref=self.send.at[c % send_slots, :, :, :width],
            dst_ref=self.held.at[c % held_slots, :, :, :width],
            send_sem=self.pair_out.at[c % send_slots],
            recv_sem=self.pair_in.at[c % held_slots],
            device_id={"dp": self.other},
            device_id_type=MESH,
        )

    def pair_finish(self, c):
        width = self.plan[c].width
        self.pair_copy(c).wait_recv()

        def block(at, carry):
            self.total[c % self.ring, at, :, :width] += self.held[c % held_slots, at, :, :width]
            return carry

        lax.fori_loop(0, self.line, block, 0)
        self.pair_copy(c).wait_send()

    def line_copy(self, c, step, way, block, target):
        width = self.plan[c].width
        return pltpu.make_async_remote_copy(
            src_ref=self.total.at[c % self.ring, block, :, :width],
            dst_ref=self.landed.at[way, step, c % 2, :, :width],
            send_sem=self.line_out.at[way, step, c % 2],
            recv_sem=self.line_in.at[way, step, c % 2],
            device_id={"dp": target},
            device_id_type=MESH,
        )

    def line_sends(self, step, way):
        place, line = self.place, self.line
        if way == 0:
            block = line - 1 - step + place
            return (place <= step) & (place < line - 1), block, self.me + 2
        block = place + step - line + 1
        return (place >= line - 1 - step) & (place > 0), block, self.me - 2

    def line_gets(self, step, way):
        place, line = self.place, self.line
        if way == 0:
            return (place > 0) & (place - 1 <= step), line - 2 - step + place, self.me - 2
        gets = (place < line - 1) & (place + 1 >= line - 1 - step)
        return gets, place + step - line + 2, self.me + 2

    def line_start(self, c, step):
        for way in range(2):
            sends, block, target = self.line_sends(step, way)

            @pl.when(sends)
            def _():
                if c >= 2:
                    pl.semaphore_wait(self.credit.at[way, step], 1)
                self.line_copy(c, step, way, block, target).start()

    def line_finish(self, c, step):
        width = self.plan[c].width
        for way in range(2):
            gets, block, source = self.line_gets(step, way)

            @pl.when(gets)
            def _():
                self.line_copy(c, step, way, block, source).wait_recv()
                self.total[c % self.ring, block, :, :width] += self.landed[
                    way, step, c % 2, :, :width
                ]
                if c + 2 < len(self.plan):
                    pl.semaphore_signal(
                        self.credit.at[way, step],
                        inc=1,
                        device_id={"dp": source},
                        device_id_type=MESH,
                    )

            sends, sent, target = self.line_sends(step, way)

            @pl.when(sends)
            def _():
                self.line_copy(c, step, way, sent, target).wait_send()

    def out_copy(self, c):
        item = self.plan[c]
        return pltpu.make_async_copy(
            self.total.at[c % self.ring, self.place, :, : item.width],
            item.out.at[:, item.first : item.first + item.width],
            self.out_sem.at[c % self.ring],
        )

    def run(self, tasks):
        count, steps = len(self.plan), self.steps
        self.compute(0)
        self.pair_copy(0).start()
        self.compute(1)
        for slot in range(count + steps + 1):
            for step in range(steps):
                c = slot - 2 - step
                if 0 <= c < count:
                    self.line_finish(c, step)
            if 0 <= slot - 1 < count:
                self.pair_finish(slot - 1)
            for step in range(steps):
                c = slot - 1 - step
                if 0 <= c < count:
                    self.line_start(c, step)
            if slot + 1 < count:
                self.pair_copy(slot + 1).start()
            done = slot - 1 - steps
            if 0 <= done < count:
                self.out_copy(done).start()
            if slot + 2 < count:
                if slot + 2 >= self.ring:
                    self.out_copy(slot + 2 - self.ring).wait()
                self.compute(slot + 2)
            for task in tasks.get(slot, ()):
                task()
        for c in range(max(0, count - self.ring), count):
            self.out_copy(c).wait()


class Chunk:
    def __init__(self, left, right, computed, out, first, width):
        self.left, self.right, self.computed = left, right, computed
        self.out, self.first, self.width = out, first, width


def for_rows(count, body):
    def step(i, carry):
        body(pl.ds(pl.multiple_of(i * row_group, row_group), row_group))
        return carry

    lax.fori_loop(0, count // row_group, step, 0)


class TensorSum:
    def __init__(self, uses, own, near, far, near_sems, far_sems, near_credit, far_credit):
        self.own, self.near, self.far = own, near, far
        self.near_sems, self.far_sems = near_sems, far_sems
        self.near_credit, self.far_credit = near_credit, far_credit
        index = lax.axis_index("tensor")
        self.core_peer = index + 1 - 2 * (index % 2)
        self.far_peer = index + 2 - 4 * (index // 2)
        self.near_left, self.far_left = 2 * uses, uses
        self.near_first, self.far_first = True, True

    def near_copy(self, source):
        return pltpu.make_async_remote_copy(
            src_ref=source, dst_ref=self.near, send_sem=self.near_sems.at[0],
            recv_sem=self.near_sems.at[1], device_id={"tensor": self.core_peer},
            device_id_type=MESH,
        )

    def far_copy(self):
        return pltpu.make_async_remote_copy(
            src_ref=self.own, dst_ref=self.far, send_sem=self.far_sems.at[0],
            recv_sem=self.far_sems.at[1], device_id={"tensor": self.far_peer},
            device_id_type=MESH,
        )

    def near_start(self, source):
        if not self.near_first:
            pl.semaphore_wait(self.near_credit, 1)
        self.near_first = False
        self.pending = source
        self.near_copy(source).start()

    def near_wait(self):
        self.near_copy(self.pending).wait()

    def near_free(self):
        self.near_left -= 1
        if self.near_left:
            pl.semaphore_signal(
                self.near_credit, inc=1, device_id={"tensor": self.core_peer}, device_id_type=MESH
            )

    def far_start(self):
        self.near_wait()

        def add(rows):
            self.own[rows, :] += self.near[rows, :]

        for_rows(self.own.shape[0], add)
        self.near_free()
        if not self.far_first:
            pl.semaphore_wait(self.far_credit, 1)
        self.far_first = False
        self.far_copy().start()

    def far_wait(self):
        self.far_copy().wait()

    def far_free(self):
        self.far_left -= 1
        if self.far_left:
            pl.semaphore_signal(
                self.far_credit, inc=1, device_id={"tensor": self.far_peer}, device_id_type=MESH
            )


def back_kernel(dp_count, *refs):
    refs = list(refs)
    take = lambda n: [refs.pop(0) for _ in range(n)]
    (lam,) = take(1)
    cot_left, two_left, one_left = [take(2) for _ in range(3)]
    hidden, gate_pre, up_pre, heads = [take(2) for _ in range(4)]
    keep_back, send_back, keep_fed, send_fed, middle = [take(2) for _ in range(5)]
    (layer_in, cotangent) = take(2)
    weights_in = take(4)
    kept_in = [take(4) for _ in range(2)]
    tables = [take(4) for _ in range(2)]
    (sub_scale, gain_one, gain_two) = take(3)
    (grad_down, grad_gate, grad_up, grad_out, grad_qkv, layer_out, grad_in, small_out) = take(8)
    reducer_refs = take(10)
    (left_a, left_b, rights, rows_qkv) = take(4)
    weights = take(4)
    kept = [take(4) for _ in range(2)]
    backward_scratch = take(4)
    (grad_sub, grad_lam) = take(2)
    sets = [take(3) for _ in range(2)]
    through = take(2)
    (spare, projected, attended, rows_in, rows_out) = take(5)
    (small, small_near, small_landed) = take(3)
    (near_sems, far_sems, near_credit, far_credit) = take(4)
    (load_sems, small_near_sems, small_send, small_recv) = take(4)
    assert not refs

    me = lax.axis_index("dp")
    tensor = lax.axis_index("tensor")
    core = tensor % 2
    core_peer = tensor + 1 - 2 * core
    far_peer = tensor + 2 - 4 * (tensor // 2)
    line = dp_count // 2
    half = middle[0].shape[0]
    row_count = 2 * half
    head_count, head_width = sub_scale.shape
    out_weight, projections = weights[0], weights[1:]
    inner = out_weight.shape[0]
    tokens = [slice(m * row_count, (m + 1) * row_count) for m in range(2)]

    barrier = pltpu.get_barrier_semaphore()
    for offset in range(1, dp_count):
        pl.semaphore_signal(
            barrier, inc=1, device_id={"dp": lax.rem(me + offset, dp_count)}, device_id_type=MESH
        )
    for peer in (core_peer, far_peer):
        pl.semaphore_signal(barrier, inc=1, device_id={"tensor": peer}, device_id_type=MESH)
    pl.semaphore_wait(barrier, dp_count + 1)

    used = [0]

    def load(source, target):
        copy = pltpu.make_async_copy(source, target, load_sems.at[used[0]])
        used[0] += 1
        copy.start()
        return copy

    def wait_all(copies):
        for copy in copies:
            copy.wait()

    reducer_width = reducer_refs[0].shape[-1]
    plan, sources, left_loads, right_loads = [], {}, {}, {}

    def load_left(sources_of, left):
        return [load(sources_of[m], left.at[:, tokens[m]]) for m in range(2)]

    def load_right(c):
        if c in sources:
            source, first, width = sources[c]
            right_loads[c] = [
                load(source[m].at[:, first : first + width], rights.at[c % 2, tokens[m], :width])
                for m in range(2)
            ]

    def get_left(c, left):
        wait_all(left_loads.pop(c, ()))
        return left

    def get_right(c, first, width):
        if c in sources:
            wait_all(right_loads[c])
            return rights.at[c % 2, :, :width]
        return rows_qkv.at[:, first : first + width]

    def computed(c):
        load_right(c + 2)
        if c == last_two:
            left_loads[first_one] = load_left(one_left, left_b)

    def add_group(left, source, columns, out):
        for first in range(0, columns, reducer_width):
            width = min(reducer_width, columns - first)
            c = len(plan)
            if source is not None:
                sources[c] = (source, first, width)
            plan.append(
                Chunk(
                    functools.partial(get_left, c, left),
                    functools.partial(get_right, c, first, width),
                    functools.partial(computed, c),
                    out,
                    first,
                    width,
                )
            )

    add_group(left_a, hidden, hidden[0].shape[1], grad_down)
    first_two = len(plan)
    add_group(left_b, gate_pre, gate_pre[0].shape[1], grad_gate)
    add_group(left_b, up_pre, up_pre[0].shape[1], grad_up)
    last_two = len(plan) - 1
    add_group(left_a, heads, inner, grad_out)
    first_one = len(plan)
    add_group(left_b, None, 3 * inner, grad_qkv)

    left_loads[0] = load_left(cot_left, left_a)
    load_right(0)
    load_right(1)
    sums = [
        TensorSum(
            3, *sets[m], near_sems.at[m], far_sems.at[m], near_credit.at[m], far_credit.at[m]
        )
        for m in range(2)
    ]
    own_loads = {}
    for m in range(2):
        own_loads[m] = load(keep_back[m], sets[m][0])
        sums[m].near_start(send_back[m])
    left_loads[first_two] = load_left(two_left, left_b)
    weight_loads = [load(*pair) for pair in zip(weights_in, weights)]
    kept_loads = [[load(*pair) for pair in zip(kept_in[m], kept[m])] for m in range(2)]
    spare_queue = [middle[0], middle[1], middle[0], middle[1]]
    rows_queue = [cotangent.at[0], cotangent.at[1]]
    rows_queue += [layer_in.at[0], cotangent.at[0], layer_in.at[1], cotangent.at[1]]
    queued = {}

    def next_spare():
        queued["spare"] = load(spare_queue.pop(0), spare) if spare_queue else None

    def next_rows():
        queued["rows"] = load(rows_queue.pop(0), rows_in) if rows_queue else None

    next_spare()
    next_rows()
    out_loads = []
    small[...] = jnp.zeros_like(small)

    def mine(rows):
        return pl.ds(pl.multiple_of(core * half + rows.start, row_group), row_group)

    def others(rows):
        return pl.ds(pl.multiple_of((1 - core) * half + rows.start, row_group), row_group)

    def exchange(m):
        if m in own_loads:
            own_loads.pop(m).wait()
        sums[m].far_start()

    def norm_two(m):
        own, near, far = sets[m]
        queued["spare"].wait()
        sums[m].far_wait()

        def body(rows):
            grads = own[rows, :] + far[rows, :]
            values = spare[rows, :]
            root = root_of(values)
            small[1:2, :] += jnp.sum(grads * values * root, axis=0, keepdims=True)
            through[m][rows, :] = rms_back(grads * gain_two[...], values, root)

        for_rows(half, body)
        sums[m].far_free()
        sums[m].near_start(through[m])
        next_spare()

    def attend(m):
        near = sets[m][1]
        queued["rows"].wait()
        sums[m].near_wait()

        def body(rows):
            attended[mine(rows), :] = (
                rows_in[mine(rows), :].astype(jnp.float32) + through[m][rows, :]
            ).astype(jnp.bfloat16)
            attended[others(rows), :] = (
                rows_in[others(rows), :].astype(jnp.float32) + near[rows, :]
            ).astype(jnp.bfloat16)

        for_rows(half, body)
        sums[m].near_free()
        next_rows()

        def flip_block(i, carry):
            at = pl.ds(pl.multiple_of(i * 128, 128), 128)
            left_a[at, tokens[m]] = attended[:, at].T
            return carry

        lax.fori_loop(0, attended.shape[1] // 128, flip_block, 0)
        if m == 0:
            wait_all(weight_loads)
        wait_all(kept_loads[m])
        backward_kernel(
            lam, attended, out_weight, *kept[m], *tables[m], sub_scale,
            rows_qkv.at[tokens[m], :], grad_sub, grad_lam, *backward_scratch,
        )
        for head in range(head_count):
            at = slice(head * head_width, (head + 1) * head_width)
            small[2:3, at] += grad_sub[head : head + 1, :]
            small[3:4, at] += grad_lam[head : head + 1, :]

    def project(m):
        def part(which, target):
            rows = pl.ds(pl.multiple_of(m * row_count + which * half, half), half)

            def block(i, carry):
                at = pl.ds(pl.multiple_of(i * 512, 512), 512)
                total = 0.0
                for p in range(3):
                    grads = rows_qkv[rows, p * inner : (p + 1) * inner]
                    total = total + dot_t(grads, projections[p][at, :])
                target[:, at] = total
                return carry

            lax.fori_loop(0, target.shape[1] // 512, block, 0)

        part(1 - core, projected)
        sums[m].near_start(projected)
        part(core, sets[m][0])

    def norm_one(m):
        own, near, far = sets[m]
        queued["rows"].wait()
        sums[m].far_wait()

        def body(rows):
            grads = own[rows, :] + far[rows, :]
            values = rows_in[mine(rows), :].astype(jnp.float32)
            root = root_of(values)
            small[0:1, :] += jnp.sum(grads * values * root, axis=0, keepdims=True)
            through[m][rows, :] += rms_back(grads * gain_one[...], values, root)

        for_rows(half, body)
        sums[m].far_free()
        sums[m].near_start(through[m])
        next_rows()
        own_loads[m] = load(keep_fed[m], own)

    def store_rows(target):
        out_loads.append(load(rows_out, target))

    def finish_in(m):
        near = sets[m][1]
        queued["rows"].wait()
        sums[m].near_wait()
        wait_all(out_loads)
        out_loads.clear()

        def body(rows):
            rows_out[mine(rows), :] = (
                rows_in[mine(rows), :].astype(jnp.float32) + through[m][rows, :]
            ).astype(jnp.bfloat16)
            rows_out[others(rows), :] = (
                rows_in[others(rows), :].astype(jnp.float32) + near[rows, :]
            ).astype(jnp.bfloat16)

        for_rows(half, body)
        sums[m].near_free()
        next_rows()
        store_rows(grad_in.at[m])
        sums[m].near_start(send_fed[m])

    def add_fed(m):
        own, near, far = sets[m]
        queued["spare"].wait()
        sums[m].far_wait()

        def body(rows):
            own[rows, :] = spare[rows, :] + (own[rows, :] + far[rows, :])

        for_rows(half, body)
        sums[m].far_free()
        sums[m].near_start(own)
        next_spare()

    def finish_out(m):
        own, near = sets[m][:2]
        sums[m].near_wait()
        wait_all(out_loads)
        out_loads.clear()

        def body(rows):
            rows_out[mine(rows), :] = own[rows, :].astype(jnp.bfloat16)
            rows_out[others(rows), :] = near[rows, :].astype(jnp.bfloat16)

        for_rows(half, body)
        sums[m].near_free()
        store_rows(layer_out.at[m])

    small_core = pltpu.make_async_remote_copy(
        src_ref=small, dst_ref=small_near, send_sem=small_near_sems.at[0],
        recv_sem=small_near_sems.at[1], device_id={"tensor": core_peer}, device_id_type=MESH,
    )

    def small_copy(offset):
        return pltpu.make_async_remote_copy(
            src_ref=small, dst_ref=small_landed.at[offset - 1], send_sem=small_send.at[offset - 1],
            recv_sem=small_recv.at[offset - 1],
            device_id={"dp": lax.rem(me + offset, dp_count)}, device_id_type=MESH,
        )

    def small_spread():
        small_core.wait()
        small[0:2, :] += small_near[0:2, :]
        for offset in range(1, dp_count):
            small_copy(offset).start()

    def small_finish():
        for offset in range(1, dp_count):
            small_copy(offset).wait()
        total = small[...]
        for offset in range(1, dp_count):
            total = total + small_landed[offset - 1]
        small_near[...] = total
        out_loads.append(load(small_near, small_out))

    order = {
        0: [lambda: exchange(0)],
        2: [lambda: norm_two(0), lambda: exchange(1)],
        3: [lambda: attend(0), lambda: project(0)],
        4: [lambda: norm_two(1), lambda: exchange(0)],
        5: [lambda: attend(1), lambda: project(1)],
        6: [lambda: norm_one(0), lambda: exchange(1)],
        7: [lambda: finish_in(0)],
        8: [lambda: norm_one(1), lambda: exchange(0), small_core.start],
        9: [lambda: finish_in(1), small_spread],
        10: [lambda: add_fed(0), lambda: exchange(1), small_finish],
        11: [lambda: finish_out(0)],
        12: [lambda: add_fed(1)],
        13: [lambda: finish_out(1)],
    }
    stretch = 256 // reducer_width
    tasks = {slot * stretch: items for slot, items in order.items()}
    Reducer(plan, line, reducer_refs).run(tasks)
    wait_all(out_loads)


def back_call(dp_count, lam, arrays, blocks, shapes):
    depth, row_count, inner, hidden_count, head_count, head_width = shapes
    line = dp_count // 2
    rows = depth // dp_count
    half = row_count // 2
    width = 256 if line <= 4 else 128
    ring = line + 4
    wide = (line, rows, width)
    bf16, f32 = jnp.bfloat16, jnp.float32
    dma, regular = pltpu.SemaphoreType.DMA, pltpu.SemaphoreType.REGULAR
    wide_half = pltpu.VMEM((half, depth), f32)
    wide_rows = pltpu.VMEM((row_count, depth), bf16)
    narrow = pltpu.VMEM((row_count, inner), bf16)
    narrow_f32 = pltpu.VMEM((row_count, inner), f32)
    small = pltpu.VMEM((8, depth), f32)
    grad = lambda columns: jax.ShapeDtypeStruct((rows, columns), f32)
    rows_shape = jax.ShapeDtypeStruct((2, row_count, depth), bf16)
    flops = 2 * 2 * row_count * depth * (3 * hidden_count + 8 * inner)
    return pl.pallas_call(
        functools.partial(back_kernel, dp_count),
        out_shape=[grad(hidden_count)] * 3
        + [grad(inner), grad(3 * inner), rows_shape, rows_shape]
        + [jax.ShapeDtypeStruct((8, depth), f32)],
        in_specs=[pl.BlockSpec(memory_space=pltpu.SMEM)]
        + [pl.BlockSpec(memory_space=pl.ANY)] * len(arrays)
        + in_vmem(len(blocks)),
        out_specs=[pl.BlockSpec(memory_space=pl.ANY)] * 8,
        scratch_shapes=[
            pltpu.VMEM((send_slots,) + wide, f32),
            pltpu.VMEM((held_slots,) + wide, f32),
            pltpu.VMEM((ring,) + wide, f32),
            pltpu.VMEM((2, line - 1, 2, rows, width), f32),
            dma((send_slots,)),
            dma((held_slots,)),
            dma((2, line - 1, 2)),
            dma((2, line - 1, 2)),
            regular((2, line - 1)),
            dma((ring,)),
            pltpu.VMEM((depth, 2 * row_count), bf16),
            pltpu.VMEM((depth, 2 * row_count), bf16),
            pltpu.VMEM((2, 2 * row_count, width), bf16),
            pltpu.VMEM((2 * row_count, 3 * inner), bf16),
            pltpu.VMEM((inner, depth), bf16),
        ]
        + [pltpu.VMEM((depth, inner), bf16)] * 3
        + [narrow, narrow, narrow, narrow_f32] * 2
        + [narrow_f32, narrow, narrow_f32, narrow_f32]
        + [pltpu.VMEM((head_count, head_width), f32)] * 2
        + [wide_half] * 10
        + [wide_rows] * 3
        + [
            small,
            small,
            pltpu.VMEM((dp_count - 1, 8, depth), f32),
            dma((2, 2)),
            dma((2, 2)),
            regular((2,)),
            regular((2,)),
            dma((128,)),
            dma((2,)),
            dma((dp_count - 1,)),
            dma((dp_count - 1,)),
        ],
        compiler_params=pltpu.CompilerParams(
            collective_id=0, has_side_effects=True, vmem_limit_bytes=60 * 1024 * 1024
        ),
        cost_estimate=pl.CostEstimate(flops=flops, bytes_accessed=64 << 20, transcendentals=0),
    )(lam, *arrays, *blocks)


def attention_forward(row_in, tables, lam, sub_scale, norm1_gain, projections):
    row_count, depth = row_in.shape
    inner = projections[0].shape[1]
    narrow = jax.ShapeDtypeStruct((row_count, inner), jnp.bfloat16)
    return pl.pallas_call(
        forward_kernel,
        out_shape=[
            jax.ShapeDtypeStruct((row_count, depth), jnp.bfloat16),
            narrow,
            narrow,
            narrow,
            jax.ShapeDtypeStruct((row_count, inner), jnp.float32),
            narrow,
        ],
        in_specs=[pl.BlockSpec(memory_space=pltpu.SMEM)] + in_vmem(10),
        out_specs=in_vmem(6),
        compiler_params=pltpu.CompilerParams(vmem_limit_bytes=32 * 1024 * 1024),
        cost_estimate=pl.CostEstimate(
            flops=12 * row_count * depth * inner, bytes_accessed=8 << 20, transcendentals=0
        ),
    )(lam, row_in, norm1_gain[None, :], *projections, *tables, sub_scale)


def feed_forward(normed_two, cot_rows, gate_weight, up_weight, down_weight):
    half = normed_two.shape[0] // 2
    gate_pre = f32_dot(normed_two, gate_weight)
    upward = f32_dot(normed_two, up_weight)
    sigmoid_gate = jax.nn.sigmoid(gate_pre)
    hidden = (gate_pre * sigmoid_gate * upward).astype(jnp.bfloat16)
    grad_hidden = dot_t(cot_rows, down_weight)
    grad_gate_pre = (
        grad_hidden * upward * sigmoid_gate * (1.0 + gate_pre * (1.0 - sigmoid_gate))
    ).astype(jnp.bfloat16)
    grad_up_pre = (grad_hidden * gate_pre * sigmoid_gate).astype(jnp.bfloat16)

    def back(at):
        return dot_t(grad_gate_pre[at], gate_weight) + dot_t(grad_up_pre[at], up_weight)

    send_back = back(slice(half, None))
    keep_back = back(slice(0, half))
    send_fed = f32_dot(hidden[half:], down_weight)
    keep_fed = f32_dot(hidden[:half], down_weight)
    return (keep_back, send_back), (keep_fed, send_fed), hidden, grad_gate_pre, grad_up_pre


def on_device(
    layer_in,
    short_lengths,
    long_lengths,
    norm1_gain,
    query_weight,
    key_weight,
    value_weight,
    lambda_param,
    sub_gain,
    out_weight,
    norm2_gain,
    gate_weight,
    up_weight,
    down_weight,
    out_cotangent,
):
    dp_count = lax.axis_size("dp")
    core = lax.axis_index("tensor") % 2
    head_count, lambda_width = lambda_param.shape
    doc_lengths = (short_lengths[0], long_lengths[0])
    map_width = lambda_width // 4
    projections = (query_weight, key_weight, value_weight)
    lambda_parts = lambda_param.reshape(head_count, 4, map_width)
    first_exp = jnp.exp(jnp.sum(lambda_parts[:, 0] * lambda_parts[:, 1], axis=-1))
    second_exp = jnp.exp(jnp.sum(lambda_parts[:, 2] * lambda_parts[:, 3], axis=-1))
    lam = first_exp - second_exp + lambda_base
    sub_scale = sub_gain * (1.0 - lambda_base)
    tables = []
    for m in range(2):
        position, segment = doc_tables(doc_lengths[m], layer_in.shape[1])
        tables.append(
            rotary_tables(position, map_width) + (segment[:, None], segment[None, :])
        )
    cots = [mine_first(out_cotangent[m], core) for m in range(2)]
    inputs = [half_rows(layer_in[m], core).astype(jnp.float32) for m in range(2)]
    front = [
        attention_forward(layer_in[m], tables[m], lam, sub_scale, norm1_gain, projections)
        for m in range(2)
    ]
    heads = [front[m][5] for m in range(2)]
    middle, normed_two, ffn = [], [], []
    for m in range(2):
        keep = f32_dot(half_rows(heads[m], core), out_weight)
        send = f32_dot(half_rows(heads[m], 1 - core), out_weight)
        middle.append(inputs[m] + tensor_sum(keep, send))
        scaled = middle[m] * root_of(middle[m])
        normed_two.append((with_other(scaled) * norm2_gain).astype(jnp.bfloat16))
        ffn.append(feed_forward(normed_two[m], cots[m], gate_weight, up_weight, down_weight))
    turned = lambda parts: [part.T for part in parts]
    arrays = turned(cots) + turned(normed_two) + turned([front[m][0] for m in range(2)])
    for index in (2, 3, 4):
        arrays += [ffn[m][index] for m in range(2)]
    arrays += heads
    for group, part in ((0, 0), (0, 1), (1, 0), (1, 1)):
        arrays += [ffn[m][group][part] for m in range(2)]
    arrays += middle + [layer_in, out_cotangent, out_weight, *projections]
    for m in range(2):
        arrays += front[m][1:5]
    blocks = [*tables[0], *tables[1], sub_scale, norm1_gain[None, :], norm2_gain[None, :]]
    depth, inner = query_weight.shape
    shapes = (
        depth, layer_in.shape[1], inner, gate_weight.shape[1], head_count, sub_gain.shape[1],
    )
    grad_down, grad_gate, grad_up, grad_out, grad_qkv, layer_out, grad_in, small = back_call(
        dp_count, lam, arrays, blocks, shapes
    )
    grad_query, grad_key, grad_value = jnp.split(grad_qkv, 3, axis=1)
    per_head = lambda row: row[:inner].reshape(head_count, -1)
    grad_lam = per_head(small[3])[:, :1]
    first_scale = grad_lam * first_exp[:, None]
    second_scale = grad_lam * second_exp[:, None]
    lambda_grad = jnp.concatenate(
        [
            first_scale * lambda_parts[:, 1],
            first_scale * lambda_parts[:, 0],
            -second_scale * lambda_parts[:, 3],
            -second_scale * lambda_parts[:, 2],
        ],
        axis=1,
    )
    index = lax.axis_index("dp")

    def block_of(values):
        size = values.shape[-1] // dp_count
        return lax.dynamic_slice_in_dim(values, index * size, size, values.ndim - 1)

    return (
        layer_out,
        grad_in,
        block_of(small[0]),
        grad_query,
        grad_key,
        grad_value,
        block_of(lambda_grad),
        block_of(per_head(small[2])),
        grad_out.T,
        block_of(small[1]),
        grad_gate,
        grad_up,
        grad_down.T,
    )


def solution(mesh):
    return jax.shard_map(
        on_device,
        mesh=mesh,
        in_specs=(
            P(None, "dp", None),
            P("dp", None),
            P("dp", None),
            P(),
            P(None, "tensor"),
            P(None, "tensor"),
            P(None, "tensor"),
            P("tensor", None),
            P("tensor", None),
            P("tensor", None),
            P(),
            P(None, "tensor"),
            P(None, "tensor"),
            P("tensor", None),
            P(None, "dp", None),
        ),
        out_specs=(
            P(None, "dp", None),
            P(None, "dp", None),
            P("dp"),
            P("dp", "tensor"),
            P("dp", "tensor"),
            P("dp", "tensor"),
            P("tensor", "dp"),
            P("tensor", "dp"),
            P("tensor", "dp"),
            P("dp"),
            P("dp", "tensor"),
            P("dp", "tensor"),
            P("tensor", "dp"),
        ),
        check_vma=False,
    )
```

```python
import functools
import math

import jax
import jax.numpy as jnp
from jax import lax
from jax.experimental import pallas as pl
from jax.experimental.pallas import tpu as pltpu
from jax.sharding import PartitionSpec as P

norm_epsilon = 1e-05
lambda_base = 0.8 - 0.6 * math.exp(-0.3 * 11.0)
rotary_base = 10000.0
closed_score = -1e30
block_rows = 128
longest_document = 256
row_group = 16
send_slots = 3
held_slots = 4
MESH = pl.DeviceIdType.MESH


def doc_tables(lengths, row_count):
    doc_ends = jnp.cumsum(lengths, dtype=jnp.int32)
    places = jnp.arange(row_count, dtype=jnp.int32)
    passed = (places[:, None] >= doc_ends[None, :]).astype(jnp.int32)
    segment = jnp.sum(passed, axis=1, dtype=jnp.int32)
    starts = jnp.sum(passed * lengths[None, :], axis=1, dtype=jnp.int32)
    return (places - starts, segment)


def rotary_tables(position, map_width):
    half_width = map_width // 2
    frequency = rotary_base ** (-2.0 * jnp.arange(half_width, dtype=jnp.float32) / map_width)
    angles = position.astype(jnp.float32)[:, None] * frequency[None, :]
    cosine, sine = jnp.cos(angles), jnp.sin(angles)
    return (
        jnp.concatenate([cosine] * 4, axis=1),
        jnp.concatenate([-sine, sine, -sine, sine], axis=1),
    )


def turn(values, cosine, sine):
    width = values.shape[-1]
    quarter = width // 4
    lane = lax.broadcasted_iota(jnp.int32, values.shape, 1)
    partner = jnp.where(
        lane % (2 * quarter) < quarter,
        pltpu.roll(values, width - quarter, 1),
        pltpu.roll(values, quarter, 1),
    )
    return values * cosine + partner * sine


def map_of(values, which):
    lane = lax.broadcasted_iota(jnp.int32, values.shape, 1)
    mine = (lane >= values.shape[-1] // 2) == (which == 1)
    return jnp.where(mine, values, jnp.zeros_like(values))


def key_range(block):
    first = max(0, block * block_rows - longest_document + 1) // block_rows * block_rows
    return first, (block + 1) * block_rows


def open_pairs(block, segment_column, segment_row):
    first, last = key_range(block)
    rows = pl.ds(block * block_rows, block_rows)
    shape = (block_rows, last - first)
    row_at = lax.broadcasted_iota(jnp.int32, shape, 0) + block * block_rows
    key_at = lax.broadcasted_iota(jnp.int32, shape, 1) + first
    return (segment_column[rows, :] == segment_row[:, first:last]) & (key_at <= row_at)


def softmax_map(query, key, opened, scale):
    scores = jnp.where(opened, dot_t(query, key) * scale, closed_score)
    expanded = jnp.exp(scores - jnp.max(scores, axis=-1, keepdims=True))
    return expanded * (1.0 / jnp.sum(expanded, axis=-1, keepdims=True))


def f32_dot(left, right):
    return jnp.dot(left, right, preferred_element_type=jnp.float32)


def dot_t(left, right):
    return lax.dot_general(
        left, right, (((1,), (1,)), ((), ())), preferred_element_type=jnp.float32
    )


def dot_rows(left, right):
    return lax.dot_general(
        left, right, (((0,), (0,)), ((), ())), preferred_element_type=jnp.float32
    )


def rms_back(incoming, values, inverse_root):
    return inverse_root * incoming - values * inverse_root**3 * jnp.mean(
        incoming * values, axis=-1, keepdims=True
    )


def root_of(values):
    return lax.rsqrt(jnp.mean(values * values, axis=-1, keepdims=True) + norm_epsilon)


def forward_kernel(
    lam, rows, gain, query_weight, key_weight, value_weight, cosine, sine, segment_column,
    segment_row, sub_scale, normed_one, query, key, value, mixed, heads_out,
):
    head_count, width = sub_scale.shape
    scale = (width // 2) ** (-0.5)
    values = rows[...].astype(jnp.float32)
    normed_one[...] = (values * root_of(values) * gain[...]).astype(jnp.bfloat16)
    raw_query = f32_dot(normed_one[...], query_weight[...])
    raw_key = f32_dot(normed_one[...], key_weight[...])
    value[...] = f32_dot(normed_one[...], value_weight[...]).astype(jnp.bfloat16)
    for head in range(head_count):
        at = slice(head * width, (head + 1) * width)
        query[:, at] = turn(raw_query[:, at], cosine[...], sine[...]).astype(jnp.bfloat16)
        key[:, at] = turn(raw_key[:, at], cosine[...], sine[...]).astype(jnp.bfloat16)
    for block in range(rows.shape[0] // block_rows):
        first, last = key_range(block)
        here = slice(block * block_rows, last)
        opened = open_pairs(block, segment_column, segment_row)
        for head in range(head_count):
            at = slice(head * width, (head + 1) * width)
            keys = key[first:last, at]
            maps = [softmax_map(map_of(query[here, at], c), keys, opened, scale) for c in range(2)]
            combined = (maps[0] - lam[head] * maps[1]).astype(jnp.bfloat16)
            out = f32_dot(combined, value[first:last, at])
            mixed[here, at] = out
            heads_out[here, at] = (out * root_of(out) * sub_scale[head : head + 1, :]).astype(
                jnp.bfloat16
            )


def backward_kernel(
    lam, grad_attended, out_weight, query, key, value, mixed, cosine, sine, segment_column,
    segment_row, sub_scale, grad_rows, grad_sub, grad_lam, grad_heads, grad_mixed, grad_key,
    grad_value,
):
    head_count, width = sub_scale.shape
    row_count = query.shape[0]
    inner = head_count * width
    scale = (width // 2) ** (-0.5)
    grad_heads[...] = dot_t(grad_attended[...], out_weight[...])
    for head in range(head_count):
        at = slice(head * width, (head + 1) * width)
        heads = mixed[:, at]
        root = root_of(heads)
        grads = grad_heads[:, at]
        grad_sub[head : head + 1, :] = jnp.sum(grads * heads * root, axis=0, keepdims=True) * (
            1.0 - lambda_base
        )
        grad_mixed[:, at] = rms_back(grads * sub_scale[head : head + 1, :], heads, root).astype(
            jnp.bfloat16
        )
    grad_key[...] = jnp.zeros_like(grad_key)
    grad_value[...] = jnp.zeros_like(grad_value)
    lam_sums = [0.0] * head_count
    for block in range(row_count // block_rows):
        first, last = key_range(block)
        here = slice(block * block_rows, last)
        opened = open_pairs(block, segment_column, segment_row)
        for head in range(head_count):
            at = slice(head * width, (head + 1) * width)
            keys = key[first:last, at]
            queries = [map_of(query[here, at], c) for c in range(2)]
            maps = [softmax_map(queries[c], keys, opened, scale) for c in range(2)]
            mixes = grad_mixed[here, at]
            combined = (maps[0] - lam[head] * maps[1]).astype(jnp.bfloat16)
            grad_value[first:last, at] += dot_rows(combined, mixes)
            grads = dot_t(mixes, value[first:last, at])
            first_sum = jnp.sum(grads * maps[0], axis=-1, keepdims=True)
            second_sum = jnp.sum(grads * maps[1], axis=-1, keepdims=True)
            lam_sums[head] = lam_sums[head] + jnp.sum(second_sum, axis=0, keepdims=True)
            score_grads = [
                (maps[0] * (grads - first_sum)).astype(jnp.bfloat16),
                (maps[1] * (-lam[head] * (grads - second_sum))).astype(jnp.bfloat16),
            ]
            grad_query = f32_dot(score_grads[0], map_of(keys, 0)) + f32_dot(
                score_grads[1], map_of(keys, 1)
            )
            grad_rows[here, at] = turn(
                grad_query * scale, cosine[here, :], -sine[here, :]
            ).astype(jnp.bfloat16)
            grad_key[first:last, at] += dot_rows(score_grads[0], queries[0]) + dot_rows(
                score_grads[1], queries[1]
            )
    for head in range(head_count):
        at = slice(head * width, (head + 1) * width)
        grad_rows[:, inner + head * width : inner + (head + 1) * width] = turn(
            grad_key[:, at] * scale, cosine[...], -sine[...]
        ).astype(jnp.bfloat16)
        grad_lam[head : head + 1, :] = jnp.broadcast_to(-lam_sums[head], (1, width))
    grad_rows[:, 2 * inner :] = grad_value[...].astype(jnp.bfloat16)


def in_vmem(count):
    return [pl.BlockSpec(memory_space=pltpu.VMEM)] * count


class Reducer:
    def __init__(self, plan, line, refs):
        self.plan, self.line = plan, line
        (
            self.send, self.held, self.total, self.landed, self.pair_out, self.pair_in,
            self.line_out, self.line_in, self.credit, self.out_sem,
        ) = refs
        self.me = lax.axis_index("dp")
        self.place, self.side = self.me // 2, self.me % 2
        self.other = self.me + 1 - 2 * self.side
        self.steps = line - 1
        self.ring = self.total.shape[0]
        self.rows = self.total.shape[2]

    def compute(self, c):
        item = self.plan[c]
        width = item.width
        left, right = item.left(), item.right()

        def block(at, carry):
            first = pl.multiple_of(2 * at * self.rows, self.rows)
            columns = right[...]
            away = left[pl.ds(first + (1 - self.side) * self.rows, self.rows), :]
            here = left[pl.ds(first + self.side * self.rows, self.rows), :]
            self.send[c % send_slots, at, :, :width] = f32_dot(away, columns)
            self.total[c % self.ring, at, :, :width] = f32_dot(here, columns)
            return carry

        lax.fori_loop(0, self.line, block, 0)
        item.computed()

    def pair_copy(self, c):
        width = self.plan[c].width
        return pltpu.make_async_remote_copy(
            src_ref=self.send.at[c % send_slots, :, :, :width],
            dst_ref=self.held.at[c % held_slots, :, :, :width],
            send_sem=self.pair_out.at[c % send_slots],
            recv_sem=self.pair_in.at[c % held_slots],
            device_id={"dp": self.other},
            device_id_type=MESH,
        )

    def pair_finish(self, c):
        width = self.plan[c].width
        self.pair_copy(c).wait_recv()

        def block(at, carry):
            self.total[c % self.ring, at, :, :width] += self.held[c % held_slots, at, :, :width]
            return carry

        lax.fori_loop(0, self.line, block, 0)
        self.pair_copy(c).wait_send()

    def line_copy(self, c, step, way, block, target):
        width = self.plan[c].width
        return pltpu.make_async_remote_copy(
            src_ref=self.total.at[c % self.ring, block, :, :width],
            dst_ref=self.landed.at[way, step, c % 2, :, :width],
            send_sem=self.line_out.at[way, step, c % 2],
            recv_sem=self.line_in.at[way, step, c % 2],
            device_id={"dp": target},
            device_id_type=MESH,
        )

    def line_sends(self, step, way):
        place, line = self.place, self.line
        if way == 0:
            block = line - 1 - step + place
            return (place <= step) & (place < line - 1), block, self.me + 2
        block = place + step - line + 1
        return (place >= line - 1 - step) & (place > 0), block, self.me - 2

    def line_gets(self, step, way):
        place, line = self.place, self.line
        if way == 0:
            return (place > 0) & (place - 1 <= step), line - 2 - step + place, self.me - 2
        gets = (place < line - 1) & (place + 1 >= line - 1 - step)
        return gets, place + step - line + 2, self.me + 2

    def line_start(self, c, step):
        for way in range(2):
            sends, block, target = self.line_sends(step, way)

            @pl.when(sends)
            def _():
                if c >= 2:
                    pl.semaphore_wait(self.credit.at[way, step], 1)
                self.line_copy(c, step, way, block, target).start()

    def line_finish(self, c, step):
        width = self.plan[c].width
        for way in range(2):
            gets, block, source = self.line_gets(step, way)

            @pl.when(gets)
            def _():
                self.line_copy(c, step, way, block, source).wait_recv()
                self.total[c % self.ring, block, :, :width] += self.landed[
                    way, step, c % 2, :, :width
                ]
                if c + 2 < len(self.plan):
                    pl.semaphore_signal(
                        self.credit.at[way, step],
                        inc=1,
                        device_id={"dp": source},
                        device_id_type=MESH,
                    )

            sends, sent, target = self.line_sends(step, way)

            @pl.when(sends)
            def _():
                self.line_copy(c, step, way, sent, target).wait_send()

    def out_copy(self, c):
        item = self.plan[c]
        return pltpu.make_async_copy(
            self.total.at[c % self.ring, self.place, :, : item.width],
            item.out.at[:, item.first : item.first + item.width],
            self.out_sem.at[c % self.ring],
        )

    def run(self, tasks):
        count, steps = len(self.plan), self.steps
        self.compute(0)
        self.pair_copy(0).start()
        self.compute(1)
        for slot in range(count + steps + 1):
            for step in range(steps):
                c = slot - 2 - step
                if 0 <= c < count:
                    self.line_finish(c, step)
            if 0 <= slot - 1 < count:
                self.pair_finish(slot - 1)
            for step in range(steps):
                c = slot - 1 - step
                if 0 <= c < count:
                    self.line_start(c, step)
            if slot + 1 < count:
                self.pair_copy(slot + 1).start()
            done = slot - 1 - steps
            if 0 <= done < count:
                self.out_copy(done).start()
            if slot + 2 < count:
                if slot + 2 >= self.ring:
                    self.out_copy(slot + 2 - self.ring).wait()
                self.compute(slot + 2)
            for task in tasks.get(slot, ()):
                task()
        for c in range(max(0, count - self.ring), count):
            self.out_copy(c).wait()


class Chunk:
    def __init__(self, left, right, computed, out, first, width):
        self.left, self.right, self.computed = left, right, computed
        self.out, self.first, self.width = out, first, width


def for_rows(count, body):
    def step(i, carry):
        body(pl.ds(pl.multiple_of(i * row_group, row_group), row_group))
        return carry

    lax.fori_loop(0, count // row_group, step, 0)


class TensorSum:
    def __init__(self, uses, own, near, far, near_sems, far_sems, near_credit, far_credit):
        self.own, self.near, self.far = own, near, far
        self.near_sems, self.far_sems = near_sems, far_sems
        self.near_credit, self.far_credit = near_credit, far_credit
        index = lax.axis_index("tensor")
        self.core_peer = index + 1 - 2 * (index % 2)
        self.far_peer = index + 2 - 4 * (index // 2)
        self.near_left, self.far_left = 2 * uses, uses
        self.near_first, self.far_first = True, True

    def near_copy(self, source):
        return pltpu.make_async_remote_copy(
            src_ref=source, dst_ref=self.near, send_sem=self.near_sems.at[0],
            recv_sem=self.near_sems.at[1], device_id={"tensor": self.core_peer},
            device_id_type=MESH,
        )

    def far_copy(self):
        return pltpu.make_async_remote_copy(
            src_ref=self.own, dst_ref=self.far, send_sem=self.far_sems.at[0],
            recv_sem=self.far_sems.at[1], device_id={"tensor": self.far_peer},
            device_id_type=MESH,
        )

    def near_start(self, source):
        if not self.near_first:
            pl.semaphore_wait(self.near_credit, 1)
        self.near_first = False
        self.pending = source
        self.near_copy(source).start()

    def near_wait(self):
        self.near_copy(self.pending).wait()

    def near_free(self):
        self.near_left -= 1
        if self.near_left:
            pl.semaphore_signal(
                self.near_credit, inc=1, device_id={"tensor": self.core_peer}, device_id_type=MESH
            )

    def near_add(self):
        self.near_wait()

        def add(rows):
            self.own[rows, :] += self.near[rows, :]

        for_rows(self.own.shape[0], add)
        self.near_free()

    def far_go(self):
        if not self.far_first:
            pl.semaphore_wait(self.far_credit, 1)
        self.far_first = False
        self.far_copy().start()

    def far_wait(self):
        self.far_copy().wait()

    def far_free(self):
        self.far_left -= 1
        if self.far_left:
            pl.semaphore_signal(
                self.far_credit, inc=1, device_id={"tensor": self.far_peer}, device_id_type=MESH
            )


def back_kernel(dp_count, *refs):
    refs = list(refs)
    take = lambda n: [refs.pop(0) for _ in range(n)]
    (lam,) = take(1)
    cot_left, two_left, one_left = [take(2) for _ in range(3)]
    hidden, gate_pre, up_pre, heads = [take(2) for _ in range(4)]
    part_back, part_fed, middle = [take(2) for _ in range(3)]
    (layer_in, cotangent) = take(2)
    weights_in = take(4)
    kept_in = [take(4) for _ in range(2)]
    tables = [take(4) for _ in range(2)]
    (sub_scale, gain_one, gain_two) = take(3)
    (grad_down, grad_gate, grad_up, grad_out, grad_qkv, layer_out, grad_in, small_out) = take(8)
    reducer_refs = take(10)
    (left_a, left_b, rights, rows_qkv) = take(4)
    weights = take(4)
    kept = [take(4) for _ in range(2)]
    backward_scratch = take(4)
    (grad_sub, grad_lam) = take(2)
    sets = [take(3) for _ in range(2)]
    through = take(2)
    (spare, projected, attended, rows_in, rows_out) = take(5)
    (small, small_near, small_landed) = take(3)
    (near_sems, far_sems, near_credit, far_credit) = take(4)
    (load_sems, small_near_sems, small_send, small_recv) = take(4)
    assert not refs

    me = lax.axis_index("dp")
    tensor = lax.axis_index("tensor")
    core = tensor % 2
    core_peer = tensor + 1 - 2 * core
    far_peer = tensor + 2 - 4 * (tensor // 2)
    line = dp_count // 2
    half = middle[0].shape[0]
    row_count = 2 * half
    head_count, head_width = sub_scale.shape
    out_weight, projections = weights[0], weights[1:]
    inner = out_weight.shape[0]
    kept_half = pl.ds(pl.multiple_of(core * half, half), half)
    sent_half = pl.ds(pl.multiple_of((1 - core) * half, half), half)
    tokens = [slice(m * row_count, (m + 1) * row_count) for m in range(2)]

    barrier = pltpu.get_barrier_semaphore()
    for offset in range(1, dp_count):
        pl.semaphore_signal(
            barrier, inc=1, device_id={"dp": lax.rem(me + offset, dp_count)}, device_id_type=MESH
        )
    for peer in (core_peer, far_peer):
        pl.semaphore_signal(barrier, inc=1, device_id={"tensor": peer}, device_id_type=MESH)
    pl.semaphore_wait(barrier, dp_count + 1)

    used = [0]

    def load(source, target):
        copy = pltpu.make_async_copy(source, target, load_sems.at[used[0]])
        used[0] += 1
        copy.start()
        return copy

    def wait_all(copies):
        for copy in copies:
            copy.wait()

    reducer_width = reducer_refs[0].shape[-1]
    plan, sources, left_loads, right_loads = [], {}, {}, {}

    def load_left(sources_of, left):
        return [load(sources_of[m], left.at[:, tokens[m]]) for m in range(2)]

    def load_right(c):
        if c in sources:
            source, first, width = sources[c]
            right_loads[c] = [
                load(source[m].at[:, first : first + width], rights.at[c % 2, tokens[m], :width])
                for m in range(2)
            ]

    def get_left(c, left):
        wait_all(left_loads.pop(c, ()))
        return left

    def get_right(c, first, width):
        if c in sources:
            wait_all(right_loads[c])
            return rights.at[c % 2, :, :width]
        return rows_qkv.at[:, first : first + width]

    def computed(c):
        load_right(c + 2)
        if c == last_two:
            left_loads[first_one] = load_left(one_left, left_b)

    def add_group(left, source, columns, out):
        for first in range(0, columns, reducer_width):
            width = min(reducer_width, columns - first)
            c = len(plan)
            if source is not None:
                sources[c] = (source, first, width)
            plan.append(
                Chunk(
                    functools.partial(get_left, c, left),
                    functools.partial(get_right, c, first, width),
                    functools.partial(computed, c),
                    out,
                    first,
                    width,
                )
            )

    add_group(left_a, hidden, hidden[0].shape[1], grad_down)
    first_two = len(plan)
    add_group(left_b, gate_pre, gate_pre[0].shape[1], grad_gate)
    add_group(left_b, up_pre, up_pre[0].shape[1], grad_up)
    last_two = len(plan) - 1
    add_group(left_a, heads, inner, grad_out)
    first_one = len(plan)
    add_group(left_b, None, 3 * inner, grad_qkv)

    left_loads[0] = load_left(cot_left, left_a)
    load_right(0)
    load_right(1)
    sums = [
        TensorSum(
            3, *sets[m], near_sems.at[m], far_sems.at[m], near_credit.at[m], far_credit.at[m]
        )
        for m in range(2)
    ]
    own_loads = {}
    for m in range(2):
        own_loads[m] = load(part_back[m].at[kept_half], sets[m][0])
        sums[m].near_start(part_back[m].at[sent_half])
    left_loads[first_two] = load_left(two_left, left_b)
    weight_loads = [load(*pair) for pair in zip(weights_in, weights)]
    kept_loads = [[load(*pair) for pair in zip(kept_in[m], kept[m])] for m in range(2)]
    spare_queue = [middle[0], middle[1], middle[0], middle[1]]
    rows_queue = [cotangent.at[0], cotangent.at[1]]
    rows_queue += [layer_in.at[0], cotangent.at[0], layer_in.at[1], cotangent.at[1]]
    queued = {}

    def next_spare():
        queued["spare"] = load(spare_queue.pop(0), spare) if spare_queue else None

    def next_rows():
        queued["rows"] = load(rows_queue.pop(0), rows_in) if rows_queue else None

    next_spare()
    next_rows()
    out_loads = []
    small[...] = jnp.zeros_like(small)

    def mine(rows):
        return pl.ds(pl.multiple_of(core * half + rows.start, row_group), row_group)

    def others(rows):
        return pl.ds(pl.multiple_of((1 - core) * half + rows.start, row_group), row_group)

    def exchange(m):
        if m in own_loads:
            own_loads.pop(m).wait()
        sums[m].near_add()
        sums[m].far_go()

    def norm_two(m):
        own, near, far = sets[m]
        queued["spare"].wait()
        sums[m].far_wait()

        def body(rows):
            grads = own[rows, :] + far[rows, :]
            values = spare[rows, :]
            root = root_of(values)
            small[1:2, :] += jnp.sum(grads * values * root, axis=0, keepdims=True)
            through[m][rows, :] = rms_back(grads * gain_two[...], values, root)

        for_rows(half, body)
        sums[m].far_free()
        sums[m].near_start(through[m])
        next_spare()

    def attend(m):
        near = sets[m][1]
        queued["rows"].wait()
        sums[m].near_wait()

        def body(rows):
            attended[mine(rows), :] = (
                rows_in[mine(rows), :].astype(jnp.float32) + through[m][rows, :]
            ).astype(jnp.bfloat16)
            attended[others(rows), :] = (
                rows_in[others(rows), :].astype(jnp.float32) + near[rows, :]
            ).astype(jnp.bfloat16)

        for_rows(half, body)
        sums[m].near_free()
        next_rows()

        def flip_block(i, carry):
            at = pl.ds(pl.multiple_of(i * 128, 128), 128)
            left_a[at, tokens[m]] = attended[:, at].T
            return carry

        lax.fori_loop(0, attended.shape[1] // 128, flip_block, 0)
        if m == 0:
            wait_all(weight_loads)
        wait_all(kept_loads[m])
        backward_kernel(
            lam, attended, out_weight, *kept[m], *tables[m], sub_scale,
            rows_qkv.at[tokens[m], :], grad_sub, grad_lam, *backward_scratch,
        )
        for head in range(head_count):
            at = slice(head * head_width, (head + 1) * head_width)
            small[2:3, at] += grad_sub[head : head + 1, :]
            small[3:4, at] += grad_lam[head : head + 1, :]

    def project(m):
        def part(which, target):
            rows = pl.ds(pl.multiple_of(m * row_count + which * half, half), half)

            def block(i, carry):
                at = pl.ds(pl.multiple_of(i * 512, 512), 512)
                total = 0.0
                for p in range(3):
                    grads = rows_qkv[rows, p * inner : (p + 1) * inner]
                    total = total + dot_t(grads, projections[p][at, :])
                target[:, at] = total
                return carry

            lax.fori_loop(0, target.shape[1] // 512, block, 0)

        part(1 - core, projected)
        sums[m].near_start(projected)
        part(core, sets[m][0])

    def norm_one(m):
        own, near, far = sets[m]
        queued["rows"].wait()
        sums[m].far_wait()

        def body(rows):
            grads = own[rows, :] + far[rows, :]
            values = rows_in[mine(rows), :].astype(jnp.float32)
            root = root_of(values)
            small[0:1, :] += jnp.sum(grads * values * root, axis=0, keepdims=True)
            through[m][rows, :] += rms_back(grads * gain_one[...], values, root)

        for_rows(half, body)
        sums[m].far_free()
        sums[m].near_start(through[m])
        next_rows()
        own_loads[m] = load(part_fed[m].at[kept_half], own)

    def store_rows(target):
        out_loads.append(load(rows_out, target))

    def finish_in(m):
        near = sets[m][1]
        queued["rows"].wait()
        sums[m].near_wait()
        wait_all(out_loads)
        out_loads.clear()

        def body(rows):
            rows_out[mine(rows), :] = (
                rows_in[mine(rows), :].astype(jnp.float32) + through[m][rows, :]
            ).astype(jnp.bfloat16)
            rows_out[others(rows), :] = (
                rows_in[others(rows), :].astype(jnp.float32) + near[rows, :]
            ).astype(jnp.bfloat16)

        for_rows(half, body)
        sums[m].near_free()
        next_rows()
        store_rows(grad_in.at[m])
        sums[m].near_start(part_fed[m].at[sent_half])

    def add_fed(m):
        own, near, far = sets[m]
        queued["spare"].wait()
        sums[m].far_wait()

        def body(rows):
            own[rows, :] = spare[rows, :] + (own[rows, :] + far[rows, :])

        for_rows(half, body)
        sums[m].far_free()
        sums[m].near_start(own)
        next_spare()

    def finish_out(m):
        own, near = sets[m][:2]
        sums[m].near_wait()
        wait_all(out_loads)
        out_loads.clear()

        def body(rows):
            rows_out[mine(rows), :] = own[rows, :].astype(jnp.bfloat16)
            rows_out[others(rows), :] = near[rows, :].astype(jnp.bfloat16)

        for_rows(half, body)
        sums[m].near_free()
        store_rows(layer_out.at[m])

    small_core = pltpu.make_async_remote_copy(
        src_ref=small, dst_ref=small_near, send_sem=small_near_sems.at[0],
        recv_sem=small_near_sems.at[1], device_id={"tensor": core_peer}, device_id_type=MESH,
    )

    def small_copy(offset):
        return pltpu.make_async_remote_copy(
            src_ref=small, dst_ref=small_landed.at[offset - 1], send_sem=small_send.at[offset - 1],
            recv_sem=small_recv.at[offset - 1],
            device_id={"dp": lax.rem(me + offset, dp_count)}, device_id_type=MESH,
        )

    def small_spread():
        small_core.wait()
        small[0:2, :] += small_near[0:2, :]
        for offset in range(1, dp_count):
            small_copy(offset).start()

    def small_finish():
        for offset in range(1, dp_count):
            small_copy(offset).wait()
        total = small[...]
        for offset in range(1, dp_count):
            total = total + small_landed[offset - 1]
        small_near[...] = total
        out_loads.append(load(small_near, small_out))

    order = {
        0: [lambda: exchange(0)],
        2: [lambda: norm_two(0), lambda: exchange(1)],
        3: [lambda: attend(0), lambda: project(0)],
        4: [lambda: norm_two(1), lambda: exchange(0)],
        5: [lambda: attend(1), lambda: project(1)],
        6: [lambda: norm_one(0), lambda: exchange(1)],
        7: [lambda: finish_in(0)],
        8: [lambda: norm_one(1), lambda: exchange(0), small_core.start],
        9: [lambda: finish_in(1), small_spread],
        10: [lambda: add_fed(0), lambda: exchange(1), small_finish],
        11: [lambda: finish_out(0)],
        12: [lambda: add_fed(1)],
        13: [lambda: finish_out(1)],
    }
    stretch = 256 // reducer_width
    tasks = {slot * stretch: items for slot, items in order.items()}
    Reducer(plan, line, reducer_refs).run(tasks)
    wait_all(out_loads)


def back_call(dp_count, lam, arrays, blocks, shapes):
    depth, row_count, inner, hidden_count, head_count, head_width = shapes
    line = dp_count // 2
    rows = depth // dp_count
    half = row_count // 2
    width = 256 if line <= 4 else 128
    ring = line + 4
    wide = (line, rows, width)
    bf16, f32 = jnp.bfloat16, jnp.float32
    dma, regular = pltpu.SemaphoreType.DMA, pltpu.SemaphoreType.REGULAR
    wide_half = pltpu.VMEM((half, depth), f32)
    wide_rows = pltpu.VMEM((row_count, depth), bf16)
    narrow = pltpu.VMEM((row_count, inner), bf16)
    narrow_f32 = pltpu.VMEM((row_count, inner), f32)
    small = pltpu.VMEM((8, depth), f32)
    grad = lambda columns: jax.ShapeDtypeStruct((rows, columns), f32)
    rows_shape = jax.ShapeDtypeStruct((2, row_count, depth), bf16)
    flops = 2 * 2 * row_count * depth * (3 * hidden_count + 8 * inner)
    return pl.pallas_call(
        functools.partial(back_kernel, dp_count),
        out_shape=[grad(hidden_count)] * 3
        + [grad(inner), grad(3 * inner), rows_shape, rows_shape]
        + [jax.ShapeDtypeStruct((8, depth), f32)],
        in_specs=[pl.BlockSpec(memory_space=pltpu.SMEM)]
        + [pl.BlockSpec(memory_space=pl.ANY)] * len(arrays)
        + in_vmem(len(blocks)),
        out_specs=[pl.BlockSpec(memory_space=pl.ANY)] * 8,
        scratch_shapes=[
            pltpu.VMEM((send_slots,) + wide, f32),
            pltpu.VMEM((held_slots,) + wide, f32),
            pltpu.VMEM((ring,) + wide, f32),
            pltpu.VMEM((2, line - 1, 2, rows, width), f32),
            dma((send_slots,)),
            dma((held_slots,)),
            dma((2, line - 1, 2)),
            dma((2, line - 1, 2)),
            regular((2, line - 1)),
            dma((ring,)),
            pltpu.VMEM((depth, 2 * row_count), bf16),
            pltpu.VMEM((depth, 2 * row_count), bf16),
            pltpu.VMEM((2, 2 * row_count, width), bf16),
            pltpu.VMEM((2 * row_count, 3 * inner), bf16),
            pltpu.VMEM((inner, depth), bf16),
        ]
        + [pltpu.VMEM((depth, inner), bf16)] * 3
        + [narrow, narrow, narrow, narrow_f32] * 2
        + [narrow_f32, narrow, narrow_f32, narrow_f32]
        + [pltpu.VMEM((head_count, head_width), f32)] * 2
        + [wide_half] * 10
        + [wide_rows] * 3
        + [
            small,
            small,
            pltpu.VMEM((dp_count - 1, 8, depth), f32),
            dma((2, 2)),
            dma((2, 2)),
            regular((2,)),
            regular((2,)),
            dma((128,)),
            dma((2,)),
            dma((dp_count - 1,)),
            dma((dp_count - 1,)),
        ],
        compiler_params=pltpu.CompilerParams(
            collective_id=0, has_side_effects=True, vmem_limit_bytes=60 * 1024 * 1024
        ),
        cost_estimate=pl.CostEstimate(flops=flops, bytes_accessed=64 << 20, transcendentals=0),
    )(lam, *arrays, *blocks)


def front_kernel(*refs):
    refs = list(refs)
    take = lambda n: [refs.pop(0) for _ in range(n)]
    (lam,) = take(1)
    layer_in, cotangent = take(2)
    weights_in = take(7)
    tables = [take(4) for _ in range(2)]
    (sub_scale, gain_one, gain_two) = take(3)
    outs = [take(14) for _ in range(2)]
    rows_in, cot_rows = take(2), take(2)
    (normed_one, normed_two, flipped) = take(3)
    weights = take(7)
    kept = [take(5) for _ in range(2)]
    sets = [take(3) for _ in range(2)]
    (projected,) = take(1)
    hidden = [take(3) for _ in range(2)]
    (back, fed) = take(2)
    (near_sems, far_sems, near_credit, load_sems) = take(4)
    assert not refs

    tensor = lax.axis_index("tensor")
    core = tensor % 2
    out_weight, gate_weight, up_weight, down_weight = weights[3:]
    row_count, depth = normed_one.shape
    half = row_count // 2
    hidden_count = gate_weight.shape[1]
    used = [0]

    def load(source, target):
        copy = pltpu.make_async_copy(source, target, load_sems.at[used[0]])
        used[0] += 1
        copy.start()
        return copy

    def wait_all(copies):
        for copy in copies:
            copy.wait()
        copies.clear()

    rows_loads = [load(layer_in.at[0], rows_in[0])]
    weight_loads = [load(*pair) for pair in zip(weights_in[:4], weights[:4])]
    rows_loads.append(load(layer_in.at[1], rows_in[1]))
    cot_loads = [load(cotangent.at[m], cot_rows[m]) for m in range(2)]
    wide_loads = [load(*pair) for pair in zip(weights_in[4:], weights[4:])]

    barrier = pltpu.get_barrier_semaphore()
    for peer in (tensor + 1 - 2 * core, tensor + 2 - 4 * (tensor // 2)):
        pl.semaphore_signal(barrier, inc=1, device_id={"tensor": peer}, device_id_type=MESH)
    pl.semaphore_wait(barrier, 2)
    sums = [
        TensorSum(1, *sets[m], near_sems.at[m], far_sems.at[m], near_credit.at[m], None)
        for m in range(2)
    ]
    out_loads, flip_loads, wide_outs = [], [], []

    def mine(rows):
        return pl.ds(pl.multiple_of(core * half + rows.start, row_group), row_group)

    def others(rows):
        return pl.ds(pl.multiple_of((1 - core) * half + rows.start, row_group), row_group)

    def flip_to(source, target):
        wait_all(flip_loads)

        def block(i, carry):
            at = pl.ds(pl.multiple_of(i * 128, 128), 128)
            flipped[at, :] = source[:, at].T
            return carry

        lax.fori_loop(0, depth // 128, block, 0)
        flip_loads.append(load(flipped, target))

    def attend(m):
        rows_loads[m].wait()
        if m == 0:
            wait_all(weight_loads)
        forward_kernel(
            lam, rows_in[m], gain_one, *weights[:3], *tables[m], sub_scale, normed_one, *kept[m]
        )
        heads = kept[m][4]

        def part(which, target):
            rows = pl.ds(pl.multiple_of(which * half, half), half)

            def block(i, carry):
                at = pl.ds(pl.multiple_of(i * 512, 512), 512)
                target[:, at] = f32_dot(heads[rows, :], out_weight[:, at])
                return carry

            lax.fori_loop(0, depth // 512, block, 0)

        part(1 - core, projected)
        sums[m].near_start(projected)
        part(core, sets[m][0])
        out_loads.extend(load(*pair) for pair in zip(kept[m], outs[m][3:8]))
        flip_to(normed_one, outs[m][2])
        sums[m].near_add()

    def norm_rows(rows, values):
        return (values * root_of(values) * gain_two[...]).astype(jnp.bfloat16)

    def join(m):
        own, near, far = sets[m]

        def add(rows):
            values = rows_in[m][mine(rows), :].astype(jnp.float32)
            own[rows, :] = values + (own[rows, :] + far[rows, :])

        def norm_mine(rows):
            normed_two[mine(rows), :] = norm_rows(rows, own[rows, :])

        def norm_others(rows):
            normed_two[others(rows), :] = norm_rows(rows, near[rows, :])

        for_rows(half, add)
        sums[m].near_start(own)
        out_loads.append(load(own, outs[m][8]))
        for_rows(half, norm_mine)
        sums[m].near_wait()
        for_rows(half, norm_others)
        sums[m].near_free()

    def feed(m):
        inside, gate_pre, up_pre = hidden[m]
        if m == 0:
            wait_all(wide_loads)

        def block(j, carry):
            at = pl.ds(pl.multiple_of(j * 256, 256), 256)
            gate = f32_dot(normed_two[...], gate_weight[:, at])
            upward = f32_dot(normed_two[...], up_weight[:, at])
            grads = dot_t(cot_rows[m][...], down_weight[at, :])
            sigmoid = jax.nn.sigmoid(gate)
            inside[:, at] = (gate * sigmoid * upward).astype(jnp.bfloat16)
            gate_pre[:, at] = (
                grads * upward * sigmoid * (1.0 + gate * (1.0 - sigmoid))
            ).astype(jnp.bfloat16)
            up_pre[:, at] = (grads * gate * sigmoid).astype(jnp.bfloat16)
            return carry

        lax.fori_loop(0, hidden_count // 256, block, 0)
        out_loads.extend(load(*pair) for pair in zip(hidden[m], outs[m][9:12]))
        wait_all(wide_outs)

        def through(i, carry):
            at = pl.ds(pl.multiple_of(i * 512, 512), 512)
            back[:, at] = dot_t(gate_pre[...], gate_weight[at, :]) + dot_t(
                up_pre[...], up_weight[at, :]
            )
            fed[:, at] = f32_dot(inside[...], down_weight[:, at])
            return carry

        lax.fori_loop(0, depth // 512, through, 0)
        wide_outs.extend([load(back, outs[m][12]), load(fed, outs[m][13])])

    attend(0)
    sums[0].far_go()
    attend(1)
    for m in range(2):
        cot_loads[m].wait()
        flip_to(cot_rows[m], outs[m][0])
    sums[0].far_wait()
    sums[1].far_go()
    join(0)
    feed(0)
    flip_to(normed_two, outs[0][1])
    sums[1].far_wait()
    join(1)
    feed(1)
    flip_to(normed_two, outs[1][1])
    wait_all(flip_loads)
    wait_all(wide_outs)
    wait_all(out_loads)


def front_call(lam, arrays, blocks, shapes):
    depth, row_count, inner, hidden_count = shapes[:4]
    bf16, f32 = jnp.bfloat16, jnp.float32
    dma, regular = pltpu.SemaphoreType.DMA, pltpu.SemaphoreType.REGULAR
    half = row_count // 2
    out_shape = []
    for m in range(2):
        out_shape += [jax.ShapeDtypeStruct((depth, row_count), bf16)] * 3
        out_shape += [jax.ShapeDtypeStruct((row_count, inner), bf16)] * 3
        out_shape += [jax.ShapeDtypeStruct((row_count, inner), f32)]
        out_shape += [jax.ShapeDtypeStruct((row_count, inner), bf16)]
        out_shape += [jax.ShapeDtypeStruct((half, depth), f32)]
        out_shape += [jax.ShapeDtypeStruct((row_count, hidden_count), bf16)] * 3
        out_shape += [jax.ShapeDtypeStruct((row_count, depth), f32)] * 2
    wide_rows = pltpu.VMEM((row_count, depth), bf16)
    narrow = pltpu.VMEM((row_count, inner), bf16)
    wide_half = pltpu.VMEM((half, depth), f32)
    return pl.pallas_call(
        front_kernel,
        out_shape=out_shape,
        in_specs=[pl.BlockSpec(memory_space=pltpu.SMEM)]
        + [pl.BlockSpec(memory_space=pl.ANY)] * len(arrays)
        + in_vmem(len(blocks)),
        out_specs=[pl.BlockSpec(memory_space=pl.ANY)] * len(out_shape),
        scratch_shapes=[wide_rows] * 6
        + [pltpu.VMEM((depth, row_count), bf16)]
        + [pltpu.VMEM((depth, inner), bf16)] * 3
        + [pltpu.VMEM((inner, depth), bf16)]
        + [pltpu.VMEM((depth, hidden_count), bf16)] * 2
        + [pltpu.VMEM((hidden_count, depth), bf16)]
        + [narrow, narrow, narrow, pltpu.VMEM((row_count, inner), f32), narrow] * 2
        + [wide_half] * 7
        + [pltpu.VMEM((row_count, hidden_count), bf16)] * 6
        + [pltpu.VMEM((row_count, depth), f32)] * 2
        + [dma((2, 2)), dma((2, 2)), regular((2,)), dma((64,))],
        compiler_params=pltpu.CompilerParams(
            collective_id=1, has_side_effects=True, vmem_limit_bytes=62 * 1024 * 1024
        ),
        cost_estimate=pl.CostEstimate(
            flops=4 * row_count * depth * (6 * hidden_count + 4 * inner),
            bytes_accessed=64 << 20,
            transcendentals=0,
        ),
    )(lam, *arrays, *blocks)


def on_device(
    layer_in,
    short_lengths,
    long_lengths,
    norm1_gain,
    query_weight,
    key_weight,
    value_weight,
    lambda_param,
    sub_gain,
    out_weight,
    norm2_gain,
    gate_weight,
    up_weight,
    down_weight,
    out_cotangent,
):
    dp_count = lax.axis_size("dp")
    head_count, lambda_width = lambda_param.shape
    doc_lengths = (short_lengths[0], long_lengths[0])
    map_width = lambda_width // 4
    projections = (query_weight, key_weight, value_weight)
    lambda_parts = lambda_param.reshape(head_count, 4, map_width)
    first_exp = jnp.exp(jnp.sum(lambda_parts[:, 0] * lambda_parts[:, 1], axis=-1))
    second_exp = jnp.exp(jnp.sum(lambda_parts[:, 2] * lambda_parts[:, 3], axis=-1))
    lam = first_exp - second_exp + lambda_base
    sub_scale = sub_gain * (1.0 - lambda_base)
    tables = []
    for m in range(2):
        position, segment = doc_tables(doc_lengths[m], layer_in.shape[1])
        tables.append(
            rotary_tables(position, map_width) + (segment[:, None], segment[None, :])
        )
    depth, inner = query_weight.shape
    shapes = (
        depth, layer_in.shape[1], inner, gate_weight.shape[1], head_count, sub_gain.shape[1],
    )
    blocks = [*tables[0], *tables[1], sub_scale, norm1_gain[None, :], norm2_gain[None, :]]
    arrays = [layer_in, out_cotangent, *projections, out_weight]
    arrays += [gate_weight, up_weight, down_weight]
    parts = front_call(lam, arrays, blocks, shapes)
    pick = lambda at: [parts[at], parts[at + 14]]
    arrays = pick(0) + pick(1) + pick(2) + pick(9) + pick(10) + pick(11) + pick(7)
    arrays += pick(12) + pick(13) + pick(8)
    arrays += [layer_in, out_cotangent, out_weight, *projections]
    arrays += parts[3:7] + parts[17:21]
    grad_down, grad_gate, grad_up, grad_out, grad_qkv, layer_out, grad_in, small = back_call(
        dp_count, lam, arrays, blocks, shapes
    )
    grad_query, grad_key, grad_value = jnp.split(grad_qkv, 3, axis=1)
    per_head = lambda row: row[:inner].reshape(head_count, -1)
    grad_lam = per_head(small[3])[:, :1]
    first_scale = grad_lam * first_exp[:, None]
    second_scale = grad_lam * second_exp[:, None]
    lambda_grad = jnp.concatenate(
        [
            first_scale * lambda_parts[:, 1],
            first_scale * lambda_parts[:, 0],
            -second_scale * lambda_parts[:, 3],
            -second_scale * lambda_parts[:, 2],
        ],
        axis=1,
    )
    index = lax.axis_index("dp")

    def block_of(values):
        size = values.shape[-1] // dp_count
        return lax.dynamic_slice_in_dim(values, index * size, size, values.ndim - 1)

    return (
        layer_out,
        grad_in,
        block_of(small[0]),
        grad_query,
        grad_key,
        grad_value,
        block_of(lambda_grad),
        block_of(per_head(small[2])),
        grad_out.T,
        block_of(small[1]),
        grad_gate,
        grad_up,
        grad_down.T,
    )


def solution(mesh):
    return jax.shard_map(
        on_device,
        mesh=mesh,
        in_specs=(
            P(None, "dp", None),
            P("dp", None),
            P("dp", None),
            P(),
            P(None, "tensor"),
            P(None, "tensor"),
            P(None, "tensor"),
            P("tensor", None),
            P("tensor", None),
            P("tensor", None),
            P(),
            P(None, "tensor"),
            P(None, "tensor"),
            P("tensor", None),
            P(None, "dp", None),
        ),
        out_specs=(
            P(None, "dp", None),
            P(None, "dp", None),
            P("dp"),
            P("dp", "tensor"),
            P("dp", "tensor"),
            P("dp", "tensor"),
            P("tensor", "dp"),
            P("tensor", "dp"),
            P("tensor", "dp"),
            P("dp"),
            P("dp", "tensor"),
            P("dp", "tensor"),
            P("tensor", "dp"),
        ),
        check_vma=False,
    )
```

```python
import functools
import math

import jax
import jax.numpy as jnp
from jax import lax
from jax.experimental import pallas as pl
from jax.experimental.pallas import tpu as pltpu
from jax.sharding import PartitionSpec as P

norm_epsilon = 1e-05
lambda_base = 0.8 - 0.6 * math.exp(-0.3 * 11.0)
rotary_base = 10000.0
closed_score = -1e30
block_rows = 128
longest_document = 256
row_group = 16
send_slots = 3
held_slots = 4
MESH = pl.DeviceIdType.MESH


def doc_tables(lengths, row_count):
    doc_ends = jnp.cumsum(lengths, dtype=jnp.int32)
    places = jnp.arange(row_count, dtype=jnp.int32)
    passed = (places[:, None] >= doc_ends[None, :]).astype(jnp.int32)
    segment = jnp.sum(passed, axis=1, dtype=jnp.int32)
    starts = jnp.sum(passed * lengths[None, :], axis=1, dtype=jnp.int32)
    return (places - starts, segment)


def rotary_tables(position, map_width):
    half_width = map_width // 2
    frequency = rotary_base ** (-2.0 * jnp.arange(half_width, dtype=jnp.float32) / map_width)
    angles = position.astype(jnp.float32)[:, None] * frequency[None, :]
    cosine, sine = jnp.cos(angles), jnp.sin(angles)
    return (
        jnp.concatenate([cosine] * 4, axis=1),
        jnp.concatenate([-sine, sine, -sine, sine], axis=1),
    )


def turn(values, cosine, sine):
    width = values.shape[-1]
    quarter = width // 4
    lane = lax.broadcasted_iota(jnp.int32, values.shape, 1)
    partner = jnp.where(
        lane % (2 * quarter) < quarter,
        pltpu.roll(values, width - quarter, 1),
        pltpu.roll(values, quarter, 1),
    )
    return values * cosine + partner * sine


def map_of(values, which):
    lane = lax.broadcasted_iota(jnp.int32, values.shape, 1)
    mine = (lane >= values.shape[-1] // 2) == (which == 1)
    return jnp.where(mine, values, jnp.zeros_like(values))


def key_range(block):
    first = max(0, block * block_rows - longest_document + 1) // block_rows * block_rows
    return first, (block + 1) * block_rows


def open_pairs(block, segment_column, segment_row):
    first, last = key_range(block)
    rows = pl.ds(block * block_rows, block_rows)
    shape = (block_rows, last - first)
    row_at = lax.broadcasted_iota(jnp.int32, shape, 0) + block * block_rows
    key_at = lax.broadcasted_iota(jnp.int32, shape, 1) + first
    return (segment_column[rows, :] == segment_row[:, first:last]) & (key_at <= row_at)


def softmax_map(query, key, opened, scale):
    scores = jnp.where(opened, dot_t(query, key) * scale, closed_score)
    expanded = jnp.exp(scores - jnp.max(scores, axis=-1, keepdims=True))
    return expanded * (1.0 / jnp.sum(expanded, axis=-1, keepdims=True))


def f32_dot(left, right):
    return jnp.dot(left, right, preferred_element_type=jnp.float32)


def dot_t(left, right):
    return lax.dot_general(
        left, right, (((1,), (1,)), ((), ())), preferred_element_type=jnp.float32
    )


def dot_rows(left, right):
    return lax.dot_general(
        left, right, (((0,), (0,)), ((), ())), preferred_element_type=jnp.float32
    )


def rms_back(incoming, values, inverse_root):
    return inverse_root * incoming - values * inverse_root**3 * jnp.mean(
        incoming * values, axis=-1, keepdims=True
    )


def root_of(values):
    return lax.rsqrt(jnp.mean(values * values, axis=-1, keepdims=True) + norm_epsilon)


def forward_kernel(
    lam, rows, gain, query_weight, key_weight, value_weight, cosine, sine, segment_column,
    segment_row, sub_scale, normed_one, query, key, value, mixed, heads_out,
):
    head_count, width = sub_scale.shape
    scale = (width // 2) ** (-0.5)
    values = rows[...].astype(jnp.float32)
    normed_one[...] = (values * root_of(values) * gain[...]).astype(jnp.bfloat16)
    raw_query = f32_dot(normed_one[...], query_weight[...])
    raw_key = f32_dot(normed_one[...], key_weight[...])
    value[...] = f32_dot(normed_one[...], value_weight[...]).astype(jnp.bfloat16)
    for head in range(head_count):
        at = slice(head * width, (head + 1) * width)
        query[:, at] = turn(raw_query[:, at], cosine[...], sine[...]).astype(jnp.bfloat16)
        key[:, at] = turn(raw_key[:, at], cosine[...], sine[...]).astype(jnp.bfloat16)
    for block in range(rows.shape[0] // block_rows):
        first, last = key_range(block)
        here = slice(block * block_rows, last)
        opened = open_pairs(block, segment_column, segment_row)
        for head in range(head_count):
            at = slice(head * width, (head + 1) * width)
            keys = key[first:last, at]
            maps = [softmax_map(map_of(query[here, at], c), keys, opened, scale) for c in range(2)]
            combined = (maps[0] - lam[head] * maps[1]).astype(jnp.bfloat16)
            out = f32_dot(combined, value[first:last, at])
            mixed[here, at] = out
            heads_out[here, at] = (out * root_of(out) * sub_scale[head : head + 1, :]).astype(
                jnp.bfloat16
            )


def backward_kernel(
    lam, grad_attended, out_weight, query, key, value, mixed, cosine, sine, segment_column,
    segment_row, sub_scale, grad_rows, grad_sub, grad_lam, grad_heads, grad_mixed, grad_key,
    grad_value,
):
    head_count, width = sub_scale.shape
    row_count = query.shape[0]
    inner = head_count * width
    scale = (width // 2) ** (-0.5)
    grad_heads[...] = dot_t(grad_attended[...], out_weight[...])
    for head in range(head_count):
        at = slice(head * width, (head + 1) * width)
        heads = mixed[:, at]
        root = root_of(heads)
        grads = grad_heads[:, at]
        grad_sub[head : head + 1, :] = jnp.sum(grads * heads * root, axis=0, keepdims=True) * (
            1.0 - lambda_base
        )
        grad_mixed[:, at] = rms_back(grads * sub_scale[head : head + 1, :], heads, root).astype(
            jnp.bfloat16
        )
    grad_key[...] = jnp.zeros_like(grad_key)
    grad_value[...] = jnp.zeros_like(grad_value)
    lam_sums = [0.0] * head_count
    for block in range(row_count // block_rows):
        first, last = key_range(block)
        here = slice(block * block_rows, last)
        opened = open_pairs(block, segment_column, segment_row)
        for head in range(head_count):
            at = slice(head * width, (head + 1) * width)
            keys = key[first:last, at]
            queries = [map_of(query[here, at], c) for c in range(2)]
            maps = [softmax_map(queries[c], keys, opened, scale) for c in range(2)]
            mixes = grad_mixed[here, at]
            combined = (maps[0] - lam[head] * maps[1]).astype(jnp.bfloat16)
            grad_value[first:last, at] += dot_rows(combined, mixes)
            grads = dot_t(mixes, value[first:last, at])
            first_sum = jnp.sum(grads * maps[0], axis=-1, keepdims=True)
            second_sum = jnp.sum(grads * maps[1], axis=-1, keepdims=True)
            lam_sums[head] = lam_sums[head] + jnp.sum(second_sum, axis=0, keepdims=True)
            score_grads = [
                (maps[0] * (grads - first_sum)).astype(jnp.bfloat16),
                (maps[1] * (-lam[head] * (grads - second_sum))).astype(jnp.bfloat16),
            ]
            grad_query = f32_dot(score_grads[0], map_of(keys, 0)) + f32_dot(
                score_grads[1], map_of(keys, 1)
            )
            grad_rows[here, at] = turn(
                grad_query * scale, cosine[here, :], -sine[here, :]
            ).astype(jnp.bfloat16)
            grad_key[first:last, at] += dot_rows(score_grads[0], queries[0]) + dot_rows(
                score_grads[1], queries[1]
            )
    for head in range(head_count):
        at = slice(head * width, (head + 1) * width)
        grad_rows[:, inner + head * width : inner + (head + 1) * width] = turn(
            grad_key[:, at] * scale, cosine[...], -sine[...]
        ).astype(jnp.bfloat16)
        grad_lam[head : head + 1, :] = jnp.broadcast_to(-lam_sums[head], (1, width))
    grad_rows[:, 2 * inner :] = grad_value[...].astype(jnp.bfloat16)


def in_vmem(count):
    return [pl.BlockSpec(memory_space=pltpu.VMEM)] * count


class Line:
    def __init__(self, line, widths, total, landed, line_out, line_in, credit):
        self.line, self.widths = line, widths
        self.total, self.landed = total, landed
        self.line_out, self.line_in, self.credit = line_out, line_in, credit
        self.me = lax.axis_index("dp")
        self.place = self.me // 2
        self.ring = total.shape[0]

    def copy(self, c, step, way, block, target):
        width = self.widths[c]
        return pltpu.make_async_remote_copy(
            src_ref=self.total.at[c % self.ring, block, :, :width],
            dst_ref=self.landed.at[way, step, c % 2, :, :width],
            send_sem=self.line_out.at[way, step, c % 2],
            recv_sem=self.line_in.at[way, step, c % 2],
            device_id={"dp": target},
            device_id_type=MESH,
        )

    def sends(self, step, way):
        place, line = self.place, self.line
        if way == 0:
            block = line - 1 - step + place
            return (place <= step) & (place < line - 1), block, self.me + 2
        block = place + step - line + 1
        return (place >= line - 1 - step) & (place > 0), block, self.me - 2

    def gets(self, step, way):
        place, line = self.place, self.line
        if way == 0:
            return (place > 0) & (place - 1 <= step), line - 2 - step + place, self.me - 2
        gets = (place < line - 1) & (place + 1 >= line - 1 - step)
        return gets, place + step - line + 2, self.me + 2

    def start(self, c, step):
        for way in range(2):
            sends, block, target = self.sends(step, way)

            @pl.when(sends)
            def _():
                if c >= 2:
                    pl.semaphore_wait(self.credit.at[way, step], 1)
                self.copy(c, step, way, block, target).start()

    def finish(self, c, step):
        width = self.widths[c]
        for way in range(2):
            gets, block, source = self.gets(step, way)

            @pl.when(gets)
            def _():
                self.copy(c, step, way, block, source).wait_recv()
                self.total[c % self.ring, block, :, :width] += self.landed[
                    way, step, c % 2, :, :width
                ]
                if c + 2 < len(self.widths):
                    pl.semaphore_signal(
                        self.credit.at[way, step],
                        inc=1,
                        device_id={"dp": source},
                        device_id_type=MESH,
                    )

            sends, sent, target = self.sends(step, way)

            @pl.when(sends)
            def _():
                self.copy(c, step, way, sent, target).wait_send()


class Reducer:
    def __init__(self, plan, line_plan, line_starts, line, refs):
        self.plan, self.line_plan, self.line_starts = plan, line_plan, line_starts
        self.line = line
        (
            self.send, self.held, self.total, landed, self.pair_out, self.pair_in,
            line_out, line_in, credit, self.out_sem,
        ) = refs[:10]
        self.first = Line(
            line, [item.width for item in plan], self.total, landed, line_out, line_in, credit
        )
        self.place = self.first.place
        self.me = self.first.me
        self.side = self.me % 2
        self.other = self.me + 1 - 2 * self.side
        self.steps = line - 1
        self.ring = self.total.shape[0]
        self.rows = self.total.shape[2]
        if line_plan:
            (
                self.line_total, landed, line_out, line_in, credit, self.last_held,
                self.last_out, self.last_in, self.line_out_sem,
            ) = refs[10:]
            self.second = Line(
                line, [item.width for item in line_plan], self.line_total, landed, line_out,
                line_in, credit,
            )

    def compute(self, c):
        item = self.plan[c]
        width = item.width
        left, right = item.left(), item.right()

        def block(at, carry):
            first = pl.multiple_of(2 * at * self.rows, self.rows)
            columns = right[...]
            away = left[pl.ds(first + (1 - self.side) * self.rows, self.rows), :]
            here = left[pl.ds(first + self.side * self.rows, self.rows), :]
            self.send[c % send_slots, at, :, :width] = f32_dot(away, columns)
            self.total[c % self.ring, at, :, :width] = f32_dot(here, columns)
            return carry

        lax.fori_loop(0, self.line, block, 0)
        item.computed()

    def line_compute(self, c):
        item = self.line_plan[c]
        left, right = item.left(), item.right()
        slot = c % self.line_total.shape[0]
        if c >= self.line_total.shape[0]:
            self.line_result(c - self.line_total.shape[0]).wait()

        def block(at, carry):
            rows = pl.ds(pl.multiple_of(2 * at * self.rows, 2 * self.rows), 2 * self.rows)
            self.line_total[slot, at] = f32_dot(left[rows, :], right[...])
            return carry

        lax.fori_loop(0, self.line, block, 0)
        item.computed()

    def side_rows(self, side):
        return pl.ds(pl.multiple_of(side * self.rows, self.rows), self.rows)

    def last_copy(self, c):
        slot = c % self.line_total.shape[0]
        return pltpu.make_async_remote_copy(
            src_ref=self.line_total.at[slot, self.place, self.side_rows(1 - self.side), :],
            dst_ref=self.last_held.at[c],
            send_sem=self.last_out.at[c],
            recv_sem=self.last_in.at[c],
            device_id={"dp": self.other},
            device_id_type=MESH,
        )

    def line_result(self, c):
        item = self.line_plan[c]
        slot = c % self.line_total.shape[0]
        return pltpu.make_async_copy(
            self.line_total.at[slot, self.place, self.side_rows(self.side), :],
            item.out.at[:, item.first : item.first + item.width],
            self.line_out_sem.at[slot],
        )

    def line_finish(self, slot):
        for c, start in enumerate(self.line_starts):
            step = slot - 1 - start
            if 0 <= step < self.steps:
                self.second.finish(c, step)
            if step == self.steps:
                self.last_copy(c).wait()
                at = c % self.line_total.shape[0]
                self.line_total[at, self.place, self.side_rows(self.side), :] += self.last_held[c]
                self.line_result(c).start()

    def line_begin(self, slot):
        for c, start in enumerate(self.line_starts):
            step = slot - start
            if 0 <= step < self.steps:
                self.second.start(c, step)
            if step == self.steps:
                self.last_copy(c).start()

    def pair_copy(self, c):
        width = self.plan[c].width
        return pltpu.make_async_remote_copy(
            src_ref=self.send.at[c % send_slots, :, :, :width],
            dst_ref=self.held.at[c % held_slots, :, :, :width],
            send_sem=self.pair_out.at[c % send_slots],
            recv_sem=self.pair_in.at[c % held_slots],
            device_id={"dp": self.other},
            device_id_type=MESH,
        )

    def pair_finish(self, c):
        width = self.plan[c].width
        self.pair_copy(c).wait_recv()

        def block(at, carry):
            self.total[c % self.ring, at, :, :width] += self.held[c % held_slots, at, :, :width]
            return carry

        lax.fori_loop(0, self.line, block, 0)
        self.pair_copy(c).wait_send()

    def out_copy(self, c):
        item = self.plan[c]
        return pltpu.make_async_copy(
            self.total.at[c % self.ring, self.place, :, : item.width],
            item.out.at[:, item.first : item.first + item.width],
            self.out_sem.at[c % self.ring],
        )

    def run(self, tasks):
        count, steps = len(self.plan), self.steps
        begun = [c for c, start in enumerate(self.line_starts) if start == 0]
        self.compute(0)
        self.pair_copy(0).start()
        for c in begun:
            self.line_compute(c)
        self.line_begin(0)
        self.compute(1)
        for slot in range(count + steps + 1):
            for step in range(steps):
                c = slot - 2 - step
                if 0 <= c < count:
                    self.first.finish(c, step)
            self.line_finish(slot)
            if 0 <= slot - 1 < count:
                self.pair_finish(slot - 1)
            for step in range(steps):
                c = slot - 1 - step
                if 0 <= c < count:
                    self.first.start(c, step)
            if slot:
                self.line_begin(slot)
            if slot + 1 < count:
                self.pair_copy(slot + 1).start()
            done = slot - 1 - steps
            if 0 <= done < count:
                self.out_copy(done).start()
            if slot + 2 < count:
                if slot + 2 >= self.ring:
                    self.out_copy(slot + 2 - self.ring).wait()
                self.compute(slot + 2)
            for c, start in enumerate(self.line_starts):
                if slot and start == slot + 1:
                    self.line_compute(c)
            for task in tasks.get(slot, ()):
                task()
        for c in range(max(0, count - self.ring), count):
            self.out_copy(c).wait()
        if self.line_plan:
            for c in range(len(self.line_plan) - self.line_total.shape[0], len(self.line_plan)):
                self.line_result(c).wait()


class Chunk:
    def __init__(self, left, right, computed, out, first, width):
        self.left, self.right, self.computed = left, right, computed
        self.out, self.first, self.width = out, first, width


def for_rows(count, body):
    def step(i, carry):
        body(pl.ds(pl.multiple_of(i * row_group, row_group), row_group))
        return carry

    lax.fori_loop(0, count // row_group, step, 0)


class TensorSum:
    def __init__(self, uses, own, near, far, near_sems, far_sems, near_credit, far_credit):
        self.own, self.near, self.far = own, near, far
        self.near_sems, self.far_sems = near_sems, far_sems
        self.near_credit, self.far_credit = near_credit, far_credit
        index = lax.axis_index("tensor")
        self.core_peer = index + 1 - 2 * (index % 2)
        self.far_peer = index + 2 - 4 * (index // 2)
        self.near_left, self.far_left = 2 * uses, uses
        self.near_first, self.far_first = True, True

    def near_copy(self, source):
        return pltpu.make_async_remote_copy(
            src_ref=source, dst_ref=self.near, send_sem=self.near_sems.at[0],
            recv_sem=self.near_sems.at[1], device_id={"tensor": self.core_peer},
            device_id_type=MESH,
        )

    def far_copy(self):
        return pltpu.make_async_remote_copy(
            src_ref=self.own, dst_ref=self.far, send_sem=self.far_sems.at[0],
            recv_sem=self.far_sems.at[1], device_id={"tensor": self.far_peer},
            device_id_type=MESH,
        )

    def near_start(self, source):
        if not self.near_first:
            pl.semaphore_wait(self.near_credit, 1)
        self.near_first = False
        self.pending = source
        self.near_copy(source).start()

    def near_wait(self):
        self.near_copy(self.pending).wait()

    def near_free(self):
        self.near_left -= 1
        if self.near_left:
            pl.semaphore_signal(
                self.near_credit, inc=1, device_id={"tensor": self.core_peer}, device_id_type=MESH
            )

    def near_add(self):
        self.near_wait()

        def add(rows):
            self.own[rows, :] += self.near[rows, :]

        for_rows(self.own.shape[0], add)
        self.near_free()

    def far_go(self):
        if not self.far_first:
            pl.semaphore_wait(self.far_credit, 1)
        self.far_first = False
        self.far_copy().start()

    def far_wait(self):
        self.far_copy().wait()

    def far_free(self):
        self.far_left -= 1
        if self.far_left:
            pl.semaphore_signal(
                self.far_credit, inc=1, device_id={"tensor": self.far_peer}, device_id_type=MESH
            )


def line_first(dp_count):
    return (0, 0, 3, 6, 9, 12) if dp_count == 8 else ()


def back_kernel(dp_count, *refs):
    refs = list(refs)
    take = lambda n: [refs.pop(0) for _ in range(n)]
    (lam,) = take(1)
    cot_left, two_left, one_left = [take(2) for _ in range(3)]
    hidden, gate_pre, up_pre, heads = [take(2) for _ in range(4)]
    part_back, part_fed, middle = [take(2) for _ in range(3)]
    (layer_in, cotangent) = take(2)
    weights_in = take(4)
    kept_in = [take(4) for _ in range(2)]
    tables = [take(4) for _ in range(2)]
    (sub_scale, gain_one, gain_two) = take(3)
    (grad_down, grad_gate, grad_up, grad_out, grad_qkv, layer_out, grad_in, small_out) = take(8)
    reducer_refs = take(20 if line_first(dp_count) else 10)
    line_rights = reducer_refs.pop() if line_first(dp_count) else None
    (left_a, left_b, rights, rows_qkv) = take(4)
    weights = take(4)
    kept = take(4)
    backward_scratch = take(4)
    (grad_sub, grad_lam) = take(2)
    sets = [take(3) for _ in range(2)]
    through = take(2)
    (spare, projected, attended, rows_in, rows_out) = take(5)
    (small, small_near, small_landed) = take(3)
    (near_sems, far_sems, near_credit, far_credit) = take(4)
    (load_sems, small_near_sems, small_send, small_recv) = take(4)
    assert not refs

    me = lax.axis_index("dp")
    tensor = lax.axis_index("tensor")
    core = tensor % 2
    core_peer = tensor + 1 - 2 * core
    far_peer = tensor + 2 - 4 * (tensor // 2)
    line = dp_count // 2
    half = middle[0].shape[0]
    row_count = 2 * half
    head_count, head_width = sub_scale.shape
    out_weight, projections = weights[0], weights[1:]
    inner = out_weight.shape[0]
    kept_half = pl.ds(pl.multiple_of(core * half, half), half)
    sent_half = pl.ds(pl.multiple_of((1 - core) * half, half), half)
    tokens = [slice(m * row_count, (m + 1) * row_count) for m in range(2)]

    barrier = pltpu.get_barrier_semaphore()
    for offset in range(1, dp_count):
        pl.semaphore_signal(
            barrier, inc=1, device_id={"dp": lax.rem(me + offset, dp_count)}, device_id_type=MESH
        )
    for peer in (core_peer, far_peer):
        pl.semaphore_signal(barrier, inc=1, device_id={"tensor": peer}, device_id_type=MESH)
    pl.semaphore_wait(barrier, dp_count + 1)

    used = [0]

    def load(source, target):
        copy = pltpu.make_async_copy(source, target, load_sems.at[used[0]])
        used[0] += 1
        copy.start()
        return copy

    def wait_all(copies):
        for copy in copies:
            copy.wait()

    reducer_width = reducer_refs[0].shape[-1]
    plan, sources, left_loads, right_loads = [], {}, {}, {}

    def load_left(sources_of, left):
        return [load(sources_of[m], left.at[:, tokens[m]]) for m in range(2)]

    def load_columns(source, first, width, target):
        return [
            load(source[m].at[:, first : first + width], target.at[tokens[m], :width])
            for m in range(2)
        ]

    def load_right(c):
        if c in sources:
            right_loads[c] = load_columns(*sources[c], rights.at[c % 2])

    def load_line_right(c):
        if c < len(line_sources):
            line_loads[c] = load_columns(*line_sources[c], line_rights.at[c % 2])

    def get_left(c, left):
        wait_all(left_loads.pop(c, ()))
        return left

    def get_line_left(left):
        if left is left_b and first_two in left_loads:
            wait_all(left_loads.pop(first_two))
        return left

    def get_right(c, first, width):
        if c in sources:
            wait_all(right_loads[c])
            return rights.at[c % 2, :, :width]
        return rows_qkv.at[:, first : first + width]

    def get_line_right(c):
        wait_all(line_loads[c])
        return line_rights.at[c % 2]

    def computed(c):
        load_right(c + 2)
        if c == last_two:
            left_loads[first_one] = load_left(one_left, left_b)

    def add_group(left, source, columns, out, line_chunks=0):
        start = line_chunks * line_width
        for first in range(0, start, line_width):
            c = len(line_plan)
            line_sources.append((source, first, line_width))
            line_plan.append(
                Chunk(
                    functools.partial(get_line_left, left),
                    functools.partial(get_line_right, c),
                    functools.partial(load_line_right, c + 2),
                    out,
                    first,
                    line_width,
                )
            )
        for first in range(start, columns, reducer_width):
            width = min(reducer_width, columns - first)
            c = len(plan)
            if source is not None:
                sources[c] = (source, first, width)
            plan.append(
                Chunk(
                    functools.partial(get_left, c, left),
                    functools.partial(get_right, c, first, width),
                    functools.partial(computed, c),
                    out,
                    first,
                    width,
                )
            )

    line_starts = line_first(dp_count)
    line_plan, line_sources, line_loads, line_width = [], [], {}, 128
    late = len(line_starts) // 3
    add_group(left_a, hidden, hidden[0].shape[1], grad_down)
    first_two = len(plan)
    add_group(left_b, gate_pre, gate_pre[0].shape[1], grad_gate, late)
    add_group(left_b, up_pre, up_pre[0].shape[1], grad_up, late)
    last_two = len(plan) - 1
    add_group(left_a, heads, inner, grad_out, late)
    first_one = len(plan)
    add_group(left_b, None, 3 * inner, grad_qkv)

    left_loads[0] = load_left(cot_left, left_a)
    load_right(0)
    left_loads[first_two] = load_left(two_left, left_b)
    load_line_right(0)
    load_line_right(1)
    load_right(1)
    sums = [
        TensorSum(
            3, *sets[m], near_sems.at[m], far_sems.at[m], near_credit.at[m], far_credit.at[m]
        )
        for m in range(2)
    ]
    own_loads = {}
    for m in range(2):
        own_loads[m] = load(part_back[m].at[kept_half], sets[m][0])
        sums[m].near_start(part_back[m].at[sent_half])
    weight_loads = [load(*pair) for pair in zip(weights_in, weights)]
    kept_loads = [load(*pair) for pair in zip(kept_in[0], kept)]
    spare_queue = [middle[0], middle[1], middle[0], middle[1]]
    rows_queue = [cotangent.at[0], cotangent.at[1]]
    rows_queue += [layer_in.at[0], cotangent.at[0], layer_in.at[1], cotangent.at[1]]
    queued = {}

    def next_spare():
        queued["spare"] = load(spare_queue.pop(0), spare) if spare_queue else None

    def next_rows():
        queued["rows"] = load(rows_queue.pop(0), rows_in) if rows_queue else None

    next_spare()
    next_rows()
    out_loads = []
    small[...] = jnp.zeros_like(small)

    def mine(rows):
        return pl.ds(pl.multiple_of(core * half + rows.start, row_group), row_group)

    def others(rows):
        return pl.ds(pl.multiple_of((1 - core) * half + rows.start, row_group), row_group)

    def exchange(m):
        if m in own_loads:
            own_loads.pop(m).wait()
        sums[m].near_add()
        sums[m].far_go()

    def norm_two(m):
        own, near, far = sets[m]
        queued["spare"].wait()
        sums[m].far_wait()

        def body(rows):
            grads = own[rows, :] + far[rows, :]
            values = spare[rows, :]
            root = root_of(values)
            small[1:2, :] += jnp.sum(grads * values * root, axis=0, keepdims=True)
            through[m][rows, :] = rms_back(grads * gain_two[...], values, root)

        for_rows(half, body)
        sums[m].far_free()
        sums[m].near_start(through[m])
        next_spare()

    def attend(m):
        near = sets[m][1]
        queued["rows"].wait()
        sums[m].near_wait()

        def body(rows):
            attended[mine(rows), :] = (
                rows_in[mine(rows), :].astype(jnp.float32) + through[m][rows, :]
            ).astype(jnp.bfloat16)
            attended[others(rows), :] = (
                rows_in[others(rows), :].astype(jnp.float32) + near[rows, :]
            ).astype(jnp.bfloat16)

        for_rows(half, body)
        sums[m].near_free()
        next_rows()

        def flip_block(i, carry):
            at = pl.ds(pl.multiple_of(i * 128, 128), 128)
            left_a[at, tokens[m]] = attended[:, at].T
            return carry

        lax.fori_loop(0, attended.shape[1] // 128, flip_block, 0)
        if m == 0:
            wait_all(weight_loads)
        wait_all(kept_loads)
        backward_kernel(
            lam, attended, out_weight, *kept, *tables[m], sub_scale,
            rows_qkv.at[tokens[m], :], grad_sub, grad_lam, *backward_scratch,
        )
        if m == 0:
            kept_loads[:] = [load(*pair) for pair in zip(kept_in[1], kept)]
        for head in range(head_count):
            at = slice(head * head_width, (head + 1) * head_width)
            small[2:3, at] += grad_sub[head : head + 1, :]
            small[3:4, at] += grad_lam[head : head + 1, :]

    def project(m):
        def part(which, target):
            rows = pl.ds(pl.multiple_of(m * row_count + which * half, half), half)

            def block(i, carry):
                at = pl.ds(pl.multiple_of(i * 512, 512), 512)
                total = 0.0
                for p in range(3):
                    grads = rows_qkv[rows, p * inner : (p + 1) * inner]
                    total = total + dot_t(grads, projections[p][at, :])
                target[:, at] = total
                return carry

            lax.fori_loop(0, target.shape[1] // 512, block, 0)

        part(1 - core, projected)
        sums[m].near_start(projected)
        part(core, sets[m][0])

    def norm_one(m):
        own, near, far = sets[m]
        queued["rows"].wait()
        sums[m].far_wait()

        def body(rows):
            grads = own[rows, :] + far[rows, :]
            values = rows_in[mine(rows), :].astype(jnp.float32)
            root = root_of(values)
            small[0:1, :] += jnp.sum(grads * values * root, axis=0, keepdims=True)
            through[m][rows, :] += rms_back(grads * gain_one[...], values, root)

        for_rows(half, body)
        sums[m].far_free()
        sums[m].near_start(through[m])
        next_rows()
        own_loads[m] = load(part_fed[m].at[kept_half], own)

    def store_rows(target):
        out_loads.append(load(rows_out, target))

    def finish_in(m):
        near = sets[m][1]
        queued["rows"].wait()
        sums[m].near_wait()
        wait_all(out_loads)
        out_loads.clear()

        def body(rows):
            rows_out[mine(rows), :] = (
                rows_in[mine(rows), :].astype(jnp.float32) + through[m][rows, :]
            ).astype(jnp.bfloat16)
            rows_out[others(rows), :] = (
                rows_in[others(rows), :].astype(jnp.float32) + near[rows, :]
            ).astype(jnp.bfloat16)

        for_rows(half, body)
        sums[m].near_free()
        next_rows()
        store_rows(grad_in.at[m])
        sums[m].near_start(part_fed[m].at[sent_half])

    def add_fed(m):
        own, near, far = sets[m]
        queued["spare"].wait()
        sums[m].far_wait()

        def body(rows):
            own[rows, :] = spare[rows, :] + (own[rows, :] + far[rows, :])

        for_rows(half, body)
        sums[m].far_free()
        sums[m].near_start(own)
        next_spare()

    def finish_out(m):
        own, near = sets[m][:2]
        sums[m].near_wait()
        wait_all(out_loads)
        out_loads.clear()

        def body(rows):
            rows_out[mine(rows), :] = own[rows, :].astype(jnp.bfloat16)
            rows_out[others(rows), :] = near[rows, :].astype(jnp.bfloat16)

        for_rows(half, body)
        sums[m].near_free()
        store_rows(layer_out.at[m])

    small_core = pltpu.make_async_remote_copy(
        src_ref=small, dst_ref=small_near, send_sem=small_near_sems.at[0],
        recv_sem=small_near_sems.at[1], device_id={"tensor": core_peer}, device_id_type=MESH,
    )

    def small_copy(offset):
        return pltpu.make_async_remote_copy(
            src_ref=small, dst_ref=small_landed.at[offset - 1], send_sem=small_send.at[offset - 1],
            recv_sem=small_recv.at[offset - 1],
            device_id={"dp": lax.rem(me + offset, dp_count)}, device_id_type=MESH,
        )

    def small_spread():
        small_core.wait()
        small[0:2, :] += small_near[0:2, :]
        for offset in range(1, dp_count):
            small_copy(offset).start()

    def small_finish():
        for offset in range(1, dp_count):
            small_copy(offset).wait()
        total = small[...]
        for offset in range(1, dp_count):
            total = total + small_landed[offset - 1]
        small_near[...] = total
        out_loads.append(load(small_near, small_out))

    order = {
        0: [lambda: exchange(0)],
        2: [lambda: norm_two(0), lambda: exchange(1)],
        3: [lambda: attend(0), lambda: project(0)],
        4: [lambda: norm_two(1), lambda: exchange(0)],
        5: [lambda: attend(1), lambda: project(1)],
        6: [lambda: norm_one(0), lambda: exchange(1)],
        7: [lambda: finish_in(0)],
        8: [lambda: norm_one(1), lambda: exchange(0), small_core.start],
        9: [lambda: finish_in(1), small_spread],
        10: [lambda: add_fed(0), lambda: exchange(1), small_finish],
        11: [lambda: finish_out(0)],
        12: [lambda: add_fed(1)],
        13: [lambda: finish_out(1)],
    }
    stretch = 256 // reducer_width
    tasks = {slot * stretch: items for slot, items in order.items()}
    Reducer(plan, line_plan, line_starts, line, reducer_refs).run(tasks)
    wait_all(out_loads)


def back_call(dp_count, lam, arrays, blocks, shapes):
    depth, row_count, inner, hidden_count, head_count, head_width = shapes
    line = dp_count // 2
    rows = depth // dp_count
    half = row_count // 2
    width = 256 if line <= 4 else 128
    ring = line + 3
    starts = line_first(dp_count)
    wide = (line, rows, width)
    bf16, f32 = jnp.bfloat16, jnp.float32
    dma, regular = pltpu.SemaphoreType.DMA, pltpu.SemaphoreType.REGULAR
    wide_half = pltpu.VMEM((half, depth), f32)
    wide_rows = pltpu.VMEM((row_count, depth), bf16)
    narrow = pltpu.VMEM((row_count, inner), bf16)
    narrow_f32 = pltpu.VMEM((row_count, inner), f32)
    small = pltpu.VMEM((8, depth), f32)
    grad = lambda columns: jax.ShapeDtypeStruct((rows, columns), f32)
    rows_shape = jax.ShapeDtypeStruct((2, row_count, depth), bf16)
    flops = 2 * 2 * row_count * depth * (3 * hidden_count + 8 * inner)
    return pl.pallas_call(
        functools.partial(back_kernel, dp_count),
        out_shape=[grad(hidden_count)] * 3
        + [grad(inner), grad(3 * inner), rows_shape, rows_shape]
        + [jax.ShapeDtypeStruct((8, depth), f32)],
        in_specs=[pl.BlockSpec(memory_space=pltpu.SMEM)]
        + [pl.BlockSpec(memory_space=pl.ANY)] * len(arrays)
        + in_vmem(len(blocks)),
        out_specs=[pl.BlockSpec(memory_space=pl.ANY)] * 8,
        scratch_shapes=[
            pltpu.VMEM((send_slots,) + wide, f32),
            pltpu.VMEM((held_slots,) + wide, f32),
            pltpu.VMEM((ring,) + wide, f32),
            pltpu.VMEM((2, line - 1, 2, rows, width), f32),
            dma((send_slots,)),
            dma((held_slots,)),
            dma((2, line - 1, 2)),
            dma((2, line - 1, 2)),
            regular((2, line - 1)),
            dma((ring,)),
        ]
        + (
            [
                pltpu.VMEM((3, line, 2 * rows, 128), f32),
                pltpu.VMEM((2, line - 1, 2, 2 * rows, 128), f32),
                dma((2, line - 1, 2)),
                dma((2, line - 1, 2)),
                regular((2, line - 1)),
                pltpu.VMEM((len(starts), rows, 128), f32),
                dma((len(starts),)),
                dma((len(starts),)),
                dma((3,)),
                pltpu.VMEM((2, 2 * row_count, 128), bf16),
            ]
            if starts
            else []
        )
        + [
            pltpu.VMEM((depth, 2 * row_count), bf16),
            pltpu.VMEM((depth, 2 * row_count), bf16),
            pltpu.VMEM((2, 2 * row_count, width), bf16),
            pltpu.VMEM((2 * row_count, 3 * inner), bf16),
            pltpu.VMEM((inner, depth), bf16),
        ]
        + [pltpu.VMEM((depth, inner), bf16)] * 3
        + [narrow, narrow, narrow, narrow_f32]
        + [narrow_f32, narrow, narrow_f32, narrow_f32]
        + [pltpu.VMEM((head_count, head_width), f32)] * 2
        + [wide_half] * 10
        + [wide_rows] * 3
        + [
            small,
            small,
            pltpu.VMEM((dp_count - 1, 8, depth), f32),
            dma((2, 2)),
            dma((2, 2)),
            regular((2,)),
            regular((2,)),
            dma((128,)),
            dma((2,)),
            dma((dp_count - 1,)),
            dma((dp_count - 1,)),
        ],
        compiler_params=pltpu.CompilerParams(
            collective_id=0, has_side_effects=True, vmem_limit_bytes=62 * 1024 * 1024
        ),
        cost_estimate=pl.CostEstimate(flops=flops, bytes_accessed=64 << 20, transcendentals=0),
    )(lam, *arrays, *blocks)


def front_kernel(*refs):
    refs = list(refs)
    take = lambda n: [refs.pop(0) for _ in range(n)]
    (lam,) = take(1)
    layer_in, cotangent = take(2)
    weights_in = take(7)
    tables = [take(4) for _ in range(2)]
    (sub_scale, gain_one, gain_two) = take(3)
    outs = [take(14) for _ in range(2)]
    rows_in, cot_rows = take(2), take(2)
    (normed_one, normed_two, flipped) = take(3)
    weights = take(7)
    kept = [take(5) for _ in range(2)]
    sets = [take(3) for _ in range(2)]
    (projected,) = take(1)
    hidden = [take(3) for _ in range(2)]
    (back, fed) = take(2)
    (near_sems, far_sems, near_credit, load_sems) = take(4)
    assert not refs

    tensor = lax.axis_index("tensor")
    core = tensor % 2
    out_weight, gate_weight, up_weight, down_weight = weights[3:]
    row_count, depth = normed_one.shape
    half = row_count // 2
    hidden_count = gate_weight.shape[1]
    used = [0]

    def load(source, target):
        copy = pltpu.make_async_copy(source, target, load_sems.at[used[0]])
        used[0] += 1
        copy.start()
        return copy

    def wait_all(copies):
        for copy in copies:
            copy.wait()
        copies.clear()

    rows_loads = [load(layer_in.at[0], rows_in[0])]
    weight_loads = [load(*pair) for pair in zip(weights_in[:4], weights[:4])]
    rows_loads.append(load(layer_in.at[1], rows_in[1]))
    cot_loads = [load(cotangent.at[m], cot_rows[m]) for m in range(2)]
    wide_loads = [load(*pair) for pair in zip(weights_in[4:], weights[4:])]

    barrier = pltpu.get_barrier_semaphore()
    for peer in (tensor + 1 - 2 * core, tensor + 2 - 4 * (tensor // 2)):
        pl.semaphore_signal(barrier, inc=1, device_id={"tensor": peer}, device_id_type=MESH)
    pl.semaphore_wait(barrier, 2)
    sums = [
        TensorSum(1, *sets[m], near_sems.at[m], far_sems.at[m], near_credit.at[m], None)
        for m in range(2)
    ]
    out_loads, flip_loads, wide_outs = [], [], []

    def mine(rows):
        return pl.ds(pl.multiple_of(core * half + rows.start, row_group), row_group)

    def others(rows):
        return pl.ds(pl.multiple_of((1 - core) * half + rows.start, row_group), row_group)

    def flip_to(source, target):
        wait_all(flip_loads)

        def block(i, carry):
            at = pl.ds(pl.multiple_of(i * 128, 128), 128)
            flipped[at, :] = source[:, at].T
            return carry

        lax.fori_loop(0, depth // 128, block, 0)
        flip_loads.append(load(flipped, target))

    def attend(m):
        rows_loads[m].wait()
        if m == 0:
            wait_all(weight_loads)
        forward_kernel(
            lam, rows_in[m], gain_one, *weights[:3], *tables[m], sub_scale, normed_one, *kept[m]
        )
        heads = kept[m][4]

        def part(which, target):
            rows = pl.ds(pl.multiple_of(which * half, half), half)

            def block(i, carry):
                at = pl.ds(pl.multiple_of(i * 512, 512), 512)
                target[:, at] = f32_dot(heads[rows, :], out_weight[:, at])
                return carry

            lax.fori_loop(0, depth // 512, block, 0)

        part(1 - core, projected)
        sums[m].near_start(projected)
        part(core, sets[m][0])
        out_loads.extend(load(*pair) for pair in zip(kept[m], outs[m][3:8]))
        flip_to(normed_one, outs[m][2])
        sums[m].near_add()

    def norm_rows(rows, values):
        return (values * root_of(values) * gain_two[...]).astype(jnp.bfloat16)

    def join(m):
        own, near, far = sets[m]

        def add(rows):
            values = rows_in[m][mine(rows), :].astype(jnp.float32)
            own[rows, :] = values + (own[rows, :] + far[rows, :])

        def norm_mine(rows):
            normed_two[mine(rows), :] = norm_rows(rows, own[rows, :])

        def norm_others(rows):
            normed_two[others(rows), :] = norm_rows(rows, near[rows, :])

        for_rows(half, add)
        sums[m].near_start(own)
        out_loads.append(load(own, outs[m][8]))
        for_rows(half, norm_mine)
        sums[m].near_wait()
        for_rows(half, norm_others)
        sums[m].near_free()

    def feed(m):
        inside, gate_pre, up_pre = hidden[m]
        if m == 0:
            wait_all(wide_loads)

        def block(j, carry):
            at = pl.ds(pl.multiple_of(j * 256, 256), 256)
            gate = f32_dot(normed_two[...], gate_weight[:, at])
            upward = f32_dot(normed_two[...], up_weight[:, at])
            grads = dot_t(cot_rows[m][...], down_weight[at, :])
            sigmoid = jax.nn.sigmoid(gate)
            inside[:, at] = (gate * sigmoid * upward).astype(jnp.bfloat16)
            gate_pre[:, at] = (
                grads * upward * sigmoid * (1.0 + gate * (1.0 - sigmoid))
            ).astype(jnp.bfloat16)
            up_pre[:, at] = (grads * gate * sigmoid).astype(jnp.bfloat16)
            return carry

        lax.fori_loop(0, hidden_count // 256, block, 0)
        out_loads.extend(load(*pair) for pair in zip(hidden[m], outs[m][9:12]))
        wait_all(wide_outs)

        def through(i, carry):
            at = pl.ds(pl.multiple_of(i * 512, 512), 512)
            back[:, at] = dot_t(gate_pre[...], gate_weight[at, :]) + dot_t(
                up_pre[...], up_weight[at, :]
            )
            fed[:, at] = f32_dot(inside[...], down_weight[:, at])
            return carry

        lax.fori_loop(0, depth // 512, through, 0)
        wide_outs.extend([load(back, outs[m][12]), load(fed, outs[m][13])])

    attend(0)
    sums[0].far_go()
    attend(1)
    for m in range(2):
        cot_loads[m].wait()
        flip_to(cot_rows[m], outs[m][0])
    sums[0].far_wait()
    sums[1].far_go()
    join(0)
    feed(0)
    flip_to(normed_two, outs[0][1])
    sums[1].far_wait()
    join(1)
    feed(1)
    flip_to(normed_two, outs[1][1])
    wait_all(flip_loads)
    wait_all(wide_outs)
    wait_all(out_loads)


def front_call(lam, arrays, blocks, shapes):
    depth, row_count, inner, hidden_count = shapes[:4]
    bf16, f32 = jnp.bfloat16, jnp.float32
    dma, regular = pltpu.SemaphoreType.DMA, pltpu.SemaphoreType.REGULAR
    half = row_count // 2
    out_shape = []
    for m in range(2):
        out_shape += [jax.ShapeDtypeStruct((depth, row_count), bf16)] * 3
        out_shape += [jax.ShapeDtypeStruct((row_count, inner), bf16)] * 3
        out_shape += [jax.ShapeDtypeStruct((row_count, inner), f32)]
        out_shape += [jax.ShapeDtypeStruct((row_count, inner), bf16)]
        out_shape += [jax.ShapeDtypeStruct((half, depth), f32)]
        out_shape += [jax.ShapeDtypeStruct((row_count, hidden_count), bf16)] * 3
        out_shape += [jax.ShapeDtypeStruct((row_count, depth), f32)] * 2
    wide_rows = pltpu.VMEM((row_count, depth), bf16)
    narrow = pltpu.VMEM((row_count, inner), bf16)
    wide_half = pltpu.VMEM((half, depth), f32)
    return pl.pallas_call(
        front_kernel,
        out_shape=out_shape,
        in_specs=[pl.BlockSpec(memory_space=pltpu.SMEM)]
        + [pl.BlockSpec(memory_space=pl.ANY)] * len(arrays)
        + in_vmem(len(blocks)),
        out_specs=[pl.BlockSpec(memory_space=pl.ANY)] * len(out_shape),
        scratch_shapes=[wide_rows] * 6
        + [pltpu.VMEM((depth, row_count), bf16)]
        + [pltpu.VMEM((depth, inner), bf16)] * 3
        + [pltpu.VMEM((inner, depth), bf16)]
        + [pltpu.VMEM((depth, hidden_count), bf16)] * 2
        + [pltpu.VMEM((hidden_count, depth), bf16)]
        + [narrow, narrow, narrow, pltpu.VMEM((row_count, inner), f32), narrow] * 2
        + [wide_half] * 7
        + [pltpu.VMEM((row_count, hidden_count), bf16)] * 6
        + [pltpu.VMEM((row_count, depth), f32)] * 2
        + [dma((2, 2)), dma((2, 2)), regular((2,)), dma((64,))],
        compiler_params=pltpu.CompilerParams(
            collective_id=1, has_side_effects=True, vmem_limit_bytes=62 * 1024 * 1024
        ),
        cost_estimate=pl.CostEstimate(
            flops=4 * row_count * depth * (6 * hidden_count + 4 * inner),
            bytes_accessed=64 << 20,
            transcendentals=0,
        ),
    )(lam, *arrays, *blocks)


def on_device(
    layer_in,
    short_lengths,
    long_lengths,
    norm1_gain,
    query_weight,
    key_weight,
    value_weight,
    lambda_param,
    sub_gain,
    out_weight,
    norm2_gain,
    gate_weight,
    up_weight,
    down_weight,
    out_cotangent,
):
    dp_count = lax.axis_size("dp")
    head_count, lambda_width = lambda_param.shape
    doc_lengths = (short_lengths[0], long_lengths[0])
    map_width = lambda_width // 4
    projections = (query_weight, key_weight, value_weight)
    lambda_parts = lambda_param.reshape(head_count, 4, map_width)
    first_exp = jnp.exp(jnp.sum(lambda_parts[:, 0] * lambda_parts[:, 1], axis=-1))
    second_exp = jnp.exp(jnp.sum(lambda_parts[:, 2] * lambda_parts[:, 3], axis=-1))
    lam = first_exp - second_exp + lambda_base
    sub_scale = sub_gain * (1.0 - lambda_base)
    tables = []
    for m in range(2):
        position, segment = doc_tables(doc_lengths[m], layer_in.shape[1])
        tables.append(
            rotary_tables(position, map_width) + (segment[:, None], segment[None, :])
        )
    depth, inner = query_weight.shape
    shapes = (
        depth, layer_in.shape[1], inner, gate_weight.shape[1], head_count, sub_gain.shape[1],
    )
    blocks = [*tables[0], *tables[1], sub_scale, norm1_gain[None, :], norm2_gain[None, :]]
    arrays = [layer_in, out_cotangent, *projections, out_weight]
    arrays += [gate_weight, up_weight, down_weight]
    parts = front_call(lam, arrays, blocks, shapes)
    pick = lambda at: [parts[at], parts[at + 14]]
    arrays = pick(0) + pick(1) + pick(2) + pick(9) + pick(10) + pick(11) + pick(7)
    arrays += pick(12) + pick(13) + pick(8)
    arrays += [layer_in, out_cotangent, out_weight, *projections]
    arrays += parts[3:7] + parts[17:21]
    grad_down, grad_gate, grad_up, grad_out, grad_qkv, layer_out, grad_in, small = back_call(
        dp_count, lam, arrays, blocks, shapes
    )
    grad_query, grad_key, grad_value = jnp.split(grad_qkv, 3, axis=1)
    per_head = lambda row: row[:inner].reshape(head_count, -1)
    grad_lam = per_head(small[3])[:, :1]
    first_scale = grad_lam * first_exp[:, None]
    second_scale = grad_lam * second_exp[:, None]
    lambda_grad = jnp.concatenate(
        [
            first_scale * lambda_parts[:, 1],
            first_scale * lambda_parts[:, 0],
            -second_scale * lambda_parts[:, 3],
            -second_scale * lambda_parts[:, 2],
        ],
        axis=1,
    )
    index = lax.axis_index("dp")

    def block_of(values):
        size = values.shape[-1] // dp_count
        return lax.dynamic_slice_in_dim(values, index * size, size, values.ndim - 1)

    return (
        layer_out,
        grad_in,
        block_of(small[0]),
        grad_query,
        grad_key,
        grad_value,
        block_of(lambda_grad),
        block_of(per_head(small[2])),
        grad_out.T,
        block_of(small[1]),
        grad_gate,
        grad_up,
        grad_down.T,
    )


def solution(mesh):
    return jax.shard_map(
        on_device,
        mesh=mesh,
        in_specs=(
            P(None, "dp", None),
            P("dp", None),
            P("dp", None),
            P(),
            P(None, "tensor"),
            P(None, "tensor"),
            P(None, "tensor"),
            P("tensor", None),
            P("tensor", None),
            P("tensor", None),
            P(),
            P(None, "tensor"),
            P(None, "tensor"),
            P("tensor", None),
            P(None, "dp", None),
        ),
        out_specs=(
            P(None, "dp", None),
            P(None, "dp", None),
            P("dp"),
            P("dp", "tensor"),
            P("dp", "tensor"),
            P("dp", "tensor"),
            P("tensor", "dp"),
            P("tensor", "dp"),
            P("tensor", "dp"),
            P("dp"),
            P("dp", "tensor"),
            P("dp", "tensor"),
            P("tensor", "dp"),
        ),
        check_vma=False,
    )
```

```python
import functools
import math

import jax
import jax.numpy as jnp
from jax import lax
from jax.experimental import pallas as pl
from jax.experimental.pallas import tpu as pltpu
from jax.sharding import PartitionSpec as P

norm_epsilon = 1e-05
lambda_base = 0.8 - 0.6 * math.exp(-0.3 * 11.0)
rotary_base = 10000.0
closed_score = -1e30
block_rows = 128
longest_document = 256
row_group = 16
send_slots = 3
held_slots = 4
MESH = pl.DeviceIdType.MESH


def doc_tables(lengths, row_count):
    doc_ends = jnp.cumsum(lengths, dtype=jnp.int32)
    places = jnp.arange(row_count, dtype=jnp.int32)
    passed = (places[:, None] >= doc_ends[None, :]).astype(jnp.int32)
    segment = jnp.sum(passed, axis=1, dtype=jnp.int32)
    starts = jnp.sum(passed * lengths[None, :], axis=1, dtype=jnp.int32)
    return (places - starts, segment)


def rotary_tables(position, map_width):
    half_width = map_width // 2
    frequency = rotary_base ** (-2.0 * jnp.arange(half_width, dtype=jnp.float32) / map_width)
    angles = position.astype(jnp.float32)[:, None] * frequency[None, :]
    cosine, sine = jnp.cos(angles), jnp.sin(angles)
    return (
        jnp.concatenate([cosine] * 4, axis=1),
        jnp.concatenate([-sine, sine, -sine, sine], axis=1),
    )


def turn(values, cosine, sine):
    width = values.shape[-1]
    quarter = width // 4
    lane = lax.broadcasted_iota(jnp.int32, values.shape, 1)
    partner = jnp.where(
        lane % (2 * quarter) < quarter,
        pltpu.roll(values, width - quarter, 1),
        pltpu.roll(values, quarter, 1),
    )
    return values * cosine + partner * sine


def map_of(values, which):
    lane = lax.broadcasted_iota(jnp.int32, values.shape, 1)
    mine = (lane >= values.shape[-1] // 2) == (which == 1)
    return jnp.where(mine, values, jnp.zeros_like(values))


def key_range(block):
    first = max(0, block * block_rows - longest_document + 1) // block_rows * block_rows
    return first, (block + 1) * block_rows


def open_pairs(block, segment_column, segment_row):
    first, last = key_range(block)
    rows = pl.ds(block * block_rows, block_rows)
    shape = (block_rows, last - first)
    row_at = lax.broadcasted_iota(jnp.int32, shape, 0) + block * block_rows
    key_at = lax.broadcasted_iota(jnp.int32, shape, 1) + first
    return (segment_column[rows, :] == segment_row[:, first:last]) & (key_at <= row_at)


def softmax_map(query, key, opened, scale):
    scores = jnp.where(opened, dot_t(query, key) * scale, closed_score)
    expanded = jnp.exp(scores - jnp.max(scores, axis=-1, keepdims=True))
    return expanded * (1.0 / jnp.sum(expanded, axis=-1, keepdims=True))


def f32_dot(left, right):
    return jnp.dot(left, right, preferred_element_type=jnp.float32)


def dot_t(left, right):
    return lax.dot_general(
        left, right, (((1,), (1,)), ((), ())), preferred_element_type=jnp.float32
    )


def dot_rows(left, right):
    return lax.dot_general(
        left, right, (((0,), (0,)), ((), ())), preferred_element_type=jnp.float32
    )


def rms_back(incoming, values, inverse_root):
    return inverse_root * incoming - values * inverse_root**3 * jnp.mean(
        incoming * values, axis=-1, keepdims=True
    )


def root_of(values):
    return lax.rsqrt(jnp.mean(values * values, axis=-1, keepdims=True) + norm_epsilon)


def forward_kernel(
    lam, rows, gain, query_weight, key_weight, value_weight, cosine, sine, segment_column,
    segment_row, sub_scale, normed_one, query, key, value, mixed, heads_out, between,
):
    head_count, width = sub_scale.shape
    scale = (width // 2) ** (-0.5)
    values = rows[...].astype(jnp.float32)
    normed_one[...] = (values * root_of(values) * gain[...]).astype(jnp.bfloat16)
    raw_query = f32_dot(normed_one[...], query_weight[...])
    raw_key = f32_dot(normed_one[...], key_weight[...])
    value[...] = f32_dot(normed_one[...], value_weight[...]).astype(jnp.bfloat16)
    for head in range(head_count):
        at = slice(head * width, (head + 1) * width)
        query[:, at] = turn(raw_query[:, at], cosine[...], sine[...]).astype(jnp.bfloat16)
        key[:, at] = turn(raw_key[:, at], cosine[...], sine[...]).astype(jnp.bfloat16)
    for block in range(rows.shape[0] // block_rows):
        first, last = key_range(block)
        here = slice(block * block_rows, last)
        opened = open_pairs(block, segment_column, segment_row)
        if block in between:
            between[block]()
        for head in range(head_count):
            at = slice(head * width, (head + 1) * width)
            keys = key[first:last, at]
            maps = [softmax_map(map_of(query[here, at], c), keys, opened, scale) for c in range(2)]
            combined = (maps[0] - lam[head] * maps[1]).astype(jnp.bfloat16)
            out = f32_dot(combined, value[first:last, at])
            mixed[here, at] = out
            heads_out[here, at] = (out * root_of(out) * sub_scale[head : head + 1, :]).astype(
                jnp.bfloat16
            )


def backward_kernel(
    lam, grad_attended, out_weight, query, key, value, mixed, cosine, sine, segment_column,
    segment_row, sub_scale, grad_rows, grad_sub, grad_lam, grad_heads, grad_mixed, grad_key,
    grad_value,
):
    head_count, width = sub_scale.shape
    row_count = query.shape[0]
    inner = head_count * width
    scale = (width // 2) ** (-0.5)
    grad_heads[...] = dot_t(grad_attended[...], out_weight[...])
    for head in range(head_count):
        at = slice(head * width, (head + 1) * width)
        heads = mixed[:, at]
        root = root_of(heads)
        grads = grad_heads[:, at]
        grad_sub[head : head + 1, :] = jnp.sum(grads * heads * root, axis=0, keepdims=True) * (
            1.0 - lambda_base
        )
        grad_mixed[:, at] = rms_back(grads * sub_scale[head : head + 1, :], heads, root).astype(
            jnp.bfloat16
        )
    grad_key[...] = jnp.zeros_like(grad_key)
    grad_value[...] = jnp.zeros_like(grad_value)
    lam_sums = [0.0] * head_count
    for block in range(row_count // block_rows):
        first, last = key_range(block)
        here = slice(block * block_rows, last)
        opened = open_pairs(block, segment_column, segment_row)
        for head in range(head_count):
            at = slice(head * width, (head + 1) * width)
            keys = key[first:last, at]
            queries = [map_of(query[here, at], c) for c in range(2)]
            maps = [softmax_map(queries[c], keys, opened, scale) for c in range(2)]
            mixes = grad_mixed[here, at]
            combined = (maps[0] - lam[head] * maps[1]).astype(jnp.bfloat16)
            grad_value[first:last, at] += dot_rows(combined, mixes)
            grads = dot_t(mixes, value[first:last, at])
            first_sum = jnp.sum(grads * maps[0], axis=-1, keepdims=True)
            second_sum = jnp.sum(grads * maps[1], axis=-1, keepdims=True)
            lam_sums[head] = lam_sums[head] + jnp.sum(second_sum, axis=0, keepdims=True)
            score_grads = [
                (maps[0] * (grads - first_sum)).astype(jnp.bfloat16),
                (maps[1] * (-lam[head] * (grads - second_sum))).astype(jnp.bfloat16),
            ]
            grad_query = f32_dot(score_grads[0], map_of(keys, 0)) + f32_dot(
                score_grads[1], map_of(keys, 1)
            )
            grad_rows[here, at] = turn(
                grad_query * scale, cosine[here, :], -sine[here, :]
            ).astype(jnp.bfloat16)
            grad_key[first:last, at] += dot_rows(score_grads[0], queries[0]) + dot_rows(
                score_grads[1], queries[1]
            )
    for head in range(head_count):
        at = slice(head * width, (head + 1) * width)
        grad_rows[:, inner + head * width : inner + (head + 1) * width] = turn(
            grad_key[:, at] * scale, cosine[...], -sine[...]
        ).astype(jnp.bfloat16)
        grad_lam[head : head + 1, :] = jnp.broadcast_to(-lam_sums[head], (1, width))
    grad_rows[:, 2 * inner :] = grad_value[...].astype(jnp.bfloat16)


def in_vmem(count):
    return [pl.BlockSpec(memory_space=pltpu.VMEM)] * count


class Line:
    def __init__(self, line, widths, total, landed, line_out, line_in, credit):
        self.line, self.widths = line, widths
        self.total, self.landed = total, landed
        self.line_out, self.line_in, self.credit = line_out, line_in, credit
        self.me = lax.axis_index("dp")
        self.place = self.me // 2
        self.ring = total.shape[0]

    def copy(self, c, step, way, block, target):
        width = self.widths[c]
        return pltpu.make_async_remote_copy(
            src_ref=self.total.at[c % self.ring, block, :, :width],
            dst_ref=self.landed.at[way, step, c % 2, :, :width],
            send_sem=self.line_out.at[way, step, c % 2],
            recv_sem=self.line_in.at[way, step, c % 2],
            device_id={"dp": target},
            device_id_type=MESH,
        )

    def sends(self, step, way):
        place, line = self.place, self.line
        if way == 0:
            block = line - 1 - step + place
            return (place <= step) & (place < line - 1), block, self.me + 2
        block = place + step - line + 1
        return (place >= line - 1 - step) & (place > 0), block, self.me - 2

    def gets(self, step, way):
        place, line = self.place, self.line
        if way == 0:
            return (place > 0) & (place - 1 <= step), line - 2 - step + place, self.me - 2
        gets = (place < line - 1) & (place + 1 >= line - 1 - step)
        return gets, place + step - line + 2, self.me + 2

    def start(self, c, step):
        for way in range(2):
            sends, block, target = self.sends(step, way)

            @pl.when(sends)
            def _():
                if c >= 2:
                    pl.semaphore_wait(self.credit.at[way, step], 1)
                self.copy(c, step, way, block, target).start()

    def finish(self, c, step):
        width = self.widths[c]
        for way in range(2):
            gets, block, source = self.gets(step, way)

            @pl.when(gets)
            def _():
                self.copy(c, step, way, block, source).wait_recv()
                self.total[c % self.ring, block, :, :width] += self.landed[
                    way, step, c % 2, :, :width
                ]
                if c + 2 < len(self.widths):
                    pl.semaphore_signal(
                        self.credit.at[way, step],
                        inc=1,
                        device_id={"dp": source},
                        device_id_type=MESH,
                    )

            sends, sent, target = self.sends(step, way)

            @pl.when(sends)
            def _():
                self.copy(c, step, way, sent, target).wait_send()


class Reducer:
    def __init__(self, plan, line_plan, line_starts, line, refs):
        self.plan, self.line_plan, self.line_starts = plan, line_plan, line_starts
        self.line = line
        (
            self.send, self.held, self.total, landed, self.pair_out, self.pair_in,
            line_out, line_in, credit, self.out_sem,
        ) = refs[:10]
        self.first = Line(
            line, [item.width for item in plan], self.total, landed, line_out, line_in, credit
        )
        self.place = self.first.place
        self.me = self.first.me
        self.side = self.me % 2
        self.other = self.me + 1 - 2 * self.side
        self.steps = line - 1
        self.ring = self.total.shape[0]
        self.rows = self.total.shape[2]
        if line_plan:
            (
                self.line_total, landed, line_out, line_in, credit, self.last_held,
                self.last_out, self.last_in, self.line_out_sem,
            ) = refs[10:]
            self.second = Line(
                line, [item.width for item in line_plan], self.line_total, landed, line_out,
                line_in, credit,
            )

    def compute(self, c):
        item = self.plan[c]
        width = item.width
        left, right = item.left(), item.right()

        def block(at, carry):
            first = pl.multiple_of(2 * at * self.rows, self.rows)
            columns = right[...]
            away = left[pl.ds(first + (1 - self.side) * self.rows, self.rows), :]
            here = left[pl.ds(first + self.side * self.rows, self.rows), :]
            self.send[c % send_slots, at, :, :width] = f32_dot(away, columns)
            self.total[c % self.ring, at, :, :width] = f32_dot(here, columns)
            return carry

        lax.fori_loop(0, self.line, block, 0)
        item.computed()

    def line_compute(self, c):
        item = self.line_plan[c]
        left, right = item.left(), item.right()
        slot = c % self.line_total.shape[0]
        if c >= self.line_total.shape[0]:
            self.line_result(c - self.line_total.shape[0]).wait()

        def block(at, carry):
            rows = pl.ds(pl.multiple_of(2 * at * self.rows, 2 * self.rows), 2 * self.rows)
            self.line_total[slot, at] = f32_dot(left[rows, :], right[...])
            return carry

        lax.fori_loop(0, self.line, block, 0)
        item.computed()

    def side_rows(self, side):
        return pl.ds(pl.multiple_of(side * self.rows, self.rows), self.rows)

    def last_copy(self, c):
        slot = c % self.line_total.shape[0]
        return pltpu.make_async_remote_copy(
            src_ref=self.line_total.at[slot, self.place, self.side_rows(1 - self.side), :],
            dst_ref=self.last_held.at[c],
            send_sem=self.last_out.at[c],
            recv_sem=self.last_in.at[c],
            device_id={"dp": self.other},
            device_id_type=MESH,
        )

    def line_result(self, c):
        item = self.line_plan[c]
        slot = c % self.line_total.shape[0]
        return pltpu.make_async_copy(
            self.line_total.at[slot, self.place, self.side_rows(self.side), :],
            item.out.at[:, item.first : item.first + item.width],
            self.line_out_sem.at[slot],
        )

    def line_finish(self, slot):
        for c, start in enumerate(self.line_starts):
            step = slot - 1 - start
            if 0 <= step < self.steps:
                self.second.finish(c, step)
            if step == self.steps:
                self.last_copy(c).wait()
                at = c % self.line_total.shape[0]
                self.line_total[at, self.place, self.side_rows(self.side), :] += self.last_held[c]
                self.line_result(c).start()

    def line_begin(self, slot):
        for c, start in enumerate(self.line_starts):
            step = slot - start
            if 0 <= step < self.steps:
                self.second.start(c, step)
            if step == self.steps:
                self.last_copy(c).start()

    def pair_copy(self, c):
        width = self.plan[c].width
        return pltpu.make_async_remote_copy(
            src_ref=self.send.at[c % send_slots, :, :, :width],
            dst_ref=self.held.at[c % held_slots, :, :, :width],
            send_sem=self.pair_out.at[c % send_slots],
            recv_sem=self.pair_in.at[c % held_slots],
            device_id={"dp": self.other},
            device_id_type=MESH,
        )

    def pair_finish(self, c):
        width = self.plan[c].width
        self.pair_copy(c).wait_recv()

        def block(at, carry):
            self.total[c % self.ring, at, :, :width] += self.held[c % held_slots, at, :, :width]
            return carry

        lax.fori_loop(0, self.line, block, 0)
        self.pair_copy(c).wait_send()

    def out_copy(self, c):
        item = self.plan[c]
        return pltpu.make_async_copy(
            self.total.at[c % self.ring, self.place, :, : item.width],
            item.out.at[:, item.first : item.first + item.width],
            self.out_sem.at[c % self.ring],
        )

    def run(self, tasks):
        count, steps = len(self.plan), self.steps
        begun = [c for c, start in enumerate(self.line_starts) if start == 0]
        for c in begun:
            self.line_compute(c)
        self.line_begin(0)
        self.compute(1)
        for slot in range(count + steps + 1):
            for step in range(steps):
                c = slot - 2 - step
                if 0 <= c < count:
                    self.first.finish(c, step)
            self.line_finish(slot)
            if 0 <= slot - 1 < count:
                self.pair_finish(slot - 1)
            for step in range(steps):
                c = slot - 1 - step
                if 0 <= c < count:
                    self.first.start(c, step)
            if slot:
                self.line_begin(slot)
            if slot + 1 < count:
                self.pair_copy(slot + 1).start()
            done = slot - 1 - steps
            if 0 <= done < count:
                self.out_copy(done).start()
            if slot + 2 < count:
                if slot + 2 >= self.ring:
                    self.out_copy(slot + 2 - self.ring).wait()
                self.compute(slot + 2)
            for c, start in enumerate(self.line_starts):
                if slot and start == slot + 1:
                    self.line_compute(c)
            for task in tasks.get(slot, ()):
                task()
        for c in range(max(0, count - self.ring), count):
            self.out_copy(c).wait()
        if self.line_plan:
            for c in range(len(self.line_plan) - self.line_total.shape[0], len(self.line_plan)):
                self.line_result(c).wait()


class Chunk:
    def __init__(self, left, right, computed, out, first, width):
        self.left, self.right, self.computed = left, right, computed
        self.out, self.first, self.width = out, first, width


def for_rows(count, body):
    def step(i, carry):
        body(pl.ds(pl.multiple_of(i * row_group, row_group), row_group))
        return carry

    lax.fori_loop(0, count // row_group, step, 0)


class TensorSum:
    def __init__(self, uses, own, near, far, near_sems, far_sems, near_credit, far_credit):
        self.own, self.near, self.far = own, near, far
        self.near_sems, self.far_sems = near_sems, far_sems
        self.near_credit, self.far_credit = near_credit, far_credit
        index = lax.axis_index("tensor")
        self.core_peer = index + 1 - 2 * (index % 2)
        self.far_peer = index + 2 - 4 * (index // 2)
        self.near_left, self.far_left = 2 * uses, uses
        self.near_first, self.far_first = True, True

    def near_copy(self, source):
        return pltpu.make_async_remote_copy(
            src_ref=source, dst_ref=self.near, send_sem=self.near_sems.at[0],
            recv_sem=self.near_sems.at[1], device_id={"tensor": self.core_peer},
            device_id_type=MESH,
        )

    def far_copy(self):
        return pltpu.make_async_remote_copy(
            src_ref=self.own, dst_ref=self.far, send_sem=self.far_sems.at[0],
            recv_sem=self.far_sems.at[1], device_id={"tensor": self.far_peer},
            device_id_type=MESH,
        )

    def near_start(self, source):
        if not self.near_first:
            pl.semaphore_wait(self.near_credit, 1)
        self.near_first = False
        self.pending = source
        self.near_copy(source).start()

    def near_wait(self):
        self.near_copy(self.pending).wait()

    def near_free(self):
        self.near_left -= 1
        if self.near_left:
            pl.semaphore_signal(
                self.near_credit, inc=1, device_id={"tensor": self.core_peer}, device_id_type=MESH
            )

    def near_add(self):
        self.near_wait()

        def add(rows):
            self.own[rows, :] += self.near[rows, :]

        for_rows(self.own.shape[0], add)
        self.near_free()

    def far_go(self):
        if not self.far_first:
            pl.semaphore_wait(self.far_credit, 1)
        self.far_first = False
        self.far_copy().start()

    def far_wait(self):
        self.far_copy().wait()

    def far_free(self):
        self.far_left -= 1
        if self.far_left:
            pl.semaphore_signal(
                self.far_credit, inc=1, device_id={"tensor": self.far_peer}, device_id_type=MESH
            )


def line_first(dp_count):
    return ((0, 0, 3, 6, 9, 12), (2, 2, 2)) if dp_count == 8 else ((), (0, 0, 0))


def back_kernel(dp_count, *refs):
    refs = list(refs)
    take = lambda n: [refs.pop(0) for _ in range(n)]
    (lam,) = take(1)
    cot_left, two_left, one_left = [take(2) for _ in range(3)]
    hidden, gate_pre, up_pre, heads = [take(2) for _ in range(4)]
    part_back, part_fed, middle = [take(2) for _ in range(3)]
    (layer_in, cotangent) = take(2)
    weights_in = take(4)
    kept_in = [take(4) for _ in range(2)]
    tables = [take(4) for _ in range(2)]
    (sub_scale, gain_one, gain_two) = take(3)
    (grad_down, grad_gate, grad_up, grad_out, grad_qkv, layer_out, grad_in, small_out) = take(8)
    reducer_refs = take(20 if line_first(dp_count)[0] else 10)
    line_rights = reducer_refs.pop() if line_first(dp_count)[0] else None
    (left_a, left_b, rights, rows_qkv) = take(4)
    weights = take(4)
    kept = take(4)
    backward_scratch = take(4)
    (grad_sub, grad_lam) = take(2)
    sets = [take(3) for _ in range(2)]
    through = take(2)
    (spare, projected, attended, rows_in, rows_out) = take(5)
    (small, small_near, small_landed) = take(3)
    (near_sems, far_sems, near_credit, far_credit) = take(4)
    (load_sems, small_near_sems, small_send, small_recv) = take(4)
    assert not refs

    me = lax.axis_index("dp")
    tensor = lax.axis_index("tensor")
    core = tensor % 2
    core_peer = tensor + 1 - 2 * core
    far_peer = tensor + 2 - 4 * (tensor // 2)
    line = dp_count // 2
    half = middle[0].shape[0]
    row_count = 2 * half
    head_count, head_width = sub_scale.shape
    out_weight, projections = weights[0], weights[1:]
    inner = out_weight.shape[0]
    kept_half = pl.ds(pl.multiple_of(core * half, half), half)
    sent_half = pl.ds(pl.multiple_of((1 - core) * half, half), half)
    tokens = [slice(m * row_count, (m + 1) * row_count) for m in range(2)]

    barrier = pltpu.get_barrier_semaphore()
    for offset in range(1, dp_count):
        pl.semaphore_signal(
            barrier, inc=1, device_id={"dp": lax.rem(me + offset, dp_count)}, device_id_type=MESH
        )
    for peer in (core_peer, far_peer):
        pl.semaphore_signal(barrier, inc=1, device_id={"tensor": peer}, device_id_type=MESH)

    used = [0]

    def load(source, target):
        copy = pltpu.make_async_copy(source, target, load_sems.at[used[0]])
        used[0] += 1
        copy.start()
        return copy

    def wait_all(copies):
        for copy in copies:
            copy.wait()

    reducer_width = reducer_refs[0].shape[-1]
    plan, sources, left_loads, right_loads = [], {}, {}, {}

    def load_left(sources_of, left):
        return [load(sources_of[m], left.at[:, tokens[m]]) for m in range(2)]

    def load_columns(source, first, width, target):
        return [
            load(source[m].at[:, first : first + width], target.at[tokens[m], :width])
            for m in range(2)
        ]

    def load_right(c):
        if c in sources:
            right_loads[c] = load_columns(*sources[c], rights.at[c % 2])

    def load_line_right(c):
        if c < len(line_sources):
            line_loads[c] = load_columns(*line_sources[c], line_rights.at[c % 2])

    def get_left(c, left):
        wait_all(left_loads.pop(c, ()))
        return left

    def get_line_left(left):
        if left is left_b and first_two in left_loads:
            wait_all(left_loads.pop(first_two))
        return left

    def get_right(c, first, width):
        if c in sources:
            wait_all(right_loads[c])
            return rights.at[c % 2, :, :width]
        return rows_qkv.at[:, first : first + width]

    def get_line_right(c):
        wait_all(line_loads[c])
        return line_rights.at[c % 2]

    def computed(c):
        load_right(c + 2)
        if c == last_two:
            left_loads[first_one] = load_left(one_left, left_b)

    def add_group(left, source, columns, out, line_chunks=0):
        start = line_chunks * line_width
        for first in range(0, start, line_width):
            c = len(line_plan)
            line_sources.append((source, first, line_width))
            line_plan.append(
                Chunk(
                    functools.partial(get_line_left, left),
                    functools.partial(get_line_right, c),
                    functools.partial(load_line_right, c + 2),
                    out,
                    first,
                    line_width,
                )
            )
        for first in range(start, columns, reducer_width):
            width = min(reducer_width, columns - first)
            c = len(plan)
            if source is not None:
                sources[c] = (source, first, width)
            plan.append(
                Chunk(
                    functools.partial(get_left, c, left),
                    functools.partial(get_right, c, first, width),
                    functools.partial(computed, c),
                    out,
                    first,
                    width,
                )
            )

    line_starts, line_counts = line_first(dp_count)
    line_plan, line_sources, line_loads, line_width = [], [], {}, 128
    add_group(left_a, hidden, hidden[0].shape[1], grad_down)
    first_two = len(plan)
    add_group(left_b, gate_pre, gate_pre[0].shape[1], grad_gate, line_counts[0])
    add_group(left_b, up_pre, up_pre[0].shape[1], grad_up, line_counts[1])
    last_two = len(plan) - 1
    add_group(left_a, heads, inner, grad_out, line_counts[2])
    first_one = len(plan)
    add_group(left_b, None, 3 * inner, grad_qkv)

    left_loads[0] = load_left(cot_left, left_a)
    load_right(0)
    left_loads[first_two] = load_left(two_left, left_b)
    load_line_right(0)
    load_line_right(1)
    load_right(1)
    sums = [
        TensorSum(
            3, *sets[m], near_sems.at[m], far_sems.at[m], near_credit.at[m], far_credit.at[m]
        )
        for m in range(2)
    ]
    own_loads = {m: load(part_back[m].at[kept_half], sets[m][0]) for m in range(2)}
    weight_loads = [load(*pair) for pair in zip(weights_in, weights)]
    kept_loads = [load(*pair) for pair in zip(kept_in[0], kept)]
    spare_queue = [middle[0], middle[1], middle[0], middle[1]]
    rows_queue = [cotangent.at[0], cotangent.at[1]]
    rows_queue += [layer_in.at[0], cotangent.at[0], layer_in.at[1], cotangent.at[1]]
    queued = {}

    def next_spare():
        queued["spare"] = load(spare_queue.pop(0), spare) if spare_queue else None

    def next_rows():
        queued["rows"] = load(rows_queue.pop(0), rows_in) if rows_queue else None

    next_spare()
    next_rows()
    out_loads = []
    small[...] = jnp.zeros_like(small)

    def mine(rows):
        return pl.ds(pl.multiple_of(core * half + rows.start, row_group), row_group)

    def others(rows):
        return pl.ds(pl.multiple_of((1 - core) * half + rows.start, row_group), row_group)

    def exchange(m):
        if m in own_loads:
            own_loads.pop(m).wait()
        sums[m].near_add()
        sums[m].far_go()

    def norm_two(m):
        own, near, far = sets[m]
        queued["spare"].wait()
        sums[m].far_wait()

        def body(rows):
            grads = own[rows, :] + far[rows, :]
            values = spare[rows, :]
            root = root_of(values)
            small[1:2, :] += jnp.sum(grads * values * root, axis=0, keepdims=True)
            through[m][rows, :] = rms_back(grads * gain_two[...], values, root)

        for_rows(half, body)
        sums[m].far_free()
        sums[m].near_start(through[m])
        next_spare()

    def attend(m):
        near = sets[m][1]
        queued["rows"].wait()
        sums[m].near_wait()

        def body(rows):
            attended[mine(rows), :] = (
                rows_in[mine(rows), :].astype(jnp.float32) + through[m][rows, :]
            ).astype(jnp.bfloat16)
            attended[others(rows), :] = (
                rows_in[others(rows), :].astype(jnp.float32) + near[rows, :]
            ).astype(jnp.bfloat16)

        for_rows(half, body)
        sums[m].near_free()
        next_rows()

        def flip_block(i, carry):
            at = pl.ds(pl.multiple_of(i * 128, 128), 128)
            left_a[at, tokens[m]] = attended[:, at].T
            return carry

        lax.fori_loop(0, attended.shape[1] // 128, flip_block, 0)
        if m == 0:
            wait_all(weight_loads)
        wait_all(kept_loads)
        backward_kernel(
            lam, attended, out_weight, *kept, *tables[m], sub_scale,
            rows_qkv.at[tokens[m], :], grad_sub, grad_lam, *backward_scratch,
        )
        if m == 0:
            kept_loads[:] = [load(*pair) for pair in zip(kept_in[1], kept)]
        for head in range(head_count):
            at = slice(head * head_width, (head + 1) * head_width)
            small[2:3, at] += grad_sub[head : head + 1, :]
            small[3:4, at] += grad_lam[head : head + 1, :]

    def project(m):
        def part(which, target):
            rows = pl.ds(pl.multiple_of(m * row_count + which * half, half), half)

            def block(i, carry):
                at = pl.ds(pl.multiple_of(i * 512, 512), 512)
                total = 0.0
                for p in range(3):
                    grads = rows_qkv[rows, p * inner : (p + 1) * inner]
                    total = total + dot_t(grads, projections[p][at, :])
                target[:, at] = total
                return carry

            lax.fori_loop(0, target.shape[1] // 512, block, 0)

        part(1 - core, projected)
        sums[m].near_start(projected)
        part(core, sets[m][0])

    def norm_one(m):
        own, near, far = sets[m]
        queued["rows"].wait()
        sums[m].far_wait()

        def body(rows):
            grads = own[rows, :] + far[rows, :]
            values = rows_in[mine(rows), :].astype(jnp.float32)
            root = root_of(values)
            small[0:1, :] += jnp.sum(grads * values * root, axis=0, keepdims=True)
            through[m][rows, :] += rms_back(grads * gain_one[...], values, root)

        for_rows(half, body)
        sums[m].far_free()
        sums[m].near_start(through[m])
        next_rows()
        own_loads[m] = load(part_fed[m].at[kept_half], own)

    def store_rows(target):
        out_loads.append(load(rows_out, target))

    def finish_in(m):
        near = sets[m][1]
        queued["rows"].wait()
        sums[m].near_wait()
        wait_all(out_loads)
        out_loads.clear()

        def body(rows):
            rows_out[mine(rows), :] = (
                rows_in[mine(rows), :].astype(jnp.float32) + through[m][rows, :]
            ).astype(jnp.bfloat16)
            rows_out[others(rows), :] = (
                rows_in[others(rows), :].astype(jnp.float32) + near[rows, :]
            ).astype(jnp.bfloat16)

        for_rows(half, body)
        sums[m].near_free()
        next_rows()
        store_rows(grad_in.at[m])
        sums[m].near_start(part_fed[m].at[sent_half])

    def add_fed(m):
        own, near, far = sets[m]
        queued["spare"].wait()
        sums[m].far_wait()

        def body(rows):
            own[rows, :] = spare[rows, :] + (own[rows, :] + far[rows, :])

        for_rows(half, body)
        sums[m].far_free()
        sums[m].near_start(own)
        next_spare()

    def finish_out(m):
        own, near = sets[m][:2]
        sums[m].near_wait()
        wait_all(out_loads)
        out_loads.clear()

        def body(rows):
            rows_out[mine(rows), :] = own[rows, :].astype(jnp.bfloat16)
            rows_out[others(rows), :] = near[rows, :].astype(jnp.bfloat16)

        for_rows(half, body)
        sums[m].near_free()
        store_rows(layer_out.at[m])

    small_core = pltpu.make_async_remote_copy(
        src_ref=small, dst_ref=small_near, send_sem=small_near_sems.at[0],
        recv_sem=small_near_sems.at[1], device_id={"tensor": core_peer}, device_id_type=MESH,
    )

    def small_copy(offset):
        return pltpu.make_async_remote_copy(
            src_ref=small, dst_ref=small_landed.at[offset - 1], send_sem=small_send.at[offset - 1],
            recv_sem=small_recv.at[offset - 1],
            device_id={"dp": lax.rem(me + offset, dp_count)}, device_id_type=MESH,
        )

    def small_spread():
        small_core.wait()
        small[0:2, :] += small_near[0:2, :]
        for offset in range(1, dp_count):
            small_copy(offset).start()

    def small_finish():
        for offset in range(1, dp_count):
            small_copy(offset).wait()
        total = small[...]
        for offset in range(1, dp_count):
            total = total + small_landed[offset - 1]
        small_near[...] = total
        out_loads.append(load(small_near, small_out))

    order = {
        0: [lambda: exchange(0)],
        2: [lambda: norm_two(0), lambda: exchange(1)],
        3: [lambda: attend(0), lambda: project(0)],
        4: [lambda: norm_two(1), lambda: exchange(0)],
        5: [lambda: attend(1), lambda: project(1)],
        6: [lambda: norm_one(0), lambda: exchange(1)],
        7: [lambda: finish_in(0)],
        8: [lambda: norm_one(1), lambda: exchange(0), small_core.start],
        9: [lambda: finish_in(1), small_spread],
        10: [lambda: add_fed(0), lambda: exchange(1), small_finish],
        11: [lambda: finish_out(0)],
        12: [lambda: add_fed(1)],
        13: [lambda: finish_out(1)],
    }
    stretch = 256 // reducer_width
    tasks = {slot * stretch: items for slot, items in order.items()}
    reducer = Reducer(plan, line_plan, line_starts, line, reducer_refs)
    reducer.compute(0)
    pl.semaphore_wait(barrier, dp_count + 1)
    reducer.pair_copy(0).start()
    for m in range(2):
        sums[m].near_start(part_back[m].at[sent_half])
    reducer.run(tasks)
    wait_all(out_loads)


def back_call(dp_count, lam, arrays, blocks, shapes):
    depth, row_count, inner, hidden_count, head_count, head_width = shapes
    line = dp_count // 2
    rows = depth // dp_count
    half = row_count // 2
    width = 256 if line <= 4 else 128
    ring = line + 3
    starts = line_first(dp_count)[0]
    wide = (line, rows, width)
    bf16, f32 = jnp.bfloat16, jnp.float32
    dma, regular = pltpu.SemaphoreType.DMA, pltpu.SemaphoreType.REGULAR
    wide_half = pltpu.VMEM((half, depth), f32)
    wide_rows = pltpu.VMEM((row_count, depth), bf16)
    narrow = pltpu.VMEM((row_count, inner), bf16)
    narrow_f32 = pltpu.VMEM((row_count, inner), f32)
    small = pltpu.VMEM((8, depth), f32)
    grad = lambda columns: jax.ShapeDtypeStruct((rows, columns), f32)
    rows_shape = jax.ShapeDtypeStruct((2, row_count, depth), bf16)
    flops = 2 * 2 * row_count * depth * (3 * hidden_count + 8 * inner)
    return pl.pallas_call(
        functools.partial(back_kernel, dp_count),
        out_shape=[grad(hidden_count)] * 3
        + [grad(inner), grad(3 * inner), rows_shape, rows_shape]
        + [jax.ShapeDtypeStruct((8, depth), f32)],
        in_specs=[pl.BlockSpec(memory_space=pltpu.SMEM)]
        + [pl.BlockSpec(memory_space=pl.ANY)] * len(arrays)
        + in_vmem(len(blocks)),
        out_specs=[pl.BlockSpec(memory_space=pl.ANY)] * 8,
        scratch_shapes=[
            pltpu.VMEM((send_slots,) + wide, f32),
            pltpu.VMEM((held_slots,) + wide, f32),
            pltpu.VMEM((ring,) + wide, f32),
            pltpu.VMEM((2, line - 1, 2, rows, width), f32),
            dma((send_slots,)),
            dma((held_slots,)),
            dma((2, line - 1, 2)),
            dma((2, line - 1, 2)),
            regular((2, line - 1)),
            dma((ring,)),
        ]
        + (
            [
                pltpu.VMEM((3, line, 2 * rows, 128), f32),
                pltpu.VMEM((2, line - 1, 2, 2 * rows, 128), f32),
                dma((2, line - 1, 2)),
                dma((2, line - 1, 2)),
                regular((2, line - 1)),
                pltpu.VMEM((len(starts), rows, 128), f32),
                dma((len(starts),)),
                dma((len(starts),)),
                dma((3,)),
                pltpu.VMEM((2, 2 * row_count, 128), bf16),
            ]
            if starts
            else []
        )
        + [
            pltpu.VMEM((depth, 2 * row_count), bf16),
            pltpu.VMEM((depth, 2 * row_count), bf16),
            pltpu.VMEM((2, 2 * row_count, width), bf16),
            pltpu.VMEM((2 * row_count, 3 * inner), bf16),
            pltpu.VMEM((inner, depth), bf16),
        ]
        + [pltpu.VMEM((depth, inner), bf16)] * 3
        + [narrow, narrow, narrow, narrow_f32]
        + [narrow_f32, narrow, narrow_f32, narrow_f32]
        + [pltpu.VMEM((head_count, head_width), f32)] * 2
        + [wide_half] * 10
        + [wide_rows] * 3
        + [
            small,
            small,
            pltpu.VMEM((dp_count - 1, 8, depth), f32),
            dma((2, 2)),
            dma((2, 2)),
            regular((2,)),
            regular((2,)),
            dma((128,)),
            dma((2,)),
            dma((dp_count - 1,)),
            dma((dp_count - 1,)),
        ],
        compiler_params=pltpu.CompilerParams(
            collective_id=0, has_side_effects=True, vmem_limit_bytes=62 * 1024 * 1024
        ),
        cost_estimate=pl.CostEstimate(flops=flops, bytes_accessed=64 << 20, transcendentals=0),
    )(lam, *arrays, *blocks)


def gathers_heads(dp_count):
    return dp_count == 8


class Gather:
    def __init__(self, own, piece, wide, far, near, far_near, full, sems):
        self.own, self.piece, self.wide = own, piece, wide
        self.far, self.near, self.far_near, self.full = far, near, far_near, full
        (
            self.cross_sems, self.line_out, self.line_in, self.pair_out, self.pair_in,
            self.near_sems,
        ) = sems
        self.me = lax.axis_index("dp")
        self.place, self.side = self.me // 2, self.me % 2
        self.line = self.line_out.shape[1] + 1
        self.rows = piece.shape[0]
        tensor = lax.axis_index("tensor")
        self.tensor = tensor
        self.core_peer = tensor + 1 - 2 * (tensor % 2)
        self.far_peer = tensor + 2 - 4 * (tensor // 2)
        self.diagonal = self.far_peer + 1 - 2 * (tensor % 2)

    def slot(self, side, place):
        start = (side * self.line + place) * self.rows
        return self.far.at[pl.ds(pl.multiple_of(start, self.rows), self.rows)]

    def remote(self, source, target, send, recv, device):
        return pltpu.make_async_remote_copy(
            src_ref=source, dst_ref=target, send_sem=send, recv_sem=recv, device_id=device,
            device_id_type=MESH,
        )

    def cross(self):
        return self.remote(
            self.piece, self.slot(self.side, self.place), self.cross_sems.at[0],
            self.cross_sems.at[1], {"tensor": self.far_peer},
        )

    def near_copy(self, index):
        half = self.line * self.rows
        if index == 0:
            source, target = self.wide, self.near
        else:
            start = (self.side if index == 1 else 1 - self.side) * half
            rows = pl.ds(pl.multiple_of(start, self.rows), half)
            source, target = self.far.at[rows], self.far_near.at[rows]
        return self.remote(
            source, target, self.near_sems.at[0, index], self.near_sems.at[1, index],
            {"tensor": self.core_peer},
        )

    def line_copy(self, way, step):
        place = self.place - step if way == 0 else self.place + step
        slot = self.slot(self.side, place)
        return self.remote(
            slot, slot, self.line_out.at[way, step], self.line_in.at[way, step],
            {"dp": self.me + 2 - 4 * way},
        )

    def line_sends(self, way, step):
        if way == 0:
            return (self.place >= step) & (self.place < self.line - 1)
        return (self.place + step <= self.line - 1) & (self.place > 0)

    def line_gets(self, way, step):
        if way == 0:
            return self.place >= step
        return self.place + step <= self.line - 1

    def pair_copy(self, index, place):
        slot = self.slot(self.side, place)
        return self.remote(
            slot, slot, self.pair_out.at[index], self.pair_in.at[index],
            {"dp": self.me + 1 - 2 * self.side},
        )

    def pair_index(self, way, step):
        return 1 + way * (self.line - 1) + step - 1

    def begin(self):
        count = self.own.shape[0]
        rows = pl.ds(pl.multiple_of(self.me * self.rows, self.rows), self.rows)
        self.piece[...] = self.own[rows, :].astype(jnp.float32)
        self.cross().start()

        def widen(rows):
            self.wide[rows, :] = self.own[rows, :].astype(jnp.float32)

        for_rows(count, widen)
        self.near_copy(0).start()

    def forward(self, step):
        if step == 0:
            self.cross().wait()
            self.pair_copy(0, self.place).start()
        for way in range(2):
            if step:

                @pl.when(self.line_gets(way, step))
                def _():
                    self.line_arrival(way, step).wait_recv()
                    place = self.place - step if way == 0 else self.place + step
                    self.pair_copy(self.pair_index(way, step), place).start()

            if step < self.line - 1:

                @pl.when(self.line_sends(way, step))
                def _():
                    self.line_copy(way, step).start()

    def line_arrival(self, way, step):
        place = self.place - step if way == 0 else self.place + step
        slot = self.slot(self.side, place)
        return self.remote(
            slot, slot, self.line_out.at[way, step - 1], self.line_in.at[way, step - 1],
            {"dp": self.me - 2 + 4 * way},
        )

    def store(self, source, tensor, first, count):
        block = self.own.shape[0]

        def narrow(rows):
            at = pl.ds(pl.multiple_of(tensor * block + first + rows.start, row_group), row_group)
            self.full[at, :] = source[rows, :].astype(jnp.bfloat16)

        for_rows(count, narrow)

    def store_far(self, source, tensor):
        for side in range(2):
            for place in range(self.line):
                rows = pl.ds((side * self.line + place) * self.rows, self.rows)
                self.store(source.at[rows], tensor, (2 * place + side) * self.rows, self.rows)

    def finish_line(self):
        self.near_copy(1).start()
        for way in range(2):
            for step in range(self.line - 1):

                @pl.when(self.line_sends(way, step))
                def _():
                    self.line_copy(way, step).wait_send()

        block = self.own.shape[0]
        self.store(self.own, self.tensor, 0, block)
        self.near_copy(0).wait()
        self.store(self.near, self.core_peer, 0, block)

    def finish(self):
        for index in range(1 + 2 * (self.line - 1)):
            if index == 0:
                self.pair_copy(0, self.place).wait()
                continue
            way, step = (index - 1) // (self.line - 1), (index - 1) % (self.line - 1) + 1

            @pl.when(self.line_gets(way, step))
            def _():
                place = self.place - step if way == 0 else self.place + step
                slot = self.slot(1 - self.side, place)
                self.pair_copy(index, place).wait_send()
                self.remote(
                    slot, slot, self.pair_out.at[index], self.pair_in.at[index],
                    {"dp": self.me + 1 - 2 * self.side},
                ).wait_recv()

        self.near_copy(2).start()
        self.store_far(self.far, self.far_peer)
        self.near_copy(1).wait()
        self.near_copy(2).wait()
        self.store_far(self.far_near, self.diagonal)


def front_kernel(dp_count, *refs):
    refs = list(refs)
    take = lambda n: [refs.pop(0) for _ in range(n)]
    (lam,) = take(1)
    layer_in, cotangent = take(2)
    weights_in = take(7)
    tables = [take(4) for _ in range(2)]
    (sub_scale, gain_one, gain_two) = take(3)
    outs = [take(14) for _ in range(2)]
    rows_in, cot_rows = take(2), take(2)
    (normed_one, normed_two, flipped) = take(3)
    weights = take(7)
    kept = take(5)
    hidden = take(3)
    (back, fed) = take(2)
    (near_sems, load_sems) = take(2)
    gathers = gathers_heads(dp_count)
    if gathers:
        sets = [take(2) for _ in range(2)]
        heads_wide, heads_landed = take(2), take(2)
        (heads_full, piece, wide, near_weight, full_weight, heads_sems) = take(6)
        gather_sems = take(6)
    else:
        sets = [take(3) for _ in range(2)]
        (projected, far_sems, near_credit) = take(3)
    assert not refs

    tensor = lax.axis_index("tensor")
    core = tensor % 2
    out_weight, gate_weight, up_weight, down_weight = weights[3:]
    row_count, depth = normed_one.shape
    half = row_count // 2
    hidden_count = gate_weight.shape[1]
    used = [0]

    def load(source, target):
        copy = pltpu.make_async_copy(source, target, load_sems.at[used[0]])
        used[0] += 1
        copy.start()
        return copy

    def wait_all(copies):
        for copy in copies:
            copy.wait()
        copies.clear()

    rows_loads = [load(layer_in.at[0], rows_in[0])]
    weight_loads = [load(*pair) for pair in zip(weights_in[:4], weights[:4])]
    rows_loads.append(load(layer_in.at[1], rows_in[1]))
    cot_loads = [load(cotangent.at[m], cot_rows[m]) for m in range(2)]
    wide_loads = [load(*pair) for pair in zip(weights_in[4:], weights[4:])]

    barrier = pltpu.get_barrier_semaphore()
    core_peer, far_peer = tensor + 1 - 2 * core, tensor + 2 - 4 * (tensor // 2)
    diagonal = far_peer + 1 - 2 * core
    me = lax.axis_index("dp")
    for peer in (core_peer, far_peer, diagonal):
        pl.semaphore_signal(barrier, inc=1, device_id={"tensor": peer}, device_id_type=MESH)
    if gathers:
        for offset in range(1, dp_count):
            target = lax.rem(me + offset, dp_count)
            pl.semaphore_signal(barrier, inc=1, device_id={"dp": target}, device_id_type=MESH)
    pl.semaphore_wait(barrier, dp_count + 2 if gathers else 3)
    if gathers:
        sums = [
            TensorSum(1, *sets[m], None, near_sems.at[m], None, None, None) for m in range(2)
        ]
        for item in sums:
            item.near_left = 1
        gather = Gather(
            weights[3], piece, wide, back, near_weight, fed, full_weight, gather_sems
        )
    else:
        sums = [
            TensorSum(1, *sets[m], near_sems.at[m], far_sems.at[m], near_credit.at[m], None)
            for m in range(2)
        ]
    out_loads, flip_loads, wide_outs, hidden_outs = [], [], [], []

    def mine(rows):
        return pl.ds(pl.multiple_of(core * half + rows.start, row_group), row_group)

    def others(rows):
        return pl.ds(pl.multiple_of((1 - core) * half + rows.start, row_group), row_group)

    def flip_to(source, target):
        wait_all(flip_loads)

        def block(i, carry):
            at = pl.ds(pl.multiple_of(i * 128, 128), 128)
            flipped[at, :] = source[:, at].T
            return carry

        lax.fori_loop(0, depth // 128, block, 0)
        flip_loads.append(load(flipped, target))

    def heads_copy(m, index):
        peer = (core_peer, far_peer, diagonal)[index]
        which = core if index == 1 else 1 - core
        rows = pl.ds(pl.multiple_of(which * half, half), half)
        return pltpu.make_async_remote_copy(
            src_ref=heads_wide[m].at[rows], dst_ref=heads_landed[m].at[index],
            send_sem=heads_sems.at[m, 0, index], recv_sem=heads_sems.at[m, 1, index],
            device_id={"tensor": peer}, device_id_type=MESH,
        )

    def join_heads(m):
        own = sets[m][0]
        inner = kept[4].shape[1]

        def place_of(index):
            return pl.ds(pl.multiple_of(index * inner, inner), inner)

        rows = pl.ds(pl.multiple_of(core * half, half), half)
        heads_full[:, place_of(tensor)] = heads_wide[m][rows, :].astype(jnp.bfloat16)
        for index, peer in enumerate((core_peer, far_peer, diagonal)):
            heads_copy(m, index).wait()
            heads_full[:, place_of(peer)] = heads_landed[m][index].astype(jnp.bfloat16)

        def block(i, carry):
            at = pl.ds(pl.multiple_of(i * 512, 512), 512)
            values = rows_in[m][rows, at].astype(jnp.float32)
            own[:, at] = values + f32_dot(heads_full[...], full_weight[:, at])
            return carry

        lax.fori_loop(0, depth // 512, block, 0)

    def attend(m, between):
        rows_loads[m].wait()
        wait_all(weight_loads)
        wait_all(out_loads)
        forward_kernel(
            lam, rows_in[m], gain_one, *weights[:3], *tables[m], sub_scale, normed_one, *kept,
            between,
        )
        heads = kept[4]
        if gathers:
            if m == 0:
                gather.forward(0)
            heads_wide[m][...] = heads[...].astype(jnp.float32)
            for index in range(3):
                heads_copy(m, index).start()
            out_loads.extend(load(*pair) for pair in zip(kept, outs[m][3:8]))
            flip_to(normed_one, outs[m][2])
            return

        def part(which, target):
            rows = pl.ds(pl.multiple_of(which * half, half), half)

            def block(i, carry):
                at = pl.ds(pl.multiple_of(i * 512, 512), 512)
                target[:, at] = f32_dot(heads[rows, :], out_weight[:, at])
                return carry

            lax.fori_loop(0, depth // 512, block, 0)

        part(1 - core, projected)
        sums[m].near_start(projected)
        part(core, sets[m][0])
        out_loads.extend(load(*pair) for pair in zip(kept, outs[m][3:8]))
        flip_to(normed_one, outs[m][2])
        sums[m].near_add()

    def norm_rows(values):
        return (values * root_of(values) * gain_two[...]).astype(jnp.bfloat16)

    def join(m):
        own = sets[m][0]
        if gathers:
            join_heads(m)
        else:
            far = sets[m][2]

            def add(rows):
                values = rows_in[m][mine(rows), :].astype(jnp.float32)
                own[rows, :] = values + (own[rows, :] + far[rows, :])

            for_rows(half, add)
        sums[m].near_start(own)
        out_loads.append(load(own, outs[m][8]))

    def norm(m):
        own, near = sets[m][:2]

        def norm_mine(rows):
            normed_two[mine(rows), :] = norm_rows(own[rows, :])

        def norm_others(rows):
            normed_two[others(rows), :] = norm_rows(near[rows, :])

        for_rows(half, norm_mine)
        sums[m].near_wait()
        for_rows(half, norm_others)
        sums[m].near_free()
        flip_to(normed_two, outs[m][1])

    def feed(m):
        inside, gate_pre, up_pre = hidden
        if m == 0:
            wait_all(wide_loads)
        wait_all(hidden_outs)

        def block(j, carry):
            at = pl.ds(pl.multiple_of(j * 256, 256), 256)
            gate = f32_dot(normed_two[...], gate_weight[:, at])
            upward = f32_dot(normed_two[...], up_weight[:, at])
            grads = dot_t(cot_rows[m][...], down_weight[at, :])
            sigmoid = jax.nn.sigmoid(gate)
            inside[:, at] = (gate * sigmoid * upward).astype(jnp.bfloat16)
            gate_pre[:, at] = (
                grads * upward * sigmoid * (1.0 + gate * (1.0 - sigmoid))
            ).astype(jnp.bfloat16)
            up_pre[:, at] = (grads * gate * sigmoid).astype(jnp.bfloat16)
            return carry

        lax.fori_loop(0, hidden_count // 256, block, 0)
        hidden_outs.extend(load(*pair) for pair in zip(hidden, outs[m][9:12]))
        wait_all(wide_outs)

        def through(i, carry):
            at = pl.ds(pl.multiple_of(i * 512, 512), 512)
            back[:, at] = dot_t(gate_pre[...], gate_weight[at, :]) + dot_t(
                up_pre[...], up_weight[at, :]
            )
            fed[:, at] = f32_dot(inside[...], down_weight[:, at])
            return carry

        lax.fori_loop(0, depth // 512, through, 0)
        wide_outs.extend([load(back, outs[m][12]), load(fed, outs[m][13])])

    def flip_cot(m):
        cot_loads[m].wait()
        flip_to(cot_rows[m], outs[m][0])

    if gathers:
        wait_all(weight_loads)
        gather.begin()
        attend(0, {})
        attend(1, {2: lambda: gather.forward(1)})
        flip_cot(0)
        gather.forward(2)
        flip_cot(1)
        gather.forward(3)
        gather.finish_line()
        gather.finish()
    else:
        attend(0, {})
        sums[0].far_go()
        attend(1, {})
        flip_cot(0)
        flip_cot(1)
        sums[0].far_wait()
        sums[1].far_go()
    join(0)
    if gathers:
        join(1)
    norm(0)
    feed(0)
    if not gathers:
        sums[1].far_wait()
        join(1)
    norm(1)
    feed(1)
    wait_all(flip_loads)
    wait_all(hidden_outs)
    wait_all(wide_outs)
    wait_all(out_loads)


def front_call(dp_count, lam, arrays, blocks, shapes):
    depth, row_count, inner, hidden_count = shapes[:4]
    bf16, f32 = jnp.bfloat16, jnp.float32
    dma, regular = pltpu.SemaphoreType.DMA, pltpu.SemaphoreType.REGULAR
    half = row_count // 2
    out_shape = []
    for m in range(2):
        out_shape += [jax.ShapeDtypeStruct((depth, row_count), bf16)] * 3
        out_shape += [jax.ShapeDtypeStruct((row_count, inner), bf16)] * 3
        out_shape += [jax.ShapeDtypeStruct((row_count, inner), f32)]
        out_shape += [jax.ShapeDtypeStruct((row_count, inner), bf16)]
        out_shape += [jax.ShapeDtypeStruct((half, depth), f32)]
        out_shape += [jax.ShapeDtypeStruct((row_count, hidden_count), bf16)] * 3
        out_shape += [jax.ShapeDtypeStruct((row_count, depth), f32)] * 2
    wide_rows = pltpu.VMEM((row_count, depth), bf16)
    narrow = pltpu.VMEM((row_count, inner), bf16)
    wide_half = pltpu.VMEM((half, depth), f32)
    if gathers_heads(dp_count):
        steps = dp_count // 2 - 1
        extra = [wide_half] * 4
        extra += [pltpu.VMEM((row_count, inner), f32)] * 2
        extra += [pltpu.VMEM((3, half, inner), f32)] * 2
        extra += [
            pltpu.VMEM((half, depth), bf16),
            pltpu.VMEM((inner // dp_count, depth), f32),
            pltpu.VMEM((inner, depth), f32),
            pltpu.VMEM((inner, depth), f32),
            pltpu.VMEM((depth, depth), bf16),
            dma((2, 2, 3)),
            dma((2,)),
            dma((2, steps)),
            dma((2, steps)),
            dma((1 + 2 * steps,)),
            dma((1 + 2 * steps,)),
            dma((2, 3)),
        ]
    else:
        extra = [wide_half] * 7 + [dma((2, 2)), regular((2,))]
    return pl.pallas_call(
        functools.partial(front_kernel, dp_count),
        out_shape=out_shape,
        in_specs=[pl.BlockSpec(memory_space=pltpu.SMEM)]
        + [pl.BlockSpec(memory_space=pl.ANY)] * len(arrays)
        + in_vmem(len(blocks)),
        out_specs=[pl.BlockSpec(memory_space=pl.ANY)] * len(out_shape),
        scratch_shapes=[wide_rows] * 6
        + [pltpu.VMEM((depth, row_count), bf16)]
        + [pltpu.VMEM((depth, inner), bf16)] * 3
        + [pltpu.VMEM((inner, depth), bf16)]
        + [pltpu.VMEM((depth, hidden_count), bf16)] * 2
        + [pltpu.VMEM((hidden_count, depth), bf16)]
        + [narrow, narrow, narrow, pltpu.VMEM((row_count, inner), f32), narrow]
        + [pltpu.VMEM((row_count, hidden_count), bf16)] * 3
        + [pltpu.VMEM((row_count, depth), f32)] * 2
        + [dma((2, 2)), dma((64,))]
        + extra,
        compiler_params=pltpu.CompilerParams(
            collective_id=1, has_side_effects=True, vmem_limit_bytes=62 * 1024 * 1024
        ),
        cost_estimate=pl.CostEstimate(
            flops=4 * row_count * depth * (6 * hidden_count + 4 * inner),
            bytes_accessed=64 << 20,
            transcendentals=0,
        ),
    )(lam, *arrays, *blocks)


def on_device(
    layer_in,
    short_lengths,
    long_lengths,
    norm1_gain,
    query_weight,
    key_weight,
    value_weight,
    lambda_param,
    sub_gain,
    out_weight,
    norm2_gain,
    gate_weight,
    up_weight,
    down_weight,
    out_cotangent,
):
    dp_count = lax.axis_size("dp")
    head_count, lambda_width = lambda_param.shape
    doc_lengths = (short_lengths[0], long_lengths[0])
    map_width = lambda_width // 4
    projections = (query_weight, key_weight, value_weight)
    lambda_parts = lambda_param.reshape(head_count, 4, map_width)
    first_exp = jnp.exp(jnp.sum(lambda_parts[:, 0] * lambda_parts[:, 1], axis=-1))
    second_exp = jnp.exp(jnp.sum(lambda_parts[:, 2] * lambda_parts[:, 3], axis=-1))
    lam = first_exp - second_exp + lambda_base
    sub_scale = sub_gain * (1.0 - lambda_base)
    tables = []
    for m in range(2):
        position, segment = doc_tables(doc_lengths[m], layer_in.shape[1])
        tables.append(
            rotary_tables(position, map_width) + (segment[:, None], segment[None, :])
        )
    depth, inner = query_weight.shape
    shapes = (
        depth, layer_in.shape[1], inner, gate_weight.shape[1], head_count, sub_gain.shape[1],
    )
    blocks = [*tables[0], *tables[1], sub_scale, norm1_gain[None, :], norm2_gain[None, :]]
    arrays = [layer_in, out_cotangent, *projections, out_weight]
    arrays += [gate_weight, up_weight, down_weight]
    parts = front_call(dp_count, lam, arrays, blocks, shapes)
    pick = lambda at: [parts[at], parts[at + 14]]
    arrays = pick(0) + pick(1) + pick(2) + pick(9) + pick(10) + pick(11) + pick(7)
    arrays += pick(12) + pick(13) + pick(8)
    arrays += [layer_in, out_cotangent, out_weight, *projections]
    arrays += parts[3:7] + parts[17:21]
    grad_down, grad_gate, grad_up, grad_out, grad_qkv, layer_out, grad_in, small = back_call(
        dp_count, lam, arrays, blocks, shapes
    )
    grad_query, grad_key, grad_value = jnp.split(grad_qkv, 3, axis=1)
    per_head = lambda row: row[:inner].reshape(head_count, -1)
    grad_lam = per_head(small[3])[:, :1]
    first_scale = grad_lam * first_exp[:, None]
    second_scale = grad_lam * second_exp[:, None]
    lambda_grad = jnp.concatenate(
        [
            first_scale * lambda_parts[:, 1],
            first_scale * lambda_parts[:, 0],
            -second_scale * lambda_parts[:, 3],
            -second_scale * lambda_parts[:, 2],
        ],
        axis=1,
    )
    index = lax.axis_index("dp")

    def block_of(values):
        size = values.shape[-1] // dp_count
        return lax.dynamic_slice_in_dim(values, index * size, size, values.ndim - 1)

    return (
        layer_out,
        grad_in,
        block_of(small[0]),
        grad_query,
        grad_key,
        grad_value,
        block_of(lambda_grad),
        block_of(per_head(small[2])),
        grad_out.T,
        block_of(small[1]),
        grad_gate,
        grad_up,
        grad_down.T,
    )


def solution(mesh):
    return jax.shard_map(
        on_device,
        mesh=mesh,
        in_specs=(
            P(None, "dp", None),
            P("dp", None),
            P("dp", None),
            P(),
            P(None, "tensor"),
            P(None, "tensor"),
            P(None, "tensor"),
            P("tensor", None),
            P("tensor", None),
            P("tensor", None),
            P(),
            P(None, "tensor"),
            P(None, "tensor"),
            P("tensor", None),
            P(None, "dp", None),
        ),
        out_specs=(
            P(None, "dp", None),
            P(None, "dp", None),
            P("dp"),
            P("dp", "tensor"),
            P("dp", "tensor"),
            P("dp", "tensor"),
            P("tensor", "dp"),
            P("tensor", "dp"),
            P("tensor", "dp"),
            P("dp"),
            P("dp", "tensor"),
            P("dp", "tensor"),
            P("tensor", "dp"),
        ),
        check_vma=False,
    )
```

```python
import functools
import math

import jax
import jax.numpy as jnp
from jax import lax
from jax.experimental import pallas as pl
from jax.experimental.pallas import tpu as pltpu
from jax.sharding import PartitionSpec as P

norm_epsilon = 1e-05
lambda_base = 0.8 - 0.6 * math.exp(-0.3 * 11.0)
rotary_base = 10000.0
closed_score = -1e30
block_rows = 128
longest_document = 256
row_group = 16
send_slots = 3
held_slots = 4
MESH = pl.DeviceIdType.MESH


def documents(lengths, places):
    end, segment, start = 0, 0, 0
    for k in range(lengths.shape[1]):
        length = lengths[0, k]
        end = end + length
        passed = (places >= end).astype(jnp.int32)
        segment = segment + passed
        start = start + passed * length
    return segment, start


def segments(lengths, column, row):
    column[...] = documents(lengths, lax.broadcasted_iota(jnp.int32, column.shape, 0))[0]
    row[...] = documents(lengths, lax.broadcasted_iota(jnp.int32, row.shape, 1))[0]


def rotary_tables(lengths, cosines, sines, map_width):
    half_width = map_width // 2
    row_count, width = cosines[0].shape
    lane = lax.broadcasted_iota(jnp.int32, (block_rows, width), 1)
    frequency = jnp.zeros((block_rows, width), jnp.float32)
    for k in range(half_width):
        value = rotary_base ** (-2.0 * k / map_width)
        frequency = jnp.where(lane % half_width == k, value, frequency)

    def block(i, carry):
        rows = pl.ds(pl.multiple_of(i * block_rows, block_rows), block_rows)
        places = lax.broadcasted_iota(jnp.int32, (block_rows, width), 0) + i * block_rows
        starts = [documents(item, places)[1] for item in lengths]
        start = jnp.where(lane < half_width, starts[0], starts[1])
        angles = (places - start).astype(jnp.float32) * frequency

        def spread(values, m):
            base = jnp.where(lane // half_width == m, values, 0.0)
            return sum(
                (pltpu.roll(base, k * half_width, 1) for k in range(1, width // half_width)), base
            )

        cosine, sine = jnp.cos(angles), jnp.sin(angles)
        for m in range(2):
            cosines[m][rows, :] = spread(cosine, m)
            signed = spread(sine, m)
            sines[m][rows, :] = jnp.where(lane % map_width < half_width, -signed, signed)
        return carry

    lax.fori_loop(0, row_count // block_rows, block, 0)


def lambda_terms(param):
    width = param.shape[1] // 4
    part = lambda k: param[:, k * width : (k + 1) * width]
    first = jnp.exp(jnp.sum(part(0) * part(1), axis=-1, keepdims=True))
    second = jnp.exp(jnp.sum(part(2) * part(3), axis=-1, keepdims=True))
    return first, second, first - second + lambda_base


def turn(values, cosine, sine):
    width = values.shape[-1]
    quarter = width // 4
    lane = lax.broadcasted_iota(jnp.int32, values.shape, 1)
    partner = jnp.where(
        lane % (2 * quarter) < quarter,
        pltpu.roll(values, width - quarter, 1),
        pltpu.roll(values, quarter, 1),
    )
    return values * cosine + partner * sine


def map_of(values, which):
    lane = lax.broadcasted_iota(jnp.int32, values.shape, 1)
    mine = (lane >= values.shape[-1] // 2) == (which == 1)
    return jnp.where(mine, values, jnp.zeros_like(values))


def key_range(block):
    first = max(0, block * block_rows - longest_document + 1) // block_rows * block_rows
    return first, (block + 1) * block_rows


def open_pairs(block, segment_column, segment_row):
    first, last = key_range(block)
    rows = pl.ds(block * block_rows, block_rows)
    shape = (block_rows, last - first)
    row_at = lax.broadcasted_iota(jnp.int32, shape, 0) + block * block_rows
    key_at = lax.broadcasted_iota(jnp.int32, shape, 1) + first
    return (segment_column[rows, :] == segment_row[:, first:last]) & (key_at <= row_at)


def softmax_map(query, key, opened, scale):
    scores = jnp.where(opened, dot_t(query, key) * scale, closed_score)
    expanded = jnp.exp(scores - jnp.max(scores, axis=-1, keepdims=True))
    return expanded * (1.0 / jnp.sum(expanded, axis=-1, keepdims=True))


def f32_dot(left, right):
    return jnp.dot(left, right, preferred_element_type=jnp.float32)


def dot_t(left, right):
    return lax.dot_general(
        left, right, (((1,), (1,)), ((), ())), preferred_element_type=jnp.float32
    )


def dot_rows(left, right):
    return lax.dot_general(
        left, right, (((0,), (0,)), ((), ())), preferred_element_type=jnp.float32
    )


def rms_back(incoming, values, inverse_root):
    return inverse_root * incoming - values * inverse_root**3 * jnp.mean(
        incoming * values, axis=-1, keepdims=True
    )


def root_of(values):
    return lax.rsqrt(jnp.mean(values * values, axis=-1, keepdims=True) + norm_epsilon)


def forward_kernel(
    lam, rows, gain, query_weight, key_weight, value_weight, cosine, sine, segment_column,
    segment_row, sub_scale, normed_one, query, key, value, mixed, heads_out, between,
):
    head_count, width = sub_scale.shape
    scale = (width // 2) ** (-0.5)
    values = rows[...].astype(jnp.float32)
    normed_one[...] = (values * root_of(values) * gain[...]).astype(jnp.bfloat16)
    raw_query = f32_dot(normed_one[...], query_weight[...])
    raw_key = f32_dot(normed_one[...], key_weight[...])
    value[...] = f32_dot(normed_one[...], value_weight[...]).astype(jnp.bfloat16)
    for head in range(head_count):
        at = slice(head * width, (head + 1) * width)
        query[:, at] = turn(raw_query[:, at], cosine[...], sine[...]).astype(jnp.bfloat16)
        key[:, at] = turn(raw_key[:, at], cosine[...], sine[...]).astype(jnp.bfloat16)
    for block in range(rows.shape[0] // block_rows):
        first, last = key_range(block)
        here = slice(block * block_rows, last)
        opened = open_pairs(block, segment_column, segment_row)
        if block in between:
            between[block]()
        for head in range(head_count):
            at = slice(head * width, (head + 1) * width)
            keys = key[first:last, at]
            maps = [softmax_map(map_of(query[here, at], c), keys, opened, scale) for c in range(2)]
            combined = (maps[0] - lam[head : head + 1, :] * maps[1]).astype(jnp.bfloat16)
            out = f32_dot(combined, value[first:last, at])
            mixed[here, at] = out
            heads_out[here, at] = (out * root_of(out) * sub_scale[head : head + 1, :]).astype(
                jnp.bfloat16
            )


def backward_kernel(
    lam, grad_attended, out_weight, query, key, value, mixed, cosine, sine, segment_column,
    segment_row, sub_scale, grad_rows, grad_sub, grad_lam, grad_heads, grad_mixed, grad_key,
    grad_value,
):
    head_count, width = sub_scale.shape
    row_count = query.shape[0]
    inner = head_count * width
    scale = (width // 2) ** (-0.5)
    grad_heads[...] = dot_t(grad_attended[...], out_weight[...])
    for head in range(head_count):
        at = slice(head * width, (head + 1) * width)
        heads = mixed[:, at]
        root = root_of(heads)
        grads = grad_heads[:, at]
        grad_sub[head : head + 1, :] = jnp.sum(grads * heads * root, axis=0, keepdims=True) * (
            1.0 - lambda_base
        )
        grad_mixed[:, at] = rms_back(grads * sub_scale[head : head + 1, :], heads, root).astype(
            jnp.bfloat16
        )
    grad_key[...] = jnp.zeros_like(grad_key)
    grad_value[...] = jnp.zeros_like(grad_value)
    lam_sums = [0.0] * head_count
    for block in range(row_count // block_rows):
        first, last = key_range(block)
        here = slice(block * block_rows, last)
        opened = open_pairs(block, segment_column, segment_row)
        for head in range(head_count):
            at = slice(head * width, (head + 1) * width)
            keys = key[first:last, at]
            queries = [map_of(query[here, at], c) for c in range(2)]
            maps = [softmax_map(queries[c], keys, opened, scale) for c in range(2)]
            mixes = grad_mixed[here, at]
            combined = (maps[0] - lam[head : head + 1, :] * maps[1]).astype(jnp.bfloat16)
            grad_value[first:last, at] += dot_rows(combined, mixes)
            grads = dot_t(mixes, value[first:last, at])
            first_sum = jnp.sum(grads * maps[0], axis=-1, keepdims=True)
            second_sum = jnp.sum(grads * maps[1], axis=-1, keepdims=True)
            lam_sums[head] = lam_sums[head] + jnp.sum(second_sum, axis=0, keepdims=True)
            score_grads = [
                (maps[0] * (grads - first_sum)).astype(jnp.bfloat16),
                (maps[1] * (-lam[head : head + 1, :] * (grads - second_sum))).astype(jnp.bfloat16),
            ]
            grad_query = f32_dot(score_grads[0], map_of(keys, 0)) + f32_dot(
                score_grads[1], map_of(keys, 1)
            )
            grad_rows[here, at] = turn(
                grad_query * scale, cosine[here, :], -sine[here, :]
            ).astype(jnp.bfloat16)
            grad_key[first:last, at] += dot_rows(score_grads[0], queries[0]) + dot_rows(
                score_grads[1], queries[1]
            )
    for head in range(head_count):
        at = slice(head * width, (head + 1) * width)
        grad_rows[:, inner + head * width : inner + (head + 1) * width] = turn(
            grad_key[:, at] * scale, cosine[...], -sine[...]
        ).astype(jnp.bfloat16)
        grad_lam[head : head + 1, :] = jnp.broadcast_to(-lam_sums[head], (1, width))
    grad_rows[:, 2 * inner :] = grad_value[...].astype(jnp.bfloat16)


def in_vmem(count):
    return [pl.BlockSpec(memory_space=pltpu.VMEM)] * count


class Line:
    def __init__(self, line, widths, total, landed, line_out, line_in, credit):
        self.line, self.widths = line, widths
        self.total, self.landed = total, landed
        self.line_out, self.line_in, self.credit = line_out, line_in, credit
        self.me = lax.axis_index("dp")
        self.place = self.me // 2
        self.ring = total.shape[0]

    def copy(self, c, step, way, block, target):
        width = self.widths[c]
        return pltpu.make_async_remote_copy(
            src_ref=self.total.at[c % self.ring, block, :, :width],
            dst_ref=self.landed.at[way, step, c % 2, :, :width],
            send_sem=self.line_out.at[way, step, c % 2],
            recv_sem=self.line_in.at[way, step, c % 2],
            device_id={"dp": target},
            device_id_type=MESH,
        )

    def sends(self, step, way):
        place, line = self.place, self.line
        if way == 0:
            block = line - 1 - step + place
            return (place <= step) & (place < line - 1), block, self.me + 2
        block = place + step - line + 1
        return (place >= line - 1 - step) & (place > 0), block, self.me - 2

    def gets(self, step, way):
        place, line = self.place, self.line
        if way == 0:
            return (place > 0) & (place - 1 <= step), line - 2 - step + place, self.me - 2
        gets = (place < line - 1) & (place + 1 >= line - 1 - step)
        return gets, place + step - line + 2, self.me + 2

    def start(self, c, step):
        for way in range(2):
            sends, block, target = self.sends(step, way)

            @pl.when(sends)
            def _():
                if c >= 2:
                    pl.semaphore_wait(self.credit.at[way, step], 1)
                self.copy(c, step, way, block, target).start()

    def finish(self, c, step):
        width = self.widths[c]
        for way in range(2):
            gets, block, source = self.gets(step, way)

            @pl.when(gets)
            def _():
                self.copy(c, step, way, block, source).wait_recv()
                self.total[c % self.ring, block, :, :width] += self.landed[
                    way, step, c % 2, :, :width
                ]
                if c + 2 < len(self.widths):
                    pl.semaphore_signal(
                        self.credit.at[way, step],
                        inc=1,
                        device_id={"dp": source},
                        device_id_type=MESH,
                    )

            sends, sent, target = self.sends(step, way)

            @pl.when(sends)
            def _():
                self.copy(c, step, way, sent, target).wait_send()


class Reducer:
    def __init__(self, plan, line_plan, line_starts, line, refs):
        self.plan, self.line_plan, self.line_starts = plan, line_plan, line_starts
        self.line = line
        (
            self.send, self.held, self.total, landed, self.pair_out, self.pair_in,
            line_out, line_in, credit, self.out_sem,
        ) = refs[:10]
        self.first = Line(
            line, [item.width for item in plan], self.total, landed, line_out, line_in, credit
        )
        self.place = self.first.place
        self.me = self.first.me
        self.side = self.me % 2
        self.other = self.me + 1 - 2 * self.side
        self.steps = line - 1
        self.ring = self.total.shape[0]
        self.rows = self.total.shape[2]
        if line_plan:
            (
                self.line_total, landed, line_out, line_in, credit, self.last_held,
                self.last_out, self.last_in, self.line_out_sem,
            ) = refs[10:]
            self.second = Line(
                line, [item.width for item in line_plan], self.line_total, landed, line_out,
                line_in, credit,
            )

    def compute(self, c):
        item = self.plan[c]
        width = item.width
        left, right = item.left(), item.right()

        def block(at, carry):
            first = pl.multiple_of(2 * at * self.rows, self.rows)
            columns = right[...]
            away = left[pl.ds(first + (1 - self.side) * self.rows, self.rows), :]
            here = left[pl.ds(first + self.side * self.rows, self.rows), :]
            self.send[c % send_slots, at, :, :width] = f32_dot(away, columns)
            self.total[c % self.ring, at, :, :width] = f32_dot(here, columns)
            return carry

        lax.fori_loop(0, self.line, block, 0)
        item.computed()

    def line_compute(self, c):
        item = self.line_plan[c]
        left, right = item.left(), item.right()
        slot = c % self.line_total.shape[0]
        if c >= self.line_total.shape[0]:
            self.line_result(c - self.line_total.shape[0]).wait()

        def block(at, carry):
            rows = pl.ds(pl.multiple_of(2 * at * self.rows, 2 * self.rows), 2 * self.rows)
            self.line_total[slot, at] = f32_dot(left[rows, :], right[...])
            return carry

        lax.fori_loop(0, self.line, block, 0)
        item.computed()

    def side_rows(self, side):
        return pl.ds(pl.multiple_of(side * self.rows, self.rows), self.rows)

    def last_copy(self, c):
        slot = c % self.line_total.shape[0]
        return pltpu.make_async_remote_copy(
            src_ref=self.line_total.at[slot, self.place, self.side_rows(1 - self.side), :],
            dst_ref=self.last_held.at[c],
            send_sem=self.last_out.at[c],
            recv_sem=self.last_in.at[c],
            device_id={"dp": self.other},
            device_id_type=MESH,
        )

    def line_result(self, c):
        item = self.line_plan[c]
        slot = c % self.line_total.shape[0]
        return pltpu.make_async_copy(
            self.line_total.at[slot, self.place, self.side_rows(self.side), :],
            item.out.at[:, item.first : item.first + item.width],
            self.line_out_sem.at[slot],
        )

    def line_finish(self, slot):
        for c, start in enumerate(self.line_starts):
            step = slot - 1 - start
            if 0 <= step < self.steps:
                self.second.finish(c, step)
            if step == self.steps:
                self.last_copy(c).wait()
                at = c % self.line_total.shape[0]
                self.line_total[at, self.place, self.side_rows(self.side), :] += self.last_held[c]
                self.line_result(c).start()

    def line_begin(self, slot):
        for c, start in enumerate(self.line_starts):
            step = slot - start
            if 0 <= step < self.steps:
                self.second.start(c, step)
            if step == self.steps:
                self.last_copy(c).start()

    def pair_copy(self, c):
        width = self.plan[c].width
        return pltpu.make_async_remote_copy(
            src_ref=self.send.at[c % send_slots, :, :, :width],
            dst_ref=self.held.at[c % held_slots, :, :, :width],
            send_sem=self.pair_out.at[c % send_slots],
            recv_sem=self.pair_in.at[c % held_slots],
            device_id={"dp": self.other},
            device_id_type=MESH,
        )

    def pair_finish(self, c):
        width = self.plan[c].width
        self.pair_copy(c).wait_recv()

        def block(at, carry):
            self.total[c % self.ring, at, :, :width] += self.held[c % held_slots, at, :, :width]
            return carry

        lax.fori_loop(0, self.line, block, 0)
        self.pair_copy(c).wait_send()

    def out_copies(self, c):
        item = self.plan[c]
        outs = item.out if isinstance(item.out, list) else [item.out]
        size = outs[0].shape[1]
        first, last = item.first, item.first + item.width
        while first < last:
            count = min(last, (first // size + 1) * size) - first
            at = first - item.first
            yield pltpu.make_async_copy(
                self.total.at[c % self.ring, self.place, :, at : at + count],
                outs[first // size].at[:, first % size : first % size + count],
                self.out_sem.at[c % self.ring, at // 128],
            )
            first += count

    def out_start(self, c):
        for copy in self.out_copies(c):
            copy.start()

    def out_wait(self, c):
        for copy in self.out_copies(c):
            copy.wait()

    def run(self, tasks):
        count, steps = len(self.plan), self.steps
        begun = [c for c, start in enumerate(self.line_starts) if start == 0]
        for c in begun:
            self.line_compute(c)
        self.line_begin(0)
        self.compute(1)
        for slot in range(count + steps + 1):
            for step in range(steps):
                c = slot - 2 - step
                if 0 <= c < count:
                    self.first.finish(c, step)
            self.line_finish(slot)
            if 0 <= slot - 1 < count:
                self.pair_finish(slot - 1)
            for step in range(steps):
                c = slot - 1 - step
                if 0 <= c < count:
                    self.first.start(c, step)
            if slot:
                self.line_begin(slot)
            if slot + 1 < count:
                self.pair_copy(slot + 1).start()
            done = slot - 1 - steps
            if 0 <= done < count:
                self.out_start(done)
            if slot + 2 < count:
                if slot + 2 >= self.ring:
                    self.out_wait(slot + 2 - self.ring)
                self.compute(slot + 2)
            for c, start in enumerate(self.line_starts):
                if slot and start == slot + 1:
                    self.line_compute(c)
            for task in tasks.get(slot, ()):
                task()
        for c in range(max(0, count - self.ring), count):
            self.out_wait(c)
        if self.line_plan:
            for c in range(len(self.line_plan) - self.line_total.shape[0], len(self.line_plan)):
                self.line_result(c).wait()


class Chunk:
    def __init__(self, left, right, computed, out, first, width):
        self.left, self.right, self.computed = left, right, computed
        self.out, self.first, self.width = out, first, width


def for_rows(count, body):
    def step(i, carry):
        body(pl.ds(pl.multiple_of(i * row_group, row_group), row_group))
        return carry

    lax.fori_loop(0, count // row_group, step, 0)


class TensorSum:
    def __init__(self, uses, own, near, far, near_sems, far_sems, near_credit, far_credit):
        self.own, self.near, self.far = own, near, far
        self.near_sems, self.far_sems = near_sems, far_sems
        self.near_credit, self.far_credit = near_credit, far_credit
        index = lax.axis_index("tensor")
        self.core_peer = index + 1 - 2 * (index % 2)
        self.far_peer = index + 2 - 4 * (index // 2)
        self.near_left, self.far_left = 2 * uses, uses
        self.near_first, self.far_first = True, True

    def near_copy(self, source):
        return pltpu.make_async_remote_copy(
            src_ref=source, dst_ref=self.near, send_sem=self.near_sems.at[0],
            recv_sem=self.near_sems.at[1], device_id={"tensor": self.core_peer},
            device_id_type=MESH,
        )

    def far_copy(self):
        return pltpu.make_async_remote_copy(
            src_ref=self.own, dst_ref=self.far, send_sem=self.far_sems.at[0],
            recv_sem=self.far_sems.at[1], device_id={"tensor": self.far_peer},
            device_id_type=MESH,
        )

    def near_start(self, source):
        if not self.near_first:
            pl.semaphore_wait(self.near_credit, 1)
        self.near_first = False
        self.pending = source
        self.near_copy(source).start()

    def near_wait(self):
        self.near_copy(self.pending).wait()

    def near_free(self):
        self.near_left -= 1
        if self.near_left:
            pl.semaphore_signal(
                self.near_credit, inc=1, device_id={"tensor": self.core_peer}, device_id_type=MESH
            )

    def near_add(self):
        self.near_wait()

        def add(rows):
            self.own[rows, :] += self.near[rows, :]

        for_rows(self.own.shape[0], add)
        self.near_free()

    def far_go(self):
        if not self.far_first:
            pl.semaphore_wait(self.far_credit, 1)
        self.far_first = False
        self.far_copy().start()

    def far_wait(self):
        self.far_copy().wait()

    def far_free(self):
        self.far_left -= 1
        if self.far_left:
            pl.semaphore_signal(
                self.far_credit, inc=1, device_id={"tensor": self.far_peer}, device_id_type=MESH
            )


def line_first(dp_count):
    return ((0, 0, 3, 6, 9, 12), (2, 2, 2)) if dp_count == 8 else ((), (0, 0, 0))


def back_kernel(dp_count, *refs):
    refs = list(refs)
    take = lambda n: [refs.pop(0) for _ in range(n)]
    lengths = take(2)
    cot_left, two_left, one_left = [take(2) for _ in range(3)]
    hidden, gate_pre, up_pre, heads = [take(2) for _ in range(4)]
    part_back, part_fed, middle = [take(2) for _ in range(3)]
    (layer_in, cotangent) = take(2)
    weights_in = take(4)
    kept_in = [take(4) for _ in range(2)]
    tables_in = [take(2) for _ in range(2)]
    (lambda_param, sub_gain, gain_one, gain_two) = take(4)
    (grad_down, grad_gate, grad_up, grad_out) = take(4)
    grad_qkv = take(3)
    (layer_out, grad_in) = take(2)
    small_outs = take(4)
    reducer_refs = take(20 if line_first(dp_count)[0] else 10)
    line_rights = reducer_refs.pop() if line_first(dp_count)[0] else None
    (left_a, left_b, rights, rows_qkv) = take(4)
    weights = take(4)
    kept = take(4)
    backward_scratch = take(4)
    (grad_sub, grad_lam) = take(2)
    sets = [take(3) for _ in range(2)]
    through = take(2)
    (spare, projected, attended, rows_in, rows_out) = take(5)
    (small, small_near, small_landed) = take(3)
    small_blocks = take(4)
    tables = take(4)
    (near_sems, far_sems, near_credit, far_credit) = take(4)
    (load_sems, small_near_sems, small_send, small_recv) = take(4)
    assert not refs

    me = lax.axis_index("dp")
    tensor = lax.axis_index("tensor")
    core = tensor % 2
    core_peer = tensor + 1 - 2 * core
    far_peer = tensor + 2 - 4 * (tensor // 2)
    line = dp_count // 2
    half = middle[0].shape[0]
    row_count = 2 * half
    head_count, head_width = sub_gain.shape
    sub_scale = sub_gain[...] * (1.0 - lambda_base)
    first_exp, second_exp, lam = lambda_terms(lambda_param)
    out_weight, projections = weights[0], weights[1:]
    inner = out_weight.shape[0]
    kept_half = pl.ds(pl.multiple_of(core * half, half), half)
    sent_half = pl.ds(pl.multiple_of((1 - core) * half, half), half)
    tokens = [slice(m * row_count, (m + 1) * row_count) for m in range(2)]

    barrier = pltpu.get_barrier_semaphore()
    for offset in range(1, dp_count):
        pl.semaphore_signal(
            barrier, inc=1, device_id={"dp": lax.rem(me + offset, dp_count)}, device_id_type=MESH
        )
    for peer in (core_peer, far_peer):
        pl.semaphore_signal(barrier, inc=1, device_id={"tensor": peer}, device_id_type=MESH)

    used = [0]

    def load(source, target):
        copy = pltpu.make_async_copy(source, target, load_sems.at[used[0]])
        used[0] += 1
        copy.start()
        return copy

    def wait_all(copies):
        for copy in copies:
            copy.wait()

    reducer_width = reducer_refs[0].shape[-1]
    plan, sources, left_loads, right_loads = [], {}, {}, {}

    def load_left(sources_of, left):
        return [load(sources_of[m], left.at[:, tokens[m]]) for m in range(2)]

    def load_columns(source, first, width, target):
        return [
            load(source[m].at[:, first : first + width], target.at[tokens[m], :width])
            for m in range(2)
        ]

    def load_right(c):
        if c in sources:
            right_loads[c] = load_columns(*sources[c], rights.at[c % 2])

    def load_line_right(c):
        if c < len(line_sources):
            line_loads[c] = load_columns(*line_sources[c], line_rights.at[c % 2])

    def get_left(c, left):
        wait_all(left_loads.pop(c, ()))
        return left

    def get_line_left(left):
        if left is left_b and first_two in left_loads:
            wait_all(left_loads.pop(first_two))
        return left

    def get_right(c, first, width):
        if c in sources:
            wait_all(right_loads[c])
            return rights.at[c % 2, :, :width]
        return rows_qkv.at[:, first : first + width]

    def get_line_right(c):
        wait_all(line_loads[c])
        return line_rights.at[c % 2]

    def computed(c):
        load_right(c + 2)
        if c == last_two:
            left_loads[first_one] = load_left(one_left, left_b)

    def add_group(left, source, columns, out, line_chunks=0):
        start = line_chunks * line_width
        for first in range(0, start, line_width):
            c = len(line_plan)
            line_sources.append((source, first, line_width))
            line_plan.append(
                Chunk(
                    functools.partial(get_line_left, left),
                    functools.partial(get_line_right, c),
                    functools.partial(load_line_right, c + 2),
                    out,
                    first,
                    line_width,
                )
            )
        for first in range(start, columns, reducer_width):
            width = min(reducer_width, columns - first)
            c = len(plan)
            if source is not None:
                sources[c] = (source, first, width)
            plan.append(
                Chunk(
                    functools.partial(get_left, c, left),
                    functools.partial(get_right, c, first, width),
                    functools.partial(computed, c),
                    out,
                    first,
                    width,
                )
            )

    line_starts, line_counts = line_first(dp_count)
    line_plan, line_sources, line_loads, line_width = [], [], {}, 128
    add_group(left_a, hidden, hidden[0].shape[1], grad_down)
    first_two = len(plan)
    add_group(left_b, gate_pre, gate_pre[0].shape[1], grad_gate, line_counts[0])
    add_group(left_b, up_pre, up_pre[0].shape[1], grad_up, line_counts[1])
    last_two = len(plan) - 1
    add_group(left_a, heads, inner, grad_out, line_counts[2])
    first_one = len(plan)
    add_group(left_b, None, 3 * inner, grad_qkv)

    left_loads[0] = load_left(cot_left, left_a)
    load_right(0)
    left_loads[first_two] = load_left(two_left, left_b)
    load_line_right(0)
    load_line_right(1)
    load_right(1)
    sums = [
        TensorSum(
            3, *sets[m], near_sems.at[m], far_sems.at[m], near_credit.at[m], far_credit.at[m]
        )
        for m in range(2)
    ]
    own_loads = {m: load(part_back[m].at[kept_half], sets[m][0]) for m in range(2)}
    weight_loads = [load(*pair) for pair in zip(weights_in, weights)]
    def load_kept(m):
        pairs = zip([*kept_in[m], *tables_in[m]], [*kept, *tables[:2]])
        return [load(*pair) for pair in pairs]

    kept_loads = load_kept(0)
    spare_queue = [middle[0], middle[1], middle[0], middle[1]]
    rows_queue = [cotangent.at[0], cotangent.at[1]]
    rows_queue += [layer_in.at[0], cotangent.at[0], layer_in.at[1], cotangent.at[1]]
    queued = {}

    def next_spare():
        queued["spare"] = load(spare_queue.pop(0), spare) if spare_queue else None

    def next_rows():
        queued["rows"] = load(rows_queue.pop(0), rows_in) if rows_queue else None

    next_spare()
    next_rows()
    out_loads = []
    small[...] = jnp.zeros_like(small)

    def mine(rows):
        return pl.ds(pl.multiple_of(core * half + rows.start, row_group), row_group)

    def others(rows):
        return pl.ds(pl.multiple_of((1 - core) * half + rows.start, row_group), row_group)

    def exchange(m):
        if m in own_loads:
            own_loads.pop(m).wait()
        sums[m].near_add()
        sums[m].far_go()

    def norm_two(m):
        own, near, far = sets[m]
        queued["spare"].wait()
        sums[m].far_wait()

        def body(rows):
            grads = own[rows, :] + far[rows, :]
            values = spare[rows, :]
            root = root_of(values)
            small[1:2, :] += jnp.sum(grads * values * root, axis=0, keepdims=True)
            through[m][rows, :] = rms_back(grads * gain_two[...], values, root)

        for_rows(half, body)
        sums[m].far_free()
        sums[m].near_start(through[m])
        next_spare()

    def attend(m):
        near = sets[m][1]
        queued["rows"].wait()
        sums[m].near_wait()

        def body(rows):
            attended[mine(rows), :] = (
                rows_in[mine(rows), :].astype(jnp.float32) + through[m][rows, :]
            ).astype(jnp.bfloat16)
            attended[others(rows), :] = (
                rows_in[others(rows), :].astype(jnp.float32) + near[rows, :]
            ).astype(jnp.bfloat16)

        for_rows(half, body)
        sums[m].near_free()
        next_rows()

        def flip_block(i, carry):
            at = pl.ds(pl.multiple_of(i * 128, 128), 128)
            left_a[at, tokens[m]] = attended[:, at].T
            return carry

        lax.fori_loop(0, attended.shape[1] // 128, flip_block, 0)
        if m == 0:
            wait_all(weight_loads)
        wait_all(kept_loads)
        segments(lengths[m], *tables[2:])
        backward_kernel(
            lam, attended, out_weight, *kept, *tables, sub_scale,
            rows_qkv.at[tokens[m], :], grad_sub, grad_lam, *backward_scratch,
        )
        if m == 0:
            kept_loads[:] = load_kept(1)
        for head in range(head_count):
            at = slice(head * head_width, (head + 1) * head_width)
            small[2:3, at] += grad_sub[head : head + 1, :]
            small[3:4, at] += grad_lam[head : head + 1, :]

    def project(m):
        def part(which, target):
            rows = pl.ds(pl.multiple_of(m * row_count + which * half, half), half)

            def block(i, carry):
                at = pl.ds(pl.multiple_of(i * 512, 512), 512)
                total = 0.0
                for p in range(3):
                    grads = rows_qkv[rows, p * inner : (p + 1) * inner]
                    total = total + dot_t(grads, projections[p][at, :])
                target[:, at] = total
                return carry

            lax.fori_loop(0, target.shape[1] // 512, block, 0)

        part(1 - core, projected)
        sums[m].near_start(projected)
        part(core, sets[m][0])

    def norm_one(m):
        own, near, far = sets[m]
        queued["rows"].wait()
        sums[m].far_wait()

        def body(rows):
            grads = own[rows, :] + far[rows, :]
            values = rows_in[mine(rows), :].astype(jnp.float32)
            root = root_of(values)
            small[0:1, :] += jnp.sum(grads * values * root, axis=0, keepdims=True)
            through[m][rows, :] += rms_back(grads * gain_one[...], values, root)

        for_rows(half, body)
        sums[m].far_free()
        sums[m].near_start(through[m])
        next_rows()
        own_loads[m] = load(part_fed[m].at[kept_half], own)

    def store_rows(target):
        out_loads.append(load(rows_out, target))

    def finish_in(m):
        near = sets[m][1]
        queued["rows"].wait()
        sums[m].near_wait()
        wait_all(out_loads)
        out_loads.clear()

        def body(rows):
            rows_out[mine(rows), :] = (
                rows_in[mine(rows), :].astype(jnp.float32) + through[m][rows, :]
            ).astype(jnp.bfloat16)
            rows_out[others(rows), :] = (
                rows_in[others(rows), :].astype(jnp.float32) + near[rows, :]
            ).astype(jnp.bfloat16)

        for_rows(half, body)
        sums[m].near_free()
        next_rows()
        store_rows(grad_in.at[m])
        sums[m].near_start(part_fed[m].at[sent_half])

    def add_fed(m):
        own, near, far = sets[m]
        queued["spare"].wait()
        sums[m].far_wait()

        def body(rows):
            own[rows, :] = spare[rows, :] + (own[rows, :] + far[rows, :])

        for_rows(half, body)
        sums[m].far_free()
        sums[m].near_start(own)
        next_spare()

    def finish_out(m):
        own, near = sets[m][:2]
        sums[m].near_wait()
        wait_all(out_loads)
        out_loads.clear()

        def body(rows):
            rows_out[mine(rows), :] = own[rows, :].astype(jnp.bfloat16)
            rows_out[others(rows), :] = near[rows, :].astype(jnp.bfloat16)

        for_rows(half, body)
        sums[m].near_free()
        store_rows(layer_out.at[m])

    small_core = pltpu.make_async_remote_copy(
        src_ref=small, dst_ref=small_near, send_sem=small_near_sems.at[0],
        recv_sem=small_near_sems.at[1], device_id={"tensor": core_peer}, device_id_type=MESH,
    )

    def small_copy(offset):
        return pltpu.make_async_remote_copy(
            src_ref=small, dst_ref=small_landed.at[offset - 1], send_sem=small_send.at[offset - 1],
            recv_sem=small_recv.at[offset - 1],
            device_id={"dp": lax.rem(me + offset, dp_count)}, device_id_type=MESH,
        )

    def small_spread():
        small_core.wait()
        small[0:2, :] += small_near[0:2, :]
        for offset in range(1, dp_count):
            small_copy(offset).start()

    def small_finish():
        for offset in range(1, dp_count):
            small_copy(offset).wait()
        total = small[...]
        for offset in range(1, dp_count):
            total = total + small_landed[offset - 1]

        def own_block(values, target):
            count = target.shape[1]
            shift = lax.rem((dp_count - me) * count, count * dp_count)
            return pltpu.roll(values, shift, 1)[: target.shape[0], :count]

        norm_blocks, lambda_block, sub_block = small_blocks[:2], small_blocks[2], small_blocks[3]
        for row in range(2):
            norm_blocks[row][...] = own_block(total, norm_blocks[row][...])
            total = pltpu.roll(total, 7, 0)
        total = pltpu.roll(total, 2, 0)
        part = head_width // 2
        for head in range(head_count):
            at = slice(head * head_width, (head + 1) * head_width)
            sub_block[head : head + 1, :] = own_block(
                jnp.broadcast_to(total[2:3, at], (8, head_width)), sub_block[0:1, :]
            )
            grad = total[3:4, head * head_width : head * head_width + 1]
            param = lambda_param[head : head + 1, :]
            first = grad * first_exp[head : head + 1, :]
            second = grad * second_exp[head : head + 1, :]
            piece = lambda k: param[:, k * part : (k + 1) * part]
            full = jnp.concatenate(
                [first * piece(1), first * piece(0), -second * piece(3), -second * piece(2)], axis=1
            )
            lambda_block[head : head + 1, :] = own_block(
                jnp.broadcast_to(full, (8, 4 * part)), lambda_block[0:1, :]
            )
        out_loads.extend(load(*pair) for pair in zip(small_blocks, small_outs))

    order = {
        0: [lambda: exchange(0)],
        2: [lambda: norm_two(0), lambda: exchange(1)],
        3: [lambda: attend(0), lambda: project(0)],
        4: [lambda: norm_two(1), lambda: exchange(0)],
        5: [lambda: attend(1), lambda: project(1)],
        6: [lambda: norm_one(0), lambda: exchange(1)],
        7: [lambda: finish_in(0)],
        8: [lambda: norm_one(1), lambda: exchange(0), small_core.start],
        9: [lambda: finish_in(1), small_spread],
        10: [lambda: add_fed(0), lambda: exchange(1), small_finish],
        11: [lambda: finish_out(0)],
        12: [lambda: add_fed(1)],
        13: [lambda: finish_out(1)],
    }
    stretch = 256 // reducer_width
    tasks = {slot * stretch: items for slot, items in order.items()}
    reducer = Reducer(plan, line_plan, line_starts, line, reducer_refs)
    reducer.compute(0)
    pl.semaphore_wait(barrier, dp_count + 1)
    reducer.pair_copy(0).start()
    for m in range(2):
        sums[m].near_start(part_back[m].at[sent_half])
    reducer.run(tasks)
    wait_all(out_loads)


def back_call(dp_count, lengths, arrays, blocks, shapes):
    depth, row_count, inner, hidden_count, head_count, head_width = shapes
    line = dp_count // 2
    rows = depth // dp_count
    half = row_count // 2
    width = 256 if line <= 4 else 128
    ring = line + 3
    starts = line_first(dp_count)[0]
    wide = (line, rows, width)
    bf16, f32 = jnp.bfloat16, jnp.float32
    dma, regular = pltpu.SemaphoreType.DMA, pltpu.SemaphoreType.REGULAR
    wide_half = pltpu.VMEM((half, depth), f32)
    wide_rows = pltpu.VMEM((row_count, depth), bf16)
    narrow = pltpu.VMEM((row_count, inner), bf16)
    narrow_f32 = pltpu.VMEM((row_count, inner), f32)
    small = pltpu.VMEM((8, depth), f32)
    grad = lambda columns: jax.ShapeDtypeStruct((rows, columns), f32)
    rows_shape = jax.ShapeDtypeStruct((2, row_count, depth), bf16)
    small_shapes = [jax.ShapeDtypeStruct((1, rows), f32)] * 2
    for count in (2 * head_width, head_width):
        small_shapes.append(jax.ShapeDtypeStruct((head_count, count // dp_count), f32))
    flops = 2 * 2 * row_count * depth * (3 * hidden_count + 8 * inner)
    return pl.pallas_call(
        functools.partial(back_kernel, dp_count),
        out_shape=[grad(hidden_count)] * 3
        + [grad(inner)] * 4
        + [rows_shape] * 2
        + small_shapes,
        in_specs=[pl.BlockSpec(memory_space=pltpu.SMEM)] * 2
        + [pl.BlockSpec(memory_space=pl.ANY)] * len(arrays)
        + in_vmem(len(blocks)),
        out_specs=[pl.BlockSpec(memory_space=pl.ANY)] * 13,
        scratch_shapes=[
            pltpu.VMEM((send_slots,) + wide, f32),
            pltpu.VMEM((held_slots,) + wide, f32),
            pltpu.VMEM((ring,) + wide, f32),
            pltpu.VMEM((2, line - 1, 2, rows, width), f32),
            dma((send_slots,)),
            dma((held_slots,)),
            dma((2, line - 1, 2)),
            dma((2, line - 1, 2)),
            regular((2, line - 1)),
            dma((ring, 2)),
        ]
        + (
            [
                pltpu.VMEM((3, line, 2 * rows, 128), f32),
                pltpu.VMEM((2, line - 1, 2, 2 * rows, 128), f32),
                dma((2, line - 1, 2)),
                dma((2, line - 1, 2)),
                regular((2, line - 1)),
                pltpu.VMEM((len(starts), rows, 128), f32),
                dma((len(starts),)),
                dma((len(starts),)),
                dma((3,)),
                pltpu.VMEM((2, 2 * row_count, 128), bf16),
            ]
            if starts
            else []
        )
        + [
            pltpu.VMEM((depth, 2 * row_count), bf16),
            pltpu.VMEM((depth, 2 * row_count), bf16),
            pltpu.VMEM((2, 2 * row_count, width), bf16),
            pltpu.VMEM((2 * row_count, 3 * inner), bf16),
            pltpu.VMEM((inner, depth), bf16),
        ]
        + [pltpu.VMEM((depth, inner), bf16)] * 3
        + [narrow, narrow, narrow, narrow_f32]
        + [narrow_f32, narrow, narrow_f32, narrow_f32]
        + [pltpu.VMEM((head_count, head_width), f32)] * 2
        + [wide_half] * 10
        + [wide_rows] * 3
        + [
            small,
            small,
            pltpu.VMEM((dp_count - 1, 8, depth), f32),
            *[pltpu.VMEM(item.shape, f32) for item in small_shapes],
            pltpu.VMEM((row_count, head_width), f32),
            pltpu.VMEM((row_count, head_width), f32),
            pltpu.VMEM((row_count, 1), jnp.int32),
            pltpu.VMEM((1, row_count), jnp.int32),
            dma((2, 2)),
            dma((2, 2)),
            regular((2,)),
            regular((2,)),
            dma((128,)),
            dma((2,)),
            dma((dp_count - 1,)),
            dma((dp_count - 1,)),
        ],
        compiler_params=pltpu.CompilerParams(
            collective_id=0, has_side_effects=True, vmem_limit_bytes=62 * 1024 * 1024
        ),
        cost_estimate=pl.CostEstimate(flops=flops, bytes_accessed=64 << 20, transcendentals=0),
    )(*lengths, *arrays, *blocks)


def gathers_heads(dp_count):
    return dp_count == 8


class Gather:
    def __init__(self, own, piece, wide, far, near, far_near, full, sems):
        self.own, self.piece, self.wide = own, piece, wide
        self.far, self.near, self.far_near, self.full = far, near, far_near, full
        (
            self.cross_sems, self.line_out, self.line_in, self.pair_out, self.pair_in,
            self.near_sems,
        ) = sems
        self.me = lax.axis_index("dp")
        self.place, self.side = self.me // 2, self.me % 2
        self.line = self.line_out.shape[1] + 1
        self.rows = piece.shape[0]
        tensor = lax.axis_index("tensor")
        self.tensor = tensor
        self.core_peer = tensor + 1 - 2 * (tensor % 2)
        self.far_peer = tensor + 2 - 4 * (tensor // 2)
        self.diagonal = self.far_peer + 1 - 2 * (tensor % 2)

    def slot(self, side, place):
        start = (side * self.line + place) * self.rows
        return self.far.at[pl.ds(pl.multiple_of(start, self.rows), self.rows)]

    def remote(self, source, target, send, recv, device):
        return pltpu.make_async_remote_copy(
            src_ref=source, dst_ref=target, send_sem=send, recv_sem=recv, device_id=device,
            device_id_type=MESH,
        )

    def cross(self):
        return self.remote(
            self.piece, self.slot(self.side, self.place), self.cross_sems.at[0],
            self.cross_sems.at[1], {"tensor": self.far_peer},
        )

    def near_copy(self, index):
        half = self.line * self.rows
        if index == 0:
            source, target = self.wide, self.near
        else:
            start = (self.side if index == 1 else 1 - self.side) * half
            rows = pl.ds(pl.multiple_of(start, self.rows), half)
            source, target = self.far.at[rows], self.far_near.at[rows]
        return self.remote(
            source, target, self.near_sems.at[0, index], self.near_sems.at[1, index],
            {"tensor": self.core_peer},
        )

    def line_copy(self, way, step):
        place = self.place - step if way == 0 else self.place + step
        slot = self.slot(self.side, place)
        return self.remote(
            slot, slot, self.line_out.at[way, step], self.line_in.at[way, step],
            {"dp": self.me + 2 - 4 * way},
        )

    def line_sends(self, way, step):
        if way == 0:
            return (self.place >= step) & (self.place < self.line - 1)
        return (self.place + step <= self.line - 1) & (self.place > 0)

    def line_gets(self, way, step):
        if way == 0:
            return self.place >= step
        return self.place + step <= self.line - 1

    def pair_copy(self, index, place):
        slot = self.slot(self.side, place)
        return self.remote(
            slot, slot, self.pair_out.at[index], self.pair_in.at[index],
            {"dp": self.me + 1 - 2 * self.side},
        )

    def pair_index(self, way, step):
        return 1 + way * (self.line - 1) + step - 1

    def begin(self):
        count = self.own.shape[0]
        rows = pl.ds(pl.multiple_of(self.me * self.rows, self.rows), self.rows)
        self.piece[...] = self.own[rows, :].astype(jnp.float32)
        self.cross().start()

        def widen(rows):
            self.wide[rows, :] = self.own[rows, :].astype(jnp.float32)

        for_rows(count, widen)
        self.near_copy(0).start()

    def forward(self, step):
        if step == 0:
            self.cross().wait()
            self.pair_copy(0, self.place).start()
        for way in range(2):
            if step:

                @pl.when(self.line_gets(way, step))
                def _():
                    self.line_arrival(way, step).wait_recv()
                    place = self.place - step if way == 0 else self.place + step
                    self.pair_copy(self.pair_index(way, step), place).start()

            if step < self.line - 1:

                @pl.when(self.line_sends(way, step))
                def _():
                    self.line_copy(way, step).start()

    def line_arrival(self, way, step):
        place = self.place - step if way == 0 else self.place + step
        slot = self.slot(self.side, place)
        return self.remote(
            slot, slot, self.line_out.at[way, step - 1], self.line_in.at[way, step - 1],
            {"dp": self.me - 2 + 4 * way},
        )

    def store(self, source, tensor, first, count):
        block = self.own.shape[0]

        def narrow(rows):
            at = pl.ds(pl.multiple_of(tensor * block + first + rows.start, row_group), row_group)
            self.full[at, :] = source[rows, :].astype(jnp.bfloat16)

        for_rows(count, narrow)

    def store_far(self, source, tensor):
        for side in range(2):
            for place in range(self.line):
                rows = pl.ds((side * self.line + place) * self.rows, self.rows)
                self.store(source.at[rows], tensor, (2 * place + side) * self.rows, self.rows)

    def finish_line(self):
        self.near_copy(1).start()
        for way in range(2):
            for step in range(self.line - 1):

                @pl.when(self.line_sends(way, step))
                def _():
                    self.line_copy(way, step).wait_send()

        block = self.own.shape[0]
        self.store(self.own, self.tensor, 0, block)
        self.near_copy(0).wait()
        self.store(self.near, self.core_peer, 0, block)

    def finish(self):
        for index in range(1 + 2 * (self.line - 1)):
            if index == 0:
                self.pair_copy(0, self.place).wait()
                continue
            way, step = (index - 1) // (self.line - 1), (index - 1) % (self.line - 1) + 1

            @pl.when(self.line_gets(way, step))
            def _():
                place = self.place - step if way == 0 else self.place + step
                slot = self.slot(1 - self.side, place)
                self.pair_copy(index, place).wait_send()
                self.remote(
                    slot, slot, self.pair_out.at[index], self.pair_in.at[index],
                    {"dp": self.me + 1 - 2 * self.side},
                ).wait_recv()

        self.near_copy(2).start()
        self.store_far(self.far, self.far_peer)
        self.near_copy(1).wait()
        self.near_copy(2).wait()
        self.store_far(self.far_near, self.diagonal)


def front_kernel(dp_count, *refs):
    refs = list(refs)
    take = lambda n: [refs.pop(0) for _ in range(n)]
    lengths = take(2)
    layer_in, cotangent = take(2)
    weights_in = take(7)
    (lambda_param, sub_gain, gain_one, gain_two) = take(4)
    outs = [take(16) for _ in range(2)]
    cosines, sines = take(2), take(2)
    (segment_column, segment_row) = take(2)
    rows_in, cot_rows = take(2), take(2)
    (normed_one, normed_two, flipped) = take(3)
    weights = take(7)
    kept = take(5)
    hidden = take(3)
    (back, fed) = take(2)
    (near_sems, load_sems) = take(2)
    gathers = gathers_heads(dp_count)
    if gathers:
        sets = [take(2) for _ in range(2)]
        heads_wide, heads_landed = take(2), take(2)
        (heads_full, piece, wide, near_weight, full_weight, heads_sems) = take(6)
        gather_sems = take(6)
    else:
        sets = [take(3) for _ in range(2)]
        (projected, far_sems, near_credit) = take(3)
    assert not refs

    tensor = lax.axis_index("tensor")
    core = tensor % 2
    out_weight, gate_weight, up_weight, down_weight = weights[3:]
    row_count, depth = normed_one.shape
    half = row_count // 2
    hidden_count = gate_weight.shape[1]
    used = [0]

    def load(source, target):
        copy = pltpu.make_async_copy(source, target, load_sems.at[used[0]])
        used[0] += 1
        copy.start()
        return copy

    def wait_all(copies):
        for copy in copies:
            copy.wait()
        copies.clear()

    rows_loads = [load(layer_in.at[0], rows_in[0])]
    weight_loads = [load(*pair) for pair in zip(weights_in[:4], weights[:4])]
    rows_loads.append(load(layer_in.at[1], rows_in[1]))
    cot_loads = [load(cotangent.at[m], cot_rows[m]) for m in range(2)]
    wide_loads = [load(*pair) for pair in zip(weights_in[4:], weights[4:])]

    sub_scale = sub_gain[...] * (1.0 - lambda_base)
    lam = lambda_terms(lambda_param)[2]
    barrier = pltpu.get_barrier_semaphore()
    core_peer, far_peer = tensor + 1 - 2 * core, tensor + 2 - 4 * (tensor // 2)
    diagonal = far_peer + 1 - 2 * core
    me = lax.axis_index("dp")
    for peer in (core_peer, far_peer, diagonal):
        pl.semaphore_signal(barrier, inc=1, device_id={"tensor": peer}, device_id_type=MESH)
    if gathers:
        for offset in range(1, dp_count):
            target = lax.rem(me + offset, dp_count)
            pl.semaphore_signal(barrier, inc=1, device_id={"dp": target}, device_id_type=MESH)
    pl.semaphore_wait(barrier, dp_count + 2 if gathers else 3)
    if gathers:
        sums = [
            TensorSum(1, *sets[m], None, near_sems.at[m], None, None, None) for m in range(2)
        ]
        for item in sums:
            item.near_left = 1
        gather = Gather(
            weights[3], piece, wide, back, near_weight, fed, full_weight, gather_sems
        )
    else:
        sums = [
            TensorSum(1, *sets[m], near_sems.at[m], far_sems.at[m], near_credit.at[m], None)
            for m in range(2)
        ]
    rotary_tables(lengths, cosines, sines, lambda_param.shape[1] // 4)
    out_loads, flip_loads, wide_outs, hidden_outs = [], [], [], []

    def mine(rows):
        return pl.ds(pl.multiple_of(core * half + rows.start, row_group), row_group)

    def others(rows):
        return pl.ds(pl.multiple_of((1 - core) * half + rows.start, row_group), row_group)

    def flip_to(source, target):
        wait_all(flip_loads)

        def block(i, carry):
            at = pl.ds(pl.multiple_of(i * 128, 128), 128)
            flipped[at, :] = source[:, at].T
            return carry

        lax.fori_loop(0, depth // 128, block, 0)
        flip_loads.append(load(flipped, target))

    def heads_copy(m, index):
        peer = (core_peer, far_peer, diagonal)[index]
        which = core if index == 1 else 1 - core
        rows = pl.ds(pl.multiple_of(which * half, half), half)
        return pltpu.make_async_remote_copy(
            src_ref=heads_wide[m].at[rows], dst_ref=heads_landed[m].at[index],
            send_sem=heads_sems.at[m, 0, index], recv_sem=heads_sems.at[m, 1, index],
            device_id={"tensor": peer}, device_id_type=MESH,
        )

    def join_heads(m):
        own = sets[m][0]
        inner = kept[4].shape[1]

        def place_of(index):
            return pl.ds(pl.multiple_of(index * inner, inner), inner)

        rows = pl.ds(pl.multiple_of(core * half, half), half)
        heads_full[:, place_of(tensor)] = heads_wide[m][rows, :].astype(jnp.bfloat16)
        for index, peer in enumerate((core_peer, far_peer, diagonal)):
            heads_copy(m, index).wait()
            heads_full[:, place_of(peer)] = heads_landed[m][index].astype(jnp.bfloat16)

        def block(i, carry):
            at = pl.ds(pl.multiple_of(i * 512, 512), 512)
            values = rows_in[m][rows, at].astype(jnp.float32)
            own[:, at] = values + f32_dot(heads_full[...], full_weight[:, at])
            return carry

        lax.fori_loop(0, depth // 512, block, 0)

    def attend(m, between):
        rows_loads[m].wait()
        wait_all(weight_loads)
        wait_all(out_loads)
        segments(lengths[m], segment_column, segment_row)
        out_loads.extend([load(cosines[m], outs[m][14]), load(sines[m], outs[m][15])])
        forward_kernel(
            lam, rows_in[m], gain_one, *weights[:3], cosines[m], sines[m], segment_column,
            segment_row, sub_scale, normed_one, *kept,
            between,
        )
        heads = kept[4]
        if gathers:
            if m == 0:
                gather.forward(0)
            heads_wide[m][...] = heads[...].astype(jnp.float32)
            for index in range(3):
                heads_copy(m, index).start()
            out_loads.extend(load(*pair) for pair in zip(kept, outs[m][3:8]))
            flip_to(normed_one, outs[m][2])
            return

        def part(which, target):
            rows = pl.ds(pl.multiple_of(which * half, half), half)

            def block(i, carry):
                at = pl.ds(pl.multiple_of(i * 512, 512), 512)
                target[:, at] = f32_dot(heads[rows, :], out_weight[:, at])
                return carry

            lax.fori_loop(0, depth // 512, block, 0)

        part(1 - core, projected)
        sums[m].near_start(projected)
        part(core, sets[m][0])
        out_loads.extend(load(*pair) for pair in zip(kept, outs[m][3:8]))
        flip_to(normed_one, outs[m][2])
        sums[m].near_add()

    def norm_rows(values):
        return (values * root_of(values) * gain_two[...]).astype(jnp.bfloat16)

    def join(m):
        own = sets[m][0]
        if gathers:
            join_heads(m)
        else:
            far = sets[m][2]

            def add(rows):
                values = rows_in[m][mine(rows), :].astype(jnp.float32)
                own[rows, :] = values + (own[rows, :] + far[rows, :])

            for_rows(half, add)
        sums[m].near_start(own)
        out_loads.append(load(own, outs[m][8]))

    def norm(m):
        own, near = sets[m][:2]

        def norm_mine(rows):
            normed_two[mine(rows), :] = norm_rows(own[rows, :])

        def norm_others(rows):
            normed_two[others(rows), :] = norm_rows(near[rows, :])

        for_rows(half, norm_mine)
        sums[m].near_wait()
        for_rows(half, norm_others)
        sums[m].near_free()
        flip_to(normed_two, outs[m][1])

    def feed(m):
        inside, gate_pre, up_pre = hidden
        if m == 0:
            wait_all(wide_loads)
        wait_all(hidden_outs)

        def block(j, carry):
            at = pl.ds(pl.multiple_of(j * 256, 256), 256)
            gate = f32_dot(normed_two[...], gate_weight[:, at])
            upward = f32_dot(normed_two[...], up_weight[:, at])
            grads = dot_t(cot_rows[m][...], down_weight[at, :])
            sigmoid = jax.nn.sigmoid(gate)
            inside[:, at] = (gate * sigmoid * upward).astype(jnp.bfloat16)
            gate_pre[:, at] = (
                grads * upward * sigmoid * (1.0 + gate * (1.0 - sigmoid))
            ).astype(jnp.bfloat16)
            up_pre[:, at] = (grads * gate * sigmoid).astype(jnp.bfloat16)
            return carry

        lax.fori_loop(0, hidden_count // 256, block, 0)
        hidden_outs.extend(load(*pair) for pair in zip(hidden, outs[m][9:12]))
        wait_all(wide_outs)

        def through(i, carry):
            at = pl.ds(pl.multiple_of(i * 512, 512), 512)
            back[:, at] = dot_t(gate_pre[...], gate_weight[at, :]) + dot_t(
                up_pre[...], up_weight[at, :]
            )
            fed[:, at] = f32_dot(inside[...], down_weight[:, at])
            return carry

        lax.fori_loop(0, depth // 512, through, 0)
        wide_outs.extend([load(back, outs[m][12]), load(fed, outs[m][13])])

    def flip_cot(m):
        cot_loads[m].wait()
        flip_to(cot_rows[m], outs[m][0])

    if gathers:
        wait_all(weight_loads)
        gather.begin()
        attend(0, {})
        attend(1, {2: lambda: gather.forward(1)})
        flip_cot(0)
        gather.forward(2)
        flip_cot(1)
        gather.forward(3)
        gather.finish_line()
        gather.finish()
    else:
        attend(0, {})
        sums[0].far_go()
        attend(1, {})
        flip_cot(0)
        flip_cot(1)
        sums[0].far_wait()
        sums[1].far_go()
    join(0)
    if gathers:
        join(1)
    norm(0)
    feed(0)
    if not gathers:
        sums[1].far_wait()
        join(1)
    norm(1)
    feed(1)
    wait_all(flip_loads)
    wait_all(hidden_outs)
    wait_all(wide_outs)
    wait_all(out_loads)


def front_call(dp_count, lengths, arrays, blocks, shapes):
    depth, row_count, inner, hidden_count, head_count, head_width = shapes
    bf16, f32 = jnp.bfloat16, jnp.float32
    dma, regular = pltpu.SemaphoreType.DMA, pltpu.SemaphoreType.REGULAR
    half = row_count // 2
    out_shape = []
    for m in range(2):
        out_shape += [jax.ShapeDtypeStruct((depth, row_count), bf16)] * 3
        out_shape += [jax.ShapeDtypeStruct((row_count, inner), bf16)] * 3
        out_shape += [jax.ShapeDtypeStruct((row_count, inner), f32)]
        out_shape += [jax.ShapeDtypeStruct((row_count, inner), bf16)]
        out_shape += [jax.ShapeDtypeStruct((half, depth), f32)]
        out_shape += [jax.ShapeDtypeStruct((row_count, hidden_count), bf16)] * 3
        out_shape += [jax.ShapeDtypeStruct((row_count, depth), f32)] * 2
        out_shape += [jax.ShapeDtypeStruct((row_count, head_width), f32)] * 2
    wide_rows = pltpu.VMEM((row_count, depth), bf16)
    narrow = pltpu.VMEM((row_count, inner), bf16)
    wide_half = pltpu.VMEM((half, depth), f32)
    if gathers_heads(dp_count):
        steps = dp_count // 2 - 1
        extra = [wide_half] * 4
        extra += [pltpu.VMEM((row_count, inner), f32)] * 2
        extra += [pltpu.VMEM((3, half, inner), f32)] * 2
        extra += [
            pltpu.VMEM((half, depth), bf16),
            pltpu.VMEM((inner // dp_count, depth), f32),
            pltpu.VMEM((inner, depth), f32),
            pltpu.VMEM((inner, depth), f32),
            pltpu.VMEM((depth, depth), bf16),
            dma((2, 2, 3)),
            dma((2,)),
            dma((2, steps)),
            dma((2, steps)),
            dma((1 + 2 * steps,)),
            dma((1 + 2 * steps,)),
            dma((2, 3)),
        ]
    else:
        extra = [wide_half] * 7 + [dma((2, 2)), regular((2,))]
    return pl.pallas_call(
        functools.partial(front_kernel, dp_count),
        out_shape=out_shape,
        in_specs=[pl.BlockSpec(memory_space=pltpu.SMEM)] * 2
        + [pl.BlockSpec(memory_space=pl.ANY)] * len(arrays)
        + in_vmem(len(blocks)),
        out_specs=[pl.BlockSpec(memory_space=pl.ANY)] * len(out_shape),
        scratch_shapes=[pltpu.VMEM((row_count, head_width), f32)] * 4
        + [pltpu.VMEM((row_count, 1), jnp.int32), pltpu.VMEM((1, row_count), jnp.int32)]
        + [wide_rows] * 6
        + [pltpu.VMEM((depth, row_count), bf16)]
        + [pltpu.VMEM((depth, inner), bf16)] * 3
        + [pltpu.VMEM((inner, depth), bf16)]
        + [pltpu.VMEM((depth, hidden_count), bf16)] * 2
        + [pltpu.VMEM((hidden_count, depth), bf16)]
        + [narrow, narrow, narrow, pltpu.VMEM((row_count, inner), f32), narrow]
        + [pltpu.VMEM((row_count, hidden_count), bf16)] * 3
        + [pltpu.VMEM((row_count, depth), f32)] * 2
        + [dma((2, 2)), dma((64,))]
        + extra,
        compiler_params=pltpu.CompilerParams(
            collective_id=1, has_side_effects=True, vmem_limit_bytes=62 * 1024 * 1024
        ),
        cost_estimate=pl.CostEstimate(
            flops=4 * row_count * depth * (6 * hidden_count + 4 * inner),
            bytes_accessed=64 << 20,
            transcendentals=0,
        ),
    )(*lengths, *arrays, *blocks)


def on_device(
    layer_in,
    short_lengths,
    long_lengths,
    norm1_gain,
    query_weight,
    key_weight,
    value_weight,
    lambda_param,
    sub_gain,
    out_weight,
    norm2_gain,
    gate_weight,
    up_weight,
    down_weight,
    out_cotangent,
):
    dp_count = lax.axis_size("dp")
    projections = [query_weight, key_weight, value_weight]
    depth, inner = query_weight.shape
    shapes = (depth, layer_in.shape[1], inner, gate_weight.shape[1], *sub_gain.shape)
    lengths = [short_lengths, long_lengths]
    blocks = [lambda_param, sub_gain, norm1_gain[None, :], norm2_gain[None, :]]
    arrays = [layer_in, out_cotangent, *projections, out_weight]
    arrays += [gate_weight, up_weight, down_weight]
    parts = front_call(dp_count, lengths, arrays, blocks, shapes)
    pick = lambda at: [parts[at], parts[at + 16]]
    arrays = pick(0) + pick(1) + pick(2) + pick(9) + pick(10) + pick(11) + pick(7)
    arrays += pick(12) + pick(13) + pick(8)
    arrays += [layer_in, out_cotangent, out_weight, *projections]
    arrays += parts[3:7] + parts[19:23] + parts[14:16] + parts[30:32]
    (
        grad_down, grad_gate, grad_up, grad_out, grad_query, grad_key, grad_value, layer_out,
        grad_in, grad_norm1, grad_norm2, grad_lambda, grad_sub,
    ) = back_call(dp_count, lengths, arrays, blocks, shapes)
    return (
        layer_out,
        grad_in,
        grad_norm1.reshape(-1),
        grad_query,
        grad_key,
        grad_value,
        grad_lambda,
        grad_sub,
        grad_out.T,
        grad_norm2.reshape(-1),
        grad_gate,
        grad_up,
        grad_down.T,
    )


def solution(mesh):
    return jax.shard_map(
        on_device,
        mesh=mesh,
        in_specs=(
            P(None, "dp", None),
            P("dp", None),
            P("dp", None),
            P(),
            P(None, "tensor"),
            P(None, "tensor"),
            P(None, "tensor"),
            P("tensor", None),
            P("tensor", None),
            P("tensor", None),
            P(),
            P(None, "tensor"),
            P(None, "tensor"),
            P("tensor", None),
            P(None, "dp", None),
        ),
        out_specs=(
            P(None, "dp", None),
            P(None, "dp", None),
            P("dp"),
            P("dp", "tensor"),
            P("dp", "tensor"),
            P("dp", "tensor"),
            P("tensor", "dp"),
            P("tensor", "dp"),
            P("tensor", "dp"),
            P("dp"),
            P("dp", "tensor"),
            P("dp", "tensor"),
            P("tensor", "dp"),
        ),
        check_vma=False,
    )
```

```python
import functools
import math

import jax
import jax.numpy as jnp
from jax import lax
from jax.experimental import pallas as pl
from jax.experimental.pallas import tpu as pltpu
from jax.sharding import PartitionSpec as P

norm_epsilon = 1e-05
lambda_base = 0.8 - 0.6 * math.exp(-0.3 * 11.0)
rotary_base = 10000.0
closed_score = -1e30
block_rows = 128
longest_document = 256
row_group = 16
send_slots = 3
held_slots = 4
MESH = pl.DeviceIdType.MESH


def documents(lengths, places):
    end, segment, start = 0, 0, 0
    for k in range(lengths.shape[1]):
        length = lengths[0, k]
        end = end + length
        passed = (places >= end).astype(jnp.int32)
        segment = segment + passed
        start = start + passed * length
    return segment, start


def segments(lengths, column, row):
    column[...] = documents(lengths, lax.broadcasted_iota(jnp.int32, column.shape, 0))[0]
    row[...] = documents(lengths, lax.broadcasted_iota(jnp.int32, row.shape, 1))[0]


def rotary_tables(lengths, cosines, sines, map_width):
    half_width = map_width // 2
    row_count, width = cosines[0].shape
    lane = lax.broadcasted_iota(jnp.int32, (block_rows, width), 1)
    frequency = jnp.zeros((block_rows, width), jnp.float32)
    for k in range(half_width):
        value = rotary_base ** (-2.0 * k / map_width)
        frequency = jnp.where(lane % half_width == k, value, frequency)

    def block(i, carry):
        rows = pl.ds(pl.multiple_of(i * block_rows, block_rows), block_rows)
        places = lax.broadcasted_iota(jnp.int32, (block_rows, width), 0) + i * block_rows
        starts = [documents(item, places)[1] for item in lengths]
        start = jnp.where(lane < half_width, starts[0], starts[1])
        angles = (places - start).astype(jnp.float32) * frequency

        def spread(values, m):
            base = jnp.where(lane // half_width == m, values, 0.0)
            return sum(
                (pltpu.roll(base, k * half_width, 1) for k in range(1, width // half_width)), base
            )

        cosine, sine = jnp.cos(angles), jnp.sin(angles)
        for m in range(2):
            cosines[m][rows, :] = spread(cosine, m)
            signed = spread(sine, m)
            sines[m][rows, :] = jnp.where(lane % map_width < half_width, -signed, signed)
        return carry

    lax.fori_loop(0, row_count // block_rows, block, 0)


def lambda_terms(param):
    width = param.shape[1] // 4
    part = lambda k: param[:, k * width : (k + 1) * width]
    first = jnp.exp(jnp.sum(part(0) * part(1), axis=-1, keepdims=True))
    second = jnp.exp(jnp.sum(part(2) * part(3), axis=-1, keepdims=True))
    return first, second, first - second + lambda_base


def turn(values, cosine, sine):
    width = values.shape[-1]
    quarter = width // 4
    lane = lax.broadcasted_iota(jnp.int32, values.shape, 1)
    partner = jnp.where(
        lane % (2 * quarter) < quarter,
        pltpu.roll(values, width - quarter, 1),
        pltpu.roll(values, quarter, 1),
    )
    return values * cosine + partner * sine


def map_of(values, which):
    lane = lax.broadcasted_iota(jnp.int32, values.shape, 1)
    mine = (lane >= values.shape[-1] // 2) == (which == 1)
    return jnp.where(mine, values, jnp.zeros_like(values))


def key_range(block):
    first = max(0, block * block_rows - longest_document + 1) // block_rows * block_rows
    return first, (block + 1) * block_rows


def open_pairs(block, segment_column, segment_row):
    first, last = key_range(block)
    rows = pl.ds(block * block_rows, block_rows)
    shape = (block_rows, last - first)
    row_at = lax.broadcasted_iota(jnp.int32, shape, 0) + block * block_rows
    key_at = lax.broadcasted_iota(jnp.int32, shape, 1) + first
    return (segment_column[rows, :] == segment_row[:, first:last]) & (key_at <= row_at)


def softmax_map(query, key, opened, scale):
    scores = jnp.where(opened, dot_t(query, key) * scale, closed_score)
    expanded = jnp.exp(scores - jnp.max(scores, axis=-1, keepdims=True))
    return expanded * (1.0 / jnp.sum(expanded, axis=-1, keepdims=True))


def f32_dot(left, right):
    return jnp.dot(left, right, preferred_element_type=jnp.float32)


def dot_t(left, right):
    return lax.dot_general(
        left, right, (((1,), (1,)), ((), ())), preferred_element_type=jnp.float32
    )


def dot_rows(left, right):
    return lax.dot_general(
        left, right, (((0,), (0,)), ((), ())), preferred_element_type=jnp.float32
    )


def rms_back(incoming, values, inverse_root):
    return inverse_root * incoming - values * inverse_root**3 * jnp.mean(
        incoming * values, axis=-1, keepdims=True
    )


def root_of(values):
    return lax.rsqrt(jnp.mean(values * values, axis=-1, keepdims=True) + norm_epsilon)


def forward_kernel(
    lam, rows, gain, query_weight, key_weight, value_weight, cosine, sine, segment_column,
    segment_row, sub_scale, normed_one, query, key, value, mixed, heads_out, between,
):
    head_count, width = sub_scale.shape
    scale = (width // 2) ** (-0.5)
    values = rows[...].astype(jnp.float32)
    normed_one[...] = (values * root_of(values) * gain[...]).astype(jnp.bfloat16)
    raw_query = f32_dot(normed_one[...], query_weight[...])
    raw_key = f32_dot(normed_one[...], key_weight[...])
    value[...] = f32_dot(normed_one[...], value_weight[...]).astype(jnp.bfloat16)
    for head in range(head_count):
        at = slice(head * width, (head + 1) * width)
        query[:, at] = turn(raw_query[:, at], cosine[...], sine[...]).astype(jnp.bfloat16)
        key[:, at] = turn(raw_key[:, at], cosine[...], sine[...]).astype(jnp.bfloat16)
    for block in range(rows.shape[0] // block_rows):
        first, last = key_range(block)
        here = slice(block * block_rows, last)
        opened = open_pairs(block, segment_column, segment_row)
        if block in between:
            between[block]()
        for head in range(head_count):
            at = slice(head * width, (head + 1) * width)
            keys = key[first:last, at]
            maps = [softmax_map(map_of(query[here, at], c), keys, opened, scale) for c in range(2)]
            combined = (maps[0] - lam[head : head + 1, :] * maps[1]).astype(jnp.bfloat16)
            out = f32_dot(combined, value[first:last, at])
            mixed[here, at] = out
            heads_out[here, at] = (out * root_of(out) * sub_scale[head : head + 1, :]).astype(
                jnp.bfloat16
            )


def backward_kernel(
    lam, grad_attended, out_weight, query, key, value, mixed, cosine, sine, segment_column,
    segment_row, sub_scale, grad_rows, grad_sub, grad_lam, grad_heads, grad_mixed, grad_key,
    grad_value,
):
    head_count, width = sub_scale.shape
    row_count = query.shape[0]
    inner = head_count * width
    scale = (width // 2) ** (-0.5)
    grad_heads[...] = dot_t(grad_attended[...], out_weight[...])
    for head in range(head_count):
        at = slice(head * width, (head + 1) * width)
        heads = mixed[:, at]
        root = root_of(heads)
        grads = grad_heads[:, at]
        grad_sub[head : head + 1, :] = jnp.sum(grads * heads * root, axis=0, keepdims=True) * (
            1.0 - lambda_base
        )
        grad_mixed[:, at] = rms_back(grads * sub_scale[head : head + 1, :], heads, root).astype(
            jnp.bfloat16
        )
    grad_key[...] = jnp.zeros_like(grad_key)
    grad_value[...] = jnp.zeros_like(grad_value)
    lam_sums = [0.0] * head_count
    for block in range(row_count // block_rows):
        first, last = key_range(block)
        here = slice(block * block_rows, last)
        opened = open_pairs(block, segment_column, segment_row)
        for head in range(head_count):
            at = slice(head * width, (head + 1) * width)
            keys = key[first:last, at]
            queries = [map_of(query[here, at], c) for c in range(2)]
            maps = [softmax_map(queries[c], keys, opened, scale) for c in range(2)]
            mixes = grad_mixed[here, at]
            combined = (maps[0] - lam[head : head + 1, :] * maps[1]).astype(jnp.bfloat16)
            grad_value[first:last, at] += dot_rows(combined, mixes)
            grads = dot_t(mixes, value[first:last, at])
            first_sum = jnp.sum(grads * maps[0], axis=-1, keepdims=True)
            second_sum = jnp.sum(grads * maps[1], axis=-1, keepdims=True)
            lam_sums[head] = lam_sums[head] + jnp.sum(second_sum, axis=0, keepdims=True)
            score_grads = [
                (maps[0] * (grads - first_sum)).astype(jnp.bfloat16),
                (maps[1] * (-lam[head : head + 1, :] * (grads - second_sum))).astype(jnp.bfloat16),
            ]
            grad_query = f32_dot(score_grads[0], map_of(keys, 0)) + f32_dot(
                score_grads[1], map_of(keys, 1)
            )
            grad_rows[here, at] = turn(
                grad_query * scale, cosine[here, :], -sine[here, :]
            ).astype(jnp.bfloat16)
            grad_key[first:last, at] += dot_rows(score_grads[0], queries[0]) + dot_rows(
                score_grads[1], queries[1]
            )
    for head in range(head_count):
        at = slice(head * width, (head + 1) * width)
        grad_rows[:, inner + head * width : inner + (head + 1) * width] = turn(
            grad_key[:, at] * scale, cosine[...], -sine[...]
        ).astype(jnp.bfloat16)
        grad_lam[head : head + 1, :] = jnp.broadcast_to(-lam_sums[head], (1, width))
    grad_rows[:, 2 * inner :] = grad_value[...].astype(jnp.bfloat16)


def in_vmem(count):
    return [pl.BlockSpec(memory_space=pltpu.VMEM)] * count


class Line:
    def __init__(self, line, widths, total, landed, line_out, line_in, credit):
        self.line, self.widths = line, widths
        self.total, self.landed = total, landed
        self.line_out, self.line_in, self.credit = line_out, line_in, credit
        self.me = lax.axis_index("dp")
        self.place = self.me // 2
        self.ring = total.shape[0]

    def copy(self, c, step, way, block, target):
        width = self.widths[c]
        return pltpu.make_async_remote_copy(
            src_ref=self.total.at[c % self.ring, block, :, :width],
            dst_ref=self.landed.at[way, step, c % 2, :, :width],
            send_sem=self.line_out.at[way, step, c % 2],
            recv_sem=self.line_in.at[way, step, c % 2],
            device_id={"dp": target},
            device_id_type=MESH,
        )

    def sends(self, step, way):
        place, line = self.place, self.line
        if way == 0:
            block = line - 1 - step + place
            return (place <= step) & (place < line - 1), block, self.me + 2
        block = place + step - line + 1
        return (place >= line - 1 - step) & (place > 0), block, self.me - 2

    def gets(self, step, way):
        place, line = self.place, self.line
        if way == 0:
            return (place > 0) & (place - 1 <= step), line - 2 - step + place, self.me - 2
        gets = (place < line - 1) & (place + 1 >= line - 1 - step)
        return gets, place + step - line + 2, self.me + 2

    def start(self, c, step):
        for way in range(2):
            sends, block, target = self.sends(step, way)

            @pl.when(sends)
            def _():
                if c >= 2:
                    pl.semaphore_wait(self.credit.at[way, step], 1)
                self.copy(c, step, way, block, target).start()

    def finish(self, c, step):
        width = self.widths[c]
        for way in range(2):
            gets, block, source = self.gets(step, way)

            @pl.when(gets)
            def _():
                self.copy(c, step, way, block, source).wait_recv()
                self.total[c % self.ring, block, :, :width] += self.landed[
                    way, step, c % 2, :, :width
                ]
                if c + 2 < len(self.widths):
                    pl.semaphore_signal(
                        self.credit.at[way, step],
                        inc=1,
                        device_id={"dp": source},
                        device_id_type=MESH,
                    )

            sends, sent, target = self.sends(step, way)

            @pl.when(sends)
            def _():
                self.copy(c, step, way, sent, target).wait_send()


class Reducer:
    def __init__(self, plan, line_plan, line_starts, line, refs):
        self.plan, self.line_plan, self.line_starts = plan, line_plan, line_starts
        self.line = line
        (
            self.send, self.held, self.total, landed, self.pair_out, self.pair_in,
            line_out, line_in, credit, self.out_sem,
        ) = refs[:10]
        self.first = Line(
            line, [item.width for item in plan], self.total, landed, line_out, line_in, credit
        )
        self.place = self.first.place
        self.me = self.first.me
        self.side = self.me % 2
        self.other = self.me + 1 - 2 * self.side
        self.steps = line - 1
        self.ring = self.total.shape[0]
        self.rows = self.total.shape[2]
        if line_plan:
            (
                self.line_total, landed, line_out, line_in, credit, self.last_held,
                self.last_out, self.last_in, self.line_out_sem,
            ) = refs[10:]
            self.second = Line(
                line, [item.width for item in line_plan], self.line_total, landed, line_out,
                line_in, credit,
            )

    def compute(self, c):
        item = self.plan[c]
        width = item.width
        left, right = item.left(), item.right()

        def block(at, carry):
            first = pl.multiple_of(2 * at * self.rows, self.rows)
            columns = right[...]
            away = left[pl.ds(first + (1 - self.side) * self.rows, self.rows), :]
            here = left[pl.ds(first + self.side * self.rows, self.rows), :]
            self.send[c % send_slots, at, :, :width] = f32_dot(away, columns)
            self.total[c % self.ring, at, :, :width] = f32_dot(here, columns)
            return carry

        lax.fori_loop(0, self.line, block, 0)
        item.computed()

    def line_compute(self, c):
        item = self.line_plan[c]
        left, right = item.left(), item.right()
        slot = c % self.line_total.shape[0]
        if c >= self.line_total.shape[0]:
            self.line_result(c - self.line_total.shape[0]).wait()

        def block(at, carry):
            rows = pl.ds(pl.multiple_of(2 * at * self.rows, 2 * self.rows), 2 * self.rows)
            self.line_total[slot, at] = f32_dot(left[rows, :], right[...])
            return carry

        lax.fori_loop(0, self.line, block, 0)
        item.computed()

    def side_rows(self, side):
        return pl.ds(pl.multiple_of(side * self.rows, self.rows), self.rows)

    def last_copy(self, c):
        slot = c % self.line_total.shape[0]
        return pltpu.make_async_remote_copy(
            src_ref=self.line_total.at[slot, self.place, self.side_rows(1 - self.side), :],
            dst_ref=self.last_held.at[c],
            send_sem=self.last_out.at[c],
            recv_sem=self.last_in.at[c],
            device_id={"dp": self.other},
            device_id_type=MESH,
        )

    def line_result(self, c):
        item = self.line_plan[c]
        slot = c % self.line_total.shape[0]
        return pltpu.make_async_copy(
            self.line_total.at[slot, self.place, self.side_rows(self.side), :],
            item.out.at[:, item.first : item.first + item.width],
            self.line_out_sem.at[slot],
        )

    def line_step(self, slot):
        for c, start in enumerate(self.line_starts):
            step = slot - start
            if 0 < step <= self.steps:
                self.second.finish(c, step - 1)
            if step == self.steps + 1:
                self.last_copy(c).wait()
                at = c % self.line_total.shape[0]
                self.line_total[at, self.place, self.side_rows(self.side), :] += self.last_held[c]
                self.line_result(c).start()
            if 0 <= step < self.steps and slot:
                self.second.start(c, step)
            if step == self.steps:
                self.last_copy(c).start()

    def pair_copy(self, c):
        width = self.plan[c].width
        return pltpu.make_async_remote_copy(
            src_ref=self.send.at[c % send_slots, :, :, :width],
            dst_ref=self.held.at[c % held_slots, :, :, :width],
            send_sem=self.pair_out.at[c % send_slots],
            recv_sem=self.pair_in.at[c % held_slots],
            device_id={"dp": self.other},
            device_id_type=MESH,
        )

    def pair_finish(self, c):
        width = self.plan[c].width
        self.pair_copy(c).wait_recv()

        def block(at, carry):
            self.total[c % self.ring, at, :, :width] += self.held[c % held_slots, at, :, :width]
            return carry

        lax.fori_loop(0, self.line, block, 0)
        self.pair_copy(c).wait_send()

    def out_copies(self, c):
        item = self.plan[c]
        outs = item.out if isinstance(item.out, list) else [item.out]
        size = outs[0].shape[1]
        first, last = item.first, item.first + item.width
        while first < last:
            count = min(last, (first // size + 1) * size) - first
            at = first - item.first
            yield pltpu.make_async_copy(
                self.total.at[c % self.ring, self.place, :, at : at + count],
                outs[first // size].at[:, first % size : first % size + count],
                self.out_sem.at[c % self.ring, at // 128],
            )
            first += count

    def out_start(self, c):
        for copy in self.out_copies(c):
            copy.start()

    def out_wait(self, c):
        for copy in self.out_copies(c):
            copy.wait()

    def run(self, tasks):
        count, steps = len(self.plan), self.steps
        begun = [c for c, start in enumerate(self.line_starts) if start == 0]
        for c in begun:
            self.line_compute(c)
        for c in begun:
            self.second.start(c, 0)
        self.compute(1)
        for slot in range(count + steps + 1):
            for step in reversed(range(steps)):
                c = slot - 2 - step
                if 0 <= c < count:
                    self.first.finish(c, step)
                    if step + 1 < steps:
                        self.first.start(c, step + 1)
            self.line_step(slot)
            if 0 <= slot - 1 < count:
                self.pair_finish(slot - 1)
                self.first.start(slot - 1, 0)
            if slot + 1 < count:
                self.pair_copy(slot + 1).start()
            done = slot - 1 - steps
            if 0 <= done < count:
                self.out_start(done)
            if slot + 2 < count:
                if slot + 2 >= self.ring:
                    self.out_wait(slot + 2 - self.ring)
                self.compute(slot + 2)
            for c, start in enumerate(self.line_starts):
                if slot and start == slot + 1:
                    self.line_compute(c)
            for task in tasks.get(slot, ()):
                task()
        for c in range(max(0, count - self.ring), count):
            self.out_wait(c)
        if self.line_plan:
            for c in range(len(self.line_plan) - self.line_total.shape[0], len(self.line_plan)):
                self.line_result(c).wait()


class Chunk:
    def __init__(self, left, right, computed, out, first, width):
        self.left, self.right, self.computed = left, right, computed
        self.out, self.first, self.width = out, first, width


def for_rows(count, body):
    def step(i, carry):
        body(pl.ds(pl.multiple_of(i * row_group, row_group), row_group))
        return carry

    lax.fori_loop(0, count // row_group, step, 0)


class TensorSum:
    def __init__(self, uses, own, near, far, near_sems, far_sems, near_credit, far_credit):
        self.own, self.near, self.far = own, near, far
        self.near_sems, self.far_sems = near_sems, far_sems
        self.near_credit, self.far_credit = near_credit, far_credit
        index = lax.axis_index("tensor")
        self.core_peer = index + 1 - 2 * (index % 2)
        self.far_peer = index + 2 - 4 * (index // 2)
        self.near_left, self.far_left = 2 * uses, uses
        self.near_first, self.far_first = True, True

    def near_copy(self, source):
        return pltpu.make_async_remote_copy(
            src_ref=source, dst_ref=self.near, send_sem=self.near_sems.at[0],
            recv_sem=self.near_sems.at[1], device_id={"tensor": self.core_peer},
            device_id_type=MESH,
        )

    def far_copy(self):
        return pltpu.make_async_remote_copy(
            src_ref=self.own, dst_ref=self.far, send_sem=self.far_sems.at[0],
            recv_sem=self.far_sems.at[1], device_id={"tensor": self.far_peer},
            device_id_type=MESH,
        )

    def near_start(self, source):
        if not self.near_first:
            pl.semaphore_wait(self.near_credit, 1)
        self.near_first = False
        self.pending = source
        self.near_copy(source).start()

    def near_wait(self):
        self.near_copy(self.pending).wait()

    def near_free(self):
        self.near_left -= 1
        if self.near_left:
            pl.semaphore_signal(
                self.near_credit, inc=1, device_id={"tensor": self.core_peer}, device_id_type=MESH
            )

    def near_add(self):
        self.near_wait()

        def add(rows):
            self.own[rows, :] += self.near[rows, :]

        for_rows(self.own.shape[0], add)
        self.near_free()

    def far_go(self):
        if not self.far_first:
            pl.semaphore_wait(self.far_credit, 1)
        self.far_first = False
        self.far_copy().start()

    def far_wait(self):
        self.far_copy().wait()

    def far_free(self):
        self.far_left -= 1
        if self.far_left:
            pl.semaphore_signal(
                self.far_credit, inc=1, device_id={"tensor": self.far_peer}, device_id_type=MESH
            )


def line_first(dp_count):
    return ((0, 0, 3, 6, 9, 12), (2, 2, 2)) if dp_count == 8 else ((), (0, 0, 0))


def back_kernel(dp_count, *refs):
    refs = list(refs)
    take = lambda n: [refs.pop(0) for _ in range(n)]
    lengths = take(2)
    cot_left, two_left, one_left = [take(2) for _ in range(3)]
    hidden, gate_pre, up_pre, heads = [take(2) for _ in range(4)]
    part_back, part_fed, middle = [take(2) for _ in range(3)]
    (layer_in, cotangent) = take(2)
    weights_in = take(4)
    kept_in = [take(4) for _ in range(2)]
    tables_in = [take(2) for _ in range(2)]
    (lambda_param, sub_gain, gain_one, gain_two) = take(4)
    (grad_down, grad_gate, grad_up, grad_out) = take(4)
    grad_qkv = take(3)
    (layer_out, grad_in) = take(2)
    small_outs = take(4)
    reducer_refs = take(20 if line_first(dp_count)[0] else 10)
    line_rights = reducer_refs.pop() if line_first(dp_count)[0] else None
    (left_a, left_b, rights, rows_qkv) = take(4)
    weights = take(4)
    kept = take(4)
    backward_scratch = take(4)
    (grad_sub, grad_lam) = take(2)
    sets = [take(3) for _ in range(2)]
    through = take(2)
    (spare, projected, attended, rows_in, rows_out) = take(5)
    (small, small_near, small_landed) = take(3)
    small_blocks = take(4)
    tables = take(4)
    (near_sems, far_sems, near_credit, far_credit) = take(4)
    (load_sems, small_near_sems, small_send, small_recv) = take(4)
    assert not refs

    me = lax.axis_index("dp")
    tensor = lax.axis_index("tensor")
    core = tensor % 2
    core_peer = tensor + 1 - 2 * core
    far_peer = tensor + 2 - 4 * (tensor // 2)
    line = dp_count // 2
    half = middle[0].shape[0]
    row_count = 2 * half
    head_count, head_width = sub_gain.shape
    sub_scale = sub_gain[...] * (1.0 - lambda_base)
    first_exp, second_exp, lam = lambda_terms(lambda_param)
    out_weight, projections = weights[0], weights[1:]
    inner = out_weight.shape[0]
    kept_half = pl.ds(pl.multiple_of(core * half, half), half)
    sent_half = pl.ds(pl.multiple_of((1 - core) * half, half), half)
    tokens = [slice(m * row_count, (m + 1) * row_count) for m in range(2)]

    barrier = pltpu.get_barrier_semaphore()
    for offset in range(1, dp_count):
        pl.semaphore_signal(
            barrier, inc=1, device_id={"dp": lax.rem(me + offset, dp_count)}, device_id_type=MESH
        )
    for peer in (core_peer, far_peer):
        pl.semaphore_signal(barrier, inc=1, device_id={"tensor": peer}, device_id_type=MESH)

    used = [0]

    def load(source, target):
        copy = pltpu.make_async_copy(source, target, load_sems.at[used[0]])
        used[0] += 1
        copy.start()
        return copy

    def wait_all(copies):
        for copy in copies:
            copy.wait()

    reducer_width = reducer_refs[0].shape[-1]
    plan, sources, left_loads, right_loads = [], {}, {}, {}

    def load_left(sources_of, left):
        return [load(sources_of[m], left.at[:, tokens[m]]) for m in range(2)]

    def load_columns(source, first, width, target):
        return [
            load(source[m].at[:, first : first + width], target.at[tokens[m], :width])
            for m in range(2)
        ]

    def load_right(c):
        if c in sources:
            right_loads[c] = load_columns(*sources[c], rights.at[c % 2])

    def load_line_right(c):
        if c < len(line_sources):
            line_loads[c] = load_columns(*line_sources[c], line_rights.at[c % 2])

    def get_left(c, left):
        wait_all(left_loads.pop(c, ()))
        return left

    def get_line_left(left):
        return left

    def get_right(c, first, width):
        if c in sources:
            wait_all(right_loads[c])
            return rights.at[c % 2, :, :width]
        return rows_qkv.at[:, first : first + width]

    def get_line_right(c):
        wait_all(line_loads[c])
        return line_rights.at[c % 2]

    def computed(c):
        load_right(c + 2)
        if c == last_two:
            left_loads[first_one] = load_left(one_left, left_b)

    def add_group(left, source, columns, out, line_chunks=0):
        start = line_chunks * line_width
        for first in range(0, start, line_width):
            c = len(line_plan)
            line_sources.append((source, first, line_width))
            line_plan.append(
                Chunk(
                    functools.partial(get_line_left, left),
                    functools.partial(get_line_right, c),
                    functools.partial(load_line_right, c + 2),
                    out,
                    first,
                    line_width,
                )
            )
        for first in range(start, columns, reducer_width):
            width = min(reducer_width, columns - first)
            c = len(plan)
            if source is not None:
                sources[c] = (source, first, width)
            plan.append(
                Chunk(
                    functools.partial(get_left, c, left),
                    functools.partial(get_right, c, first, width),
                    functools.partial(computed, c),
                    out,
                    first,
                    width,
                )
            )

    line_starts, line_counts = line_first(dp_count)
    line_plan, line_sources, line_loads, line_width = [], [], {}, 128
    add_group(left_a, hidden, hidden[0].shape[1], grad_down, line_counts[0])
    add_group(left_b, gate_pre, gate_pre[0].shape[1], grad_gate, line_counts[1])
    add_group(left_b, up_pre, up_pre[0].shape[1], grad_up)
    last_two = len(plan) - 1
    add_group(left_a, heads, inner, grad_out, line_counts[2])
    first_one = len(plan)
    add_group(left_b, None, 3 * inner, grad_qkv)

    left_loads[0] = load_left(cot_left, left_a)
    load_right(0)
    two_loads = [load(two_left[m], (attended, rows_out)[m]) for m in range(2)]
    load_line_right(0)
    load_line_right(1)
    load_right(1)
    sums = [
        TensorSum(
            3, *sets[m], near_sems.at[m], far_sems.at[m], near_credit.at[m], far_credit.at[m]
        )
        for m in range(2)
    ]
    own_loads = {m: load(part_back[m].at[kept_half], sets[m][0]) for m in range(2)}
    weight_loads = [load(*pair) for pair in zip(weights_in, weights)]
    def load_kept(m):
        pairs = zip([*kept_in[m], *tables_in[m]], [*kept, *tables[:2]])
        return [load(*pair) for pair in pairs]

    kept_loads = load_kept(0)
    spare_queue = [middle[0], middle[1], middle[0], middle[1]]
    rows_queue = [cotangent.at[0], cotangent.at[1]]
    rows_queue += [layer_in.at[0], cotangent.at[0], layer_in.at[1], cotangent.at[1]]
    queued = {}

    def next_spare():
        queued["spare"] = load(spare_queue.pop(0), spare) if spare_queue else None

    def next_rows():
        queued["rows"] = load(rows_queue.pop(0), rows_in) if rows_queue else None

    next_spare()
    next_rows()
    out_loads = []
    small[...] = jnp.zeros_like(small)

    def mine(rows):
        return pl.ds(pl.multiple_of(core * half + rows.start, row_group), row_group)

    def others(rows):
        return pl.ds(pl.multiple_of((1 - core) * half + rows.start, row_group), row_group)

    def flip_rows(source, left, m):
        def block(i, carry):
            at = pl.ds(pl.multiple_of(i * 128, 128), 128)
            left[at, tokens[m]] = source[:, at].T
            return carry

        lax.fori_loop(0, source.shape[1] // 128, block, 0)

    def flip_two():
        wait_all(two_loads)
        for m in range(2):
            flip_rows((attended, rows_out)[m], left_b, m)

    def exchange(m):
        if m in own_loads:
            own_loads.pop(m).wait()
        sums[m].near_add()
        sums[m].far_go()

    def norm_two(m):
        own, near, far = sets[m]
        queued["spare"].wait()
        sums[m].far_wait()

        def body(rows):
            grads = own[rows, :] + far[rows, :]
            values = spare[rows, :]
            root = root_of(values)
            small[1:2, :] += jnp.sum(grads * values * root, axis=0, keepdims=True)
            through[m][rows, :] = rms_back(grads * gain_two[...], values, root)

        for_rows(half, body)
        sums[m].far_free()
        sums[m].near_start(through[m])
        next_spare()

    def attend(m):
        near = sets[m][1]
        queued["rows"].wait()
        sums[m].near_wait()

        def body(rows):
            attended[mine(rows), :] = (
                rows_in[mine(rows), :].astype(jnp.float32) + through[m][rows, :]
            ).astype(jnp.bfloat16)
            attended[others(rows), :] = (
                rows_in[others(rows), :].astype(jnp.float32) + near[rows, :]
            ).astype(jnp.bfloat16)

        for_rows(half, body)
        sums[m].near_free()
        next_rows()

        flip_rows(attended, left_a, m)
        if m == 0:
            wait_all(weight_loads)
        wait_all(kept_loads)
        segments(lengths[m], *tables[2:])
        backward_kernel(
            lam, attended, out_weight, *kept, *tables, sub_scale,
            rows_qkv.at[tokens[m], :], grad_sub, grad_lam, *backward_scratch,
        )
        if m == 0:
            kept_loads[:] = load_kept(1)
        for head in range(head_count):
            at = slice(head * head_width, (head + 1) * head_width)
            small[2:3, at] += grad_sub[head : head + 1, :]
            small[3:4, at] += grad_lam[head : head + 1, :]

    def project(m):
        def part(which, target):
            rows = pl.ds(pl.multiple_of(m * row_count + which * half, half), half)

            def block(i, carry):
                at = pl.ds(pl.multiple_of(i * 512, 512), 512)
                total = 0.0
                for p in range(3):
                    grads = rows_qkv[rows, p * inner : (p + 1) * inner]
                    total = total + dot_t(grads, projections[p][at, :])
                target[:, at] = total
                return carry

            lax.fori_loop(0, target.shape[1] // 512, block, 0)

        part(1 - core, projected)
        sums[m].near_start(projected)
        part(core, sets[m][0])

    def norm_one(m):
        own, near, far = sets[m]
        queued["rows"].wait()
        sums[m].far_wait()

        def body(rows):
            grads = own[rows, :] + far[rows, :]
            values = rows_in[mine(rows), :].astype(jnp.float32)
            root = root_of(values)
            small[0:1, :] += jnp.sum(grads * values * root, axis=0, keepdims=True)
            through[m][rows, :] += rms_back(grads * gain_one[...], values, root)

        for_rows(half, body)
        sums[m].far_free()
        sums[m].near_start(through[m])
        next_rows()
        own_loads[m] = load(part_fed[m].at[kept_half], own)

    def store_rows(target):
        out_loads.append(load(rows_out, target))

    def finish_in(m):
        near = sets[m][1]
        queued["rows"].wait()
        sums[m].near_wait()
        wait_all(out_loads)
        out_loads.clear()

        def body(rows):
            rows_out[mine(rows), :] = (
                rows_in[mine(rows), :].astype(jnp.float32) + through[m][rows, :]
            ).astype(jnp.bfloat16)
            rows_out[others(rows), :] = (
                rows_in[others(rows), :].astype(jnp.float32) + near[rows, :]
            ).astype(jnp.bfloat16)

        for_rows(half, body)
        sums[m].near_free()
        next_rows()
        store_rows(grad_in.at[m])
        sums[m].near_start(part_fed[m].at[sent_half])

    def add_fed(m):
        own, near, far = sets[m]
        queued["spare"].wait()
        sums[m].far_wait()

        def body(rows):
            own[rows, :] = spare[rows, :] + (own[rows, :] + far[rows, :])

        for_rows(half, body)
        sums[m].far_free()
        sums[m].near_start(own)
        next_spare()

    def finish_out(m):
        own, near = sets[m][:2]
        sums[m].near_wait()
        wait_all(out_loads)
        out_loads.clear()

        def body(rows):
            rows_out[mine(rows), :] = own[rows, :].astype(jnp.bfloat16)
            rows_out[others(rows), :] = near[rows, :].astype(jnp.bfloat16)

        for_rows(half, body)
        sums[m].near_free()
        store_rows(layer_out.at[m])

    small_core = pltpu.make_async_remote_copy(
        src_ref=small, dst_ref=small_near, send_sem=small_near_sems.at[0],
        recv_sem=small_near_sems.at[1], device_id={"tensor": core_peer}, device_id_type=MESH,
    )

    def small_copy(offset):
        return pltpu.make_async_remote_copy(
            src_ref=small, dst_ref=small_landed.at[offset - 1], send_sem=small_send.at[offset - 1],
            recv_sem=small_recv.at[offset - 1],
            device_id={"dp": lax.rem(me + offset, dp_count)}, device_id_type=MESH,
        )

    def small_spread():
        small_core.wait()
        small[0:2, :] += small_near[0:2, :]
        for offset in range(1, dp_count):
            small_copy(offset).start()

    def small_finish():
        for offset in range(1, dp_count):
            small_copy(offset).wait()
        total = small[...]
        for offset in range(1, dp_count):
            total = total + small_landed[offset - 1]

        def own_block(values, target):
            count = target.shape[1]
            shift = lax.rem((dp_count - me) * count, count * dp_count)
            return pltpu.roll(values, shift, 1)[: target.shape[0], :count]

        norm_blocks, lambda_block, sub_block = small_blocks[:2], small_blocks[2], small_blocks[3]
        for row in range(2):
            norm_blocks[row][...] = own_block(total, norm_blocks[row][...])
            total = pltpu.roll(total, 7, 0)
        total = pltpu.roll(total, 2, 0)
        part = head_width // 2
        for head in range(head_count):
            at = slice(head * head_width, (head + 1) * head_width)
            sub_block[head : head + 1, :] = own_block(
                jnp.broadcast_to(total[2:3, at], (8, head_width)), sub_block[0:1, :]
            )
            grad = total[3:4, head * head_width : head * head_width + 1]
            param = lambda_param[head : head + 1, :]
            first = grad * first_exp[head : head + 1, :]
            second = grad * second_exp[head : head + 1, :]
            piece = lambda k: param[:, k * part : (k + 1) * part]
            full = jnp.concatenate(
                [first * piece(1), first * piece(0), -second * piece(3), -second * piece(2)], axis=1
            )
            lambda_block[head : head + 1, :] = own_block(
                jnp.broadcast_to(full, (8, 4 * part)), lambda_block[0:1, :]
            )
        out_loads.extend(load(*pair) for pair in zip(small_blocks, small_outs))

    order = {
        0: [flip_two, lambda: exchange(0)],
        2: [lambda: norm_two(0), lambda: exchange(1)],
        3: [lambda: attend(0), lambda: project(0)],
        4: [lambda: norm_two(1), lambda: exchange(0)],
        5: [lambda: attend(1), lambda: project(1)],
        6: [lambda: norm_one(0), lambda: exchange(1)],
        7: [lambda: finish_in(0)],
        8: [lambda: norm_one(1), lambda: exchange(0), small_core.start],
        9: [lambda: finish_in(1), small_spread],
        10: [lambda: add_fed(0), lambda: exchange(1), small_finish],
        11: [lambda: finish_out(0)],
        12: [lambda: add_fed(1)],
        13: [lambda: finish_out(1)],
    }
    stretch = 256 // reducer_width
    tasks = {slot * stretch: items for slot, items in order.items()}
    reducer = Reducer(plan, line_plan, line_starts, line, reducer_refs)
    reducer.compute(0)
    pl.semaphore_wait(barrier, dp_count + 1)
    reducer.pair_copy(0).start()
    for m in range(2):
        sums[m].near_start(part_back[m].at[sent_half])
    reducer.run(tasks)
    wait_all(out_loads)


def back_call(dp_count, lengths, arrays, blocks, shapes):
    depth, row_count, inner, hidden_count, head_count, head_width = shapes
    line = dp_count // 2
    rows = depth // dp_count
    half = row_count // 2
    width = 256 if line <= 4 else 128
    ring = line + 3
    starts = line_first(dp_count)[0]
    wide = (line, rows, width)
    bf16, f32 = jnp.bfloat16, jnp.float32
    dma, regular = pltpu.SemaphoreType.DMA, pltpu.SemaphoreType.REGULAR
    wide_half = pltpu.VMEM((half, depth), f32)
    wide_rows = pltpu.VMEM((row_count, depth), bf16)
    narrow = pltpu.VMEM((row_count, inner), bf16)
    narrow_f32 = pltpu.VMEM((row_count, inner), f32)
    small = pltpu.VMEM((8, depth), f32)
    grad = lambda columns: jax.ShapeDtypeStruct((rows, columns), f32)
    rows_shape = jax.ShapeDtypeStruct((2, row_count, depth), bf16)
    small_shapes = [jax.ShapeDtypeStruct((1, rows), f32)] * 2
    for count in (2 * head_width, head_width):
        small_shapes.append(jax.ShapeDtypeStruct((head_count, count // dp_count), f32))
    flops = 2 * 2 * row_count * depth * (3 * hidden_count + 8 * inner)
    return pl.pallas_call(
        functools.partial(back_kernel, dp_count),
        out_shape=[grad(hidden_count)] * 3
        + [grad(inner)] * 4
        + [rows_shape] * 2
        + small_shapes,
        in_specs=[pl.BlockSpec(memory_space=pltpu.SMEM)] * 2
        + [pl.BlockSpec(memory_space=pl.ANY)] * len(arrays)
        + in_vmem(len(blocks)),
        out_specs=[pl.BlockSpec(memory_space=pl.ANY)] * 13,
        scratch_shapes=[
            pltpu.VMEM((send_slots,) + wide, f32),
            pltpu.VMEM((held_slots,) + wide, f32),
            pltpu.VMEM((ring,) + wide, f32),
            pltpu.VMEM((2, line - 1, 2, rows, width), f32),
            dma((send_slots,)),
            dma((held_slots,)),
            dma((2, line - 1, 2)),
            dma((2, line - 1, 2)),
            regular((2, line - 1)),
            dma((ring, 2)),
        ]
        + (
            [
                pltpu.VMEM((3, line, 2 * rows, 128), f32),
                pltpu.VMEM((2, line - 1, 2, 2 * rows, 128), f32),
                dma((2, line - 1, 2)),
                dma((2, line - 1, 2)),
                regular((2, line - 1)),
                pltpu.VMEM((len(starts), rows, 128), f32),
                dma((len(starts),)),
                dma((len(starts),)),
                dma((3,)),
                pltpu.VMEM((2, 2 * row_count, 128), bf16),
            ]
            if starts
            else []
        )
        + [
            pltpu.VMEM((depth, 2 * row_count), bf16),
            pltpu.VMEM((depth, 2 * row_count), bf16),
            pltpu.VMEM((2, 2 * row_count, width), bf16),
            pltpu.VMEM((2 * row_count, 3 * inner), bf16),
            pltpu.VMEM((inner, depth), bf16),
        ]
        + [pltpu.VMEM((depth, inner), bf16)] * 3
        + [narrow, narrow, narrow, narrow_f32]
        + [narrow_f32, narrow, narrow_f32, narrow_f32]
        + [pltpu.VMEM((head_count, head_width), f32)] * 2
        + [wide_half] * 10
        + [wide_rows] * 3
        + [
            small,
            small,
            pltpu.VMEM((dp_count - 1, 8, depth), f32),
            *[pltpu.VMEM(item.shape, f32) for item in small_shapes],
            pltpu.VMEM((row_count, head_width), f32),
            pltpu.VMEM((row_count, head_width), f32),
            pltpu.VMEM((row_count, 1), jnp.int32),
            pltpu.VMEM((1, row_count), jnp.int32),
            dma((2, 2)),
            dma((2, 2)),
            regular((2,)),
            regular((2,)),
            dma((128,)),
            dma((2,)),
            dma((dp_count - 1,)),
            dma((dp_count - 1,)),
        ],
        compiler_params=pltpu.CompilerParams(
            collective_id=0, has_side_effects=True, vmem_limit_bytes=62 * 1024 * 1024
        ),
        cost_estimate=pl.CostEstimate(flops=flops, bytes_accessed=64 << 20, transcendentals=0),
    )(*lengths, *arrays, *blocks)


def gathers_heads(dp_count):
    return dp_count == 8


class Gather:
    def __init__(self, own, piece, wide, far, near, far_near, full, sems):
        self.own, self.piece, self.wide = own, piece, wide
        self.far, self.near, self.far_near, self.full = far, near, far_near, full
        (
            self.cross_sems, self.line_out, self.line_in, self.pair_out, self.pair_in,
            self.near_sems,
        ) = sems
        self.me = lax.axis_index("dp")
        self.place, self.side = self.me // 2, self.me % 2
        self.line = self.line_out.shape[1] + 1
        self.rows = piece.shape[0]
        tensor = lax.axis_index("tensor")
        self.tensor = tensor
        self.core_peer = tensor + 1 - 2 * (tensor % 2)
        self.far_peer = tensor + 2 - 4 * (tensor // 2)
        self.diagonal = self.far_peer + 1 - 2 * (tensor % 2)

    def slot(self, side, place):
        start = (side * self.line + place) * self.rows
        return self.far.at[pl.ds(pl.multiple_of(start, self.rows), self.rows)]

    def remote(self, source, target, send, recv, device):
        return pltpu.make_async_remote_copy(
            src_ref=source, dst_ref=target, send_sem=send, recv_sem=recv, device_id=device,
            device_id_type=MESH,
        )

    def cross(self):
        return self.remote(
            self.piece, self.slot(self.side, self.place), self.cross_sems.at[0],
            self.cross_sems.at[1], {"tensor": self.far_peer},
        )

    def near_copy(self, index):
        half = self.line * self.rows
        if index == 0:
            source, target = self.wide, self.near
        else:
            start = (self.side if index == 1 else 1 - self.side) * half
            rows = pl.ds(pl.multiple_of(start, self.rows), half)
            source, target = self.far.at[rows], self.far_near.at[rows]
        return self.remote(
            source, target, self.near_sems.at[0, index], self.near_sems.at[1, index],
            {"tensor": self.core_peer},
        )

    def line_copy(self, way, step):
        place = self.place - step if way == 0 else self.place + step
        slot = self.slot(self.side, place)
        return self.remote(
            slot, slot, self.line_out.at[way, step], self.line_in.at[way, step],
            {"dp": self.me + 2 - 4 * way},
        )

    def line_sends(self, way, step):
        if way == 0:
            return (self.place >= step) & (self.place < self.line - 1)
        return (self.place + step <= self.line - 1) & (self.place > 0)

    def line_gets(self, way, step):
        if way == 0:
            return self.place >= step
        return self.place + step <= self.line - 1

    def pair_copy(self, index, place):
        slot = self.slot(self.side, place)
        return self.remote(
            slot, slot, self.pair_out.at[index], self.pair_in.at[index],
            {"dp": self.me + 1 - 2 * self.side},
        )

    def pair_index(self, way, step):
        return 1 + way * (self.line - 1) + step - 1

    def begin(self):
        count = self.own.shape[0]
        rows = pl.ds(pl.multiple_of(self.me * self.rows, self.rows), self.rows)
        self.piece[...] = self.own[rows, :].astype(jnp.float32)
        self.cross().start()

        def widen(rows):
            self.wide[rows, :] = self.own[rows, :].astype(jnp.float32)

        for_rows(count, widen)
        self.near_copy(0).start()

    def forward(self, step):
        if step == 0:
            self.cross().wait()
            self.pair_copy(0, self.place).start()
        for way in range(2):
            if step:

                @pl.when(self.line_gets(way, step))
                def _():
                    self.line_arrival(way, step).wait_recv()
                    place = self.place - step if way == 0 else self.place + step
                    self.pair_copy(self.pair_index(way, step), place).start()

            if step < self.line - 1:

                @pl.when(self.line_sends(way, step))
                def _():
                    self.line_copy(way, step).start()

    def line_arrival(self, way, step):
        place = self.place - step if way == 0 else self.place + step
        slot = self.slot(self.side, place)
        return self.remote(
            slot, slot, self.line_out.at[way, step - 1], self.line_in.at[way, step - 1],
            {"dp": self.me - 2 + 4 * way},
        )

    def store(self, source, tensor, first, count):
        block = self.own.shape[0]

        def narrow(rows):
            at = pl.ds(pl.multiple_of(tensor * block + first + rows.start, row_group), row_group)
            self.full[at, :] = source[rows, :].astype(jnp.bfloat16)

        for_rows(count, narrow)

    def store_far(self, source, tensor):
        for side in range(2):
            for place in range(self.line):
                rows = pl.ds((side * self.line + place) * self.rows, self.rows)
                self.store(source.at[rows], tensor, (2 * place + side) * self.rows, self.rows)

    def finish_line(self):
        self.near_copy(1).start()
        for way in range(2):
            for step in range(self.line - 1):

                @pl.when(self.line_sends(way, step))
                def _():
                    self.line_copy(way, step).wait_send()

        block = self.own.shape[0]
        self.store(self.own, self.tensor, 0, block)
        self.near_copy(0).wait()
        self.store(self.near, self.core_peer, 0, block)

    def finish(self):
        for index in range(1 + 2 * (self.line - 1)):
            if index == 0:
                self.pair_copy(0, self.place).wait()
                continue
            way, step = (index - 1) // (self.line - 1), (index - 1) % (self.line - 1) + 1

            @pl.when(self.line_gets(way, step))
            def _():
                place = self.place - step if way == 0 else self.place + step
                slot = self.slot(1 - self.side, place)
                self.pair_copy(index, place).wait_send()
                self.remote(
                    slot, slot, self.pair_out.at[index], self.pair_in.at[index],
                    {"dp": self.me + 1 - 2 * self.side},
                ).wait_recv()

        self.near_copy(2).start()
        self.store_far(self.far, self.far_peer)
        self.near_copy(1).wait()
        self.near_copy(2).wait()
        self.store_far(self.far_near, self.diagonal)


def front_kernel(dp_count, *refs):
    refs = list(refs)
    take = lambda n: [refs.pop(0) for _ in range(n)]
    lengths = take(2)
    layer_in, cotangent = take(2)
    weights_in = take(7)
    (lambda_param, sub_gain, gain_one, gain_two) = take(4)
    outs = [take(16) for _ in range(2)]
    cosines, sines = take(2), take(2)
    (segment_column, segment_row) = take(2)
    rows_in, cot_rows = take(2), take(2)
    (normed_one, normed_two, flipped) = take(3)
    weights = take(7)
    kept = take(5)
    hidden = take(3)
    (back, fed) = take(2)
    (near_sems, load_sems) = take(2)
    gathers = gathers_heads(dp_count)
    if gathers:
        sets = [take(2) for _ in range(2)]
        heads_wide, heads_landed = take(2), take(2)
        (heads_full, piece, wide, near_weight, full_weight, heads_sems) = take(6)
        gather_sems = take(6)
    else:
        sets = [take(3) for _ in range(2)]
        (projected, far_sems, near_credit) = take(3)
    assert not refs

    tensor = lax.axis_index("tensor")
    core = tensor % 2
    out_weight, gate_weight, up_weight, down_weight = weights[3:]
    row_count, depth = normed_one.shape
    half = row_count // 2
    hidden_count = gate_weight.shape[1]
    used = [0]

    def load(source, target):
        copy = pltpu.make_async_copy(source, target, load_sems.at[used[0]])
        used[0] += 1
        copy.start()
        return copy

    def wait_all(copies):
        for copy in copies:
            copy.wait()
        copies.clear()

    out_weight_load = load(weights_in[3], weights[3])
    rows_loads = [load(layer_in.at[0], rows_in[0])]
    weight_loads = [load(*pair) for pair in zip(weights_in[:3], weights[:3])]
    rows_loads.append(load(layer_in.at[1], rows_in[1]))
    cot_loads = [load(cotangent.at[m], cot_rows[m]) for m in range(2)]
    wide_loads = [load(*pair) for pair in zip(weights_in[4:], weights[4:])]

    sub_scale = sub_gain[...] * (1.0 - lambda_base)
    lam = lambda_terms(lambda_param)[2]
    barrier = pltpu.get_barrier_semaphore()
    core_peer, far_peer = tensor + 1 - 2 * core, tensor + 2 - 4 * (tensor // 2)
    diagonal = far_peer + 1 - 2 * core
    me = lax.axis_index("dp")
    for peer in (core_peer, far_peer, diagonal):
        pl.semaphore_signal(barrier, inc=1, device_id={"tensor": peer}, device_id_type=MESH)
    if gathers:
        for offset in range(1, dp_count):
            target = lax.rem(me + offset, dp_count)
            pl.semaphore_signal(barrier, inc=1, device_id={"dp": target}, device_id_type=MESH)
    pl.semaphore_wait(barrier, dp_count + 2 if gathers else 3)
    if gathers:
        sums = [
            TensorSum(1, *sets[m], None, near_sems.at[m], None, None, None) for m in range(2)
        ]
        for item in sums:
            item.near_left = 1
        gather = Gather(
            weights[3], piece, wide, back, near_weight, fed, full_weight, gather_sems
        )
    else:
        sums = [
            TensorSum(1, *sets[m], near_sems.at[m], far_sems.at[m], near_credit.at[m], None)
            for m in range(2)
        ]
    out_loads, flip_loads, wide_outs, hidden_outs = [], [], [], []

    def mine(rows):
        return pl.ds(pl.multiple_of(core * half + rows.start, row_group), row_group)

    def others(rows):
        return pl.ds(pl.multiple_of((1 - core) * half + rows.start, row_group), row_group)

    def flip_to(source, target):
        wait_all(flip_loads)

        def block(i, carry):
            at = pl.ds(pl.multiple_of(i * 128, 128), 128)
            flipped[at, :] = source[:, at].T
            return carry

        lax.fori_loop(0, depth // 128, block, 0)
        flip_loads.append(load(flipped, target))

    def heads_copy(m, index):
        peer = (core_peer, far_peer, diagonal)[index]
        which = core if index == 1 else 1 - core
        rows = pl.ds(pl.multiple_of(which * half, half), half)
        return pltpu.make_async_remote_copy(
            src_ref=heads_wide[m].at[rows], dst_ref=heads_landed[m].at[index],
            send_sem=heads_sems.at[m, 0, index], recv_sem=heads_sems.at[m, 1, index],
            device_id={"tensor": peer}, device_id_type=MESH,
        )

    def join_heads(m):
        own = sets[m][0]
        inner = kept[4].shape[1]

        def place_of(index):
            return pl.ds(pl.multiple_of(index * inner, inner), inner)

        rows = pl.ds(pl.multiple_of(core * half, half), half)
        heads_full[:, place_of(tensor)] = heads_wide[m][rows, :].astype(jnp.bfloat16)
        for index, peer in enumerate((core_peer, far_peer, diagonal)):
            heads_copy(m, index).wait()
            heads_full[:, place_of(peer)] = heads_landed[m][index].astype(jnp.bfloat16)

        def block(i, carry):
            at = pl.ds(pl.multiple_of(i * 512, 512), 512)
            values = rows_in[m][rows, at].astype(jnp.float32)
            own[:, at] = values + f32_dot(heads_full[...], full_weight[:, at])
            return carry

        lax.fori_loop(0, depth // 512, block, 0)

    def attend(m, between):
        rows_loads[m].wait()
        wait_all(weight_loads)
        wait_all(out_loads)
        segments(lengths[m], segment_column, segment_row)
        out_loads.extend([load(cosines[m], outs[m][14]), load(sines[m], outs[m][15])])
        forward_kernel(
            lam, rows_in[m], gain_one, *weights[:3], cosines[m], sines[m], segment_column,
            segment_row, sub_scale, normed_one, *kept,
            between,
        )
        heads = kept[4]
        if gathers:
            heads_wide[m][...] = heads[...].astype(jnp.float32)
            for index in range(3):
                heads_copy(m, index).start()
            out_loads.extend(load(*pair) for pair in zip(kept, outs[m][3:8]))
            flip_to(normed_one, outs[m][2])
            return

        def part(which, target):
            rows = pl.ds(pl.multiple_of(which * half, half), half)

            def block(i, carry):
                at = pl.ds(pl.multiple_of(i * 512, 512), 512)
                target[:, at] = f32_dot(heads[rows, :], out_weight[:, at])
                return carry

            lax.fori_loop(0, depth // 512, block, 0)

        part(1 - core, projected)
        sums[m].near_start(projected)
        part(core, sets[m][0])
        out_loads.extend(load(*pair) for pair in zip(kept, outs[m][3:8]))
        flip_to(normed_one, outs[m][2])
        sums[m].near_add()

    def norm_rows(values):
        return (values * root_of(values) * gain_two[...]).astype(jnp.bfloat16)

    def join(m):
        own = sets[m][0]
        if gathers:
            join_heads(m)
        else:
            far = sets[m][2]

            def add(rows):
                values = rows_in[m][mine(rows), :].astype(jnp.float32)
                own[rows, :] = values + (own[rows, :] + far[rows, :])

            for_rows(half, add)
        sums[m].near_start(own)
        out_loads.append(load(own, outs[m][8]))

    def norm(m):
        own, near = sets[m][:2]

        def norm_mine(rows):
            normed_two[mine(rows), :] = norm_rows(own[rows, :])

        def norm_others(rows):
            normed_two[others(rows), :] = norm_rows(near[rows, :])

        wait_all(out_loads)
        for_rows(half, norm_mine)
        sums[m].near_wait()
        for_rows(half, norm_others)
        sums[m].near_free()
        out_loads.append(load(normed_two, outs[m][1]))

    def feed(m, between):
        inside, gate_pre, up_pre = hidden
        if m == 0:
            wait_all(wide_loads)
        wait_all(hidden_outs)

        def block(j, carry):
            at = pl.ds(pl.multiple_of(j * 256, 256), 256)
            gate = f32_dot(normed_two[...], gate_weight[:, at])
            upward = f32_dot(normed_two[...], up_weight[:, at])
            grads = dot_t(cot_rows[m][...], down_weight[at, :])
            sigmoid = jax.nn.sigmoid(gate)
            inside[:, at] = (gate * sigmoid * upward).astype(jnp.bfloat16)
            gate_pre[:, at] = (
                grads * upward * sigmoid * (1.0 + gate * (1.0 - sigmoid))
            ).astype(jnp.bfloat16)
            up_pre[:, at] = (grads * gate * sigmoid).astype(jnp.bfloat16)
            return carry

        lax.fori_loop(0, hidden_count // 256, block, 0)
        hidden_outs.extend(load(*pair) for pair in zip(hidden, outs[m][9:12]))
        between()
        wait_all(wide_outs)

        for i in range(depth // 512):
            at = slice(i * 512, (i + 1) * 512)
            back[:, at] = dot_t(gate_pre[...], gate_weight[at, :]) + dot_t(
                up_pre[...], up_weight[at, :]
            )
            fed[:, at] = f32_dot(inside[...], down_weight[:, at])
            wide_outs.append(load(back.at[:, at], outs[m][12].at[:, at]))
            wide_outs.append(load(fed.at[:, at], outs[m][13].at[:, at]))

    def flip_cot(m):
        cot_loads[m].wait()
        flip_to(cot_rows[m], outs[m][0])

    if gathers:
        out_weight_load.wait()
        gather.begin()
        rotary_tables(lengths, cosines, sines, lambda_param.shape[1] // 4)
        attend(0, {1: lambda: gather.forward(0)})
        attend(1, {0: lambda: gather.forward(1)})
        gather.forward(2)
        flip_cot(0)
        flip_cot(1)
        gather.forward(3)
        gather.finish_line()
        gather.finish()
    else:
        out_weight_load.wait()
        rotary_tables(lengths, cosines, sines, lambda_param.shape[1] // 4)
        attend(0, {})
        sums[0].far_go()
        attend(1, {})
        flip_cot(0)
        flip_cot(1)
        sums[0].far_wait()
        sums[1].far_go()
    join(0)
    norm(0)
    if gathers:
        feed(0, lambda: join(1))
    else:
        feed(0, lambda: None)
        sums[1].far_wait()
        join(1)
    norm(1)
    feed(1, lambda: None)
    wait_all(flip_loads)
    wait_all(hidden_outs)
    wait_all(wide_outs)
    wait_all(out_loads)


def front_call(dp_count, lengths, arrays, blocks, shapes):
    depth, row_count, inner, hidden_count, head_count, head_width = shapes
    bf16, f32 = jnp.bfloat16, jnp.float32
    dma, regular = pltpu.SemaphoreType.DMA, pltpu.SemaphoreType.REGULAR
    half = row_count // 2
    out_shape = []
    for m in range(2):
        out_shape += [jax.ShapeDtypeStruct((depth, row_count), bf16)]
        out_shape += [jax.ShapeDtypeStruct((row_count, depth), bf16)]
        out_shape += [jax.ShapeDtypeStruct((depth, row_count), bf16)]
        out_shape += [jax.ShapeDtypeStruct((row_count, inner), bf16)] * 3
        out_shape += [jax.ShapeDtypeStruct((row_count, inner), f32)]
        out_shape += [jax.ShapeDtypeStruct((row_count, inner), bf16)]
        out_shape += [jax.ShapeDtypeStruct((half, depth), f32)]
        out_shape += [jax.ShapeDtypeStruct((row_count, hidden_count), bf16)] * 3
        out_shape += [jax.ShapeDtypeStruct((row_count, depth), f32)] * 2
        out_shape += [jax.ShapeDtypeStruct((row_count, head_width), f32)] * 2
    wide_rows = pltpu.VMEM((row_count, depth), bf16)
    narrow = pltpu.VMEM((row_count, inner), bf16)
    wide_half = pltpu.VMEM((half, depth), f32)
    if gathers_heads(dp_count):
        steps = dp_count // 2 - 1
        extra = [wide_half] * 4
        extra += [pltpu.VMEM((row_count, inner), f32)] * 2
        extra += [pltpu.VMEM((3, half, inner), f32)] * 2
        extra += [
            pltpu.VMEM((half, depth), bf16),
            pltpu.VMEM((inner // dp_count, depth), f32),
            pltpu.VMEM((inner, depth), f32),
            pltpu.VMEM((inner, depth), f32),
            pltpu.VMEM((depth, depth), bf16),
            dma((2, 2, 3)),
            dma((2,)),
            dma((2, steps)),
            dma((2, steps)),
            dma((1 + 2 * steps,)),
            dma((1 + 2 * steps,)),
            dma((2, 3)),
        ]
    else:
        extra = [wide_half] * 7 + [dma((2, 2)), regular((2,))]
    return pl.pallas_call(
        functools.partial(front_kernel, dp_count),
        out_shape=out_shape,
        in_specs=[pl.BlockSpec(memory_space=pltpu.SMEM)] * 2
        + [pl.BlockSpec(memory_space=pl.ANY)] * len(arrays)
        + in_vmem(len(blocks)),
        out_specs=[pl.BlockSpec(memory_space=pl.ANY)] * len(out_shape),
        scratch_shapes=[pltpu.VMEM((row_count, head_width), f32)] * 4
        + [pltpu.VMEM((row_count, 1), jnp.int32), pltpu.VMEM((1, row_count), jnp.int32)]
        + [wide_rows] * 6
        + [pltpu.VMEM((depth, row_count), bf16)]
        + [pltpu.VMEM((depth, inner), bf16)] * 3
        + [pltpu.VMEM((inner, depth), bf16)]
        + [pltpu.VMEM((depth, hidden_count), bf16)] * 2
        + [pltpu.VMEM((hidden_count, depth), bf16)]
        + [narrow, narrow, narrow, pltpu.VMEM((row_count, inner), f32), narrow]
        + [pltpu.VMEM((row_count, hidden_count), bf16)] * 3
        + [pltpu.VMEM((row_count, depth), f32)] * 2
        + [dma((2, 2)), dma((64,))]
        + extra,
        compiler_params=pltpu.CompilerParams(
            collective_id=1, has_side_effects=True, vmem_limit_bytes=62 * 1024 * 1024
        ),
        cost_estimate=pl.CostEstimate(
            flops=4 * row_count * depth * (6 * hidden_count + 4 * inner),
            bytes_accessed=64 << 20,
            transcendentals=0,
        ),
    )(*lengths, *arrays, *blocks)


def on_device(
    layer_in,
    short_lengths,
    long_lengths,
    norm1_gain,
    query_weight,
    key_weight,
    value_weight,
    lambda_param,
    sub_gain,
    out_weight,
    norm2_gain,
    gate_weight,
    up_weight,
    down_weight,
    out_cotangent,
):
    dp_count = lax.axis_size("dp")
    projections = [query_weight, key_weight, value_weight]
    depth, inner = query_weight.shape
    shapes = (depth, layer_in.shape[1], inner, gate_weight.shape[1], *sub_gain.shape)
    lengths = [short_lengths, long_lengths]
    blocks = [lambda_param, sub_gain, norm1_gain[None, :], norm2_gain[None, :]]
    arrays = [layer_in, out_cotangent, *projections, out_weight]
    arrays += [gate_weight, up_weight, down_weight]
    parts = front_call(dp_count, lengths, arrays, blocks, shapes)
    pick = lambda at: [parts[at], parts[at + 16]]
    arrays = pick(0) + pick(1) + pick(2) + pick(9) + pick(10) + pick(11) + pick(7)
    arrays += pick(12) + pick(13) + pick(8)
    arrays += [layer_in, out_cotangent, out_weight, *projections]
    arrays += parts[3:7] + parts[19:23] + parts[14:16] + parts[30:32]
    (
        grad_down, grad_gate, grad_up, grad_out, grad_query, grad_key, grad_value, layer_out,
        grad_in, grad_norm1, grad_norm2, grad_lambda, grad_sub,
    ) = back_call(dp_count, lengths, arrays, blocks, shapes)
    return (
        layer_out,
        grad_in,
        grad_norm1.reshape(-1),
        grad_query,
        grad_key,
        grad_value,
        grad_lambda,
        grad_sub,
        grad_out.T,
        grad_norm2.reshape(-1),
        grad_gate,
        grad_up,
        grad_down.T,
    )


def solution(mesh):
    return jax.shard_map(
        on_device,
        mesh=mesh,
        in_specs=(
            P(None, "dp", None),
            P("dp", None),
            P("dp", None),
            P(),
            P(None, "tensor"),
            P(None, "tensor"),
            P(None, "tensor"),
            P("tensor", None),
            P("tensor", None),
            P("tensor", None),
            P(),
            P(None, "tensor"),
            P(None, "tensor"),
            P("tensor", None),
            P(None, "dp", None),
        ),
        out_specs=(
            P(None, "dp", None),
            P(None, "dp", None),
            P("dp"),
            P("dp", "tensor"),
            P("dp", "tensor"),
            P("dp", "tensor"),
            P("tensor", "dp"),
            P("tensor", "dp"),
            P("tensor", "dp"),
            P("dp"),
            P("dp", "tensor"),
            P("dp", "tensor"),
            P("tensor", "dp"),
        ),
        check_vma=False,
    )
```

```python
import functools
import math

import jax
import jax.numpy as jnp
from jax import lax
from jax.experimental import pallas as pl
from jax.experimental.pallas import tpu as pltpu
from jax.sharding import PartitionSpec as P

norm_epsilon = 1e-05
lambda_base = 0.8 - 0.6 * math.exp(-0.3 * 11.0)
rotary_base = 10000.0
closed_score = -1e30
block_rows = 128
longest_document = 256
row_group = 16
send_slots = 3
held_slots = 4
MESH = pl.DeviceIdType.MESH


def documents(lengths, places):
    end, segment, start = 0, 0, 0
    for k in range(lengths.shape[1]):
        length = lengths[0, k]
        end = end + length
        passed = (places >= end).astype(jnp.int32)
        segment = segment + passed
        start = start + passed * length
    return segment, start


def segments(lengths, column, row):
    column[...] = documents(lengths, lax.broadcasted_iota(jnp.int32, column.shape, 0))[0]
    row[...] = documents(lengths, lax.broadcasted_iota(jnp.int32, row.shape, 1))[0]


def rotary_tables(lengths, cosines, sines, map_width):
    half_width = map_width // 2
    row_count, width = cosines[0].shape
    lane = lax.broadcasted_iota(jnp.int32, (block_rows, width), 1)
    frequency = jnp.zeros((block_rows, width), jnp.float32)
    for k in range(half_width):
        value = rotary_base ** (-2.0 * k / map_width)
        frequency = jnp.where(lane % half_width == k, value, frequency)

    def block(i, carry):
        rows = pl.ds(pl.multiple_of(i * block_rows, block_rows), block_rows)
        places = lax.broadcasted_iota(jnp.int32, (block_rows, width), 0) + i * block_rows
        starts = [documents(item, places)[1] for item in lengths]
        start = jnp.where(lane < half_width, starts[0], starts[1])
        angles = (places - start).astype(jnp.float32) * frequency

        def spread(values, m):
            base = jnp.where(lane // half_width == m, values, 0.0)
            return sum(
                (pltpu.roll(base, k * half_width, 1) for k in range(1, width // half_width)), base
            )

        cosine, sine = jnp.cos(angles), jnp.sin(angles)
        for m in range(2):
            cosines[m][rows, :] = spread(cosine, m)
            signed = spread(sine, m)
            sines[m][rows, :] = jnp.where(lane % map_width < half_width, -signed, signed)
        return carry

    lax.fori_loop(0, row_count // block_rows, block, 0)


def lambda_terms(param):
    width = param.shape[1] // 4
    part = lambda k: param[:, k * width : (k + 1) * width]
    first = jnp.exp(jnp.sum(part(0) * part(1), axis=-1, keepdims=True))
    second = jnp.exp(jnp.sum(part(2) * part(3), axis=-1, keepdims=True))
    return first, second, first - second + lambda_base


def turn(values, cosine, sine):
    width = values.shape[-1]
    quarter = width // 4
    lane = lax.broadcasted_iota(jnp.int32, values.shape, 1)
    partner = jnp.where(
        lane % (2 * quarter) < quarter,
        pltpu.roll(values, width - quarter, 1),
        pltpu.roll(values, quarter, 1),
    )
    return values * cosine + partner * sine


def map_of(values, which):
    lane = lax.broadcasted_iota(jnp.int32, values.shape, 1)
    mine = (lane >= values.shape[-1] // 2) == (which == 1)
    return jnp.where(mine, values, jnp.zeros_like(values))


def key_range(block):
    first = max(0, block * block_rows - longest_document + 1) // block_rows * block_rows
    return first, (block + 1) * block_rows


def open_pairs(block, segment_column, segment_row):
    first, last = key_range(block)
    rows = pl.ds(block * block_rows, block_rows)
    shape = (block_rows, last - first)
    row_at = lax.broadcasted_iota(jnp.int32, shape, 0) + block * block_rows
    key_at = lax.broadcasted_iota(jnp.int32, shape, 1) + first
    return (segment_column[rows, :] == segment_row[:, first:last]) & (key_at <= row_at)


def softmax_map(query, key, opened, scale):
    scores = jnp.where(opened, dot_t(query, key) * scale, closed_score)
    expanded = jnp.exp(scores - jnp.max(scores, axis=-1, keepdims=True))
    return expanded * (1.0 / jnp.sum(expanded, axis=-1, keepdims=True))


def f32_dot(left, right):
    return jnp.dot(left, right, preferred_element_type=jnp.float32)


def dot_t(left, right):
    return lax.dot_general(
        left, right, (((1,), (1,)), ((), ())), preferred_element_type=jnp.float32
    )


def dot_rows(left, right):
    return lax.dot_general(
        left, right, (((0,), (0,)), ((), ())), preferred_element_type=jnp.float32
    )


def rms_back(incoming, values, inverse_root):
    return inverse_root * incoming - values * inverse_root**3 * jnp.mean(
        incoming * values, axis=-1, keepdims=True
    )


def root_of(values):
    return lax.rsqrt(jnp.mean(values * values, axis=-1, keepdims=True) + norm_epsilon)


def forward_kernel(
    lam, rows, gain, query_weight, key_weight, value_weight, cosine, sine, segment_column,
    segment_row, sub_scale, normed_one, query, key, value, mixed, heads_out, between,
):
    head_count, width = sub_scale.shape
    scale = (width // 2) ** (-0.5)
    values = rows[...].astype(jnp.float32)
    normed_one[...] = (values * root_of(values) * gain[...]).astype(jnp.bfloat16)
    raw_query = f32_dot(normed_one[...], query_weight[...])
    raw_key = f32_dot(normed_one[...], key_weight[...])
    value[...] = f32_dot(normed_one[...], value_weight[...]).astype(jnp.bfloat16)
    for head in range(head_count):
        at = slice(head * width, (head + 1) * width)
        query[:, at] = turn(raw_query[:, at], cosine[...], sine[...]).astype(jnp.bfloat16)
        key[:, at] = turn(raw_key[:, at], cosine[...], sine[...]).astype(jnp.bfloat16)
    for block in range(rows.shape[0] // block_rows):
        first, last = key_range(block)
        here = slice(block * block_rows, last)
        opened = open_pairs(block, segment_column, segment_row)
        if block in between:
            between[block]()
        for head in range(head_count):
            at = slice(head * width, (head + 1) * width)
            keys = key[first:last, at]
            maps = [softmax_map(map_of(query[here, at], c), keys, opened, scale) for c in range(2)]
            combined = (maps[0] - lam[head : head + 1, :] * maps[1]).astype(jnp.bfloat16)
            out = f32_dot(combined, value[first:last, at])
            mixed[here, at] = out
            heads_out[here, at] = (out * root_of(out) * sub_scale[head : head + 1, :]).astype(
                jnp.bfloat16
            )


def backward_kernel(
    lam, grad_attended, out_weight, query, key, value, mixed, cosine, sine, segment_column,
    segment_row, sub_scale, grad_rows, grad_sub, grad_lam, grad_heads, grad_mixed, grad_key,
    grad_value,
):
    head_count, width = sub_scale.shape
    row_count = query.shape[0]
    inner = head_count * width
    scale = (width // 2) ** (-0.5)
    grad_heads[...] = dot_t(grad_attended[...], out_weight[...])
    for head in range(head_count):
        at = slice(head * width, (head + 1) * width)
        heads = mixed[:, at]
        root = root_of(heads)
        grads = grad_heads[:, at]
        grad_sub[head : head + 1, :] = jnp.sum(grads * heads * root, axis=0, keepdims=True) * (
            1.0 - lambda_base
        )
        grad_mixed[:, at] = rms_back(grads * sub_scale[head : head + 1, :], heads, root).astype(
            jnp.bfloat16
        )
    grad_key[...] = jnp.zeros_like(grad_key)
    grad_value[...] = jnp.zeros_like(grad_value)
    lam_sums = [0.0] * head_count
    for block in range(row_count // block_rows):
        first, last = key_range(block)
        here = slice(block * block_rows, last)
        opened = open_pairs(block, segment_column, segment_row)
        for head in range(head_count):
            at = slice(head * width, (head + 1) * width)
            keys = key[first:last, at]
            queries = [map_of(query[here, at], c) for c in range(2)]
            maps = [softmax_map(queries[c], keys, opened, scale) for c in range(2)]
            mixes = grad_mixed[here, at]
            combined = (maps[0] - lam[head : head + 1, :] * maps[1]).astype(jnp.bfloat16)
            grad_value[first:last, at] += dot_rows(combined, mixes)
            grads = dot_t(mixes, value[first:last, at])
            first_sum = jnp.sum(grads * maps[0], axis=-1, keepdims=True)
            second_sum = jnp.sum(grads * maps[1], axis=-1, keepdims=True)
            lam_sums[head] = lam_sums[head] + jnp.sum(second_sum, axis=0, keepdims=True)
            score_grads = [
                (maps[0] * (grads - first_sum)).astype(jnp.bfloat16),
                (maps[1] * (-lam[head : head + 1, :] * (grads - second_sum))).astype(jnp.bfloat16),
            ]
            grad_query = f32_dot(score_grads[0], map_of(keys, 0)) + f32_dot(
                score_grads[1], map_of(keys, 1)
            )
            grad_rows[here, at] = turn(
                grad_query * scale, cosine[here, :], -sine[here, :]
            ).astype(jnp.bfloat16)
            grad_key[first:last, at] += dot_rows(score_grads[0], queries[0]) + dot_rows(
                score_grads[1], queries[1]
            )
    for head in range(head_count):
        at = slice(head * width, (head + 1) * width)
        grad_rows[:, inner + head * width : inner + (head + 1) * width] = turn(
            grad_key[:, at] * scale, cosine[...], -sine[...]
        ).astype(jnp.bfloat16)
        grad_lam[head : head + 1, :] = jnp.broadcast_to(-lam_sums[head], (1, width))
    grad_rows[:, 2 * inner :] = grad_value[...].astype(jnp.bfloat16)


def in_vmem(count):
    return [pl.BlockSpec(memory_space=pltpu.VMEM)] * count


class Line:
    def __init__(self, line, widths, total, landed, line_out, line_in, credit):
        self.line, self.widths = line, widths
        self.total, self.landed = total, landed
        self.line_out, self.line_in, self.credit = line_out, line_in, credit
        self.me = lax.axis_index("dp")
        self.place = self.me // 2
        self.ring = total.shape[0]

    def copy(self, c, step, way, block, target):
        width = self.widths[c]
        return pltpu.make_async_remote_copy(
            src_ref=self.total.at[c % self.ring, block, :, :width],
            dst_ref=self.landed.at[way, step, c % 2, :, :width],
            send_sem=self.line_out.at[way, step, c % 2],
            recv_sem=self.line_in.at[way, step, c % 2],
            device_id={"dp": target},
            device_id_type=MESH,
        )

    def sends(self, step, way):
        place, line = self.place, self.line
        if way == 0:
            block = line - 1 - step + place
            return (place <= step) & (place < line - 1), block, self.me + 2
        block = place + step - line + 1
        return (place >= line - 1 - step) & (place > 0), block, self.me - 2

    def gets(self, step, way):
        place, line = self.place, self.line
        if way == 0:
            return (place > 0) & (place - 1 <= step), line - 2 - step + place, self.me - 2
        gets = (place < line - 1) & (place + 1 >= line - 1 - step)
        return gets, place + step - line + 2, self.me + 2

    def start(self, c, step):
        for way in range(2):
            sends, block, target = self.sends(step, way)

            @pl.when(sends)
            def _():
                if c >= 2:
                    pl.semaphore_wait(self.credit.at[way, step], 1)
                self.copy(c, step, way, block, target).start()

    def finish(self, c, step):
        width = self.widths[c]
        for way in range(2):
            gets, block, source = self.gets(step, way)

            @pl.when(gets)
            def _():
                self.copy(c, step, way, block, source).wait_recv()
                self.total[c % self.ring, block, :, :width] += self.landed[
                    way, step, c % 2, :, :width
                ]
                if c + 2 < len(self.widths):
                    pl.semaphore_signal(
                        self.credit.at[way, step],
                        inc=1,
                        device_id={"dp": source},
                        device_id_type=MESH,
                    )

            sends, sent, target = self.sends(step, way)

            @pl.when(sends)
            def _():
                self.copy(c, step, way, sent, target).wait_send()


class Reducer:
    def __init__(self, plan, line_plan, line_starts, line, refs):
        self.plan, self.line_plan, self.line_starts = plan, line_plan, line_starts
        self.line = line
        (
            self.send, self.held, self.total, landed, self.pair_out, self.pair_in,
            line_out, line_in, credit, self.out_sem,
        ) = refs[:10]
        self.first = Line(
            line, [item.width for item in plan], self.total, landed, line_out, line_in, credit
        )
        self.place = self.first.place
        self.me = self.first.me
        self.side = self.me % 2
        self.other = self.me + 1 - 2 * self.side
        self.steps = line - 1
        self.ring = self.total.shape[0]
        self.rows = self.total.shape[2]
        if line_plan:
            (
                self.line_total, landed, line_out, line_in, credit, self.last_held,
                self.last_out, self.last_in, self.line_out_sem,
            ) = refs[10:]
            self.second = Line(
                line, [item.width for item in line_plan], self.line_total, landed, line_out,
                line_in, credit,
            )

    def compute(self, c):
        item = self.plan[c]
        width = item.width
        left, right = item.left(), item.right()

        def block(at, carry):
            first = pl.multiple_of(2 * at * self.rows, self.rows)
            columns = right[...]
            away = left[pl.ds(first + (1 - self.side) * self.rows, self.rows), :]
            here = left[pl.ds(first + self.side * self.rows, self.rows), :]
            self.send[c % send_slots, at, :, :width] = f32_dot(away, columns)
            self.total[c % self.ring, at, :, :width] = f32_dot(here, columns)
            return carry

        lax.fori_loop(0, self.line, block, 0)
        item.computed()

    def line_compute(self, c):
        item = self.line_plan[c]
        left, right = item.left(), item.right()
        slot = c % self.line_total.shape[0]
        if c >= self.line_total.shape[0]:
            self.line_result(c - self.line_total.shape[0]).wait()

        def block(at, carry):
            rows = pl.ds(pl.multiple_of(2 * at * self.rows, 2 * self.rows), 2 * self.rows)
            self.line_total[slot, at] = f32_dot(left[rows, :], right[...])
            return carry

        lax.fori_loop(0, self.line, block, 0)
        item.computed()

    def side_rows(self, side):
        return pl.ds(pl.multiple_of(side * self.rows, self.rows), self.rows)

    def last_copy(self, c):
        slot = c % self.line_total.shape[0]
        return pltpu.make_async_remote_copy(
            src_ref=self.line_total.at[slot, self.place, self.side_rows(1 - self.side), :],
            dst_ref=self.last_held.at[c],
            send_sem=self.last_out.at[c],
            recv_sem=self.last_in.at[c],
            device_id={"dp": self.other},
            device_id_type=MESH,
        )

    def line_result(self, c):
        item = self.line_plan[c]
        slot = c % self.line_total.shape[0]
        return pltpu.make_async_copy(
            self.line_total.at[slot, self.place, self.side_rows(self.side), :],
            item.out.at[:, item.first : item.first + item.width],
            self.line_out_sem.at[slot],
        )

    def line_step(self, slot):
        for c, start in enumerate(self.line_starts):
            step = slot - start
            if 0 < step <= self.steps:
                self.second.finish(c, step - 1)
            if step == self.steps + 1:
                self.last_copy(c).wait()
                at = c % self.line_total.shape[0]
                self.line_total[at, self.place, self.side_rows(self.side), :] += self.last_held[c]
                self.line_result(c).start()
            if 0 <= step < self.steps and slot:
                self.second.start(c, step)
            if step == self.steps:
                self.last_copy(c).start()

    def pair_copy(self, c):
        width = self.plan[c].width
        return pltpu.make_async_remote_copy(
            src_ref=self.send.at[c % send_slots, :, :, :width],
            dst_ref=self.held.at[c % held_slots, :, :, :width],
            send_sem=self.pair_out.at[c % send_slots],
            recv_sem=self.pair_in.at[c % held_slots],
            device_id={"dp": self.other},
            device_id_type=MESH,
        )

    def pair_finish(self, c):
        width = self.plan[c].width
        self.pair_copy(c).wait_recv()

        def block(at, carry):
            self.total[c % self.ring, at, :, :width] += self.held[c % held_slots, at, :, :width]
            return carry

        lax.fori_loop(0, self.line, block, 0)
        self.pair_copy(c).wait_send()

    def out_copies(self, c):
        item = self.plan[c]
        outs = item.out if isinstance(item.out, list) else [item.out]
        size = outs[0].shape[1]
        first, last = item.first, item.first + item.width
        while first < last:
            count = min(last, (first // size + 1) * size) - first
            at = first - item.first
            yield pltpu.make_async_copy(
                self.total.at[c % self.ring, self.place, :, at : at + count],
                outs[first // size].at[:, first % size : first % size + count],
                self.out_sem.at[c % self.ring, at // 128],
            )
            first += count

    def out_start(self, c):
        for copy in self.out_copies(c):
            copy.start()

    def out_wait(self, c):
        for copy in self.out_copies(c):
            copy.wait()

    def run(self, tasks):
        count, steps = len(self.plan), self.steps
        begun = [c for c, start in enumerate(self.line_starts) if start == 0]
        for c in begun:
            self.line_compute(c)
        for c in begun:
            self.second.start(c, 0)
        self.compute(1)
        for slot in range(count + steps + 1):
            for step in reversed(range(steps)):
                c = slot - 2 - step
                if 0 <= c < count:
                    self.first.finish(c, step)
                    if step + 1 < steps:
                        self.first.start(c, step + 1)
            self.line_step(slot)
            if 0 <= slot - 1 < count:
                self.pair_finish(slot - 1)
                self.first.start(slot - 1, 0)
            if slot + 1 < count:
                self.pair_copy(slot + 1).start()
            done = slot - 1 - steps
            if 0 <= done < count:
                self.out_start(done)
            if slot + 2 < count:
                if slot + 2 >= self.ring:
                    self.out_wait(slot + 2 - self.ring)
                self.compute(slot + 2)
            for c, start in enumerate(self.line_starts):
                if slot and start == slot + 1:
                    self.line_compute(c)
            for task in tasks.get(slot, ()):
                task()
        for c in range(max(0, count - self.ring), count):
            self.out_wait(c)
        if self.line_plan:
            for c in range(len(self.line_plan) - self.line_total.shape[0], len(self.line_plan)):
                self.line_result(c).wait()


class Chunk:
    def __init__(self, left, right, computed, out, first, width):
        self.left, self.right, self.computed = left, right, computed
        self.out, self.first, self.width = out, first, width


def for_rows(count, body):
    def step(i, carry):
        body(pl.ds(pl.multiple_of(i * row_group, row_group), row_group))
        return carry

    lax.fori_loop(0, count // row_group, step, 0)


class TensorSum:
    def __init__(self, uses, own, near, far, near_sems, far_sems, near_credit, far_credit):
        self.own, self.near, self.far = own, near, far
        self.near_sems, self.far_sems = near_sems, far_sems
        self.near_credit, self.far_credit = near_credit, far_credit
        index = lax.axis_index("tensor")
        self.core_peer = index + 1 - 2 * (index % 2)
        self.far_peer = index + 2 - 4 * (index // 2)
        self.near_left, self.far_left = 2 * uses, uses
        self.near_first, self.far_first = True, True

    def near_copy(self, source):
        return pltpu.make_async_remote_copy(
            src_ref=source, dst_ref=self.near, send_sem=self.near_sems.at[0],
            recv_sem=self.near_sems.at[1], device_id={"tensor": self.core_peer},
            device_id_type=MESH,
        )

    def far_copy(self):
        return pltpu.make_async_remote_copy(
            src_ref=self.own, dst_ref=self.far, send_sem=self.far_sems.at[0],
            recv_sem=self.far_sems.at[1], device_id={"tensor": self.far_peer},
            device_id_type=MESH,
        )

    def near_start(self, source):
        if not self.near_first:
            pl.semaphore_wait(self.near_credit, 1)
        self.near_first = False
        self.pending = source
        self.near_copy(source).start()

    def near_wait(self):
        self.near_copy(self.pending).wait()

    def near_free(self):
        self.near_left -= 1
        if self.near_left:
            pl.semaphore_signal(
                self.near_credit, inc=1, device_id={"tensor": self.core_peer}, device_id_type=MESH
            )

    def near_add(self):
        self.near_wait()

        def add(rows):
            self.own[rows, :] += self.near[rows, :]

        for_rows(self.own.shape[0], add)
        self.near_free()

    def far_go(self):
        if not self.far_first:
            pl.semaphore_wait(self.far_credit, 1)
        self.far_first = False
        self.far_copy().start()

    def far_wait(self):
        self.far_copy().wait()

    def far_free(self):
        self.far_left -= 1
        if self.far_left:
            pl.semaphore_signal(
                self.far_credit, inc=1, device_id={"tensor": self.far_peer}, device_id_type=MESH
            )


def line_first(dp_count):
    return ((0, 0, 3, 6, 9, 12), (2, 2, 2)) if dp_count == 8 else ((), (0, 0, 0))


def back_kernel(dp_count, *refs):
    refs = list(refs)
    take = lambda n: [refs.pop(0) for _ in range(n)]
    lengths = take(2)
    cot_left, two_left, one_left = [take(2) for _ in range(3)]
    hidden, gate_pre, up_pre, heads = [take(2) for _ in range(4)]
    part_back, part_fed, middle = [take(2) for _ in range(3)]
    (layer_in, cotangent) = take(2)
    weights_in = take(4)
    kept_in = [take(4) for _ in range(2)]
    tables_in = [take(2) for _ in range(2)]
    (lambda_param, sub_gain, gain_one, gain_two) = take(4)
    (grad_down, grad_gate, grad_up, grad_out) = take(4)
    grad_qkv = take(3)
    (layer_out, grad_in) = take(2)
    small_outs = take(4)
    reducer_refs = take(20 if line_first(dp_count)[0] else 10)
    line_rights = reducer_refs.pop() if line_first(dp_count)[0] else None
    (left_a, left_b, rights, rows_qkv) = take(4)
    weights = take(4)
    kept = take(4)
    backward_scratch = take(4)
    (grad_sub, grad_lam) = take(2)
    sets = [take(3) for _ in range(2)]
    through = take(2)
    (spare, projected, attended, rows_in, rows_out) = take(5)
    (small, small_near, small_landed) = take(3)
    small_blocks = take(4)
    tables = take(4)
    (near_sems, far_sems, near_credit, far_credit) = take(4)
    (load_sems, small_near_sems, small_send, small_recv) = take(4)
    assert not refs

    me = lax.axis_index("dp")
    tensor = lax.axis_index("tensor")
    core = tensor % 2
    core_peer = tensor + 1 - 2 * core
    far_peer = tensor + 2 - 4 * (tensor // 2)
    line = dp_count // 2
    half = middle[0].shape[0]
    row_count = 2 * half
    head_count, head_width = sub_gain.shape
    sub_scale = sub_gain[...] * (1.0 - lambda_base)
    first_exp, second_exp, lam = lambda_terms(lambda_param)
    out_weight, projections = weights[0], weights[1:]
    inner = out_weight.shape[0]
    kept_half = pl.ds(pl.multiple_of(core * half, half), half)
    sent_half = pl.ds(pl.multiple_of((1 - core) * half, half), half)
    tokens = [slice(m * row_count, (m + 1) * row_count) for m in range(2)]

    barrier = pltpu.get_barrier_semaphore()
    for offset in range(1, dp_count):
        pl.semaphore_signal(
            barrier, inc=1, device_id={"dp": lax.rem(me + offset, dp_count)}, device_id_type=MESH
        )
    for peer in (core_peer, far_peer):
        pl.semaphore_signal(barrier, inc=1, device_id={"tensor": peer}, device_id_type=MESH)

    used = [0]

    def load(source, target):
        copy = pltpu.make_async_copy(source, target, load_sems.at[used[0]])
        used[0] += 1
        copy.start()
        return copy

    def wait_all(copies):
        for copy in copies:
            copy.wait()

    reducer_width = reducer_refs[0].shape[-1]
    plan, sources, left_loads, right_loads = [], {}, {}, {}

    def load_left(sources_of, left):
        return [load(sources_of[m], left.at[:, tokens[m]]) for m in range(2)]

    def load_columns(source, first, width, target):
        return [
            load(source[m].at[:, first : first + width], target.at[tokens[m], :width])
            for m in range(2)
        ]

    def load_right(c):
        if c in sources:
            right_loads[c] = load_columns(*sources[c], rights.at[c % 2])

    def load_line_right(c):
        if c < len(line_sources):
            line_loads[c] = load_columns(*line_sources[c], line_rights.at[c % 2])

    def get_left(c, left):
        wait_all(left_loads.pop(c, ()))
        return left

    def get_line_left(left):
        return left

    def get_right(c, first, width):
        if c in sources:
            wait_all(right_loads[c])
            return rights.at[c % 2, :, :width]
        return rows_qkv.at[:, first : first + width]

    def get_line_right(c):
        wait_all(line_loads[c])
        return line_rights.at[c % 2]

    def computed(c):
        load_right(c + 2)
        if c == last_two:
            left_loads[first_one] = load_left(one_left, left_b)

    def add_group(left, source, columns, out, line_chunks=0):
        start = line_chunks * line_width
        for first in range(0, start, line_width):
            c = len(line_plan)
            line_sources.append((source, first, line_width))
            line_plan.append(
                Chunk(
                    functools.partial(get_line_left, left),
                    functools.partial(get_line_right, c),
                    functools.partial(load_line_right, c + 2),
                    out,
                    first,
                    line_width,
                )
            )
        for first in range(start, columns, reducer_width):
            width = min(reducer_width, columns - first)
            c = len(plan)
            if source is not None:
                sources[c] = (source, first, width)
            plan.append(
                Chunk(
                    functools.partial(get_left, c, left),
                    functools.partial(get_right, c, first, width),
                    functools.partial(computed, c),
                    out,
                    first,
                    width,
                )
            )

    line_starts, line_counts = line_first(dp_count)
    line_plan, line_sources, line_loads, line_width = [], [], {}, 128
    add_group(left_a, hidden, hidden[0].shape[1], grad_down, line_counts[0])
    add_group(left_b, gate_pre, gate_pre[0].shape[1], grad_gate, line_counts[1])
    add_group(left_b, up_pre, up_pre[0].shape[1], grad_up)
    last_two = len(plan) - 1
    add_group(left_a, heads, inner, grad_out, line_counts[2])
    first_one = len(plan)
    add_group(left_b, None, 3 * inner, grad_qkv)

    left_loads[0] = load_left(cot_left, left_a)
    load_right(0)
    two_loads = [load(two_left[m], (attended, rows_out)[m]) for m in range(2)]
    load_line_right(0)
    load_line_right(1)
    load_right(1)
    sums = [
        TensorSum(
            3, *sets[m], near_sems.at[m], far_sems.at[m], near_credit.at[m], far_credit.at[m]
        )
        for m in range(2)
    ]
    own_loads = {m: load(part_back[m].at[kept_half], sets[m][0]) for m in range(2)}
    weight_loads = [load(*pair) for pair in zip(weights_in, weights)]
    def load_kept(m):
        pairs = zip([*kept_in[m], *tables_in[m]], [*kept, *tables[:2]])
        return [load(*pair) for pair in pairs]

    kept_loads = load_kept(0)
    spare_queue = [middle[0], middle[1], middle[0], middle[1]]
    rows_queue = [cotangent.at[0], cotangent.at[1]]
    rows_queue += [layer_in.at[0], cotangent.at[0], layer_in.at[1], cotangent.at[1]]
    queued = {}

    def next_spare():
        queued["spare"] = load(spare_queue.pop(0), spare) if spare_queue else None

    def next_rows():
        queued["rows"] = load(rows_queue.pop(0), rows_in) if rows_queue else None

    next_spare()
    next_rows()
    out_loads = []
    small[...] = jnp.zeros_like(small)

    def mine(rows):
        return pl.ds(pl.multiple_of(core * half + rows.start, row_group), row_group)

    def others(rows):
        return pl.ds(pl.multiple_of((1 - core) * half + rows.start, row_group), row_group)

    def flip_rows(source, left, m):
        def block(i, carry):
            at = pl.ds(pl.multiple_of(i * 128, 128), 128)
            left[at, tokens[m]] = source[:, at].T
            return carry

        lax.fori_loop(0, source.shape[1] // 128, block, 0)

    def flip_two():
        wait_all(two_loads)
        for m in range(2):
            flip_rows((attended, rows_out)[m], left_b, m)

    def exchange(m):
        if m in own_loads:
            own_loads.pop(m).wait()
        sums[m].near_add()
        sums[m].far_go()

    def norm_two(m):
        own, near, far = sets[m]
        queued["spare"].wait()
        sums[m].far_wait()

        def body(rows):
            grads = own[rows, :] + far[rows, :]
            values = spare[rows, :]
            root = root_of(values)
            small[1:2, :] += jnp.sum(grads * values * root, axis=0, keepdims=True)
            through[m][rows, :] = rms_back(grads * gain_two[...], values, root)

        for_rows(half, body)
        sums[m].far_free()
        sums[m].near_start(through[m])
        next_spare()

    def attend(m):
        near = sets[m][1]
        queued["rows"].wait()
        sums[m].near_wait()

        def body(rows):
            attended[mine(rows), :] = (
                rows_in[mine(rows), :].astype(jnp.float32) + through[m][rows, :]
            ).astype(jnp.bfloat16)
            attended[others(rows), :] = (
                rows_in[others(rows), :].astype(jnp.float32) + near[rows, :]
            ).astype(jnp.bfloat16)

        for_rows(half, body)
        sums[m].near_free()
        next_rows()

        flip_rows(attended, left_a, m)
        if m == 0:
            wait_all(weight_loads)
        wait_all(kept_loads)
        segments(lengths[m], *tables[2:])
        backward_kernel(
            lam, attended, out_weight, *kept, *tables, sub_scale,
            rows_qkv.at[tokens[m], :], grad_sub, grad_lam, *backward_scratch,
        )
        if m == 0:
            kept_loads[:] = load_kept(1)
        for head in range(head_count):
            at = slice(head * head_width, (head + 1) * head_width)
            small[2:3, at] += grad_sub[head : head + 1, :]
            small[3:4, at] += grad_lam[head : head + 1, :]

    def project(m):
        def part(which, target):
            rows = pl.ds(pl.multiple_of(m * row_count + which * half, half), half)

            def block(i, carry):
                at = pl.ds(pl.multiple_of(i * 512, 512), 512)
                total = 0.0
                for p in range(3):
                    grads = rows_qkv[rows, p * inner : (p + 1) * inner]
                    total = total + dot_t(grads, projections[p][at, :])
                target[:, at] = total
                return carry

            lax.fori_loop(0, target.shape[1] // 512, block, 0)

        part(1 - core, projected)
        sums[m].near_start(projected)
        part(core, sets[m][0])

    def norm_one(m):
        own, near, far = sets[m]
        queued["rows"].wait()
        sums[m].far_wait()

        def body(rows):
            grads = own[rows, :] + far[rows, :]
            values = rows_in[mine(rows), :].astype(jnp.float32)
            root = root_of(values)
            small[0:1, :] += jnp.sum(grads * values * root, axis=0, keepdims=True)
            through[m][rows, :] += rms_back(grads * gain_one[...], values, root)

        for_rows(half, body)
        sums[m].far_free()
        sums[m].near_start(through[m])
        next_rows()
        own_loads[m] = load(part_fed[m].at[kept_half], own)

    def store_rows(target):
        out_loads.append(load(rows_out, target))

    def finish_in(m):
        near = sets[m][1]
        queued["rows"].wait()
        sums[m].near_wait()
        wait_all(out_loads)
        out_loads.clear()

        def body(rows):
            rows_out[mine(rows), :] = (
                rows_in[mine(rows), :].astype(jnp.float32) + through[m][rows, :]
            ).astype(jnp.bfloat16)
            rows_out[others(rows), :] = (
                rows_in[others(rows), :].astype(jnp.float32) + near[rows, :]
            ).astype(jnp.bfloat16)

        for_rows(half, body)
        sums[m].near_free()
        next_rows()
        store_rows(grad_in.at[m])
        sums[m].near_start(part_fed[m].at[sent_half])

    def add_fed(m):
        own, near, far = sets[m]
        queued["spare"].wait()
        sums[m].far_wait()

        def body(rows):
            own[rows, :] = spare[rows, :] + (own[rows, :] + far[rows, :])

        for_rows(half, body)
        sums[m].far_free()
        sums[m].near_start(own)
        next_spare()

    def finish_out(m):
        own, near = sets[m][:2]
        sums[m].near_wait()
        wait_all(out_loads)
        out_loads.clear()

        def body(rows):
            rows_out[mine(rows), :] = own[rows, :].astype(jnp.bfloat16)
            rows_out[others(rows), :] = near[rows, :].astype(jnp.bfloat16)

        for_rows(half, body)
        sums[m].near_free()
        store_rows(layer_out.at[m])

    small_core = pltpu.make_async_remote_copy(
        src_ref=small, dst_ref=small_near, send_sem=small_near_sems.at[0],
        recv_sem=small_near_sems.at[1], device_id={"tensor": core_peer}, device_id_type=MESH,
    )

    def small_copy(offset):
        return pltpu.make_async_remote_copy(
            src_ref=small, dst_ref=small_landed.at[offset - 1], send_sem=small_send.at[offset - 1],
            recv_sem=small_recv.at[offset - 1],
            device_id={"dp": lax.rem(me + offset, dp_count)}, device_id_type=MESH,
        )

    def small_spread():
        small_core.wait()
        small[0:2, :] += small_near[0:2, :]
        for offset in range(1, dp_count):
            small_copy(offset).start()

    def small_finish():
        for offset in range(1, dp_count):
            small_copy(offset).wait()
        total = small[...]
        for offset in range(1, dp_count):
            total = total + small_landed[offset - 1]

        def own_block(values, target):
            count = target.shape[1]
            shift = lax.rem((dp_count - me) * count, count * dp_count)
            return pltpu.roll(values, shift, 1)[: target.shape[0], :count]

        norm_blocks, lambda_block, sub_block = small_blocks[:2], small_blocks[2], small_blocks[3]
        for row in range(2):
            norm_blocks[row][...] = own_block(total, norm_blocks[row][...])
            total = pltpu.roll(total, 7, 0)
        total = pltpu.roll(total, 2, 0)
        part = head_width // 2
        for head in range(head_count):
            at = slice(head * head_width, (head + 1) * head_width)
            sub_block[head : head + 1, :] = own_block(
                jnp.broadcast_to(total[2:3, at], (8, head_width)), sub_block[0:1, :]
            )
            grad = total[3:4, head * head_width : head * head_width + 1]
            param = lambda_param[head : head + 1, :]
            first = grad * first_exp[head : head + 1, :]
            second = grad * second_exp[head : head + 1, :]
            piece = lambda k: param[:, k * part : (k + 1) * part]
            full = jnp.concatenate(
                [first * piece(1), first * piece(0), -second * piece(3), -second * piece(2)], axis=1
            )
            lambda_block[head : head + 1, :] = own_block(
                jnp.broadcast_to(full, (8, 4 * part)), lambda_block[0:1, :]
            )
        out_loads.extend(load(*pair) for pair in zip(small_blocks, small_outs))

    order = {
        0: [flip_two, lambda: exchange(0)],
        2: [lambda: norm_two(0), lambda: exchange(1)],
        3: [lambda: attend(0), lambda: project(0)],
        4: [lambda: norm_two(1), lambda: exchange(0)],
        5: [lambda: attend(1), lambda: project(1)],
        6: [lambda: norm_one(0), lambda: exchange(1)],
        7: [lambda: finish_in(0)],
        8: [lambda: norm_one(1), lambda: exchange(0), small_core.start],
        9: [lambda: finish_in(1), small_spread],
        10: [lambda: add_fed(0), lambda: exchange(1), small_finish],
        11: [lambda: finish_out(0)],
        12: [lambda: add_fed(1)],
        13: [lambda: finish_out(1)],
    }
    stretch = 256 // reducer_width
    tasks = {slot * stretch: items for slot, items in order.items()}
    reducer = Reducer(plan, line_plan, line_starts, line, reducer_refs)
    reducer.compute(0)
    pl.semaphore_wait(barrier, dp_count + 1)
    reducer.pair_copy(0).start()
    for m in range(2):
        sums[m].near_start(part_back[m].at[sent_half])
    reducer.run(tasks)
    wait_all(out_loads)


def back_call(dp_count, lengths, arrays, blocks, shapes):
    depth, row_count, inner, hidden_count, head_count, head_width = shapes
    line = dp_count // 2
    rows = depth // dp_count
    half = row_count // 2
    width = 256 if line <= 4 else 128
    ring = line + 3
    starts = line_first(dp_count)[0]
    wide = (line, rows, width)
    bf16, f32 = jnp.bfloat16, jnp.float32
    dma, regular = pltpu.SemaphoreType.DMA, pltpu.SemaphoreType.REGULAR
    wide_half = pltpu.VMEM((half, depth), f32)
    wide_rows = pltpu.VMEM((row_count, depth), bf16)
    narrow = pltpu.VMEM((row_count, inner), bf16)
    narrow_f32 = pltpu.VMEM((row_count, inner), f32)
    small = pltpu.VMEM((8, depth), f32)
    grad = lambda columns: jax.ShapeDtypeStruct((rows, columns), f32)
    rows_shape = jax.ShapeDtypeStruct((2, row_count, depth), bf16)
    small_shapes = [jax.ShapeDtypeStruct((1, rows), f32)] * 2
    for count in (2 * head_width, head_width):
        small_shapes.append(jax.ShapeDtypeStruct((head_count, count // dp_count), f32))
    flops = 2 * 2 * row_count * depth * (3 * hidden_count + 8 * inner)
    return pl.pallas_call(
        functools.partial(back_kernel, dp_count),
        out_shape=[grad(hidden_count)] * 3
        + [grad(inner)] * 4
        + [rows_shape] * 2
        + small_shapes,
        in_specs=[pl.BlockSpec(memory_space=pltpu.SMEM)] * 2
        + [pl.BlockSpec(memory_space=pl.ANY)] * len(arrays)
        + in_vmem(len(blocks)),
        out_specs=[pl.BlockSpec(memory_space=pl.ANY)] * 13,
        scratch_shapes=[
            pltpu.VMEM((send_slots,) + wide, f32),
            pltpu.VMEM((held_slots,) + wide, f32),
            pltpu.VMEM((ring,) + wide, f32),
            pltpu.VMEM((2, line - 1, 2, rows, width), f32),
            dma((send_slots,)),
            dma((held_slots,)),
            dma((2, line - 1, 2)),
            dma((2, line - 1, 2)),
            regular((2, line - 1)),
            dma((ring, 2)),
        ]
        + (
            [
                pltpu.VMEM((3, line, 2 * rows, 128), f32),
                pltpu.VMEM((2, line - 1, 2, 2 * rows, 128), f32),
                dma((2, line - 1, 2)),
                dma((2, line - 1, 2)),
                regular((2, line - 1)),
                pltpu.VMEM((len(starts), rows, 128), f32),
                dma((len(starts),)),
                dma((len(starts),)),
                dma((3,)),
                pltpu.VMEM((2, 2 * row_count, 128), bf16),
            ]
            if starts
            else []
        )
        + [
            pltpu.VMEM((depth, 2 * row_count), bf16),
            pltpu.VMEM((depth, 2 * row_count), bf16),
            pltpu.VMEM((2, 2 * row_count, width), bf16),
            pltpu.VMEM((2 * row_count, 3 * inner), bf16),
            pltpu.VMEM((inner, depth), bf16),
        ]
        + [pltpu.VMEM((depth, inner), bf16)] * 3
        + [narrow, narrow, narrow, narrow_f32]
        + [narrow_f32, narrow, narrow_f32, narrow_f32]
        + [pltpu.VMEM((head_count, head_width), f32)] * 2
        + [wide_half] * 10
        + [wide_rows] * 3
        + [
            small,
            small,
            pltpu.VMEM((dp_count - 1, 8, depth), f32),
            *[pltpu.VMEM(item.shape, f32) for item in small_shapes],
            pltpu.VMEM((row_count, head_width), f32),
            pltpu.VMEM((row_count, head_width), f32),
            pltpu.VMEM((row_count, 1), jnp.int32),
            pltpu.VMEM((1, row_count), jnp.int32),
            dma((2, 2)),
            dma((2, 2)),
            regular((2,)),
            regular((2,)),
            dma((128,)),
            dma((2,)),
            dma((dp_count - 1,)),
            dma((dp_count - 1,)),
        ],
        compiler_params=pltpu.CompilerParams(
            collective_id=0, has_side_effects=True, vmem_limit_bytes=62 * 1024 * 1024
        ),
        cost_estimate=pl.CostEstimate(flops=flops, bytes_accessed=64 << 20, transcendentals=0),
    )(*lengths, *arrays, *blocks)


def gathers_heads(dp_count):
    return dp_count == 8


class Gather:
    def __init__(self, own, piece, wide, far, near, far_near, full, sems):
        self.own, self.piece, self.wide = own, piece, wide
        self.far, self.near, self.far_near, self.full = far, near, far_near, full
        (
            self.cross_sems, self.line_out, self.line_in, self.pair_out, self.pair_in,
            self.near_sems,
        ) = sems
        self.me = lax.axis_index("dp")
        self.place, self.side = self.me // 2, self.me % 2
        self.line = self.line_out.shape[1] + 1
        self.rows = piece.shape[0]
        tensor = lax.axis_index("tensor")
        self.tensor = tensor
        self.core_peer = tensor + 1 - 2 * (tensor % 2)
        self.far_peer = tensor + 2 - 4 * (tensor // 2)
        self.diagonal = self.far_peer + 1 - 2 * (tensor % 2)

    def slot(self, side, place):
        start = (side * self.line + place) * self.rows
        return self.far.at[pl.ds(pl.multiple_of(start, self.rows), self.rows)]

    def remote(self, source, target, send, recv, device):
        return pltpu.make_async_remote_copy(
            src_ref=source, dst_ref=target, send_sem=send, recv_sem=recv, device_id=device,
            device_id_type=MESH,
        )

    def cross(self):
        return self.remote(
            self.piece, self.slot(self.side, self.place), self.cross_sems.at[0],
            self.cross_sems.at[1], {"tensor": self.far_peer},
        )

    def near_copy(self, index):
        half = self.line * self.rows
        if index == 0:
            source, target = self.wide, self.near
        else:
            start = (self.side if index == 1 else 1 - self.side) * half
            rows = pl.ds(pl.multiple_of(start, self.rows), half)
            source, target = self.far.at[rows], self.far_near.at[rows]
        return self.remote(
            source, target, self.near_sems.at[0, index], self.near_sems.at[1, index],
            {"tensor": self.core_peer},
        )

    def line_copy(self, way, step):
        place = self.place - step if way == 0 else self.place + step
        slot = self.slot(self.side, place)
        return self.remote(
            slot, slot, self.line_out.at[way, step], self.line_in.at[way, step],
            {"dp": self.me + 2 - 4 * way},
        )

    def line_sends(self, way, step):
        if way == 0:
            return (self.place >= step) & (self.place < self.line - 1)
        return (self.place + step <= self.line - 1) & (self.place > 0)

    def line_gets(self, way, step):
        if way == 0:
            return self.place >= step
        return self.place + step <= self.line - 1

    def pair_copy(self, index, place):
        slot = self.slot(self.side, place)
        return self.remote(
            slot, slot, self.pair_out.at[index], self.pair_in.at[index],
            {"dp": self.me + 1 - 2 * self.side},
        )

    def pair_index(self, way, step):
        return 1 + way * (self.line - 1) + step - 1

    def begin(self):
        count = self.own.shape[0]
        rows = pl.ds(pl.multiple_of(self.me * self.rows, self.rows), self.rows)
        self.piece[...] = self.own[rows, :].astype(jnp.float32)
        self.cross().start()

        def widen(rows):
            self.wide[rows, :] = self.own[rows, :].astype(jnp.float32)

        for_rows(count, widen)
        self.near_copy(0).start()

    def forward(self, step):
        if step == 0:
            self.cross().wait()
            self.pair_copy(0, self.place).start()
        for way in range(2):
            if step:

                @pl.when(self.line_gets(way, step))
                def _():
                    self.line_arrival(way, step).wait_recv()
                    place = self.place - step if way == 0 else self.place + step
                    self.pair_copy(self.pair_index(way, step), place).start()

            if step < self.line - 1:

                @pl.when(self.line_sends(way, step))
                def _():
                    self.line_copy(way, step).start()

    def line_arrival(self, way, step):
        place = self.place - step if way == 0 else self.place + step
        slot = self.slot(self.side, place)
        return self.remote(
            slot, slot, self.line_out.at[way, step - 1], self.line_in.at[way, step - 1],
            {"dp": self.me - 2 + 4 * way},
        )

    def store(self, source, tensor, first, count):
        block = self.own.shape[0]

        def narrow(rows):
            at = pl.ds(pl.multiple_of(tensor * block + first + rows.start, row_group), row_group)
            self.full[at, :] = source[rows, :].astype(jnp.bfloat16)

        for_rows(count, narrow)

    def store_far(self, source, tensor):
        for side in range(2):
            for place in range(self.line):
                rows = pl.ds((side * self.line + place) * self.rows, self.rows)
                self.store(source.at[rows], tensor, (2 * place + side) * self.rows, self.rows)

    def finish_line(self):
        self.near_copy(1).start()
        for way in range(2):
            for step in range(self.line - 1):

                @pl.when(self.line_sends(way, step))
                def _():
                    self.line_copy(way, step).wait_send()

        block = self.own.shape[0]
        self.store(self.own, self.tensor, 0, block)
        self.near_copy(0).wait()
        self.store(self.near, self.core_peer, 0, block)

    def finish(self):
        for index in range(1 + 2 * (self.line - 1)):
            if index == 0:
                self.pair_copy(0, self.place).wait()
                continue
            way, step = (index - 1) // (self.line - 1), (index - 1) % (self.line - 1) + 1

            @pl.when(self.line_gets(way, step))
            def _():
                place = self.place - step if way == 0 else self.place + step
                slot = self.slot(1 - self.side, place)
                self.pair_copy(index, place).wait_send()
                self.remote(
                    slot, slot, self.pair_out.at[index], self.pair_in.at[index],
                    {"dp": self.me + 1 - 2 * self.side},
                ).wait_recv()

        self.near_copy(2).start()
        self.store_far(self.far, self.far_peer)
        self.near_copy(1).wait()
        self.near_copy(2).wait()
        self.store_far(self.far_near, self.diagonal)


def front_kernel(dp_count, *refs):
    refs = list(refs)
    take = lambda n: [refs.pop(0) for _ in range(n)]
    lengths = take(2)
    layer_in, cotangent = take(2)
    weights_in = take(7)
    (lambda_param, sub_gain, gain_one, gain_two) = take(4)
    outs = [take(16) for _ in range(2)]
    cosines, sines = take(2), take(2)
    (segment_column, segment_row) = take(2)
    rows_in, cot_rows = take(2), take(2)
    (normed_one, normed_two, flipped) = take(3)
    weights = take(7)
    kept = take(5)
    hidden = take(3)
    (back, fed) = take(2)
    (near_sems, load_sems) = take(2)
    gathers = gathers_heads(dp_count)
    if gathers:
        sets = [take(2) for _ in range(2)]
        heads_wide, heads_landed = take(2), take(2)
        (heads_full, piece, wide, near_weight, full_weight, heads_sems) = take(6)
        gather_sems = take(6)
    else:
        sets = [take(3) for _ in range(2)]
        (projected, far_sems, near_credit) = take(3)
    assert not refs

    tensor = lax.axis_index("tensor")
    core = tensor % 2
    out_weight, gate_weight, up_weight, down_weight = weights[3:]
    row_count, depth = normed_one.shape
    half = row_count // 2
    hidden_count = gate_weight.shape[1]
    used = [0]

    def load(source, target):
        copy = pltpu.make_async_copy(source, target, load_sems.at[used[0]])
        used[0] += 1
        copy.start()
        return copy

    def wait_all(copies):
        for copy in copies:
            copy.wait()
        copies.clear()

    out_weight_load = load(weights_in[3], weights[3])
    rows_loads = [load(layer_in.at[0], rows_in[0])]
    weight_loads = [load(*pair) for pair in zip(weights_in[:3], weights[:3])]
    rows_loads.append(load(layer_in.at[1], rows_in[1]))
    cot_loads = [load(cotangent.at[m], cot_rows[m]) for m in range(2)]
    wide_loads = [load(*pair) for pair in zip(weights_in[4:], weights[4:])]

    sub_scale = sub_gain[...] * (1.0 - lambda_base)
    lam = lambda_terms(lambda_param)[2]
    barrier = pltpu.get_barrier_semaphore()
    core_peer, far_peer = tensor + 1 - 2 * core, tensor + 2 - 4 * (tensor // 2)
    diagonal = far_peer + 1 - 2 * core
    me = lax.axis_index("dp")
    for peer in (core_peer, far_peer, diagonal):
        pl.semaphore_signal(barrier, inc=1, device_id={"tensor": peer}, device_id_type=MESH)
    if gathers:
        for offset in range(1, dp_count):
            target = lax.rem(me + offset, dp_count)
            pl.semaphore_signal(barrier, inc=1, device_id={"dp": target}, device_id_type=MESH)
    pl.semaphore_wait(barrier, dp_count + 2 if gathers else 3)
    if gathers:
        sums = [
            TensorSum(1, *sets[m], None, near_sems.at[m], None, None, None) for m in range(2)
        ]
        for item in sums:
            item.near_left = 1
        gather = Gather(
            weights[3], piece, wide, back, near_weight, fed, full_weight, gather_sems
        )
    else:
        sums = [
            TensorSum(1, *sets[m], near_sems.at[m], far_sems.at[m], near_credit.at[m], None)
            for m in range(2)
        ]
    out_loads, flip_loads, wide_outs, hidden_outs = [], [], [], []

    def mine(rows):
        return pl.ds(pl.multiple_of(core * half + rows.start, row_group), row_group)

    def others(rows):
        return pl.ds(pl.multiple_of((1 - core) * half + rows.start, row_group), row_group)

    def flip_to(source, target):
        wait_all(flip_loads)

        def block(i, carry):
            at = pl.ds(pl.multiple_of(i * 128, 128), 128)
            flipped[at, :] = source[:, at].T
            return carry

        lax.fori_loop(0, depth // 128, block, 0)
        flip_loads.append(load(flipped, target))

    def heads_copy(m, index):
        peer = (core_peer, far_peer, diagonal)[index]
        which = core if index == 1 else 1 - core
        rows = pl.ds(pl.multiple_of(which * half, half), half)
        return pltpu.make_async_remote_copy(
            src_ref=heads_wide[m].at[rows], dst_ref=heads_landed[m].at[index],
            send_sem=heads_sems.at[m, 0, index], recv_sem=heads_sems.at[m, 1, index],
            device_id={"tensor": peer}, device_id_type=MESH,
        )

    def join_heads(m):
        own = sets[m][0]
        inner = kept[4].shape[1]

        def place_of(index):
            return pl.ds(pl.multiple_of(index * inner, inner), inner)

        rows = pl.ds(pl.multiple_of(core * half, half), half)
        heads_full[:, place_of(tensor)] = heads_wide[m][rows, :].astype(jnp.bfloat16)
        for index, peer in enumerate((core_peer, far_peer, diagonal)):
            heads_copy(m, index).wait()
            heads_full[:, place_of(peer)] = heads_landed[m][index].astype(jnp.bfloat16)

        def block(i, carry):
            at = pl.ds(pl.multiple_of(i * 512, 512), 512)
            values = rows_in[m][rows, at].astype(jnp.float32)
            own[:, at] = values + f32_dot(heads_full[...], full_weight[:, at])
            return carry

        lax.fori_loop(0, depth // 512, block, 0)

    def attend(m, between):
        rows_loads[m].wait()
        wait_all(weight_loads)
        wait_all(out_loads)
        segments(lengths[m], segment_column, segment_row)
        out_loads.extend([load(cosines[m], outs[m][14]), load(sines[m], outs[m][15])])
        forward_kernel(
            lam, rows_in[m], gain_one, *weights[:3], cosines[m], sines[m], segment_column,
            segment_row, sub_scale, normed_one, *kept,
            between,
        )
        heads = kept[4]
        if gathers:
            heads_wide[m][...] = heads[...].astype(jnp.float32)
            for index in range(3):
                heads_copy(m, index).start()
            out_loads.extend(load(*pair) for pair in zip(kept, outs[m][3:8]))
            flip_to(normed_one, outs[m][2])
            return

        def part(which, target):
            rows = pl.ds(pl.multiple_of(which * half, half), half)

            def block(i, carry):
                at = pl.ds(pl.multiple_of(i * 512, 512), 512)
                target[:, at] = f32_dot(heads[rows, :], out_weight[:, at])
                return carry

            lax.fori_loop(0, depth // 512, block, 0)

        part(1 - core, projected)
        sums[m].near_start(projected)
        part(core, sets[m][0])
        out_loads.extend(load(*pair) for pair in zip(kept, outs[m][3:8]))
        flip_to(normed_one, outs[m][2])
        sums[m].near_add()

    def norm_rows(values):
        return (values * root_of(values) * gain_two[...]).astype(jnp.bfloat16)

    def join(m):
        own = sets[m][0]
        if gathers:
            join_heads(m)
        else:
            far = sets[m][2]

            def add(rows):
                values = rows_in[m][mine(rows), :].astype(jnp.float32)
                own[rows, :] = values + (own[rows, :] + far[rows, :])

            for_rows(half, add)
        sums[m].near_start(own)
        out_loads.append(load(own, outs[m][8]))

    def norm(m):
        own, near = sets[m][:2]

        def norm_mine(rows):
            normed_two[mine(rows), :] = norm_rows(own[rows, :])

        def norm_others(rows):
            normed_two[others(rows), :] = norm_rows(near[rows, :])

        wait_all(out_loads)
        for_rows(half, norm_mine)
        sums[m].near_wait()
        for_rows(half, norm_others)
        sums[m].near_free()
        out_loads.append(load(normed_two, outs[m][1]))

    def feed(m, between):
        inside, gate_pre, up_pre = hidden
        if m == 0:
            wait_all(wide_loads)
        wait_all(hidden_outs)

        def block(j, carry):
            at = pl.ds(pl.multiple_of(j * 256, 256), 256)
            gate = f32_dot(normed_two[...], gate_weight[:, at])
            upward = f32_dot(normed_two[...], up_weight[:, at])
            grads = dot_t(cot_rows[m][...], down_weight[at, :])
            sigmoid = jax.nn.sigmoid(gate)
            inside[:, at] = (gate * sigmoid * upward).astype(jnp.bfloat16)
            gate_pre[:, at] = (
                grads * upward * sigmoid * (1.0 + gate * (1.0 - sigmoid))
            ).astype(jnp.bfloat16)
            up_pre[:, at] = (grads * gate * sigmoid).astype(jnp.bfloat16)
            return carry

        lax.fori_loop(0, hidden_count // 256, block, 0)
        hidden_outs.extend(load(*pair) for pair in zip(hidden, outs[m][9:12]))
        between()
        wait_all(wide_outs)

        for i in range(depth // 512):
            at = slice(i * 512, (i + 1) * 512)
            back[:, at] = dot_t(gate_pre[...], gate_weight[at, :]) + dot_t(
                up_pre[...], up_weight[at, :]
            )
            fed[:, at] = f32_dot(inside[...], down_weight[:, at])
            wide_outs.append(load(back.at[:, at], outs[m][12].at[:, at]))
            wide_outs.append(load(fed.at[:, at], outs[m][13].at[:, at]))

    def flip_cot(m):
        cot_loads[m].wait()
        flip_to(cot_rows[m], outs[m][0])

    if gathers:
        out_weight_load.wait()
        gather.begin()
        rotary_tables(lengths, cosines, sines, lambda_param.shape[1] // 4)
        attend(0, {1: lambda: gather.forward(0)})
        attend(1, {0: lambda: gather.forward(1)})
        gather.forward(2)
        flip_cot(0)
        flip_cot(1)
        gather.forward(3)
        gather.finish_line()
        gather.finish()
    else:
        out_weight_load.wait()
        rotary_tables(lengths, cosines, sines, lambda_param.shape[1] // 4)
        attend(0, {})
        sums[0].far_go()
        attend(1, {})
        flip_cot(0)
        flip_cot(1)
        sums[0].far_wait()
        sums[1].far_go()
    join(0)
    norm(0)
    if gathers:
        feed(0, lambda: join(1))
    else:
        feed(0, lambda: None)
        sums[1].far_wait()
        join(1)
    norm(1)
    feed(1, lambda: None)
    wait_all(flip_loads)
    wait_all(hidden_outs)
    wait_all(wide_outs)
    wait_all(out_loads)


def front_call(dp_count, lengths, arrays, blocks, shapes):
    depth, row_count, inner, hidden_count, head_count, head_width = shapes
    bf16, f32 = jnp.bfloat16, jnp.float32
    dma, regular = pltpu.SemaphoreType.DMA, pltpu.SemaphoreType.REGULAR
    half = row_count // 2
    out_shape = []
    for m in range(2):
        out_shape += [jax.ShapeDtypeStruct((depth, row_count), bf16)]
        out_shape += [jax.ShapeDtypeStruct((row_count, depth), bf16)]
        out_shape += [jax.ShapeDtypeStruct((depth, row_count), bf16)]
        out_shape += [jax.ShapeDtypeStruct((row_count, inner), bf16)] * 3
        out_shape += [jax.ShapeDtypeStruct((row_count, inner), f32)]
        out_shape += [jax.ShapeDtypeStruct((row_count, inner), bf16)]
        out_shape += [jax.ShapeDtypeStruct((half, depth), f32)]
        out_shape += [jax.ShapeDtypeStruct((row_count, hidden_count), bf16)] * 3
        out_shape += [jax.ShapeDtypeStruct((row_count, depth), f32)] * 2
        out_shape += [jax.ShapeDtypeStruct((row_count, head_width), f32)] * 2
    wide_rows = pltpu.VMEM((row_count, depth), bf16)
    narrow = pltpu.VMEM((row_count, inner), bf16)
    wide_half = pltpu.VMEM((half, depth), f32)
    if gathers_heads(dp_count):
        steps = dp_count // 2 - 1
        extra = [wide_half] * 4
        extra += [pltpu.VMEM((row_count, inner), f32)] * 2
        extra += [pltpu.VMEM((3, half, inner), f32)] * 2
        extra += [
            pltpu.VMEM((half, depth), bf16),
            pltpu.VMEM((inner // dp_count, depth), f32),
            pltpu.VMEM((inner, depth), f32),
            pltpu.VMEM((inner, depth), f32),
            pltpu.VMEM((depth, depth), bf16),
            dma((2, 2, 3)),
            dma((2,)),
            dma((2, steps)),
            dma((2, steps)),
            dma((1 + 2 * steps,)),
            dma((1 + 2 * steps,)),
            dma((2, 3)),
        ]
    else:
        extra = [wide_half] * 7 + [dma((2, 2)), regular((2,))]
    return pl.pallas_call(
        functools.partial(front_kernel, dp_count),
        out_shape=out_shape,
        in_specs=[pl.BlockSpec(memory_space=pltpu.SMEM)] * 2
        + [pl.BlockSpec(memory_space=pl.ANY)] * len(arrays)
        + in_vmem(len(blocks)),
        out_specs=[pl.BlockSpec(memory_space=pl.ANY)] * len(out_shape),
        scratch_shapes=[pltpu.VMEM((row_count, head_width), f32)] * 4
        + [pltpu.VMEM((row_count, 1), jnp.int32), pltpu.VMEM((1, row_count), jnp.int32)]
        + [wide_rows] * 6
        + [pltpu.VMEM((depth, row_count), bf16)]
        + [pltpu.VMEM((depth, inner), bf16)] * 3
        + [pltpu.VMEM((inner, depth), bf16)]
        + [pltpu.VMEM((depth, hidden_count), bf16)] * 2
        + [pltpu.VMEM((hidden_count, depth), bf16)]
        + [narrow, narrow, narrow, pltpu.VMEM((row_count, inner), f32), narrow]
        + [pltpu.VMEM((row_count, hidden_count), bf16)] * 3
        + [pltpu.VMEM((row_count, depth), f32)] * 2
        + [dma((2, 2)), dma((64,))]
        + extra,
        compiler_params=pltpu.CompilerParams(
            collective_id=1, has_side_effects=True, vmem_limit_bytes=62 * 1024 * 1024
        ),
        cost_estimate=pl.CostEstimate(
            flops=4 * row_count * depth * (6 * hidden_count + 4 * inner),
            bytes_accessed=64 << 20,
            transcendentals=0,
        ),
    )(*lengths, *arrays, *blocks)


def settle_kernel(count, *refs):
    sources, targets, held = refs[:count], refs[count : 2 * count], refs[2 * count : 3 * count]
    in_sems, out_sems = refs[3 * count :]

    def parts(k):
        rows = sources[k].shape[0]
        pieces = rows if len(sources[k].shape) == 3 else 1
        return [slice(i * rows // pieces, (i + 1) * rows // pieces) for i in range(pieces)]

    pieces = [(k, i, at) for k in range(count) for i, at in enumerate(parts(k))]
    loads = [
        pltpu.make_async_copy(sources[k].at[at], held[k].at[at], in_sems.at[k, i])
        for k, i, at in pieces
    ]
    stores = [
        pltpu.make_async_copy(held[k].at[at], targets[k].at[at], out_sems.at[k, i])
        for k, i, at in pieces
    ]
    for copy in loads:
        copy.start()
    for load, store in zip(loads, stores):
        load.wait()
        store.start()
    for store in stores:
        store.wait()


def settle(arrays):
    count = len(arrays)
    return pl.pallas_call(
        functools.partial(settle_kernel, count),
        out_shape=[jax.ShapeDtypeStruct(item.shape, item.dtype) for item in arrays],
        in_specs=[pl.BlockSpec(memory_space=pl.ANY)] * count,
        out_specs=[pl.BlockSpec(memory_space=pl.ANY)] * count,
        scratch_shapes=[pltpu.VMEM(item.shape, item.dtype) for item in arrays]
        + [pltpu.SemaphoreType.DMA((count, 2))] * 2,
        compiler_params=pltpu.CompilerParams(vmem_limit_bytes=62 * 1024 * 1024),
    )(*arrays)


def on_device(
    layer_in,
    short_lengths,
    long_lengths,
    norm1_gain,
    query_weight,
    key_weight,
    value_weight,
    lambda_param,
    sub_gain,
    out_weight,
    norm2_gain,
    gate_weight,
    up_weight,
    down_weight,
    out_cotangent,
):
    dp_count = lax.axis_size("dp")
    projections = [query_weight, key_weight, value_weight]
    depth, inner = query_weight.shape
    shapes = (depth, layer_in.shape[1], inner, gate_weight.shape[1], *sub_gain.shape)
    lengths = [short_lengths, long_lengths]
    blocks = [lambda_param, sub_gain, norm1_gain, norm2_gain]
    arrays = [layer_in, out_cotangent, *projections, out_weight]
    arrays += [gate_weight, up_weight, down_weight]
    parts = front_call(dp_count, lengths, arrays, blocks, shapes)
    pick = lambda at: [parts[at], parts[at + 16]]
    arrays = pick(0) + pick(1) + pick(2) + pick(9) + pick(10) + pick(11) + pick(7)
    arrays += pick(12) + pick(13) + pick(8)
    arrays += [layer_in, out_cotangent, out_weight, *projections]
    arrays += parts[3:7] + parts[19:23] + parts[14:16] + parts[30:32]
    (
        grad_down, grad_gate, grad_up, grad_out, grad_query, grad_key, grad_value, layer_out,
        grad_in, grad_norm1, grad_norm2, grad_lambda, grad_sub,
    ) = back_call(dp_count, lengths, arrays, blocks, shapes)
    (
        layer_out, grad_in, grad_down, grad_out, grad_query, grad_key, grad_value, grad_gate,
        grad_up, grad_lambda, grad_sub,
    ) = settle(
        [
            layer_out, grad_in, grad_down, grad_out, grad_query, grad_key, grad_value, grad_gate,
            grad_up, grad_lambda, grad_sub,
        ]
    )
    return (
        layer_out,
        grad_in,
        grad_norm1.reshape(-1),
        grad_query,
        grad_key,
        grad_value,
        grad_lambda,
        grad_sub,
        grad_out.T,
        grad_norm2.reshape(-1),
        grad_gate,
        grad_up,
        grad_down.T,
    )


def solution(mesh):
    return jax.shard_map(
        on_device,
        mesh=mesh,
        in_specs=(
            P(None, "dp", None),
            P("dp", None),
            P("dp", None),
            P(),
            P(None, "tensor"),
            P(None, "tensor"),
            P(None, "tensor"),
            P("tensor", None),
            P("tensor", None),
            P("tensor", None),
            P(),
            P(None, "tensor"),
            P(None, "tensor"),
            P("tensor", None),
            P(None, "dp", None),
        ),
        out_specs=(
            P(None, "dp", None),
            P(None, "dp", None),
            P("dp"),
            P("dp", "tensor"),
            P("dp", "tensor"),
            P("dp", "tensor"),
            P("tensor", "dp"),
            P("tensor", "dp"),
            P("tensor", "dp"),
            P("dp"),
            P("dp", "tensor"),
            P("dp", "tensor"),
            P("tensor", "dp"),
        ),
        check_vma=False,
    )
```

```python
import functools
import math

import jax
import jax.numpy as jnp
from jax import lax
from jax.experimental import pallas as pl
from jax.experimental.pallas import tpu as pltpu
from jax.sharding import PartitionSpec as P

norm_epsilon = 1e-05
lambda_base = 0.8 - 0.6 * math.exp(-0.3 * 11.0)
rotary_base = 10000.0
closed_score = -1e30
block_rows = 128
longest_document = 256
row_group = 16
send_slots = 3
held_slots = 4
MESH = pl.DeviceIdType.MESH


def documents(lengths, places):
    end, segment, start = 0, 0, 0
    for k in range(lengths.shape[1]):
        length = lengths[0, k]
        end = end + length
        passed = (places >= end).astype(jnp.int32)
        segment = segment + passed
        start = start + passed * length
    return segment, start


def segments(lengths, column, row):
    column[...] = documents(lengths, lax.broadcasted_iota(jnp.int32, column.shape, 0))[0]
    row[...] = documents(lengths, lax.broadcasted_iota(jnp.int32, row.shape, 1))[0]


def rotary_tables(lengths, cosines, sines, map_width):
    half_width = map_width // 2
    row_count, width = cosines[0].shape
    lane = lax.broadcasted_iota(jnp.int32, (block_rows, width), 1)
    frequency = jnp.zeros((block_rows, width), jnp.float32)
    for k in range(half_width):
        value = rotary_base ** (-2.0 * k / map_width)
        frequency = jnp.where(lane % half_width == k, value, frequency)

    def block(i, carry):
        rows = pl.ds(pl.multiple_of(i * block_rows, block_rows), block_rows)
        places = lax.broadcasted_iota(jnp.int32, (block_rows, width), 0) + i * block_rows
        starts = [documents(item, places)[1] for item in lengths]
        start = jnp.where(lane < half_width, starts[0], starts[1])
        angles = (places - start).astype(jnp.float32) * frequency

        def spread(values, m):
            base = jnp.where(lane // half_width == m, values, 0.0)
            return sum(
                (pltpu.roll(base, k * half_width, 1) for k in range(1, width // half_width)), base
            )

        cosine, sine = jnp.cos(angles), jnp.sin(angles)
        for m in range(2):
            cosines[m][rows, :] = spread(cosine, m)
            signed = spread(sine, m)
            sines[m][rows, :] = jnp.where(lane % map_width < half_width, -signed, signed)
        return carry

    lax.fori_loop(0, row_count // block_rows, block, 0)


def lambda_terms(param):
    width = param.shape[1] // 4
    part = lambda k: param[:, k * width : (k + 1) * width]
    first = jnp.exp(jnp.sum(part(0) * part(1), axis=-1, keepdims=True))
    second = jnp.exp(jnp.sum(part(2) * part(3), axis=-1, keepdims=True))
    return first, second, first - second + lambda_base


def turn(values, cosine, sine):
    width = values.shape[-1]
    quarter = width // 4
    lane = lax.broadcasted_iota(jnp.int32, values.shape, 1)
    partner = jnp.where(
        lane % (2 * quarter) < quarter,
        pltpu.roll(values, width - quarter, 1),
        pltpu.roll(values, quarter, 1),
    )
    return values * cosine + partner * sine


def map_of(values, which):
    lane = lax.broadcasted_iota(jnp.int32, values.shape, 1)
    mine = (lane >= values.shape[-1] // 2) == (which == 1)
    return jnp.where(mine, values, jnp.zeros_like(values))


def key_range(block):
    first = max(0, block * block_rows - longest_document + 1) // block_rows * block_rows
    return first, (block + 1) * block_rows


def open_pairs(block, segment_column, segment_row):
    first, last = key_range(block)
    rows = pl.ds(block * block_rows, block_rows)
    shape = (block_rows, last - first)
    row_at = lax.broadcasted_iota(jnp.int32, shape, 0) + block * block_rows
    key_at = lax.broadcasted_iota(jnp.int32, shape, 1) + first
    return (segment_column[rows, :] == segment_row[:, first:last]) & (key_at <= row_at)


def softmax_map(query, key, opened, scale):
    scores = jnp.where(opened, dot_t(query, key) * scale, closed_score)
    expanded = jnp.exp(scores - jnp.max(scores, axis=-1, keepdims=True))
    return expanded * (1.0 / jnp.sum(expanded, axis=-1, keepdims=True))


def f32_dot(left, right):
    return jnp.dot(left, right, preferred_element_type=jnp.float32)


def dot_t(left, right):
    return lax.dot_general(
        left, right, (((1,), (1,)), ((), ())), preferred_element_type=jnp.float32
    )


def dot_rows(left, right):
    return lax.dot_general(
        left, right, (((0,), (0,)), ((), ())), preferred_element_type=jnp.float32
    )


def rms_back(incoming, values, inverse_root):
    return inverse_root * incoming - values * inverse_root**3 * jnp.mean(
        incoming * values, axis=-1, keepdims=True
    )


def root_of(values):
    return lax.rsqrt(jnp.mean(values * values, axis=-1, keepdims=True) + norm_epsilon)


def forward_kernel(
    lam, rows, gain, query_weight, key_weight, value_weight, cosine, sine, segment_column,
    segment_row, sub_scale, normed_one, query, key, value, mixed, heads_out, between,
):
    head_count, width = sub_scale.shape
    scale = (width // 2) ** (-0.5)
    values = rows[...].astype(jnp.float32)
    normed_one[...] = (values * root_of(values) * gain[...]).astype(jnp.bfloat16)
    raw_query = f32_dot(normed_one[...], query_weight[...])
    raw_key = f32_dot(normed_one[...], key_weight[...])
    value[...] = f32_dot(normed_one[...], value_weight[...]).astype(jnp.bfloat16)
    for head in range(head_count):
        at = slice(head * width, (head + 1) * width)
        query[:, at] = turn(raw_query[:, at], cosine[...], sine[...]).astype(jnp.bfloat16)
        key[:, at] = turn(raw_key[:, at], cosine[...], sine[...]).astype(jnp.bfloat16)
    for block in range(rows.shape[0] // block_rows):
        first, last = key_range(block)
        here = slice(block * block_rows, last)
        opened = open_pairs(block, segment_column, segment_row)
        if block in between:
            between[block]()
        for head in range(head_count):
            at = slice(head * width, (head + 1) * width)
            keys = key[first:last, at]
            maps = [softmax_map(map_of(query[here, at], c), keys, opened, scale) for c in range(2)]
            combined = (maps[0] - lam[head : head + 1, :] * maps[1]).astype(jnp.bfloat16)
            out = f32_dot(combined, value[first:last, at])
            mixed[here, at] = out
            heads_out[here, at] = (out * root_of(out) * sub_scale[head : head + 1, :]).astype(
                jnp.bfloat16
            )


def backward_kernel(
    lam, grad_attended, out_weight, query, key, value, mixed, cosine, sine, segment_column,
    segment_row, sub_scale, grad_rows, grad_sub, grad_lam, grad_heads, grad_mixed, grad_key,
    grad_value,
):
    head_count, width = sub_scale.shape
    row_count = query.shape[0]
    inner = head_count * width
    scale = (width // 2) ** (-0.5)
    grad_heads[...] = dot_t(grad_attended[...], out_weight[...])
    for head in range(head_count):
        at = slice(head * width, (head + 1) * width)
        heads = mixed[:, at]
        root = root_of(heads)
        grads = grad_heads[:, at]
        grad_sub[head : head + 1, :] = jnp.sum(grads * heads * root, axis=0, keepdims=True) * (
            1.0 - lambda_base
        )
        grad_mixed[:, at] = rms_back(grads * sub_scale[head : head + 1, :], heads, root).astype(
            jnp.bfloat16
        )
    grad_key[...] = jnp.zeros_like(grad_key)
    grad_value[...] = jnp.zeros_like(grad_value)
    lam_sums = [0.0] * head_count
    for block in range(row_count // block_rows):
        first, last = key_range(block)
        here = slice(block * block_rows, last)
        opened = open_pairs(block, segment_column, segment_row)
        for head in range(head_count):
            at = slice(head * width, (head + 1) * width)
            keys = key[first:last, at]
            queries = [map_of(query[here, at], c) for c in range(2)]
            maps = [softmax_map(queries[c], keys, opened, scale) for c in range(2)]
            mixes = grad_mixed[here, at]
            combined = (maps[0] - lam[head : head + 1, :] * maps[1]).astype(jnp.bfloat16)
            grad_value[first:last, at] += dot_rows(combined, mixes)
            grads = dot_t(mixes, value[first:last, at])
            first_sum = jnp.sum(grads * maps[0], axis=-1, keepdims=True)
            second_sum = jnp.sum(grads * maps[1], axis=-1, keepdims=True)
            lam_sums[head] = lam_sums[head] + jnp.sum(second_sum, axis=0, keepdims=True)
            score_grads = [
                (maps[0] * (grads - first_sum)).astype(jnp.bfloat16),
                (maps[1] * (-lam[head : head + 1, :] * (grads - second_sum))).astype(jnp.bfloat16),
            ]
            grad_query = f32_dot(score_grads[0], map_of(keys, 0)) + f32_dot(
                score_grads[1], map_of(keys, 1)
            )
            grad_rows[here, at] = turn(
                grad_query * scale, cosine[here, :], -sine[here, :]
            ).astype(jnp.bfloat16)
            grad_key[first:last, at] += dot_rows(score_grads[0], queries[0]) + dot_rows(
                score_grads[1], queries[1]
            )
    for head in range(head_count):
        at = slice(head * width, (head + 1) * width)
        grad_rows[:, inner + head * width : inner + (head + 1) * width] = turn(
            grad_key[:, at] * scale, cosine[...], -sine[...]
        ).astype(jnp.bfloat16)
        grad_lam[head : head + 1, :] = jnp.broadcast_to(-lam_sums[head], (1, width))
    grad_rows[:, 2 * inner :] = grad_value[...].astype(jnp.bfloat16)


def in_vmem(count):
    return [pl.BlockSpec(memory_space=pltpu.VMEM)] * count


class Line:
    def __init__(self, line, widths, total, landed, line_out, line_in, credit):
        self.line, self.widths = line, widths
        self.total, self.landed = total, landed
        self.line_out, self.line_in, self.credit = line_out, line_in, credit
        self.me = lax.axis_index("dp")
        self.place = self.me // 2
        self.ring = total.shape[0]

    def copy(self, c, step, way, block, target):
        width = self.widths[c]
        return pltpu.make_async_remote_copy(
            src_ref=self.total.at[c % self.ring, block, :, :width],
            dst_ref=self.landed.at[way, step, c % 2, :, :width],
            send_sem=self.line_out.at[way, step, c % 2],
            recv_sem=self.line_in.at[way, step, c % 2],
            device_id={"dp": target},
            device_id_type=MESH,
        )

    def sends(self, step, way):
        place, line = self.place, self.line
        if way == 0:
            block = line - 1 - step + place
            return (place <= step) & (place < line - 1), block, self.me + 2
        block = place + step - line + 1
        return (place >= line - 1 - step) & (place > 0), block, self.me - 2

    def gets(self, step, way):
        place, line = self.place, self.line
        if way == 0:
            return (place > 0) & (place - 1 <= step), line - 2 - step + place, self.me - 2
        gets = (place < line - 1) & (place + 1 >= line - 1 - step)
        return gets, place + step - line + 2, self.me + 2

    def start(self, c, step):
        for way in range(2):
            sends, block, target = self.sends(step, way)

            @pl.when(sends)
            def _():
                if c >= 2:
                    pl.semaphore_wait(self.credit.at[way, step], 1)
                self.copy(c, step, way, block, target).start()

    def finish(self, c, step):
        width = self.widths[c]
        for way in range(2):
            gets, block, source = self.gets(step, way)

            @pl.when(gets)
            def _():
                self.copy(c, step, way, block, source).wait_recv()
                self.total[c % self.ring, block, :, :width] += self.landed[
                    way, step, c % 2, :, :width
                ]
                if c + 2 < len(self.widths):
                    pl.semaphore_signal(
                        self.credit.at[way, step],
                        inc=1,
                        device_id={"dp": source},
                        device_id_type=MESH,
                    )

            sends, sent, target = self.sends(step, way)

            @pl.when(sends)
            def _():
                self.copy(c, step, way, sent, target).wait_send()


class Reducer:
    def __init__(self, plan, line_plan, line_starts, line, refs):
        self.plan, self.line_plan, self.line_starts = plan, line_plan, line_starts
        self.line = line
        (
            self.send, self.held, self.total, landed, self.pair_out, self.pair_in,
            line_out, line_in, credit, self.out_sem,
        ) = refs[:10]
        self.first = Line(
            line, [item.width for item in plan], self.total, landed, line_out, line_in, credit
        )
        self.place = self.first.place
        self.me = self.first.me
        self.side = self.me % 2
        self.other = self.me + 1 - 2 * self.side
        self.steps = line - 1
        self.ring = self.total.shape[0]
        self.rows = self.total.shape[2]
        if line_plan:
            (
                self.line_total, landed, line_out, line_in, credit, self.last_held,
                self.last_out, self.last_in, self.line_out_sem,
            ) = refs[10:]
            self.second = Line(
                line, [item.width for item in line_plan], self.line_total, landed, line_out,
                line_in, credit,
            )

    def compute(self, c):
        item = self.plan[c]
        width = item.width
        left, right = item.left(), item.right()

        def block(at, carry):
            first = pl.multiple_of(2 * at * self.rows, self.rows)
            columns = right[...]
            away = left[pl.ds(first + (1 - self.side) * self.rows, self.rows), :]
            here = left[pl.ds(first + self.side * self.rows, self.rows), :]
            self.send[c % send_slots, at, :, :width] = f32_dot(away, columns)
            self.total[c % self.ring, at, :, :width] = f32_dot(here, columns)
            return carry

        lax.fori_loop(0, self.line, block, 0)
        item.computed()

    def line_compute(self, c):
        item = self.line_plan[c]
        left, right = item.left(), item.right()
        slot = c % self.line_total.shape[0]
        if c >= self.line_total.shape[0]:
            self.line_result(c - self.line_total.shape[0]).wait()

        def block(at, carry):
            rows = pl.ds(pl.multiple_of(2 * at * self.rows, 2 * self.rows), 2 * self.rows)
            self.line_total[slot, at] = f32_dot(left[rows, :], right[...])
            return carry

        lax.fori_loop(0, self.line, block, 0)
        item.computed()

    def side_rows(self, side):
        return pl.ds(pl.multiple_of(side * self.rows, self.rows), self.rows)

    def last_copy(self, c):
        slot = c % self.line_total.shape[0]
        return pltpu.make_async_remote_copy(
            src_ref=self.line_total.at[slot, self.place, self.side_rows(1 - self.side), :],
            dst_ref=self.last_held.at[c],
            send_sem=self.last_out.at[c],
            recv_sem=self.last_in.at[c],
            device_id={"dp": self.other},
            device_id_type=MESH,
        )

    def line_result(self, c):
        item = self.line_plan[c]
        slot = c % self.line_total.shape[0]
        return pltpu.make_async_copy(
            self.line_total.at[slot, self.place, self.side_rows(self.side), :],
            item.out.at[:, item.first : item.first + item.width],
            self.line_out_sem.at[slot],
        )

    def line_step(self, slot):
        for c, start in enumerate(self.line_starts):
            step = slot - start
            if 0 < step <= self.steps:
                self.second.finish(c, step - 1)
            if step == self.steps + 1:
                self.last_copy(c).wait()
                at = c % self.line_total.shape[0]
                self.line_total[at, self.place, self.side_rows(self.side), :] += self.last_held[c]
                self.line_result(c).start()
            if 0 <= step < self.steps and slot:
                self.second.start(c, step)
            if step == self.steps:
                self.last_copy(c).start()

    def pair_copy(self, c):
        width = self.plan[c].width
        return pltpu.make_async_remote_copy(
            src_ref=self.send.at[c % send_slots, :, :, :width],
            dst_ref=self.held.at[c % held_slots, :, :, :width],
            send_sem=self.pair_out.at[c % send_slots],
            recv_sem=self.pair_in.at[c % held_slots],
            device_id={"dp": self.other},
            device_id_type=MESH,
        )

    def pair_finish(self, c):
        width = self.plan[c].width
        self.pair_copy(c).wait_recv()

        def block(at, carry):
            self.total[c % self.ring, at, :, :width] += self.held[c % held_slots, at, :, :width]
            return carry

        lax.fori_loop(0, self.line, block, 0)
        self.pair_copy(c).wait_send()

    def out_copies(self, c):
        item = self.plan[c]
        outs = item.out if isinstance(item.out, list) else [item.out]
        size = outs[0].shape[1]
        first, last = item.first, item.first + item.width
        while first < last:
            count = min(last, (first // size + 1) * size) - first
            at = first - item.first
            yield pltpu.make_async_copy(
                self.total.at[c % self.ring, self.place, :, at : at + count],
                outs[first // size].at[:, first % size : first % size + count],
                self.out_sem.at[c % self.ring, at // 128],
            )
            first += count

    def out_start(self, c):
        for copy in self.out_copies(c):
            copy.start()

    def out_wait(self, c):
        for copy in self.out_copies(c):
            copy.wait()

    def run(self, tasks):
        count, steps = len(self.plan), self.steps
        begun = [c for c, start in enumerate(self.line_starts) if start == 0]
        for c in begun:
            self.line_compute(c)
        for c in begun:
            self.second.start(c, 0)
        self.compute(1)
        for slot in range(count + steps + 1):
            for step in reversed(range(steps)):
                c = slot - 2 - step
                if 0 <= c < count:
                    self.first.finish(c, step)
                    if step + 1 < steps:
                        self.first.start(c, step + 1)
            self.line_step(slot)
            if 0 <= slot - 1 < count:
                self.pair_finish(slot - 1)
                self.first.start(slot - 1, 0)
            if slot + 1 < count:
                self.pair_copy(slot + 1).start()
            done = slot - 1 - steps
            if 0 <= done < count:
                self.out_start(done)
            if slot + 2 < count:
                if slot + 2 >= self.ring:
                    self.out_wait(slot + 2 - self.ring)
                self.compute(slot + 2)
            for c, start in enumerate(self.line_starts):
                if slot and start == slot + 1:
                    self.line_compute(c)
            for task in tasks.get(slot, ()):
                task()
        for c in range(max(0, count - self.ring), count):
            self.out_wait(c)
        if self.line_plan:
            for c in range(len(self.line_plan) - self.line_total.shape[0], len(self.line_plan)):
                self.line_result(c).wait()


class Chunk:
    def __init__(self, left, right, computed, out, first, width):
        self.left, self.right, self.computed = left, right, computed
        self.out, self.first, self.width = out, first, width


def for_rows(count, body):
    def step(i, carry):
        body(pl.ds(pl.multiple_of(i * row_group, row_group), row_group))
        return carry

    lax.fori_loop(0, count // row_group, step, 0)


class TensorSum:
    def __init__(self, uses, own, near, far, near_sems, far_sems, near_credit, far_credit):
        self.own, self.near, self.far = own, near, far
        self.near_sems, self.far_sems = near_sems, far_sems
        self.near_credit, self.far_credit = near_credit, far_credit
        index = lax.axis_index("tensor")
        self.core_peer = index + 1 - 2 * (index % 2)
        self.far_peer = index + 2 - 4 * (index // 2)
        self.near_left, self.far_left = 2 * uses, uses
        self.near_first, self.far_first = True, True

    def near_copy(self, source):
        return pltpu.make_async_remote_copy(
            src_ref=source, dst_ref=self.near, send_sem=self.near_sems.at[0],
            recv_sem=self.near_sems.at[1], device_id={"tensor": self.core_peer},
            device_id_type=MESH,
        )

    def far_copy(self):
        return pltpu.make_async_remote_copy(
            src_ref=self.own, dst_ref=self.far, send_sem=self.far_sems.at[0],
            recv_sem=self.far_sems.at[1], device_id={"tensor": self.far_peer},
            device_id_type=MESH,
        )

    def near_start(self, source):
        if not self.near_first:
            pl.semaphore_wait(self.near_credit, 1)
        self.near_first = False
        self.pending = source
        self.near_copy(source).start()

    def near_wait(self):
        self.near_copy(self.pending).wait()

    def near_free(self):
        self.near_left -= 1
        if self.near_left:
            pl.semaphore_signal(
                self.near_credit, inc=1, device_id={"tensor": self.core_peer}, device_id_type=MESH
            )

    def near_add(self):
        self.near_wait()

        def add(rows):
            self.own[rows, :] += self.near[rows, :]

        for_rows(self.own.shape[0], add)
        self.near_free()

    def far_go(self):
        if not self.far_first:
            pl.semaphore_wait(self.far_credit, 1)
        self.far_first = False
        self.far_copy().start()

    def far_wait(self):
        self.far_copy().wait()

    def far_free(self):
        self.far_left -= 1
        if self.far_left:
            pl.semaphore_signal(
                self.far_credit, inc=1, device_id={"tensor": self.far_peer}, device_id_type=MESH
            )


def line_first(dp_count):
    return ((0, 0, 3, 6, 9, 12), (2, 2, 2)) if dp_count == 8 else ((), (0, 0, 0))


def back_kernel(dp_count, *refs):
    refs = list(refs)
    take = lambda n: [refs.pop(0) for _ in range(n)]
    lengths = take(2)
    cot_left, two_left, one_left = [take(2) for _ in range(3)]
    hidden, gate_pre, up_pre, heads = [take(2) for _ in range(4)]
    part_back, part_fed, middle = [take(2) for _ in range(3)]
    (layer_in, cotangent) = take(2)
    weights_in = take(4)
    kept_in = [take(4) for _ in range(2)]
    tables_in = [take(2) for _ in range(2)]
    (lambda_param, sub_gain, gain_one, gain_two) = take(4)
    (grad_down, grad_gate, grad_up, grad_out) = take(4)
    grad_qkv = take(3)
    (layer_out, grad_in) = take(2)
    small_outs = take(4)
    reducer_refs = take(20 if line_first(dp_count)[0] else 10)
    line_rights = reducer_refs.pop() if line_first(dp_count)[0] else None
    (left_a, left_b, rights, rows_qkv) = take(4)
    weights = take(4)
    kept = take(4)
    backward_scratch = take(4)
    (grad_sub, grad_lam) = take(2)
    sets = [take(3) for _ in range(2)]
    through = take(2)
    (spare, projected, attended, rows_in, rows_out) = take(5)
    (small, small_near, small_landed) = take(3)
    small_blocks = take(4)
    tables = take(4)
    (near_sems, far_sems, near_credit, far_credit) = take(4)
    (load_sems, small_near_sems, small_send, small_recv) = take(4)
    assert not refs

    me = lax.axis_index("dp")
    tensor = lax.axis_index("tensor")
    core = tensor % 2
    core_peer = tensor + 1 - 2 * core
    far_peer = tensor + 2 - 4 * (tensor // 2)
    line = dp_count // 2
    half = middle[0].shape[0]
    row_count = 2 * half
    head_count, head_width = sub_gain.shape
    sub_scale = sub_gain[...] * (1.0 - lambda_base)
    first_exp, second_exp, lam = lambda_terms(lambda_param)
    out_weight, projections = weights[0], weights[1:]
    inner = out_weight.shape[0]
    kept_half = pl.ds(pl.multiple_of(core * half, half), half)
    sent_half = pl.ds(pl.multiple_of((1 - core) * half, half), half)
    tokens = [slice(m * row_count, (m + 1) * row_count) for m in range(2)]

    barrier = pltpu.get_barrier_semaphore()
    for offset in range(1, dp_count):
        pl.semaphore_signal(
            barrier, inc=1, device_id={"dp": lax.rem(me + offset, dp_count)}, device_id_type=MESH
        )
    for peer in (core_peer, far_peer):
        pl.semaphore_signal(barrier, inc=1, device_id={"tensor": peer}, device_id_type=MESH)

    used = [0]

    def load(source, target):
        copy = pltpu.make_async_copy(source, target, load_sems.at[used[0]])
        used[0] += 1
        copy.start()
        return copy

    def wait_all(copies):
        for copy in copies:
            copy.wait()

    reducer_width = reducer_refs[0].shape[-1]
    plan, sources, left_loads, right_loads = [], {}, {}, {}

    def load_left(sources_of, left):
        return [load(sources_of[m], left.at[:, tokens[m]]) for m in range(2)]

    def load_columns(source, first, width, target):
        return [
            load(source[m].at[:, first : first + width], target.at[tokens[m], :width])
            for m in range(2)
        ]

    def load_right(c):
        if c in sources:
            right_loads[c] = load_columns(*sources[c], rights.at[c % 2])

    def load_line_right(c):
        if c < len(line_sources):
            line_loads[c] = load_columns(*line_sources[c], line_rights.at[c % 2])

    def get_left(c, left):
        wait_all(left_loads.pop(c, ()))
        return left

    def get_line_left(left):
        return left

    def get_right(c, first, width):
        if c in sources:
            wait_all(right_loads[c])
            return rights.at[c % 2, :, :width]
        return rows_qkv.at[:, first : first + width]

    def get_line_right(c):
        wait_all(line_loads[c])
        return line_rights.at[c % 2]

    def computed(c):
        load_right(c + 2)
        if c == last_two:
            left_loads[first_one] = load_left(one_left, left_b)

    def add_group(left, source, columns, out, line_chunks=0):
        start = line_chunks * line_width
        for first in range(0, start, line_width):
            c = len(line_plan)
            line_sources.append((source, first, line_width))
            line_plan.append(
                Chunk(
                    functools.partial(get_line_left, left),
                    functools.partial(get_line_right, c),
                    functools.partial(load_line_right, c + 2),
                    out,
                    first,
                    line_width,
                )
            )
        for first in range(start, columns, reducer_width):
            width = min(reducer_width, columns - first)
            c = len(plan)
            if source is not None:
                sources[c] = (source, first, width)
            plan.append(
                Chunk(
                    functools.partial(get_left, c, left),
                    functools.partial(get_right, c, first, width),
                    functools.partial(computed, c),
                    out,
                    first,
                    width,
                )
            )

    line_starts, line_counts = line_first(dp_count)
    line_plan, line_sources, line_loads, line_width = [], [], {}, 128
    add_group(left_a, hidden, hidden[0].shape[1], grad_down, line_counts[0])
    add_group(left_b, gate_pre, gate_pre[0].shape[1], grad_gate, line_counts[1])
    add_group(left_b, up_pre, up_pre[0].shape[1], grad_up)
    last_two = len(plan) - 1
    add_group(left_a, heads, inner, grad_out, line_counts[2])
    first_one = len(plan)
    add_group(left_b, None, 3 * inner, grad_qkv)

    left_loads[0] = load_left(cot_left, left_a)
    load_right(0)
    two_loads = [load(two_left[m], (attended, rows_out)[m]) for m in range(2)]
    load_line_right(0)
    load_line_right(1)
    load_right(1)
    sums = [
        TensorSum(
            3, *sets[m], near_sems.at[m], far_sems.at[m], near_credit.at[m], far_credit.at[m]
        )
        for m in range(2)
    ]
    own_loads = {m: load(part_back[m].at[kept_half], sets[m][0]) for m in range(2)}
    weight_loads = [load(*pair) for pair in zip(weights_in, weights)]
    def load_kept(m):
        pairs = zip([*kept_in[m], *tables_in[m]], [*kept, *tables[:2]])
        return [load(*pair) for pair in pairs]

    kept_loads = load_kept(0)
    spare_queue = [middle[0], middle[1], middle[0], middle[1]]
    rows_queue = [cotangent.at[0], cotangent.at[1]]
    rows_queue += [layer_in.at[0], cotangent.at[0], layer_in.at[1], cotangent.at[1]]
    queued = {}

    def next_spare():
        queued["spare"] = load(spare_queue.pop(0), spare) if spare_queue else None

    def next_rows():
        queued["rows"] = load(rows_queue.pop(0), rows_in) if rows_queue else None

    next_spare()
    next_rows()
    out_loads = []
    small[...] = jnp.zeros_like(small)

    def mine(rows):
        return pl.ds(pl.multiple_of(core * half + rows.start, row_group), row_group)

    def others(rows):
        return pl.ds(pl.multiple_of((1 - core) * half + rows.start, row_group), row_group)

    def flip_rows(source, left, m):
        def block(i, carry):
            at = pl.ds(pl.multiple_of(i * 128, 128), 128)
            left[at, tokens[m]] = source[:, at].T
            return carry

        lax.fori_loop(0, source.shape[1] // 128, block, 0)

    def flip_two():
        wait_all(two_loads)
        for m in range(2):
            flip_rows((attended, rows_out)[m], left_b, m)

    def exchange(m):
        if m in own_loads:
            own_loads.pop(m).wait()
        sums[m].near_add()
        sums[m].far_go()

    def norm_two(m):
        own, near, far = sets[m]
        queued["spare"].wait()
        sums[m].far_wait()

        def body(rows):
            grads = own[rows, :] + far[rows, :]
            values = spare[rows, :]
            root = root_of(values)
            small[1:2, :] += jnp.sum(grads * values * root, axis=0, keepdims=True)
            through[m][rows, :] = rms_back(grads * gain_two[...], values, root)

        for_rows(half, body)
        sums[m].far_free()
        sums[m].near_start(through[m])
        next_spare()

    def attend(m):
        near = sets[m][1]
        queued["rows"].wait()
        sums[m].near_wait()

        def body(rows):
            attended[mine(rows), :] = (
                rows_in[mine(rows), :].astype(jnp.float32) + through[m][rows, :]
            ).astype(jnp.bfloat16)
            attended[others(rows), :] = (
                rows_in[others(rows), :].astype(jnp.float32) + near[rows, :]
            ).astype(jnp.bfloat16)

        for_rows(half, body)
        sums[m].near_free()
        next_rows()

        flip_rows(attended, left_a, m)
        if m == 0:
            wait_all(weight_loads)
        wait_all(kept_loads)
        segments(lengths[m], *tables[2:])
        backward_kernel(
            lam, attended, out_weight, *kept, *tables, sub_scale,
            rows_qkv.at[tokens[m], :], grad_sub, grad_lam, *backward_scratch,
        )
        if m == 0:
            kept_loads[:] = load_kept(1)
        for head in range(head_count):
            at = slice(head * head_width, (head + 1) * head_width)
            small[2:3, at] += grad_sub[head : head + 1, :]
            small[3:4, at] += grad_lam[head : head + 1, :]

    def project(m):
        def part(which, target):
            rows = pl.ds(pl.multiple_of(m * row_count + which * half, half), half)

            def block(i, carry):
                at = pl.ds(pl.multiple_of(i * 512, 512), 512)
                total = 0.0
                for p in range(3):
                    grads = rows_qkv[rows, p * inner : (p + 1) * inner]
                    total = total + dot_t(grads, projections[p][at, :])
                target[:, at] = total
                return carry

            lax.fori_loop(0, target.shape[1] // 512, block, 0)

        part(1 - core, projected)
        sums[m].near_start(projected)
        part(core, sets[m][0])

    def norm_one(m):
        own, near, far = sets[m]
        queued["rows"].wait()
        sums[m].far_wait()

        def body(rows):
            grads = own[rows, :] + far[rows, :]
            values = rows_in[mine(rows), :].astype(jnp.float32)
            root = root_of(values)
            small[0:1, :] += jnp.sum(grads * values * root, axis=0, keepdims=True)
            through[m][rows, :] += rms_back(grads * gain_one[...], values, root)

        for_rows(half, body)
        sums[m].far_free()
        sums[m].near_start(through[m])
        next_rows()
        own_loads[m] = load(part_fed[m].at[kept_half], own)

    def store_rows(target):
        out_loads.append(load(rows_out, target))

    def finish_in(m):
        near = sets[m][1]
        queued["rows"].wait()
        sums[m].near_wait()
        wait_all(out_loads)
        out_loads.clear()

        def body(rows):
            rows_out[mine(rows), :] = (
                rows_in[mine(rows), :].astype(jnp.float32) + through[m][rows, :]
            ).astype(jnp.bfloat16)
            rows_out[others(rows), :] = (
                rows_in[others(rows), :].astype(jnp.float32) + near[rows, :]
            ).astype(jnp.bfloat16)

        for_rows(half, body)
        sums[m].near_free()
        next_rows()
        store_rows(grad_in.at[m])
        sums[m].near_start(part_fed[m].at[sent_half])

    def add_fed(m):
        own, near, far = sets[m]
        queued["spare"].wait()
        sums[m].far_wait()

        def body(rows):
            own[rows, :] = spare[rows, :] + (own[rows, :] + far[rows, :])

        for_rows(half, body)
        sums[m].far_free()
        sums[m].near_start(own)
        next_spare()

    def finish_out(m):
        own, near = sets[m][:2]
        sums[m].near_wait()
        wait_all(out_loads)
        out_loads.clear()

        def body(rows):
            rows_out[mine(rows), :] = own[rows, :].astype(jnp.bfloat16)
            rows_out[others(rows), :] = near[rows, :].astype(jnp.bfloat16)

        for_rows(half, body)
        sums[m].near_free()
        store_rows(layer_out.at[m])

    small_core = pltpu.make_async_remote_copy(
        src_ref=small, dst_ref=small_near, send_sem=small_near_sems.at[0],
        recv_sem=small_near_sems.at[1], device_id={"tensor": core_peer}, device_id_type=MESH,
    )

    def small_copy(offset):
        return pltpu.make_async_remote_copy(
            src_ref=small, dst_ref=small_landed.at[offset - 1], send_sem=small_send.at[offset - 1],
            recv_sem=small_recv.at[offset - 1],
            device_id={"dp": lax.rem(me + offset, dp_count)}, device_id_type=MESH,
        )

    def small_spread():
        small_core.wait()
        small[0:2, :] += small_near[0:2, :]
        for offset in range(1, dp_count):
            small_copy(offset).start()

    def small_finish():
        for offset in range(1, dp_count):
            small_copy(offset).wait()
        total = small[...]
        for offset in range(1, dp_count):
            total = total + small_landed[offset - 1]

        def own_block(values, target):
            count = target.shape[1]
            shift = lax.rem((dp_count - me) * count, count * dp_count)
            return pltpu.roll(values, shift, 1)[: target.shape[0], :count]

        norm_blocks, lambda_block, sub_block = small_blocks[:2], small_blocks[2], small_blocks[3]
        for row in range(2):
            norm_blocks[row][...] = own_block(total, norm_blocks[row][...])
            total = pltpu.roll(total, 7, 0)
        total = pltpu.roll(total, 2, 0)
        part = head_width // 2
        for head in range(head_count):
            at = slice(head * head_width, (head + 1) * head_width)
            sub_block[head : head + 1, :] = own_block(
                jnp.broadcast_to(total[2:3, at], (8, head_width)), sub_block[0:1, :]
            )
            grad = total[3:4, head * head_width : head * head_width + 1]
            param = lambda_param[head : head + 1, :]
            first = grad * first_exp[head : head + 1, :]
            second = grad * second_exp[head : head + 1, :]
            piece = lambda k: param[:, k * part : (k + 1) * part]
            full = jnp.concatenate(
                [first * piece(1), first * piece(0), -second * piece(3), -second * piece(2)], axis=1
            )
            lambda_block[head : head + 1, :] = own_block(
                jnp.broadcast_to(full, (8, 4 * part)), lambda_block[0:1, :]
            )
        out_loads.extend(load(*pair) for pair in zip(small_blocks, small_outs))

    order = {
        0: [flip_two, lambda: exchange(0)],
        2: [lambda: norm_two(0), lambda: exchange(1)],
        3: [lambda: attend(0), lambda: project(0)],
        4: [lambda: norm_two(1), lambda: exchange(0)],
        5: [lambda: attend(1), lambda: project(1)],
        6: [lambda: norm_one(0), lambda: exchange(1)],
        7: [lambda: finish_in(0)],
        8: [lambda: norm_one(1), lambda: exchange(0), small_core.start],
        9: [lambda: finish_in(1), small_spread],
        10: [lambda: add_fed(0), lambda: exchange(1), small_finish],
        11: [lambda: finish_out(0)],
        12: [lambda: add_fed(1)],
        13: [lambda: finish_out(1)],
    }
    stretch = 256 // reducer_width
    tasks = {slot * stretch: items for slot, items in order.items()}
    reducer = Reducer(plan, line_plan, line_starts, line, reducer_refs)
    reducer.compute(0)
    pl.semaphore_wait(barrier, dp_count + 1)
    reducer.pair_copy(0).start()
    for m in range(2):
        sums[m].near_start(part_back[m].at[sent_half])
    reducer.run(tasks)
    wait_all(out_loads)


def back_call(dp_count, lengths, arrays, blocks, shapes):
    depth, row_count, inner, hidden_count, head_count, head_width = shapes
    line = dp_count // 2
    rows = depth // dp_count
    half = row_count // 2
    width = 256 if line <= 4 else 128
    ring = line + 3
    starts = line_first(dp_count)[0]
    wide = (line, rows, width)
    bf16, f32 = jnp.bfloat16, jnp.float32
    dma, regular = pltpu.SemaphoreType.DMA, pltpu.SemaphoreType.REGULAR
    wide_half = pltpu.VMEM((half, depth), f32)
    wide_rows = pltpu.VMEM((row_count, depth), bf16)
    narrow = pltpu.VMEM((row_count, inner), bf16)
    narrow_f32 = pltpu.VMEM((row_count, inner), f32)
    small = pltpu.VMEM((8, depth), f32)
    grad = lambda columns: jax.ShapeDtypeStruct((rows, columns), f32)
    rows_shape = jax.ShapeDtypeStruct((2, row_count, depth), bf16)
    small_shapes = [jax.ShapeDtypeStruct((1, rows), f32)] * 2
    for count in (2 * head_width, head_width):
        small_shapes.append(jax.ShapeDtypeStruct((head_count, count // dp_count), f32))
    flops = 2 * 2 * row_count * depth * (3 * hidden_count + 8 * inner)
    return pl.pallas_call(
        functools.partial(back_kernel, dp_count),
        out_shape=[grad(hidden_count)] * 3
        + [grad(inner)] * 4
        + [rows_shape] * 2
        + small_shapes,
        in_specs=[pl.BlockSpec(memory_space=pltpu.SMEM)] * 2
        + [pl.BlockSpec(memory_space=pl.ANY)] * len(arrays)
        + in_vmem(len(blocks)),
        out_specs=[pl.BlockSpec(memory_space=pl.ANY)] * 13,
        scratch_shapes=[
            pltpu.VMEM((send_slots,) + wide, f32),
            pltpu.VMEM((held_slots,) + wide, f32),
            pltpu.VMEM((ring,) + wide, f32),
            pltpu.VMEM((2, line - 1, 2, rows, width), f32),
            dma((send_slots,)),
            dma((held_slots,)),
            dma((2, line - 1, 2)),
            dma((2, line - 1, 2)),
            regular((2, line - 1)),
            dma((ring, 2)),
        ]
        + (
            [
                pltpu.VMEM((3, line, 2 * rows, 128), f32),
                pltpu.VMEM((2, line - 1, 2, 2 * rows, 128), f32),
                dma((2, line - 1, 2)),
                dma((2, line - 1, 2)),
                regular((2, line - 1)),
                pltpu.VMEM((len(starts), rows, 128), f32),
                dma((len(starts),)),
                dma((len(starts),)),
                dma((3,)),
                pltpu.VMEM((2, 2 * row_count, 128), bf16),
            ]
            if starts
            else []
        )
        + [
            pltpu.VMEM((depth, 2 * row_count), bf16),
            pltpu.VMEM((depth, 2 * row_count), bf16),
            pltpu.VMEM((2, 2 * row_count, width), bf16),
            pltpu.VMEM((2 * row_count, 3 * inner), bf16),
            pltpu.VMEM((inner, depth), bf16),
        ]
        + [pltpu.VMEM((depth, inner), bf16)] * 3
        + [narrow, narrow, narrow, narrow_f32]
        + [narrow_f32, narrow, narrow_f32, narrow_f32]
        + [pltpu.VMEM((head_count, head_width), f32)] * 2
        + [wide_half] * 10
        + [wide_rows] * 3
        + [
            small,
            small,
            pltpu.VMEM((dp_count - 1, 8, depth), f32),
            *[pltpu.VMEM(item.shape, f32) for item in small_shapes],
            pltpu.VMEM((row_count, head_width), f32),
            pltpu.VMEM((row_count, head_width), f32),
            pltpu.VMEM((row_count, 1), jnp.int32),
            pltpu.VMEM((1, row_count), jnp.int32),
            dma((2, 2)),
            dma((2, 2)),
            regular((2,)),
            regular((2,)),
            dma((128,)),
            dma((2,)),
            dma((dp_count - 1,)),
            dma((dp_count - 1,)),
        ],
        compiler_params=pltpu.CompilerParams(
            collective_id=0, has_side_effects=True, vmem_limit_bytes=62 * 1024 * 1024
        ),
        cost_estimate=pl.CostEstimate(flops=flops, bytes_accessed=64 << 20, transcendentals=0),
    )(*lengths, *arrays, *blocks)


def gathers_heads(dp_count):
    return dp_count == 8


class Gather:
    def __init__(self, own, piece, wide, far, near, far_near, full, sems):
        self.own, self.piece, self.wide = own, piece, wide
        self.far, self.near, self.far_near, self.full = far, near, far_near, full
        (
            self.cross_sems, self.line_out, self.line_in, self.pair_out, self.pair_in,
            self.near_sems,
        ) = sems
        self.me = lax.axis_index("dp")
        self.place, self.side = self.me // 2, self.me % 2
        self.line = self.line_out.shape[1] + 1
        self.rows = piece.shape[0]
        tensor = lax.axis_index("tensor")
        self.tensor = tensor
        self.core_peer = tensor + 1 - 2 * (tensor % 2)
        self.far_peer = tensor + 2 - 4 * (tensor // 2)
        self.diagonal = self.far_peer + 1 - 2 * (tensor % 2)

    def slot(self, side, place):
        start = (side * self.line + place) * self.rows
        return self.far.at[pl.ds(pl.multiple_of(start, self.rows), self.rows)]

    def remote(self, source, target, send, recv, device):
        return pltpu.make_async_remote_copy(
            src_ref=source, dst_ref=target, send_sem=send, recv_sem=recv, device_id=device,
            device_id_type=MESH,
        )

    def cross(self):
        return self.remote(
            self.piece, self.slot(self.side, self.place), self.cross_sems.at[0],
            self.cross_sems.at[1], {"tensor": self.far_peer},
        )

    def near_copy(self, index):
        half = self.line * self.rows
        if index == 0:
            source, target = self.wide, self.near
        else:
            start = (self.side if index == 1 else 1 - self.side) * half
            rows = pl.ds(pl.multiple_of(start, self.rows), half)
            source, target = self.far.at[rows], self.far_near.at[rows]
        return self.remote(
            source, target, self.near_sems.at[0, index], self.near_sems.at[1, index],
            {"tensor": self.core_peer},
        )

    def line_copy(self, way, step):
        place = self.place - step if way == 0 else self.place + step
        slot = self.slot(self.side, place)
        return self.remote(
            slot, slot, self.line_out.at[way, step], self.line_in.at[way, step],
            {"dp": self.me + 2 - 4 * way},
        )

    def line_sends(self, way, step):
        if way == 0:
            return (self.place >= step) & (self.place < self.line - 1)
        return (self.place + step <= self.line - 1) & (self.place > 0)

    def line_gets(self, way, step):
        if way == 0:
            return self.place >= step
        return self.place + step <= self.line - 1

    def pair_copy(self, index, place):
        slot = self.slot(self.side, place)
        return self.remote(
            slot, slot, self.pair_out.at[index], self.pair_in.at[index],
            {"dp": self.me + 1 - 2 * self.side},
        )

    def pair_index(self, way, step):
        return 1 + way * (self.line - 1) + step - 1

    def begin(self):
        count = self.own.shape[0]
        rows = pl.ds(pl.multiple_of(self.me * self.rows, self.rows), self.rows)
        self.piece[...] = self.own[rows, :].astype(jnp.float32)
        self.cross().start()

        def widen(rows):
            self.wide[rows, :] = self.own[rows, :].astype(jnp.float32)

        for_rows(count, widen)
        self.near_copy(0).start()

    def forward(self, step):
        if step == 0:
            self.cross().wait()
            self.pair_copy(0, self.place).start()
        for way in range(2):
            if step:

                @pl.when(self.line_gets(way, step))
                def _():
                    self.line_arrival(way, step).wait_recv()
                    place = self.place - step if way == 0 else self.place + step
                    self.pair_copy(self.pair_index(way, step), place).start()

            if step < self.line - 1:

                @pl.when(self.line_sends(way, step))
                def _():
                    self.line_copy(way, step).start()

    def line_arrival(self, way, step):
        place = self.place - step if way == 0 else self.place + step
        slot = self.slot(self.side, place)
        return self.remote(
            slot, slot, self.line_out.at[way, step - 1], self.line_in.at[way, step - 1],
            {"dp": self.me - 2 + 4 * way},
        )

    def store(self, source, tensor, first, count):
        block = self.own.shape[0]

        def narrow(rows):
            at = pl.ds(pl.multiple_of(tensor * block + first + rows.start, row_group), row_group)
            self.full[at, :] = source[rows, :].astype(jnp.bfloat16)

        for_rows(count, narrow)

    def store_far(self, source, tensor):
        for side in range(2):
            for place in range(self.line):
                rows = pl.ds((side * self.line + place) * self.rows, self.rows)
                self.store(source.at[rows], tensor, (2 * place + side) * self.rows, self.rows)

    def finish_line(self):
        self.near_copy(1).start()
        for way in range(2):
            for step in range(self.line - 1):

                @pl.when(self.line_sends(way, step))
                def _():
                    self.line_copy(way, step).wait_send()

        block = self.own.shape[0]
        self.store(self.own, self.tensor, 0, block)
        self.near_copy(0).wait()
        self.store(self.near, self.core_peer, 0, block)

    def finish(self):
        for index in range(1 + 2 * (self.line - 1)):
            if index == 0:
                self.pair_copy(0, self.place).wait()
                continue
            way, step = (index - 1) // (self.line - 1), (index - 1) % (self.line - 1) + 1

            @pl.when(self.line_gets(way, step))
            def _():
                place = self.place - step if way == 0 else self.place + step
                slot = self.slot(1 - self.side, place)
                self.pair_copy(index, place).wait_send()
                self.remote(
                    slot, slot, self.pair_out.at[index], self.pair_in.at[index],
                    {"dp": self.me + 1 - 2 * self.side},
                ).wait_recv()

        self.near_copy(2).start()
        self.store_far(self.far, self.far_peer)
        self.near_copy(1).wait()
        self.near_copy(2).wait()
        self.store_far(self.far_near, self.diagonal)


def front_kernel(dp_count, *refs):
    refs = list(refs)
    take = lambda n: [refs.pop(0) for _ in range(n)]
    lengths = take(2)
    layer_in, cotangent = take(2)
    weights_in = take(7)
    (lambda_param, sub_gain, gain_one, gain_two) = take(4)
    outs = [take(16) for _ in range(2)]
    cosines, sines = take(2), take(2)
    (segment_column, segment_row) = take(2)
    rows_in, cot_rows = take(2), take(2)
    (normed_one, normed_two, flipped) = take(3)
    weights = take(7)
    kept = take(5)
    hidden = take(3)
    (back, fed) = take(2)
    (near_sems, load_sems) = take(2)
    gathers = gathers_heads(dp_count)
    if gathers:
        sets = [take(2) for _ in range(2)]
        heads_wide, heads_landed = take(2), take(2)
        (heads_full, piece, wide, near_weight, full_weight, heads_sems) = take(6)
        gather_sems = take(6)
    else:
        sets = [take(3) for _ in range(2)]
        (projected, far_sems, near_credit) = take(3)
    assert not refs

    tensor = lax.axis_index("tensor")
    core = tensor % 2
    out_weight, gate_weight, up_weight, down_weight = weights[3:]
    row_count, depth = normed_one.shape
    half = row_count // 2
    hidden_count = gate_weight.shape[1]
    used = [0]

    def load(source, target):
        copy = pltpu.make_async_copy(source, target, load_sems.at[used[0]])
        used[0] += 1
        copy.start()
        return copy

    def wait_all(copies):
        for copy in copies:
            copy.wait()
        copies.clear()

    out_weight_load = load(weights_in[3], weights[3])
    rows_loads = [load(layer_in.at[0], rows_in[0])]
    weight_loads = [load(*pair) for pair in zip(weights_in[:3], weights[:3])]
    rows_loads.append(load(layer_in.at[1], rows_in[1]))
    cot_loads = [load(cotangent.at[m], cot_rows[m]) for m in range(2)]
    wide_loads = [load(*pair) for pair in zip(weights_in[4:], weights[4:])]

    sub_scale = sub_gain[...] * (1.0 - lambda_base)
    lam = lambda_terms(lambda_param)[2]
    barrier = pltpu.get_barrier_semaphore()
    core_peer, far_peer = tensor + 1 - 2 * core, tensor + 2 - 4 * (tensor // 2)
    diagonal = far_peer + 1 - 2 * core
    me = lax.axis_index("dp")
    for peer in (core_peer, far_peer, diagonal):
        pl.semaphore_signal(barrier, inc=1, device_id={"tensor": peer}, device_id_type=MESH)
    if gathers:
        for offset in range(1, dp_count):
            target = lax.rem(me + offset, dp_count)
            pl.semaphore_signal(barrier, inc=1, device_id={"dp": target}, device_id_type=MESH)
    pl.semaphore_wait(barrier, dp_count + 2 if gathers else 3)
    if gathers:
        sums = [
            TensorSum(1, *sets[m], None, near_sems.at[m], None, None, None) for m in range(2)
        ]
        for item in sums:
            item.near_left = 1
        gather = Gather(
            weights[3], piece, wide, back, near_weight, fed, full_weight, gather_sems
        )
    else:
        sums = [
            TensorSum(1, *sets[m], near_sems.at[m], far_sems.at[m], near_credit.at[m], None)
            for m in range(2)
        ]
    out_loads, flip_loads, wide_outs, hidden_outs = [], [], [], []

    def mine(rows):
        return pl.ds(pl.multiple_of(core * half + rows.start, row_group), row_group)

    def others(rows):
        return pl.ds(pl.multiple_of((1 - core) * half + rows.start, row_group), row_group)

    def flip_to(source, target):
        wait_all(flip_loads)

        def block(i, carry):
            at = pl.ds(pl.multiple_of(i * 128, 128), 128)
            flipped[at, :] = source[:, at].T
            return carry

        lax.fori_loop(0, depth // 128, block, 0)
        flip_loads.append(load(flipped, target))

    def heads_copy(m, index):
        peer = (core_peer, far_peer, diagonal)[index]
        which = core if index == 1 else 1 - core
        rows = pl.ds(pl.multiple_of(which * half, half), half)
        return pltpu.make_async_remote_copy(
            src_ref=heads_wide[m].at[rows], dst_ref=heads_landed[m].at[index],
            send_sem=heads_sems.at[m, 0, index], recv_sem=heads_sems.at[m, 1, index],
            device_id={"tensor": peer}, device_id_type=MESH,
        )

    def join_heads(m):
        own = sets[m][0]
        inner = kept[4].shape[1]

        def place_of(index):
            return pl.ds(pl.multiple_of(index * inner, inner), inner)

        rows = pl.ds(pl.multiple_of(core * half, half), half)
        heads_full[:, place_of(tensor)] = heads_wide[m][rows, :].astype(jnp.bfloat16)
        for index, peer in enumerate((core_peer, far_peer, diagonal)):
            heads_copy(m, index).wait()
            heads_full[:, place_of(peer)] = heads_landed[m][index].astype(jnp.bfloat16)

        def block(i, carry):
            at = pl.ds(pl.multiple_of(i * 512, 512), 512)
            values = rows_in[m][rows, at].astype(jnp.float32)
            own[:, at] = values + f32_dot(heads_full[...], full_weight[:, at])
            return carry

        lax.fori_loop(0, depth // 512, block, 0)

    def attend(m, between):
        rows_loads[m].wait()
        wait_all(weight_loads)
        wait_all(out_loads)
        segments(lengths[m], segment_column, segment_row)
        out_loads.extend([load(cosines[m], outs[m][14]), load(sines[m], outs[m][15])])
        forward_kernel(
            lam, rows_in[m], gain_one, *weights[:3], cosines[m], sines[m], segment_column,
            segment_row, sub_scale, normed_one, *kept,
            between,
        )
        heads = kept[4]
        if gathers:
            heads_wide[m][...] = heads[...].astype(jnp.float32)
            for index in range(3):
                heads_copy(m, index).start()
            out_loads.extend(load(*pair) for pair in zip(kept, outs[m][3:8]))
            flip_to(normed_one, outs[m][2])
            return

        def part(which, target):
            rows = pl.ds(pl.multiple_of(which * half, half), half)

            def block(i, carry):
                at = pl.ds(pl.multiple_of(i * 512, 512), 512)
                target[:, at] = f32_dot(heads[rows, :], out_weight[:, at])
                return carry

            lax.fori_loop(0, depth // 512, block, 0)

        part(1 - core, projected)
        sums[m].near_start(projected)
        part(core, sets[m][0])
        out_loads.extend(load(*pair) for pair in zip(kept, outs[m][3:8]))
        flip_to(normed_one, outs[m][2])
        sums[m].near_add()

    def norm_rows(values):
        return (values * root_of(values) * gain_two[...]).astype(jnp.bfloat16)

    def join(m):
        own = sets[m][0]
        if gathers:
            join_heads(m)
        else:
            far = sets[m][2]

            def add(rows):
                values = rows_in[m][mine(rows), :].astype(jnp.float32)
                own[rows, :] = values + (own[rows, :] + far[rows, :])

            for_rows(half, add)
        sums[m].near_start(own)
        out_loads.append(load(own, outs[m][8]))

    def norm(m):
        own, near = sets[m][:2]

        def norm_mine(rows):
            normed_two[mine(rows), :] = norm_rows(own[rows, :])

        def norm_others(rows):
            normed_two[others(rows), :] = norm_rows(near[rows, :])

        wait_all(out_loads)
        for_rows(half, norm_mine)
        sums[m].near_wait()
        for_rows(half, norm_others)
        sums[m].near_free()
        out_loads.append(load(normed_two, outs[m][1]))

    def feed(m, between):
        inside, gate_pre, up_pre = hidden
        if m == 0:
            wait_all(wide_loads)
        wait_all(hidden_outs)

        def block(j, carry):
            at = pl.ds(pl.multiple_of(j * 256, 256), 256)
            gate = f32_dot(normed_two[...], gate_weight[:, at])
            upward = f32_dot(normed_two[...], up_weight[:, at])
            grads = dot_t(cot_rows[m][...], down_weight[at, :])
            sigmoid = jax.nn.sigmoid(gate)
            inside[:, at] = (gate * sigmoid * upward).astype(jnp.bfloat16)
            gate_pre[:, at] = (
                grads * upward * sigmoid * (1.0 + gate * (1.0 - sigmoid))
            ).astype(jnp.bfloat16)
            up_pre[:, at] = (grads * gate * sigmoid).astype(jnp.bfloat16)
            return carry

        lax.fori_loop(0, hidden_count // 256, block, 0, unroll=True)
        hidden_outs.extend(load(*pair) for pair in zip(hidden, outs[m][9:12]))
        between()
        wait_all(wide_outs)

        for i in range(depth // 512):
            at = slice(i * 512, (i + 1) * 512)
            back[:, at] = dot_t(gate_pre[...], gate_weight[at, :]) + dot_t(
                up_pre[...], up_weight[at, :]
            )
            fed[:, at] = f32_dot(inside[...], down_weight[:, at])
            wide_outs.append(load(back.at[:, at], outs[m][12].at[:, at]))
            wide_outs.append(load(fed.at[:, at], outs[m][13].at[:, at]))

    def flip_cot(m):
        cot_loads[m].wait()
        flip_to(cot_rows[m], outs[m][0])

    if gathers:
        out_weight_load.wait()
        gather.begin()
        rotary_tables(lengths, cosines, sines, lambda_param.shape[1] // 4)
        attend(0, {1: lambda: gather.forward(0)})
        attend(1, {0: lambda: gather.forward(1)})
        gather.forward(2)
        flip_cot(0)
        flip_cot(1)
        gather.forward(3)
        gather.finish_line()
        gather.finish()
    else:
        out_weight_load.wait()
        rotary_tables(lengths, cosines, sines, lambda_param.shape[1] // 4)
        attend(0, {})
        sums[0].far_go()
        attend(1, {})
        flip_cot(0)
        flip_cot(1)
        sums[0].far_wait()
        sums[1].far_go()
    join(0)
    norm(0)
    if gathers:
        feed(0, lambda: join(1))
    else:
        feed(0, lambda: None)
        sums[1].far_wait()
        join(1)
    norm(1)
    feed(1, lambda: None)
    wait_all(flip_loads)
    wait_all(hidden_outs)
    wait_all(wide_outs)
    wait_all(out_loads)


def front_call(dp_count, lengths, arrays, blocks, shapes):
    depth, row_count, inner, hidden_count, head_count, head_width = shapes
    bf16, f32 = jnp.bfloat16, jnp.float32
    dma, regular = pltpu.SemaphoreType.DMA, pltpu.SemaphoreType.REGULAR
    half = row_count // 2
    out_shape = []
    for m in range(2):
        out_shape += [jax.ShapeDtypeStruct((depth, row_count), bf16)]
        out_shape += [jax.ShapeDtypeStruct((row_count, depth), bf16)]
        out_shape += [jax.ShapeDtypeStruct((depth, row_count), bf16)]
        out_shape += [jax.ShapeDtypeStruct((row_count, inner), bf16)] * 3
        out_shape += [jax.ShapeDtypeStruct((row_count, inner), f32)]
        out_shape += [jax.ShapeDtypeStruct((row_count, inner), bf16)]
        out_shape += [jax.ShapeDtypeStruct((half, depth), f32)]
        out_shape += [jax.ShapeDtypeStruct((row_count, hidden_count), bf16)] * 3
        out_shape += [jax.ShapeDtypeStruct((row_count, depth), f32)] * 2
        out_shape += [jax.ShapeDtypeStruct((row_count, head_width), f32)] * 2
    wide_rows = pltpu.VMEM((row_count, depth), bf16)
    narrow = pltpu.VMEM((row_count, inner), bf16)
    wide_half = pltpu.VMEM((half, depth), f32)
    if gathers_heads(dp_count):
        steps = dp_count // 2 - 1
        extra = [wide_half] * 4
        extra += [pltpu.VMEM((row_count, inner), f32)] * 2
        extra += [pltpu.VMEM((3, half, inner), f32)] * 2
        extra += [
            pltpu.VMEM((half, depth), bf16),
            pltpu.VMEM((inner // dp_count, depth), f32),
            pltpu.VMEM((inner, depth), f32),
            pltpu.VMEM((inner, depth), f32),
            pltpu.VMEM((depth, depth), bf16),
            dma((2, 2, 3)),
            dma((2,)),
            dma((2, steps)),
            dma((2, steps)),
            dma((1 + 2 * steps,)),
            dma((1 + 2 * steps,)),
            dma((2, 3)),
        ]
    else:
        extra = [wide_half] * 7 + [dma((2, 2)), regular((2,))]
    return pl.pallas_call(
        functools.partial(front_kernel, dp_count),
        out_shape=out_shape,
        in_specs=[pl.BlockSpec(memory_space=pltpu.SMEM)] * 2
        + [pl.BlockSpec(memory_space=pl.ANY)] * len(arrays)
        + in_vmem(len(blocks)),
        out_specs=[pl.BlockSpec(memory_space=pl.ANY)] * len(out_shape),
        scratch_shapes=[pltpu.VMEM((row_count, head_width), f32)] * 4
        + [pltpu.VMEM((row_count, 1), jnp.int32), pltpu.VMEM((1, row_count), jnp.int32)]
        + [wide_rows] * 6
        + [pltpu.VMEM((depth, row_count), bf16)]
        + [pltpu.VMEM((depth, inner), bf16)] * 3
        + [pltpu.VMEM((inner, depth), bf16)]
        + [pltpu.VMEM((depth, hidden_count), bf16)] * 2
        + [pltpu.VMEM((hidden_count, depth), bf16)]
        + [narrow, narrow, narrow, pltpu.VMEM((row_count, inner), f32), narrow]
        + [pltpu.VMEM((row_count, hidden_count), bf16)] * 3
        + [pltpu.VMEM((row_count, depth), f32)] * 2
        + [dma((2, 2)), dma((64,))]
        + extra,
        compiler_params=pltpu.CompilerParams(
            collective_id=1, has_side_effects=True, vmem_limit_bytes=62 * 1024 * 1024
        ),
        cost_estimate=pl.CostEstimate(
            flops=4 * row_count * depth * (6 * hidden_count + 4 * inner),
            bytes_accessed=64 << 20,
            transcendentals=0,
        ),
    )(*lengths, *arrays, *blocks)


def settle_kernel(count, *refs):
    sources, targets, held = refs[:count], refs[count : 2 * count], refs[2 * count : 3 * count]
    in_sems, out_sems = refs[3 * count :]

    def parts(k):
        rows = sources[k].shape[0]
        pieces = rows if len(sources[k].shape) == 3 else 1
        return [slice(i * rows // pieces, (i + 1) * rows // pieces) for i in range(pieces)]

    pieces = [(k, i, at) for k in range(count) for i, at in enumerate(parts(k))]
    loads = [
        pltpu.make_async_copy(sources[k].at[at], held[k].at[at], in_sems.at[k, i])
        for k, i, at in pieces
    ]
    stores = [
        pltpu.make_async_copy(held[k].at[at], targets[k].at[at], out_sems.at[k, i])
        for k, i, at in pieces
    ]
    for copy in loads:
        copy.start()
    for load, store in zip(loads, stores):
        load.wait()
        store.start()
    for store in stores:
        store.wait()


def settle(arrays):
    count = len(arrays)
    return pl.pallas_call(
        functools.partial(settle_kernel, count),
        out_shape=[jax.ShapeDtypeStruct(item.shape, item.dtype) for item in arrays],
        in_specs=[pl.BlockSpec(memory_space=pl.ANY)] * count,
        out_specs=[pl.BlockSpec(memory_space=pl.ANY)] * count,
        scratch_shapes=[pltpu.VMEM(item.shape, item.dtype) for item in arrays]
        + [pltpu.SemaphoreType.DMA((count, 2))] * 2,
        compiler_params=pltpu.CompilerParams(vmem_limit_bytes=62 * 1024 * 1024),
    )(*arrays)


def on_device(
    layer_in,
    short_lengths,
    long_lengths,
    norm1_gain,
    query_weight,
    key_weight,
    value_weight,
    lambda_param,
    sub_gain,
    out_weight,
    norm2_gain,
    gate_weight,
    up_weight,
    down_weight,
    out_cotangent,
):
    dp_count = lax.axis_size("dp")
    projections = [query_weight, key_weight, value_weight]
    depth, inner = query_weight.shape
    shapes = (depth, layer_in.shape[1], inner, gate_weight.shape[1], *sub_gain.shape)
    lengths = [short_lengths, long_lengths]
    blocks = [lambda_param, sub_gain, norm1_gain, norm2_gain]
    arrays = [layer_in, out_cotangent, *projections, out_weight]
    arrays += [gate_weight, up_weight, down_weight]
    parts = front_call(dp_count, lengths, arrays, blocks, shapes)
    pick = lambda at: [parts[at], parts[at + 16]]
    arrays = pick(0) + pick(1) + pick(2) + pick(9) + pick(10) + pick(11) + pick(7)
    arrays += pick(12) + pick(13) + pick(8)
    arrays += [layer_in, out_cotangent, out_weight, *projections]
    arrays += parts[3:7] + parts[19:23] + parts[14:16] + parts[30:32]
    (
        grad_down, grad_gate, grad_up, grad_out, grad_query, grad_key, grad_value, layer_out,
        grad_in, grad_norm1, grad_norm2, grad_lambda, grad_sub,
    ) = back_call(dp_count, lengths, arrays, blocks, shapes)
    (
        layer_out, grad_in, grad_down, grad_out, grad_query, grad_key, grad_value, grad_gate,
        grad_up, grad_lambda, grad_sub,
    ) = settle(
        [
            layer_out, grad_in, grad_down, grad_out, grad_query, grad_key, grad_value, grad_gate,
            grad_up, grad_lambda, grad_sub,
        ]
    )
    return (
        layer_out,
        grad_in,
        grad_norm1.reshape(-1),
        grad_query,
        grad_key,
        grad_value,
        grad_lambda,
        grad_sub,
        grad_out.T,
        grad_norm2.reshape(-1),
        grad_gate,
        grad_up,
        grad_down.T,
    )


def solution(mesh):
    return jax.shard_map(
        on_device,
        mesh=mesh,
        in_specs=(
            P(None, "dp", None),
            P("dp", None),
            P("dp", None),
            P(),
            P(None, "tensor"),
            P(None, "tensor"),
            P(None, "tensor"),
            P("tensor", None),
            P("tensor", None),
            P("tensor", None),
            P(),
            P(None, "tensor"),
            P(None, "tensor"),
            P("tensor", None),
            P(None, "dp", None),
        ),
        out_specs=(
            P(None, "dp", None),
            P(None, "dp", None),
            P("dp"),
            P("dp", "tensor"),
            P("dp", "tensor"),
            P("dp", "tensor"),
            P("tensor", "dp"),
            P("tensor", "dp"),
            P("tensor", "dp"),
            P("dp"),
            P("dp", "tensor"),
            P("dp", "tensor"),
            P("tensor", "dp"),
        ),
        check_vma=False,
    )
```

```python
import functools
import math

import jax
import jax.numpy as jnp
from jax import lax
from jax.experimental import pallas as pl
from jax.experimental.pallas import tpu as pltpu
from jax.sharding import PartitionSpec as P

norm_epsilon = 1e-05
lambda_base = 0.8 - 0.6 * math.exp(-0.3 * 11.0)
rotary_base = 10000.0
closed_score = -1e30
block_rows = 128
longest_document = 256
row_group = 16
send_slots = 3
held_slots = 4
MESH = pl.DeviceIdType.MESH


def documents(lengths, places):
    end, segment, start = 0, 0, 0
    for k in range(lengths.shape[1]):
        length = lengths[0, k]
        end = end + length
        passed = (places >= end).astype(jnp.int32)
        segment = segment + passed
        start = start + passed * length
    return segment, start


def segments(lengths, column, row):
    column[...] = documents(lengths, lax.broadcasted_iota(jnp.int32, column.shape, 0))[0]
    row[...] = documents(lengths, lax.broadcasted_iota(jnp.int32, row.shape, 1))[0]


def rotary_tables(lengths, cosines, sines, map_width):
    half_width = map_width // 2
    row_count, width = cosines[0].shape
    lane = lax.broadcasted_iota(jnp.int32, (block_rows, width), 1)
    frequency = jnp.zeros((block_rows, width), jnp.float32)
    for k in range(half_width):
        value = rotary_base ** (-2.0 * k / map_width)
        frequency = jnp.where(lane % half_width == k, value, frequency)

    def block(i, carry):
        rows = pl.ds(pl.multiple_of(i * block_rows, block_rows), block_rows)
        places = lax.broadcasted_iota(jnp.int32, (block_rows, width), 0) + i * block_rows
        starts = [documents(item, places)[1] for item in lengths]
        start = jnp.where(lane < half_width, starts[0], starts[1])
        angles = (places - start).astype(jnp.float32) * frequency

        def spread(values, m):
            base = jnp.where(lane // half_width == m, values, 0.0)
            return sum(
                (pltpu.roll(base, k * half_width, 1) for k in range(1, width // half_width)), base
            )

        cosine, sine = jnp.cos(angles), jnp.sin(angles)
        for m in range(2):
            cosines[m][rows, :] = spread(cosine, m)
            signed = spread(sine, m)
            sines[m][rows, :] = jnp.where(lane % map_width < half_width, -signed, signed)
        return carry

    lax.fori_loop(0, row_count // block_rows, block, 0)


def lambda_terms(param):
    width = param.shape[1] // 4
    part = lambda k: param[:, k * width : (k + 1) * width]
    first = jnp.exp(jnp.sum(part(0) * part(1), axis=-1, keepdims=True))
    second = jnp.exp(jnp.sum(part(2) * part(3), axis=-1, keepdims=True))
    return first, second, first - second + lambda_base


def turn(values, cosine, sine):
    width = values.shape[-1]
    quarter = width // 4
    lane = lax.broadcasted_iota(jnp.int32, values.shape, 1)
    partner = jnp.where(
        lane % (2 * quarter) < quarter,
        pltpu.roll(values, width - quarter, 1),
        pltpu.roll(values, quarter, 1),
    )
    return values * cosine + partner * sine


def map_of(values, which):
    lane = lax.broadcasted_iota(jnp.int32, values.shape, 1)
    mine = (lane >= values.shape[-1] // 2) == (which == 1)
    return jnp.where(mine, values, jnp.zeros_like(values))


def key_range(block):
    first = max(0, block * block_rows - longest_document + 1) // block_rows * block_rows
    return first, (block + 1) * block_rows


def open_pairs(block, segment_column, segment_row):
    first, last = key_range(block)
    rows = pl.ds(block * block_rows, block_rows)
    shape = (block_rows, last - first)
    row_at = lax.broadcasted_iota(jnp.int32, shape, 0) + block * block_rows
    key_at = lax.broadcasted_iota(jnp.int32, shape, 1) + first
    return (segment_column[rows, :] == segment_row[:, first:last]) & (key_at <= row_at)


def softmax_map(query, key, opened, scale):
    scores = jnp.where(opened, dot_t(query, key) * scale, closed_score)
    expanded = jnp.exp(scores - jnp.max(scores, axis=-1, keepdims=True))
    return expanded * (1.0 / jnp.sum(expanded, axis=-1, keepdims=True))


def f32_dot(left, right):
    return jnp.dot(left, right, preferred_element_type=jnp.float32)


def dot_t(left, right):
    return lax.dot_general(
        left, right, (((1,), (1,)), ((), ())), preferred_element_type=jnp.float32
    )


def dot_rows(left, right):
    return lax.dot_general(
        left, right, (((0,), (0,)), ((), ())), preferred_element_type=jnp.float32
    )


def rms_back(incoming, values, inverse_root):
    return inverse_root * incoming - values * inverse_root**3 * jnp.mean(
        incoming * values, axis=-1, keepdims=True
    )


def root_of(values):
    return lax.rsqrt(jnp.mean(values * values, axis=-1, keepdims=True) + norm_epsilon)


def forward_kernel(
    lam, rows, gain, query_weight, key_weight, value_weight, cosine, sine, segment_column,
    segment_row, sub_scale, normed_one, query, key, value, mixed, heads_out, between,
):
    head_count, width = sub_scale.shape
    scale = (width // 2) ** (-0.5)
    values = rows[...].astype(jnp.float32)
    normed_one[...] = (values * root_of(values) * gain[...]).astype(jnp.bfloat16)
    raw_query = f32_dot(normed_one[...], query_weight[...])
    raw_key = f32_dot(normed_one[...], key_weight[...])
    value[...] = f32_dot(normed_one[...], value_weight[...]).astype(jnp.bfloat16)
    for head in range(head_count):
        at = slice(head * width, (head + 1) * width)
        query[:, at] = turn(raw_query[:, at], cosine[...], sine[...]).astype(jnp.bfloat16)
        key[:, at] = turn(raw_key[:, at], cosine[...], sine[...]).astype(jnp.bfloat16)
    for block in range(rows.shape[0] // block_rows):
        first, last = key_range(block)
        here = slice(block * block_rows, last)
        opened = open_pairs(block, segment_column, segment_row)
        if block in between:
            between[block]()
        for head in range(head_count):
            at = slice(head * width, (head + 1) * width)
            keys = key[first:last, at]
            maps = [softmax_map(map_of(query[here, at], c), keys, opened, scale) for c in range(2)]
            combined = (maps[0] - lam[head : head + 1, :] * maps[1]).astype(jnp.bfloat16)
            out = f32_dot(combined, value[first:last, at])
            mixed[here, at] = out
            heads_out[here, at] = (out * root_of(out) * sub_scale[head : head + 1, :]).astype(
                jnp.bfloat16
            )


def backward_kernel(
    lam, grad_attended, out_weight, query, key, value, mixed, cosine, sine, segment_column,
    segment_row, sub_scale, grad_rows, grad_sub, grad_lam, grad_heads, grad_mixed, grad_key,
    grad_value,
):
    head_count, width = sub_scale.shape
    row_count = query.shape[0]
    inner = head_count * width
    scale = (width // 2) ** (-0.5)
    grad_heads[...] = dot_t(grad_attended[...], out_weight[...])
    for head in range(head_count):
        at = slice(head * width, (head + 1) * width)
        heads = mixed[:, at]
        root = root_of(heads)
        grads = grad_heads[:, at]
        grad_sub[head : head + 1, :] = jnp.sum(grads * heads * root, axis=0, keepdims=True) * (
            1.0 - lambda_base
        )
        grad_mixed[:, at] = rms_back(grads * sub_scale[head : head + 1, :], heads, root).astype(
            jnp.bfloat16
        )
    grad_key[...] = jnp.zeros_like(grad_key)
    grad_value[...] = jnp.zeros_like(grad_value)
    lam_sums = [0.0] * head_count
    for block in range(row_count // block_rows):
        first, last = key_range(block)
        here = slice(block * block_rows, last)
        opened = open_pairs(block, segment_column, segment_row)
        for head in range(head_count):
            at = slice(head * width, (head + 1) * width)
            keys = key[first:last, at]
            queries = [map_of(query[here, at], c) for c in range(2)]
            maps = [softmax_map(queries[c], keys, opened, scale) for c in range(2)]
            mixes = grad_mixed[here, at]
            combined = (maps[0] - lam[head : head + 1, :] * maps[1]).astype(jnp.bfloat16)
            grad_value[first:last, at] += dot_rows(combined, mixes)
            grads = dot_t(mixes, value[first:last, at])
            first_sum = jnp.sum(grads * maps[0], axis=-1, keepdims=True)
            second_sum = jnp.sum(grads * maps[1], axis=-1, keepdims=True)
            lam_sums[head] = lam_sums[head] + jnp.sum(second_sum, axis=0, keepdims=True)
            score_grads = [
                (maps[0] * (grads - first_sum)).astype(jnp.bfloat16),
                (maps[1] * (-lam[head : head + 1, :] * (grads - second_sum))).astype(jnp.bfloat16),
            ]
            grad_query = f32_dot(score_grads[0], map_of(keys, 0)) + f32_dot(
                score_grads[1], map_of(keys, 1)
            )
            grad_rows[here, at] = turn(
                grad_query * scale, cosine[here, :], -sine[here, :]
            ).astype(jnp.bfloat16)
            grad_key[first:last, at] += dot_rows(score_grads[0], queries[0]) + dot_rows(
                score_grads[1], queries[1]
            )
    for head in range(head_count):
        at = slice(head * width, (head + 1) * width)
        grad_rows[:, inner + head * width : inner + (head + 1) * width] = turn(
            grad_key[:, at] * scale, cosine[...], -sine[...]
        ).astype(jnp.bfloat16)
        grad_lam[head : head + 1, :] = jnp.broadcast_to(-lam_sums[head], (1, width))
    grad_rows[:, 2 * inner :] = grad_value[...].astype(jnp.bfloat16)


def in_vmem(count):
    return [pl.BlockSpec(memory_space=pltpu.VMEM)] * count


class Line:
    def __init__(self, line, widths, total, landed, line_out, line_in, credit):
        self.line, self.widths = line, widths
        self.total, self.landed = total, landed
        self.line_out, self.line_in, self.credit = line_out, line_in, credit
        self.me = lax.axis_index("dp")
        self.place = self.me // 2
        self.ring = total.shape[0]

    def copy(self, c, step, way, block, target):
        width = self.widths[c]
        return pltpu.make_async_remote_copy(
            src_ref=self.total.at[c % self.ring, block, :, :width],
            dst_ref=self.landed.at[way, step, c % 2, :, :width],
            send_sem=self.line_out.at[way, step, c % 2],
            recv_sem=self.line_in.at[way, step, c % 2],
            device_id={"dp": target},
            device_id_type=MESH,
        )

    def sends(self, step, way):
        place, line = self.place, self.line
        if way == 0:
            block = line - 1 - step + place
            return (place <= step) & (place < line - 1), block, self.me + 2
        block = place + step - line + 1
        return (place >= line - 1 - step) & (place > 0), block, self.me - 2

    def gets(self, step, way):
        place, line = self.place, self.line
        if way == 0:
            return (place > 0) & (place - 1 <= step), line - 2 - step + place, self.me - 2
        gets = (place < line - 1) & (place + 1 >= line - 1 - step)
        return gets, place + step - line + 2, self.me + 2

    def start(self, c, step):
        for way in range(2):
            sends, block, target = self.sends(step, way)

            @pl.when(sends)
            def _():
                if c >= 2:
                    pl.semaphore_wait(self.credit.at[way, step], 1)
                self.copy(c, step, way, block, target).start()

    def finish(self, c, step):
        width = self.widths[c]
        for way in range(2):
            gets, block, source = self.gets(step, way)

            @pl.when(gets)
            def _():
                self.copy(c, step, way, block, source).wait_recv()
                self.total[c % self.ring, block, :, :width] += self.landed[
                    way, step, c % 2, :, :width
                ]
                if c + 2 < len(self.widths):
                    pl.semaphore_signal(
                        self.credit.at[way, step],
                        inc=1,
                        device_id={"dp": source},
                        device_id_type=MESH,
                    )

            sends, sent, target = self.sends(step, way)

            @pl.when(sends)
            def _():
                self.copy(c, step, way, sent, target).wait_send()


class Reducer:
    def __init__(self, plan, line_plan, line_starts, line, refs):
        self.plan, self.line_plan, self.line_starts = plan, line_plan, line_starts
        self.line = line
        (
            self.send, self.held, self.total, landed, self.pair_out, self.pair_in,
            line_out, line_in, credit, self.out_sem,
        ) = refs[:10]
        self.first = Line(
            line, [item.width for item in plan], self.total, landed, line_out, line_in, credit
        )
        self.place = self.first.place
        self.me = self.first.me
        self.side = self.me % 2
        self.other = self.me + 1 - 2 * self.side
        self.steps = line - 1
        self.ring = self.total.shape[0]
        self.rows = self.total.shape[2]
        if line_plan:
            (
                self.line_total, landed, line_out, line_in, credit, self.last_held,
                self.last_out, self.last_in, self.line_out_sem,
            ) = refs[10:]
            self.second = Line(
                line, [item.width for item in line_plan], self.line_total, landed, line_out,
                line_in, credit,
            )

    def compute(self, c):
        item = self.plan[c]
        width = item.width
        left, right = item.left(), item.right()

        def block(at, carry):
            first = pl.multiple_of(2 * at * self.rows, self.rows)
            columns = right[...]
            away = left[pl.ds(first + (1 - self.side) * self.rows, self.rows), :]
            here = left[pl.ds(first + self.side * self.rows, self.rows), :]
            self.send[c % send_slots, at, :, :width] = f32_dot(away, columns)
            self.total[c % self.ring, at, :, :width] = f32_dot(here, columns)
            return carry

        lax.fori_loop(0, self.line, block, 0)
        item.computed()

    def line_compute(self, c):
        item = self.line_plan[c]
        left, right = item.left(), item.right()
        slot = c % self.line_total.shape[0]
        if c >= self.line_total.shape[0]:
            self.line_result(c - self.line_total.shape[0]).wait()

        def block(at, carry):
            rows = pl.ds(pl.multiple_of(2 * at * self.rows, 2 * self.rows), 2 * self.rows)
            self.line_total[slot, at] = f32_dot(left[rows, :], right[...])
            return carry

        lax.fori_loop(0, self.line, block, 0)
        item.computed()

    def side_rows(self, side):
        return pl.ds(pl.multiple_of(side * self.rows, self.rows), self.rows)

    def last_copy(self, c):
        slot = c % self.line_total.shape[0]
        return pltpu.make_async_remote_copy(
            src_ref=self.line_total.at[slot, self.place, self.side_rows(1 - self.side), :],
            dst_ref=self.last_held.at[c],
            send_sem=self.last_out.at[c],
            recv_sem=self.last_in.at[c],
            device_id={"dp": self.other},
            device_id_type=MESH,
        )

    def line_result(self, c):
        item = self.line_plan[c]
        slot = c % self.line_total.shape[0]
        return pltpu.make_async_copy(
            self.line_total.at[slot, self.place, self.side_rows(self.side), :],
            item.out.at[:, item.first : item.first + item.width],
            self.line_out_sem.at[slot],
        )

    def line_step(self, slot):
        for c, start in enumerate(self.line_starts):
            step = slot - start
            if 0 < step <= self.steps:
                self.second.finish(c, step - 1)
            if step == self.steps + 1:
                self.last_copy(c).wait()
                at = c % self.line_total.shape[0]
                self.line_total[at, self.place, self.side_rows(self.side), :] += self.last_held[c]
                self.line_result(c).start()
            if 0 <= step < self.steps and slot:
                self.second.start(c, step)
            if step == self.steps:
                self.last_copy(c).start()

    def pair_copy(self, c):
        width = self.plan[c].width
        return pltpu.make_async_remote_copy(
            src_ref=self.send.at[c % send_slots, :, :, :width],
            dst_ref=self.held.at[c % held_slots, :, :, :width],
            send_sem=self.pair_out.at[c % send_slots],
            recv_sem=self.pair_in.at[c % held_slots],
            device_id={"dp": self.other},
            device_id_type=MESH,
        )

    def pair_finish(self, c):
        width = self.plan[c].width
        self.pair_copy(c).wait_recv()

        def block(at, carry):
            self.total[c % self.ring, at, :, :width] += self.held[c % held_slots, at, :, :width]
            return carry

        lax.fori_loop(0, self.line, block, 0)
        self.pair_copy(c).wait_send()

    def out_copies(self, c):
        item = self.plan[c]
        outs = item.out if isinstance(item.out, list) else [item.out]
        size = outs[0].shape[1]
        first, last = item.first, item.first + item.width
        while first < last:
            count = min(last, (first // size + 1) * size) - first
            at = first - item.first
            yield pltpu.make_async_copy(
                self.total.at[c % self.ring, self.place, :, at : at + count],
                outs[first // size].at[:, first % size : first % size + count],
                self.out_sem.at[c % self.ring, at // 128],
            )
            first += count

    def out_start(self, c):
        for copy in self.out_copies(c):
            copy.start()

    def out_wait(self, c):
        for copy in self.out_copies(c):
            copy.wait()

    def run(self, tasks):
        count, steps = len(self.plan), self.steps
        begun = [c for c, start in enumerate(self.line_starts) if start == 0]
        for c in begun:
            self.line_compute(c)
        for c in begun:
            self.second.start(c, 0)
        self.compute(1)
        for slot in range(count + steps + 1):
            for step in reversed(range(steps)):
                c = slot - 2 - step
                if 0 <= c < count:
                    self.first.finish(c, step)
                    if step + 1 < steps:
                        self.first.start(c, step + 1)
            self.line_step(slot)
            if 0 <= slot - 1 < count:
                self.pair_finish(slot - 1)
                self.first.start(slot - 1, 0)
            if slot + 1 < count:
                self.pair_copy(slot + 1).start()
            done = slot - 1 - steps
            if 0 <= done < count:
                self.out_start(done)
            if slot + 2 < count:
                if slot + 2 >= self.ring:
                    self.out_wait(slot + 2 - self.ring)
                self.compute(slot + 2)
            for c, start in enumerate(self.line_starts):
                if slot and start == slot + 1:
                    self.line_compute(c)
            for task in tasks.get(slot, ()):
                task()
        for c in range(max(0, count - self.ring), count):
            self.out_wait(c)
        if self.line_plan:
            for c in range(len(self.line_plan) - self.line_total.shape[0], len(self.line_plan)):
                self.line_result(c).wait()


class Chunk:
    def __init__(self, left, right, computed, out, first, width):
        self.left, self.right, self.computed = left, right, computed
        self.out, self.first, self.width = out, first, width


def for_rows(count, body):
    def step(i, carry):
        body(pl.ds(pl.multiple_of(i * row_group, row_group), row_group))
        return carry

    lax.fori_loop(0, count // row_group, step, 0)


class TensorSum:
    def __init__(self, uses, own, near, far, near_sems, far_sems, near_credit, far_credit):
        self.own, self.near, self.far = own, near, far
        self.near_sems, self.far_sems = near_sems, far_sems
        self.near_credit, self.far_credit = near_credit, far_credit
        index = lax.axis_index("tensor")
        self.core_peer = index + 1 - 2 * (index % 2)
        self.far_peer = index + 2 - 4 * (index // 2)
        self.near_left, self.far_left = 2 * uses, uses
        self.near_first, self.far_first = True, True

    def near_copy(self, source):
        return pltpu.make_async_remote_copy(
            src_ref=source, dst_ref=self.near, send_sem=self.near_sems.at[0],
            recv_sem=self.near_sems.at[1], device_id={"tensor": self.core_peer},
            device_id_type=MESH,
        )

    def far_copy(self):
        return pltpu.make_async_remote_copy(
            src_ref=self.own, dst_ref=self.far, send_sem=self.far_sems.at[0],
            recv_sem=self.far_sems.at[1], device_id={"tensor": self.far_peer},
            device_id_type=MESH,
        )

    def near_start(self, source):
        if not self.near_first:
            pl.semaphore_wait(self.near_credit, 1)
        self.near_first = False
        self.pending = source
        self.near_copy(source).start()

    def near_wait(self):
        self.near_copy(self.pending).wait()

    def near_free(self):
        self.near_left -= 1
        if self.near_left:
            pl.semaphore_signal(
                self.near_credit, inc=1, device_id={"tensor": self.core_peer}, device_id_type=MESH
            )

    def near_add(self):
        self.near_wait()

        def add(rows):
            self.own[rows, :] += self.near[rows, :]

        for_rows(self.own.shape[0], add)
        self.near_free()

    def far_go(self):
        if not self.far_first:
            pl.semaphore_wait(self.far_credit, 1)
        self.far_first = False
        self.far_copy().start()

    def far_wait(self):
        self.far_copy().wait()

    def far_free(self):
        self.far_left -= 1
        if self.far_left:
            pl.semaphore_signal(
                self.far_credit, inc=1, device_id={"tensor": self.far_peer}, device_id_type=MESH
            )


def line_first(dp_count):
    return ((0, 0, 3, 6, 9, 12), (2, 2, 2)) if dp_count == 8 else ((), (0, 0, 0))


def back_kernel(dp_count, *refs):
    refs = list(refs)
    take = lambda n: [refs.pop(0) for _ in range(n)]
    lengths = take(2)
    cot_left, two_left, one_left = [take(2) for _ in range(3)]
    hidden, gate_pre, up_pre, heads = [take(2) for _ in range(4)]
    part_back, part_fed, middle = [take(2) for _ in range(3)]
    (layer_in, cotangent) = take(2)
    weights_in = take(4)
    kept_in = [take(4) for _ in range(2)]
    tables_in = [take(2) for _ in range(2)]
    (lambda_param, sub_gain, gain_one, gain_two) = take(4)
    (grad_down, grad_gate, grad_up, grad_out) = take(4)
    grad_qkv = take(3)
    (layer_out, grad_in) = take(2)
    small_outs = take(4)
    reducer_refs = take(20 if line_first(dp_count)[0] else 10)
    line_rights = reducer_refs.pop() if line_first(dp_count)[0] else None
    (left_a, left_b, rights, rows_qkv) = take(4)
    weights = take(4)
    kept = take(4)
    backward_scratch = take(4)
    (grad_sub, grad_lam) = take(2)
    sets = [take(3) for _ in range(2)]
    through = take(2)
    (spare, projected, attended, rows_in, rows_out) = take(5)
    (small, small_near, small_landed) = take(3)
    small_blocks = take(4)
    tables = take(4)
    (near_sems, far_sems, near_credit, far_credit) = take(4)
    (load_sems, small_near_sems, small_send, small_recv) = take(4)
    assert not refs

    me = lax.axis_index("dp")
    tensor = lax.axis_index("tensor")
    core = tensor % 2
    core_peer = tensor + 1 - 2 * core
    far_peer = tensor + 2 - 4 * (tensor // 2)
    line = dp_count // 2
    half = middle[0].shape[0]
    row_count = 2 * half
    head_count, head_width = sub_gain.shape
    sub_scale = sub_gain[...] * (1.0 - lambda_base)
    first_exp, second_exp, lam = lambda_terms(lambda_param)
    out_weight, projections = weights[0], weights[1:]
    inner = out_weight.shape[0]
    kept_half = pl.ds(pl.multiple_of(core * half, half), half)
    sent_half = pl.ds(pl.multiple_of((1 - core) * half, half), half)
    tokens = [slice(m * row_count, (m + 1) * row_count) for m in range(2)]

    barrier = pltpu.get_barrier_semaphore()
    for offset in range(1, dp_count):
        pl.semaphore_signal(
            barrier, inc=1, device_id={"dp": lax.rem(me + offset, dp_count)}, device_id_type=MESH
        )
    for peer in (core_peer, far_peer):
        pl.semaphore_signal(barrier, inc=1, device_id={"tensor": peer}, device_id_type=MESH)

    used = [0]

    def load(source, target):
        copy = pltpu.make_async_copy(source, target, load_sems.at[used[0]])
        used[0] += 1
        copy.start()
        return copy

    def wait_all(copies):
        for copy in copies:
            copy.wait()

    reducer_width = reducer_refs[0].shape[-1]
    plan, sources, left_loads, right_loads = [], {}, {}, {}

    def load_left(sources_of, left):
        return [load(sources_of[m], left.at[:, tokens[m]]) for m in range(2)]

    def load_columns(source, first, width, target):
        return [
            load(source[m].at[:, first : first + width], target.at[tokens[m], :width])
            for m in range(2)
        ]

    def load_right(c):
        if c in sources:
            right_loads[c] = load_columns(*sources[c], rights.at[c % 2])

    def load_line_right(c):
        if c < len(line_sources):
            line_loads[c] = load_columns(*line_sources[c], line_rights.at[c % 2])

    def get_left(c, left):
        wait_all(left_loads.pop(c, ()))
        return left

    def get_line_left(left):
        return left

    def get_right(c, first, width):
        if c in sources:
            wait_all(right_loads[c])
            return rights.at[c % 2, :, :width]
        return rows_qkv.at[:, first : first + width]

    def get_line_right(c):
        wait_all(line_loads[c])
        return line_rights.at[c % 2]

    def computed(c):
        load_right(c + 2)
        if c == last_two:
            left_loads[first_one] = load_left(one_left, left_b)

    def add_group(left, source, columns, out, line_chunks=0):
        start = line_chunks * line_width
        for first in range(0, start, line_width):
            c = len(line_plan)
            line_sources.append((source, first, line_width))
            line_plan.append(
                Chunk(
                    functools.partial(get_line_left, left),
                    functools.partial(get_line_right, c),
                    functools.partial(load_line_right, c + 2),
                    out,
                    first,
                    line_width,
                )
            )
        for first in range(start, columns, reducer_width):
            width = min(reducer_width, columns - first)
            c = len(plan)
            if source is not None:
                sources[c] = (source, first, width)
            plan.append(
                Chunk(
                    functools.partial(get_left, c, left),
                    functools.partial(get_right, c, first, width),
                    functools.partial(computed, c),
                    out,
                    first,
                    width,
                )
            )

    line_starts, line_counts = line_first(dp_count)
    line_plan, line_sources, line_loads, line_width = [], [], {}, 128
    add_group(left_a, hidden, hidden[0].shape[1], grad_down, line_counts[0])
    add_group(left_b, gate_pre, gate_pre[0].shape[1], grad_gate, line_counts[1])
    add_group(left_b, up_pre, up_pre[0].shape[1], grad_up)
    last_two = len(plan) - 1
    add_group(left_a, heads, inner, grad_out, line_counts[2])
    first_one = len(plan)
    add_group(left_b, None, 3 * inner, grad_qkv)

    left_loads[0] = load_left(cot_left, left_a)
    load_right(0)
    two_loads = [load(two_left[m], (attended, rows_out)[m]) for m in range(2)]
    load_line_right(0)
    load_line_right(1)
    load_right(1)
    sums = [
        TensorSum(
            3, *sets[m], near_sems.at[m], far_sems.at[m], near_credit.at[m], far_credit.at[m]
        )
        for m in range(2)
    ]
    own_loads = {m: load(part_back[m].at[kept_half], sets[m][0]) for m in range(2)}
    weight_loads = [load(*pair) for pair in zip(weights_in, weights)]
    def load_kept(m):
        pairs = zip([*kept_in[m], *tables_in[m]], [*kept, *tables[:2]])
        return [load(*pair) for pair in pairs]

    kept_loads = load_kept(0)
    spare_queue = [middle[0], middle[1], middle[0], middle[1]]
    rows_queue = [cotangent.at[0], cotangent.at[1]]
    rows_queue += [layer_in.at[0], cotangent.at[0], layer_in.at[1], cotangent.at[1]]
    queued = {}

    def next_spare():
        queued["spare"] = load(spare_queue.pop(0), spare) if spare_queue else None

    def next_rows():
        queued["rows"] = load(rows_queue.pop(0), rows_in) if rows_queue else None

    next_spare()
    next_rows()
    out_loads = []
    small[...] = jnp.zeros_like(small)

    def mine(rows):
        return pl.ds(pl.multiple_of(core * half + rows.start, row_group), row_group)

    def others(rows):
        return pl.ds(pl.multiple_of((1 - core) * half + rows.start, row_group), row_group)

    def flip_rows(source, left, m):
        def block(i, carry):
            at = pl.ds(pl.multiple_of(i * 128, 128), 128)
            left[at, tokens[m]] = source[:, at].T
            return carry

        lax.fori_loop(0, source.shape[1] // 128, block, 0)

    def flip_two():
        wait_all(two_loads)
        for m in range(2):
            flip_rows((attended, rows_out)[m], left_b, m)

    def exchange(m):
        if m in own_loads:
            own_loads.pop(m).wait()
        sums[m].near_add()
        sums[m].far_go()

    def norm_two(m):
        own, near, far = sets[m]
        queued["spare"].wait()
        sums[m].far_wait()

        def body(rows):
            grads = own[rows, :] + far[rows, :]
            values = spare[rows, :]
            root = root_of(values)
            small[1:2, :] += jnp.sum(grads * values * root, axis=0, keepdims=True)
            through[m][rows, :] = rms_back(grads * gain_two[...], values, root)

        for_rows(half, body)
        sums[m].far_free()
        sums[m].near_start(through[m])
        next_spare()

    def attend(m):
        near = sets[m][1]
        queued["rows"].wait()
        sums[m].near_wait()

        def body(rows):
            attended[mine(rows), :] = (
                rows_in[mine(rows), :].astype(jnp.float32) + through[m][rows, :]
            ).astype(jnp.bfloat16)
            attended[others(rows), :] = (
                rows_in[others(rows), :].astype(jnp.float32) + near[rows, :]
            ).astype(jnp.bfloat16)

        for_rows(half, body)
        sums[m].near_free()
        next_rows()

        flip_rows(attended, left_a, m)
        if m == 0:
            wait_all(weight_loads)
        wait_all(kept_loads)
        segments(lengths[m], *tables[2:])
        backward_kernel(
            lam, attended, out_weight, *kept, *tables, sub_scale,
            rows_qkv.at[tokens[m], :], grad_sub, grad_lam, *backward_scratch,
        )
        if m == 0:
            kept_loads[:] = load_kept(1)
        for head in range(head_count):
            at = slice(head * head_width, (head + 1) * head_width)
            small[2:3, at] += grad_sub[head : head + 1, :]
            small[3:4, at] += grad_lam[head : head + 1, :]

    def project(m):
        def part(which, target):
            rows = pl.ds(pl.multiple_of(m * row_count + which * half, half), half)

            def block(i, carry):
                at = pl.ds(pl.multiple_of(i * 512, 512), 512)
                total = 0.0
                for p in range(3):
                    grads = rows_qkv[rows, p * inner : (p + 1) * inner]
                    total = total + dot_t(grads, projections[p][at, :])
                target[:, at] = total
                return carry

            lax.fori_loop(0, target.shape[1] // 512, block, 0)

        part(1 - core, projected)
        sums[m].near_start(projected)
        part(core, sets[m][0])

    def norm_one(m):
        own, near, far = sets[m]
        queued["rows"].wait()
        sums[m].far_wait()

        def body(rows):
            grads = own[rows, :] + far[rows, :]
            values = rows_in[mine(rows), :].astype(jnp.float32)
            root = root_of(values)
            small[0:1, :] += jnp.sum(grads * values * root, axis=0, keepdims=True)
            through[m][rows, :] += rms_back(grads * gain_one[...], values, root)

        for_rows(half, body)
        sums[m].far_free()
        sums[m].near_start(through[m])
        next_rows()
        own_loads[m] = load(part_fed[m].at[kept_half], own)

    def store_rows(target):
        out_loads.append(load(rows_out, target))

    def finish_in(m):
        near = sets[m][1]
        queued["rows"].wait()
        sums[m].near_wait()
        wait_all(out_loads)
        out_loads.clear()

        def body(rows):
            rows_out[mine(rows), :] = (
                rows_in[mine(rows), :].astype(jnp.float32) + through[m][rows, :]
            ).astype(jnp.bfloat16)
            rows_out[others(rows), :] = (
                rows_in[others(rows), :].astype(jnp.float32) + near[rows, :]
            ).astype(jnp.bfloat16)

        for_rows(half, body)
        sums[m].near_free()
        next_rows()
        store_rows(grad_in.at[m])
        sums[m].near_start(part_fed[m].at[sent_half])

    def add_fed(m):
        own, near, far = sets[m]
        queued["spare"].wait()
        sums[m].far_wait()

        def body(rows):
            own[rows, :] = spare[rows, :] + (own[rows, :] + far[rows, :])

        for_rows(half, body)
        sums[m].far_free()
        sums[m].near_start(own)
        next_spare()

    def finish_out(m):
        own, near = sets[m][:2]
        sums[m].near_wait()
        wait_all(out_loads)
        out_loads.clear()

        def body(rows):
            rows_out[mine(rows), :] = own[rows, :].astype(jnp.bfloat16)
            rows_out[others(rows), :] = near[rows, :].astype(jnp.bfloat16)

        for_rows(half, body)
        sums[m].near_free()
        store_rows(layer_out.at[m])

    small_core = pltpu.make_async_remote_copy(
        src_ref=small, dst_ref=small_near, send_sem=small_near_sems.at[0],
        recv_sem=small_near_sems.at[1], device_id={"tensor": core_peer}, device_id_type=MESH,
    )

    def small_copy(offset):
        return pltpu.make_async_remote_copy(
            src_ref=small, dst_ref=small_landed.at[offset - 1], send_sem=small_send.at[offset - 1],
            recv_sem=small_recv.at[offset - 1],
            device_id={"dp": lax.rem(me + offset, dp_count)}, device_id_type=MESH,
        )

    def small_spread():
        small_core.wait()
        small[0:2, :] += small_near[0:2, :]
        for offset in range(1, dp_count):
            small_copy(offset).start()

    def small_finish():
        for offset in range(1, dp_count):
            small_copy(offset).wait()
        total = small[...]
        for offset in range(1, dp_count):
            total = total + small_landed[offset - 1]

        def own_block(values, target):
            count = target.shape[1]
            shift = lax.rem((dp_count - me) * count, count * dp_count)
            return pltpu.roll(values, shift, 1)[: target.shape[0], :count]

        norm_blocks, lambda_block, sub_block = small_blocks[:2], small_blocks[2], small_blocks[3]
        for row in range(2):
            norm_blocks[row][...] = own_block(total, norm_blocks[row][...])
            total = pltpu.roll(total, 7, 0)
        total = pltpu.roll(total, 2, 0)
        part = head_width // 2
        for head in range(head_count):
            at = slice(head * head_width, (head + 1) * head_width)
            sub_block[head : head + 1, :] = own_block(
                jnp.broadcast_to(total[2:3, at], (8, head_width)), sub_block[0:1, :]
            )
            grad = total[3:4, head * head_width : head * head_width + 1]
            param = lambda_param[head : head + 1, :]
            first = grad * first_exp[head : head + 1, :]
            second = grad * second_exp[head : head + 1, :]
            piece = lambda k: param[:, k * part : (k + 1) * part]
            full = jnp.concatenate(
                [first * piece(1), first * piece(0), -second * piece(3), -second * piece(2)], axis=1
            )
            lambda_block[head : head + 1, :] = own_block(
                jnp.broadcast_to(full, (8, 4 * part)), lambda_block[0:1, :]
            )
        out_loads.extend(load(*pair) for pair in zip(small_blocks, small_outs))

    order = {
        0: [flip_two, lambda: exchange(0)],
        2: [lambda: norm_two(0), lambda: exchange(1)],
        3: [lambda: attend(0), lambda: project(0)],
        4: [lambda: norm_two(1), lambda: exchange(0)],
        5: [lambda: attend(1), lambda: project(1)],
        6: [lambda: norm_one(0), lambda: exchange(1)],
        7: [lambda: finish_in(0)],
        8: [lambda: norm_one(1), lambda: exchange(0), small_core.start],
        9: [lambda: finish_in(1), small_spread],
        10: [lambda: add_fed(0), lambda: exchange(1), small_finish],
        11: [lambda: finish_out(0)],
        12: [lambda: add_fed(1)],
        13: [lambda: finish_out(1)],
    }
    stretch = 256 // reducer_width
    tasks = {slot * stretch: items for slot, items in order.items()}
    reducer = Reducer(plan, line_plan, line_starts, line, reducer_refs)
    reducer.compute(0)
    pl.semaphore_wait(barrier, dp_count + 1)
    reducer.pair_copy(0).start()
    for m in range(2):
        sums[m].near_start(part_back[m].at[sent_half])
    reducer.run(tasks)
    wait_all(out_loads)


def back_call(dp_count, lengths, arrays, blocks, shapes):
    depth, row_count, inner, hidden_count, head_count, head_width = shapes
    line = dp_count // 2
    rows = depth // dp_count
    half = row_count // 2
    width = 256 if line <= 4 else 128
    ring = line + 3
    starts = line_first(dp_count)[0]
    wide = (line, rows, width)
    bf16, f32 = jnp.bfloat16, jnp.float32
    dma, regular = pltpu.SemaphoreType.DMA, pltpu.SemaphoreType.REGULAR
    wide_half = pltpu.VMEM((half, depth), f32)
    wide_rows = pltpu.VMEM((row_count, depth), bf16)
    narrow = pltpu.VMEM((row_count, inner), bf16)
    narrow_f32 = pltpu.VMEM((row_count, inner), f32)
    small = pltpu.VMEM((8, depth), f32)
    grad = lambda columns: jax.ShapeDtypeStruct((rows, columns), f32)
    rows_shape = jax.ShapeDtypeStruct((2, row_count, depth), bf16)
    small_shapes = [jax.ShapeDtypeStruct((1, rows), f32)] * 2
    for count in (2 * head_width, head_width):
        small_shapes.append(jax.ShapeDtypeStruct((head_count, count // dp_count), f32))
    flops = 2 * 2 * row_count * depth * (3 * hidden_count + 8 * inner)
    return pl.pallas_call(
        functools.partial(back_kernel, dp_count),
        out_shape=[grad(hidden_count)] * 3
        + [grad(inner)] * 4
        + [rows_shape] * 2
        + small_shapes,
        in_specs=[pl.BlockSpec(memory_space=pltpu.SMEM)] * 2
        + [pl.BlockSpec(memory_space=pl.ANY)] * len(arrays)
        + in_vmem(len(blocks)),
        out_specs=[pl.BlockSpec(memory_space=pl.ANY)] * 13,
        scratch_shapes=[
            pltpu.VMEM((send_slots,) + wide, f32),
            pltpu.VMEM((held_slots,) + wide, f32),
            pltpu.VMEM((ring,) + wide, f32),
            pltpu.VMEM((2, line - 1, 2, rows, width), f32),
            dma((send_slots,)),
            dma((held_slots,)),
            dma((2, line - 1, 2)),
            dma((2, line - 1, 2)),
            regular((2, line - 1)),
            dma((ring, 2)),
        ]
        + (
            [
                pltpu.VMEM((3, line, 2 * rows, 128), f32),
                pltpu.VMEM((2, line - 1, 2, 2 * rows, 128), f32),
                dma((2, line - 1, 2)),
                dma((2, line - 1, 2)),
                regular((2, line - 1)),
                pltpu.VMEM((len(starts), rows, 128), f32),
                dma((len(starts),)),
                dma((len(starts),)),
                dma((3,)),
                pltpu.VMEM((2, 2 * row_count, 128), bf16),
            ]
            if starts
            else []
        )
        + [
            pltpu.VMEM((depth, 2 * row_count), bf16),
            pltpu.VMEM((depth, 2 * row_count), bf16),
            pltpu.VMEM((2, 2 * row_count, width), bf16),
            pltpu.VMEM((2 * row_count, 3 * inner), bf16),
            pltpu.VMEM((inner, depth), bf16),
        ]
        + [pltpu.VMEM((depth, inner), bf16)] * 3
        + [narrow, narrow, narrow, narrow_f32]
        + [narrow_f32, narrow, narrow_f32, narrow_f32]
        + [pltpu.VMEM((head_count, head_width), f32)] * 2
        + [wide_half] * 10
        + [wide_rows] * 3
        + [
            small,
            small,
            pltpu.VMEM((dp_count - 1, 8, depth), f32),
            *[pltpu.VMEM(item.shape, f32) for item in small_shapes],
            pltpu.VMEM((row_count, head_width), f32),
            pltpu.VMEM((row_count, head_width), f32),
            pltpu.VMEM((row_count, 1), jnp.int32),
            pltpu.VMEM((1, row_count), jnp.int32),
            dma((2, 2)),
            dma((2, 2)),
            regular((2,)),
            regular((2,)),
            dma((128,)),
            dma((2,)),
            dma((dp_count - 1,)),
            dma((dp_count - 1,)),
        ],
        compiler_params=pltpu.CompilerParams(
            collective_id=0, has_side_effects=True, vmem_limit_bytes=62 * 1024 * 1024
        ),
        cost_estimate=pl.CostEstimate(flops=flops, bytes_accessed=64 << 20, transcendentals=0),
    )(*lengths, *arrays, *blocks)


def gathers_heads(dp_count):
    return dp_count == 8


class Gather:
    def __init__(self, own, piece, wide, far, near, far_near, full, sems):
        self.own, self.piece, self.wide = own, piece, wide
        self.far, self.near, self.far_near, self.full = far, near, far_near, full
        (
            self.cross_sems, self.line_out, self.line_in, self.pair_out, self.pair_in,
            self.near_sems,
        ) = sems
        self.me = lax.axis_index("dp")
        self.place, self.side = self.me // 2, self.me % 2
        self.line = self.line_out.shape[1] + 1
        self.rows = piece.shape[0]
        tensor = lax.axis_index("tensor")
        self.tensor = tensor
        self.core_peer = tensor + 1 - 2 * (tensor % 2)
        self.far_peer = tensor + 2 - 4 * (tensor // 2)
        self.diagonal = self.far_peer + 1 - 2 * (tensor % 2)

    def slot(self, side, place):
        start = (side * self.line + place) * self.rows
        return self.far.at[pl.ds(pl.multiple_of(start, self.rows), self.rows)]

    def remote(self, source, target, send, recv, device):
        return pltpu.make_async_remote_copy(
            src_ref=source, dst_ref=target, send_sem=send, recv_sem=recv, device_id=device,
            device_id_type=MESH,
        )

    def cross(self):
        return self.remote(
            self.piece, self.slot(self.side, self.place), self.cross_sems.at[0],
            self.cross_sems.at[1], {"tensor": self.far_peer},
        )

    def near_copy(self, index):
        half = self.line * self.rows
        if index == 0:
            source, target = self.wide, self.near
        else:
            start = (self.side if index == 1 else 1 - self.side) * half
            rows = pl.ds(pl.multiple_of(start, self.rows), half)
            source, target = self.far.at[rows], self.far_near.at[rows]
        return self.remote(
            source, target, self.near_sems.at[0, index], self.near_sems.at[1, index],
            {"tensor": self.core_peer},
        )

    def line_copy(self, way, step):
        place = self.place - step if way == 0 else self.place + step
        slot = self.slot(self.side, place)
        return self.remote(
            slot, slot, self.line_out.at[way, step], self.line_in.at[way, step],
            {"dp": self.me + 2 - 4 * way},
        )

    def line_sends(self, way, step):
        if way == 0:
            return (self.place >= step) & (self.place < self.line - 1)
        return (self.place + step <= self.line - 1) & (self.place > 0)

    def line_gets(self, way, step):
        if way == 0:
            return self.place >= step
        return self.place + step <= self.line - 1

    def pair_copy(self, index, place):
        slot = self.slot(self.side, place)
        return self.remote(
            slot, slot, self.pair_out.at[index], self.pair_in.at[index],
            {"dp": self.me + 1 - 2 * self.side},
        )

    def pair_index(self, way, step):
        return 1 + way * (self.line - 1) + step - 1

    def begin(self):
        count = self.own.shape[0]
        rows = pl.ds(pl.multiple_of(self.me * self.rows, self.rows), self.rows)
        self.piece[...] = self.own[rows, :].astype(jnp.float32)
        self.cross().start()

        def widen(rows):
            self.wide[rows, :] = self.own[rows, :].astype(jnp.float32)

        for_rows(count, widen)
        self.near_copy(0).start()

    def forward(self, step):
        if step == 0:
            self.cross().wait()
            self.pair_copy(0, self.place).start()
        for way in range(2):
            if step:

                @pl.when(self.line_gets(way, step))
                def _():
                    self.line_arrival(way, step).wait_recv()
                    place = self.place - step if way == 0 else self.place + step
                    self.pair_copy(self.pair_index(way, step), place).start()

            if step < self.line - 1:

                @pl.when(self.line_sends(way, step))
                def _():
                    self.line_copy(way, step).start()

    def line_arrival(self, way, step):
        place = self.place - step if way == 0 else self.place + step
        slot = self.slot(self.side, place)
        return self.remote(
            slot, slot, self.line_out.at[way, step - 1], self.line_in.at[way, step - 1],
            {"dp": self.me - 2 + 4 * way},
        )

    def store(self, source, tensor, first, count):
        block = self.own.shape[0]

        def narrow(rows):
            at = pl.ds(pl.multiple_of(tensor * block + first + rows.start, row_group), row_group)
            self.full[at, :] = source[rows, :].astype(jnp.bfloat16)

        for_rows(count, narrow)

    def store_far(self, source, tensor):
        for side in range(2):
            for place in range(self.line):
                rows = pl.ds((side * self.line + place) * self.rows, self.rows)
                self.store(source.at[rows], tensor, (2 * place + side) * self.rows, self.rows)

    def finish_line(self):
        self.near_copy(1).start()
        for way in range(2):
            for step in range(self.line - 1):

                @pl.when(self.line_sends(way, step))
                def _():
                    self.line_copy(way, step).wait_send()

        block = self.own.shape[0]
        self.store(self.own, self.tensor, 0, block)
        self.near_copy(0).wait()
        self.store(self.near, self.core_peer, 0, block)

    def finish(self):
        for index in range(1 + 2 * (self.line - 1)):
            if index == 0:
                self.pair_copy(0, self.place).wait()
                continue
            way, step = (index - 1) // (self.line - 1), (index - 1) % (self.line - 1) + 1

            @pl.when(self.line_gets(way, step))
            def _():
                place = self.place - step if way == 0 else self.place + step
                slot = self.slot(1 - self.side, place)
                self.pair_copy(index, place).wait_send()
                self.remote(
                    slot, slot, self.pair_out.at[index], self.pair_in.at[index],
                    {"dp": self.me + 1 - 2 * self.side},
                ).wait_recv()

        self.near_copy(2).start()
        self.store_far(self.far, self.far_peer)
        self.near_copy(1).wait()
        self.near_copy(2).wait()
        self.store_far(self.far_near, self.diagonal)


def front_kernel(dp_count, *refs):
    refs = list(refs)
    take = lambda n: [refs.pop(0) for _ in range(n)]
    lengths = take(2)
    layer_in, cotangent = take(2)
    weights_in = take(7)
    (lambda_param, sub_gain, gain_one, gain_two) = take(4)
    outs = [take(16) for _ in range(2)]
    cosines, sines = take(2), take(2)
    (segment_column, segment_row) = take(2)
    rows_in, cot_rows = take(2), take(2)
    (normed_one, normed_two, flipped) = take(3)
    weights = take(7)
    kept = take(5)
    hidden = take(3)
    (back, fed) = take(2)
    (near_sems, load_sems) = take(2)
    gathers = gathers_heads(dp_count)
    if gathers:
        sets = [take(2) for _ in range(2)]
        heads_wide, heads_landed = take(2), take(2)
        (heads_full, piece, wide, near_weight, full_weight, heads_sems) = take(6)
        gather_sems = take(6)
    else:
        sets = [take(3) for _ in range(2)]
        (projected, far_sems, near_credit) = take(3)
    assert not refs

    tensor = lax.axis_index("tensor")
    core = tensor % 2
    out_weight, gate_weight, up_weight, down_weight = weights[3:]
    row_count, depth = normed_one.shape
    half = row_count // 2
    hidden_count = gate_weight.shape[1]
    used = [0]

    def load(source, target):
        copy = pltpu.make_async_copy(source, target, load_sems.at[used[0]])
        used[0] += 1
        copy.start()
        return copy

    def wait_all(copies):
        for copy in copies:
            copy.wait()
        copies.clear()

    out_weight_load = load(weights_in[3], weights[3])
    rows_loads = [load(layer_in.at[0], rows_in[0])]
    weight_loads = [load(*pair) for pair in zip(weights_in[:3], weights[:3])]
    rows_loads.append(load(layer_in.at[1], rows_in[1]))
    cot_loads = [load(cotangent.at[m], cot_rows[m]) for m in range(2)]
    wide_loads = [load(*pair) for pair in zip(weights_in[4:], weights[4:])]

    sub_scale = sub_gain[...] * (1.0 - lambda_base)
    lam = lambda_terms(lambda_param)[2]
    barrier = pltpu.get_barrier_semaphore()
    core_peer, far_peer = tensor + 1 - 2 * core, tensor + 2 - 4 * (tensor // 2)
    diagonal = far_peer + 1 - 2 * core
    me = lax.axis_index("dp")
    for peer in (core_peer, far_peer, diagonal):
        pl.semaphore_signal(barrier, inc=1, device_id={"tensor": peer}, device_id_type=MESH)
    if gathers:
        for offset in range(1, dp_count):
            target = lax.rem(me + offset, dp_count)
            pl.semaphore_signal(barrier, inc=1, device_id={"dp": target}, device_id_type=MESH)
    pl.semaphore_wait(barrier, dp_count + 2 if gathers else 3)
    if gathers:
        sums = [
            TensorSum(1, *sets[m], None, near_sems.at[m], None, None, None) for m in range(2)
        ]
        for item in sums:
            item.near_left = 1
        gather = Gather(
            weights[3], piece, wide, back, near_weight, fed, full_weight, gather_sems
        )
    else:
        sums = [
            TensorSum(1, *sets[m], near_sems.at[m], far_sems.at[m], near_credit.at[m], None)
            for m in range(2)
        ]
    out_loads, flip_loads, wide_outs, hidden_outs = [], [], [], []

    def mine(rows):
        return pl.ds(pl.multiple_of(core * half + rows.start, row_group), row_group)

    def others(rows):
        return pl.ds(pl.multiple_of((1 - core) * half + rows.start, row_group), row_group)

    def flip_to(source, target):
        wait_all(flip_loads)

        def block(i, carry):
            at = pl.ds(pl.multiple_of(i * 128, 128), 128)
            flipped[at, :] = source[:, at].T
            return carry

        lax.fori_loop(0, depth // 128, block, 0)
        flip_loads.append(load(flipped, target))

    def heads_copy(m, index):
        peer = (core_peer, far_peer, diagonal)[index]
        which = core if index == 1 else 1 - core
        rows = pl.ds(pl.multiple_of(which * half, half), half)
        return pltpu.make_async_remote_copy(
            src_ref=heads_wide[m].at[rows], dst_ref=heads_landed[m].at[index],
            send_sem=heads_sems.at[m, 0, index], recv_sem=heads_sems.at[m, 1, index],
            device_id={"tensor": peer}, device_id_type=MESH,
        )

    def join_heads(m):
        own = sets[m][0]
        inner = kept[4].shape[1]

        def place_of(index):
            return pl.ds(pl.multiple_of(index * inner, inner), inner)

        rows = pl.ds(pl.multiple_of(core * half, half), half)
        heads_full[:, place_of(tensor)] = heads_wide[m][rows, :].astype(jnp.bfloat16)
        for index, peer in enumerate((core_peer, far_peer, diagonal)):
            heads_copy(m, index).wait()
            heads_full[:, place_of(peer)] = heads_landed[m][index].astype(jnp.bfloat16)

        def block(i, carry):
            at = pl.ds(pl.multiple_of(i * 512, 512), 512)
            values = rows_in[m][rows, at].astype(jnp.float32)
            own[:, at] = values + f32_dot(heads_full[...], full_weight[:, at])
            return carry

        lax.fori_loop(0, depth // 512, block, 0)

    def attend(m, between):
        rows_loads[m].wait()
        wait_all(weight_loads)
        wait_all(out_loads)
        segments(lengths[m], segment_column, segment_row)
        out_loads.extend([load(cosines[m], outs[m][14]), load(sines[m], outs[m][15])])
        forward_kernel(
            lam, rows_in[m], gain_one, *weights[:3], cosines[m], sines[m], segment_column,
            segment_row, sub_scale, normed_one, *kept,
            between,
        )
        heads = kept[4]
        if gathers:
            heads_wide[m][...] = heads[...].astype(jnp.float32)
            for index in range(3):
                heads_copy(m, index).start()
            out_loads.extend(load(*pair) for pair in zip(kept, outs[m][3:8]))
            flip_to(normed_one, outs[m][2])
            return

        def part(which, target):
            rows = pl.ds(pl.multiple_of(which * half, half), half)

            def block(i, carry):
                at = pl.ds(pl.multiple_of(i * 512, 512), 512)
                target[:, at] = f32_dot(heads[rows, :], out_weight[:, at])
                return carry

            lax.fori_loop(0, depth // 512, block, 0)

        part(1 - core, projected)
        sums[m].near_start(projected)
        part(core, sets[m][0])
        out_loads.extend(load(*pair) for pair in zip(kept, outs[m][3:8]))
        flip_to(normed_one, outs[m][2])
        sums[m].near_add()

    def norm_rows(values):
        return (values * root_of(values) * gain_two[...]).astype(jnp.bfloat16)

    def join(m):
        own = sets[m][0]
        if gathers:
            join_heads(m)
        else:
            far = sets[m][2]

            def add(rows):
                values = rows_in[m][mine(rows), :].astype(jnp.float32)
                own[rows, :] = values + (own[rows, :] + far[rows, :])

            for_rows(half, add)
        sums[m].near_start(own)
        out_loads.append(load(own, outs[m][8]))

    def norm(m):
        own, near = sets[m][:2]

        def norm_mine(rows):
            normed_two[mine(rows), :] = norm_rows(own[rows, :])

        def norm_others(rows):
            normed_two[others(rows), :] = norm_rows(near[rows, :])

        wait_all(out_loads)
        for_rows(half, norm_mine)
        sums[m].near_wait()
        for_rows(half, norm_others)
        sums[m].near_free()
        out_loads.append(load(normed_two, outs[m][1]))

    def feed(m, between):
        inside, gate_pre, up_pre = hidden
        if m == 0:
            wait_all(wide_loads)
        wait_all(hidden_outs)

        def block(j, carry):
            at = pl.ds(pl.multiple_of(j * 256, 256), 256)
            grads = dot_t(cot_rows[m][...], down_weight[at, :])
            gate = f32_dot(normed_two[...], gate_weight[:, at])
            upward = f32_dot(normed_two[...], up_weight[:, at])
            sigmoid = jax.nn.sigmoid(gate)
            inside[:, at] = (gate * sigmoid * upward).astype(jnp.bfloat16)
            gate_pre[:, at] = (
                grads * upward * sigmoid * (1.0 + gate * (1.0 - sigmoid))
            ).astype(jnp.bfloat16)
            up_pre[:, at] = (grads * gate * sigmoid).astype(jnp.bfloat16)
            return carry

        lax.fori_loop(0, hidden_count // 256, block, 0, unroll=True)
        hidden_outs.extend(load(*pair) for pair in zip(hidden, outs[m][9:12]))
        between()
        wait_all(wide_outs)

        for i in range(depth // 512):
            at = slice(i * 512, (i + 1) * 512)
            back[:, at] = dot_t(gate_pre[...], gate_weight[at, :]) + dot_t(
                up_pre[...], up_weight[at, :]
            )
            fed[:, at] = f32_dot(inside[...], down_weight[:, at])
            wide_outs.append(load(back.at[:, at], outs[m][12].at[:, at]))
            wide_outs.append(load(fed.at[:, at], outs[m][13].at[:, at]))

    def flip_cot(m):
        cot_loads[m].wait()
        flip_to(cot_rows[m], outs[m][0])

    if gathers:
        out_weight_load.wait()
        gather.begin()
        rotary_tables(lengths, cosines, sines, lambda_param.shape[1] // 4)
        attend(0, {1: lambda: gather.forward(0)})
        attend(1, {0: lambda: gather.forward(1)})
        gather.forward(2)
        flip_cot(0)
        flip_cot(1)
        gather.forward(3)
        gather.finish_line()
        gather.finish()
    else:
        out_weight_load.wait()
        rotary_tables(lengths, cosines, sines, lambda_param.shape[1] // 4)
        attend(0, {})
        sums[0].far_go()
        attend(1, {})
        flip_cot(0)
        flip_cot(1)
        sums[0].far_wait()
        sums[1].far_go()
    join(0)
    norm(0)
    if gathers:
        feed(0, lambda: join(1))
    else:
        feed(0, lambda: None)
        sums[1].far_wait()
        join(1)
    norm(1)
    feed(1, lambda: None)
    wait_all(flip_loads)
    wait_all(hidden_outs)
    wait_all(wide_outs)
    wait_all(out_loads)


def front_call(dp_count, lengths, arrays, blocks, shapes):
    depth, row_count, inner, hidden_count, head_count, head_width = shapes
    bf16, f32 = jnp.bfloat16, jnp.float32
    dma, regular = pltpu.SemaphoreType.DMA, pltpu.SemaphoreType.REGULAR
    half = row_count // 2
    out_shape = []
    for m in range(2):
        out_shape += [jax.ShapeDtypeStruct((depth, row_count), bf16)]
        out_shape += [jax.ShapeDtypeStruct((row_count, depth), bf16)]
        out_shape += [jax.ShapeDtypeStruct((depth, row_count), bf16)]
        out_shape += [jax.ShapeDtypeStruct((row_count, inner), bf16)] * 3
        out_shape += [jax.ShapeDtypeStruct((row_count, inner), f32)]
        out_shape += [jax.ShapeDtypeStruct((row_count, inner), bf16)]
        out_shape += [jax.ShapeDtypeStruct((half, depth), f32)]
        out_shape += [jax.ShapeDtypeStruct((row_count, hidden_count), bf16)] * 3
        out_shape += [jax.ShapeDtypeStruct((row_count, depth), f32)] * 2
        out_shape += [jax.ShapeDtypeStruct((row_count, head_width), f32)] * 2
    wide_rows = pltpu.VMEM((row_count, depth), bf16)
    narrow = pltpu.VMEM((row_count, inner), bf16)
    wide_half = pltpu.VMEM((half, depth), f32)
    if gathers_heads(dp_count):
        steps = dp_count // 2 - 1
        extra = [wide_half] * 4
        extra += [pltpu.VMEM((row_count, inner), f32)] * 2
        extra += [pltpu.VMEM((3, half, inner), f32)] * 2
        extra += [
            pltpu.VMEM((half, depth), bf16),
            pltpu.VMEM((inner // dp_count, depth), f32),
            pltpu.VMEM((inner, depth), f32),
            pltpu.VMEM((inner, depth), f32),
            pltpu.VMEM((depth, depth), bf16),
            dma((2, 2, 3)),
            dma((2,)),
            dma((2, steps)),
            dma((2, steps)),
            dma((1 + 2 * steps,)),
            dma((1 + 2 * steps,)),
            dma((2, 3)),
        ]
    else:
        extra = [wide_half] * 7 + [dma((2, 2)), regular((2,))]
    return pl.pallas_call(
        functools.partial(front_kernel, dp_count),
        out_shape=out_shape,
        in_specs=[pl.BlockSpec(memory_space=pltpu.SMEM)] * 2
        + [pl.BlockSpec(memory_space=pl.ANY)] * len(arrays)
        + in_vmem(len(blocks)),
        out_specs=[pl.BlockSpec(memory_space=pl.ANY)] * len(out_shape),
        scratch_shapes=[pltpu.VMEM((row_count, head_width), f32)] * 4
        + [pltpu.VMEM((row_count, 1), jnp.int32), pltpu.VMEM((1, row_count), jnp.int32)]
        + [wide_rows] * 6
        + [pltpu.VMEM((depth, row_count), bf16)]
        + [pltpu.VMEM((depth, inner), bf16)] * 3
        + [pltpu.VMEM((inner, depth), bf16)]
        + [pltpu.VMEM((depth, hidden_count), bf16)] * 2
        + [pltpu.VMEM((hidden_count, depth), bf16)]
        + [narrow, narrow, narrow, pltpu.VMEM((row_count, inner), f32), narrow]
        + [pltpu.VMEM((row_count, hidden_count), bf16)] * 3
        + [pltpu.VMEM((row_count, depth), f32)] * 2
        + [dma((2, 2)), dma((64,))]
        + extra,
        compiler_params=pltpu.CompilerParams(
            collective_id=1, has_side_effects=True, vmem_limit_bytes=62 * 1024 * 1024
        ),
        cost_estimate=pl.CostEstimate(
            flops=4 * row_count * depth * (6 * hidden_count + 4 * inner),
            bytes_accessed=64 << 20,
            transcendentals=0,
        ),
    )(*lengths, *arrays, *blocks)


def settle_kernel(count, *refs):
    sources, targets, held = refs[:count], refs[count : 2 * count], refs[2 * count : 3 * count]
    in_sems, out_sems = refs[3 * count :]

    def parts(k):
        rows = sources[k].shape[0]
        pieces = rows if len(sources[k].shape) == 3 else 1
        return [slice(i * rows // pieces, (i + 1) * rows // pieces) for i in range(pieces)]

    pieces = [(k, i, at) for k in range(count) for i, at in enumerate(parts(k))]
    loads = [
        pltpu.make_async_copy(sources[k].at[at], held[k].at[at], in_sems.at[k, i])
        for k, i, at in pieces
    ]
    stores = [
        pltpu.make_async_copy(held[k].at[at], targets[k].at[at], out_sems.at[k, i])
        for k, i, at in pieces
    ]
    for copy in loads:
        copy.start()
    for load, store in zip(loads, stores):
        load.wait()
        store.start()
    for store in stores:
        store.wait()


def settle(arrays):
    count = len(arrays)
    return pl.pallas_call(
        functools.partial(settle_kernel, count),
        out_shape=[jax.ShapeDtypeStruct(item.shape, item.dtype) for item in arrays],
        in_specs=[pl.BlockSpec(memory_space=pl.ANY)] * count,
        out_specs=[pl.BlockSpec(memory_space=pl.ANY)] * count,
        scratch_shapes=[pltpu.VMEM(item.shape, item.dtype) for item in arrays]
        + [pltpu.SemaphoreType.DMA((count, 2))] * 2,
        compiler_params=pltpu.CompilerParams(vmem_limit_bytes=62 * 1024 * 1024),
    )(*arrays)


def on_device(
    layer_in,
    short_lengths,
    long_lengths,
    norm1_gain,
    query_weight,
    key_weight,
    value_weight,
    lambda_param,
    sub_gain,
    out_weight,
    norm2_gain,
    gate_weight,
    up_weight,
    down_weight,
    out_cotangent,
):
    dp_count = lax.axis_size("dp")
    projections = [query_weight, key_weight, value_weight]
    depth, inner = query_weight.shape
    shapes = (depth, layer_in.shape[1], inner, gate_weight.shape[1], *sub_gain.shape)
    lengths = [short_lengths, long_lengths]
    blocks = [lambda_param, sub_gain, norm1_gain, norm2_gain]
    arrays = [layer_in, out_cotangent, *projections, out_weight]
    arrays += [gate_weight, up_weight, down_weight]
    parts = front_call(dp_count, lengths, arrays, blocks, shapes)
    pick = lambda at: [parts[at], parts[at + 16]]
    arrays = pick(0) + pick(1) + pick(2) + pick(9) + pick(10) + pick(11) + pick(7)
    arrays += pick(12) + pick(13) + pick(8)
    arrays += [layer_in, out_cotangent, out_weight, *projections]
    arrays += parts[3:7] + parts[19:23] + parts[14:16] + parts[30:32]
    (
        grad_down, grad_gate, grad_up, grad_out, grad_query, grad_key, grad_value, layer_out,
        grad_in, grad_norm1, grad_norm2, grad_lambda, grad_sub,
    ) = back_call(dp_count, lengths, arrays, blocks, shapes)
    (
        layer_out, grad_in, grad_down, grad_out, grad_query, grad_key, grad_value, grad_gate,
        grad_up, grad_lambda, grad_sub,
    ) = settle(
        [
            layer_out, grad_in, grad_down, grad_out, grad_query, grad_key, grad_value, grad_gate,
            grad_up, grad_lambda, grad_sub,
        ]
    )
    return (
        layer_out,
        grad_in,
        grad_norm1.reshape(-1),
        grad_query,
        grad_key,
        grad_value,
        grad_lambda,
        grad_sub,
        grad_out.T,
        grad_norm2.reshape(-1),
        grad_gate,
        grad_up,
        grad_down.T,
    )


def solution(mesh):
    return jax.shard_map(
        on_device,
        mesh=mesh,
        in_specs=(
            P(None, "dp", None),
            P("dp", None),
            P("dp", None),
            P(),
            P(None, "tensor"),
            P(None, "tensor"),
            P(None, "tensor"),
            P("tensor", None),
            P("tensor", None),
            P("tensor", None),
            P(),
            P(None, "tensor"),
            P(None, "tensor"),
            P("tensor", None),
            P(None, "dp", None),
        ),
        out_specs=(
            P(None, "dp", None),
            P(None, "dp", None),
            P("dp"),
            P("dp", "tensor"),
            P("dp", "tensor"),
            P("dp", "tensor"),
            P("tensor", "dp"),
            P("tensor", "dp"),
            P("tensor", "dp"),
            P("dp"),
            P("dp", "tensor"),
            P("dp", "tensor"),
            P("tensor", "dp"),
        ),
        check_vma=False,
    )
```
